32 devices in a mesh: fsdp: 8 (over z, y), sub: 4 (over x, core).
Axes of the slice: x: 2, y: 2, z: 4, core: 2. Of those that a mesh axis runs over, the one named last changes fastest.
Arguments:
- code_vectors: bfloat16 [32768, 32], P(('fsdp', 'sub')), may hold values from -6 to 6
- scale_ids: int32 [32768], P(('fsdp', 'sub')), may hold values from 0 to 9, as said below
- segment_ids: int32 [32768], P(('fsdp', 'sub')), may hold values from 0 to 1, as said below
- real_mask: int32 [32768], P(('fsdp', 'sub')), may hold values from 0 to 1, as said below
- labels: int32 [64], P(('fsdp', 'sub')), may hold values from 0 to 999
- targets: int32 [32768], P(('fsdp', 'sub')), may hold values from 0 to 4095
- loss_weight: int32 [32768], P(('fsdp', 'sub')), may hold values from 0 to 9, as said below
- tables: float32 [1024, 1042], P(('fsdp', 'sub')), may hold values from -10 to 10
- vectors: float32 [1024, 9], P(('fsdp', 'sub')), may hold values from -1.2 to 1.6
- ada_weight: float32 [1024, 6144], P(('fsdp', 'sub')), may hold values from -0.15625 to 0.15625
- qkv_weight: float32 [1024, 3072], P(('fsdp', 'sub')), may hold values from -0.3125 to 0.3125
- out_weight: float32 [1024, 1024], P(('fsdp', 'sub')), may hold values from -1.25 to 1.25
- up_weight: float32 [1024, 4096], P(('fsdp', 'sub')), may hold values from -0.3125 to 0.3125
- down_weight: float32 [4096, 1024], P(('fsdp', 'sub')), may hold values from -0.15625 to 0.15625
- head_weight: float32 [1024, 4096], P(('fsdp', 'sub')), may hold values from -0.3125 to 0.3125
- tables_moment: float32 [1024], P(('fsdp', 'sub')), may hold values from 5.79834e-09 to 2.319336e-08
- ada_moment: float32 [1024], P(('fsdp', 'sub')), may hold values from 5.79834e-09 to 2.319336e-08
- qkv_moment: float32 [1024], P(('fsdp', 'sub')), may hold values from 5.79834e-09 to 2.319336e-08
- out_moment: float32 [1024], P(('fsdp', 'sub')), may hold values from 5.79834e-09 to 2.319336e-08
- up_moment: float32 [1024], P(('fsdp', 'sub')), may hold values from 5.79834e-09 to 2.319336e-08
- down_moment: float32 [4096], P(('fsdp', 'sub')), may hold values from 5.79834e-09 to 2.319336e-08
- head_moment: float32 [1024], P(('fsdp', 'sub')), may hold values from 5.79834e-09 to 2.319336e-08
- vector_moment: float32 [1024, 9], P(('fsdp', 'sub')), may hold values from 5.79834e-09 to 2.319336e-08
- column_moment: float32 [20498], replicated, may hold values from 5.79834e-09 to 2.319336e-08
Outputs:
- loss_sum: float32 [], replicated
- weight_total: float32 [], replicated
- tables_grad: float32 [1024, 1042], P(('fsdp', 'sub'))
- tables_stat: float32 [1024], P(('fsdp', 'sub'))
- tables_next: float32 [1024, 1042], P(('fsdp', 'sub'))
- vectors_grad: float32 [1024, 9], P(('fsdp', 'sub'))
- vectors_stat: float32 [1024, 9], P(('fsdp', 'sub'))
- vectors_next: float32 [1024, 9], P(('fsdp', 'sub'))
- ada_grad: float32 [1024, 6144], P(('fsdp', 'sub'))
- ada_stat: float32 [1024], P(('fsdp', 'sub'))
- ada_next: float32 [1024, 6144], P(('fsdp', 'sub'))
- qkv_grad: float32 [1024, 3072], P(('fsdp', 'sub'))
- qkv_stat: float32 [1024], P(('fsdp', 'sub'))
- qkv_next: float32 [1024, 3072], P(('fsdp', 'sub'))
- out_grad: float32 [1024, 1024], P(('fsdp', 'sub'))
- out_stat: float32 [1024], P(('fsdp', 'sub'))
- out_next: float32 [1024, 1024], P(('fsdp', 'sub'))
- up_grad: float32 [1024, 4096], P(('fsdp', 'sub'))
- up_stat: float32 [1024], P(('fsdp', 'sub'))
- up_next: float32 [1024, 4096], P(('fsdp', 'sub'))
- down_grad: float32 [4096, 1024], P(('fsdp', 'sub'))
- down_stat: float32 [4096], P(('fsdp', 'sub'))
- down_next: float32 [4096, 1024], P(('fsdp', 'sub'))
- head_grad: float32 [1024, 4096], P(('fsdp', 'sub'))
- head_stat: float32 [1024], P(('fsdp', 'sub'))
- head_next: float32 [1024, 4096], P(('fsdp', 'sub'))
- column_stat: float32 [20498], replicated
- clip_spread: float32 [8], replicated
The draws below stay inside these ranges and needn't reach their ends.
Inputs may be any that keep to these rules, and one draw needn't show every extreme that they name: `scale_ids`: each row holds one whole item of 680 tokens and one item cut after fewer scales, in either order, then padding; scales count from 0 within each item, padding has scale 0. `segment_ids`: 0 for the first item of a row, 1 for the second and for padding. `real_mask`: padding only after both items. `loss_weight`: 0 exactly on padding.
All inputs are finite; a program needn't handle non-finite values.
Results may differ from the reference program's by a relative error of at most 0.0075.
The reference program's roundings to bfloat16 on the way count: a program that leaves them out, or rounds other values in their place, can miss the bound.
Values may be sent and summed in bfloat16 or wider, within the bound.
A program may use at most 512 MiB of HBM per device.

```python
import math
import jax
import jax.numpy as jnp
import numpy as np
from jax import lax

D = 1024
HEADS = 16
HEAD_DIM = 64
FF = 4096
CLASSES = 1000
CODES = 4096
CODE_DIM = 32
LEVELS = 10
ITEM = 680
TOK_DEV = 1024
STEP = 10
SUBS = 4
SPANS = 8
TOKENS = 32768
COLS = 20498
DEVICES = 32


SIDES = (1, 2, 3, 4, 5, 6, 8, 10, 13, 16)


def layout(key):
    level_ends = np.cumsum(np.array(SIDES[:LEVELS]) ** 2)
    spare_room = TOK_DEV - ITEM
    short_count = max(int(np.sum(level_ends <= spare_room)), 1)
    short_lengths = jnp.array(level_ends[:short_count].astype(np.int32))
    order_bits = jax.random.randint(jax.random.fold_in(key, 11), (DEVICES, 1), 0, 2)
    short_pick = jax.random.randint(jax.random.fold_in(key, 12), (DEVICES, 1), 0, short_count)
    short_len = jnp.take(short_lengths, short_pick)
    first_len = jnp.where(order_bits == 0, ITEM, short_len)
    second_len = jnp.where(order_bits == 0, short_len, ITEM)
    position = jnp.arange(TOK_DEV, dtype=jnp.int32)[None, :]
    in_second = position >= first_len
    local_pos = jnp.where(in_second, position - first_len, position)
    is_real = position < first_len + second_len
    level_starts = jnp.array(level_ends[:-1].astype(np.int32))
    levels = jnp.sum((local_pos[:, :, None] >= level_starts[None, None, :]).astype(jnp.int32), axis=-1)
    scales = jnp.where(is_real, levels, 0)
    return (scales.reshape(-1).astype(jnp.int32), in_second.astype(jnp.int32).reshape(-1), is_real.astype(jnp.int32).reshape(-1))


def draw_scale_ids(key, part):
    return layout(key)[0]


def draw_segment_ids(key, part):
    return layout(key)[1]


def draw_real_mask(key, part):
    return layout(key)[2]


def draw_loss_weight(key, part):
    real_rows = layout(key)[2].reshape(DEVICES, TOK_DEV)
    key = jax.random.fold_in(key, 5)
    device = jnp.arange(DEVICES, dtype=jnp.int32)[:, None]
    fsdp_index = device // SUBS
    sub_index = device % SUBS
    ceiling = 1 + 4 * fsdp_index // max(SPANS - 1, 1) + 4 * sub_index // max(SUBS - 1, 1)
    weight_draw = jax.random.randint(key, (DEVICES, TOK_DEV), 1, ceiling + 1)
    return jnp.where(real_rows == 1, weight_draw, 0).reshape(-1).astype(jnp.int32)


def rising(key, rows, columns, spread, ramp_top):
    row_ramp = 0.3 + (ramp_top - 0.3) * jnp.arange(rows, dtype=jnp.float32) / (rows - 1)
    noise_part = jnp.clip(jax.random.normal(key, (rows, columns), jnp.float32), -4.0, 4.0)
    return noise_part * row_ramp[:, None] * spread


def draw_tables(key, part):
    key = jax.random.fold_in(key, 20)
    ramp_top = 2.4
    column_scale = jnp.concatenate([jnp.ones((CLASSES,), jnp.float32), jnp.full((CODE_DIM,), CODE_DIM ** (-0.5), jnp.float32), jnp.full((LEVELS,), 0.5, jnp.float32)])
    return rising(key, D, CLASSES + CODE_DIM + LEVELS, 1.0, ramp_top) * column_scale[None, :]


def draw_vectors(key, part):
    key = jax.random.fold_in(key, 27)
    uniform_part = jax.random.uniform(key, (D, 9), jnp.float32)
    normal_part = jnp.clip(jax.random.normal(jax.random.fold_in(key, 1), (D, 9), jnp.float32), -4.0, 4.0)
    lower_ends = jnp.array([0.6, 0.6, 0.0, 0.0, 0.0, 0.0, 1.0, 1.0, 0.7], jnp.float32)
    upper_ends = jnp.array([1.2, 1.2, 0.0, 0.0, 0.0, 0.0, 1.6, 1.6, 1.5], jnp.float32)
    noise_scale = jnp.array([0.0, 0.0, 0.3, 0.3, 0.3, 0.3, 0.0, 0.0, 0.0], jnp.float32)
    return lower_ends + (upper_ends - lower_ends) * uniform_part + noise_scale * normal_part


def draw_ada_weight(key, part):
    key = jax.random.fold_in(key, 21)
    ramp_top = 2.4
    return rising(key, D, 6 * D, 0.5 * D ** (-0.5), ramp_top)


def draw_qkv_weight(key, part):
    key = jax.random.fold_in(key, 22)
    ramp_top = 2.4
    return rising(key, D, 3 * D, D ** (-0.5), ramp_top)


def draw_out_weight(key, part):
    key = jax.random.fold_in(key, 23)
    ramp_top = 2.4
    return rising(key, D, D, 4.0 * D ** (-0.5), ramp_top)


def draw_up_weight(key, part):
    key = jax.random.fold_in(key, 24)
    ramp_top = 2.4
    return rising(key, D, FF, D ** (-0.5), ramp_top)


def draw_down_weight(key, part):
    key = jax.random.fold_in(key, 25)
    ramp_top = 2.4
    return rising(key, FF, D, FF ** (-0.5), ramp_top)


def draw_head_weight(key, part):
    key = jax.random.fold_in(key, 26)
    ramp_top = 2.4
    return rising(key, D, CODES, D ** (-0.5), ramp_top)


def plant(drawn, rng, low, top_value):
    dims = drawn.shape
    index_at = [jax.random.randint(jax.random.fold_in(rng, axis), (), 0, dims[axis]) for axis in range(len(dims))]
    drawn = drawn.at[tuple(index_at)].set(low)
    longest = dims.index(max(dims))
    index_at[longest] = (index_at[longest] + 1) % dims[longest]
    return drawn.at[tuple(index_at)].set(top_value)


def steps_of(stream_key, shape, cuts, least, top_value):
    def one(dim, parts):
        steps = jax.random.uniform(jax.random.fold_in(jax.random.fold_in(stream_key, 6), dim), (parts,), jnp.float32, least / len(cuts), top_value / len(cuts))
        return jnp.repeat(jnp.exp(steps), shape[dim] // parts).reshape((-1,) + (1,) * (len(shape) - dim - 1))

    factor_of = one(*cuts[0])
    for cut in cuts[1:]:
        factor_of = factor_of * one(*cut)
    return factor_of


def scatter_about(stream_key, shape, width, most, shards=(), kind=jnp.bfloat16):
    level = steps_of(stream_key, shape, shards, -0.22, 0.18) if shards else 1.0
    values = jax.random.normal(stream_key, shape, jnp.float32) * width * level
    return jnp.minimum(jnp.maximum(values, -most), most).astype(kind)


def setup_inputs(seed: int = 0) -> dict:
    key_of = jax.random.split(jax.random.key(seed), 25)
    code_vectors = scatter_about(key_of[0], (TOKENS, CODE_DIM), 1.0, 6.0, ((0, 32),))
    scale_ids = draw_scale_ids(jax.random.fold_in(key_of[24], 71), 0)
    segment_ids = draw_segment_ids(jax.random.fold_in(key_of[24], 71), 0)
    real_mask = draw_real_mask(jax.random.fold_in(key_of[24], 71), 0)
    labels = plant(jax.random.randint(key_of[4], (2 * DEVICES,), 0, CLASSES), jax.random.fold_in(key_of[4], 1), 0, CLASSES - 1).astype(jnp.int32)
    targets = plant(jax.random.randint(key_of[5], (TOKENS,), 0, CODES), jax.random.fold_in(key_of[5], 1), 0, CODES - 1).astype(jnp.int32)
    loss_weight = draw_loss_weight(jax.random.fold_in(key_of[24], 71), 0)
    tables = draw_tables(jax.random.fold_in(key_of[24], 71), 0)
    vectors = draw_vectors(jax.random.fold_in(key_of[24], 71), 0)
    ada_weight = draw_ada_weight(jax.random.fold_in(key_of[24], 71), 0)
    qkv_weight = draw_qkv_weight(jax.random.fold_in(key_of[24], 71), 0)
    out_weight = draw_out_weight(jax.random.fold_in(key_of[24], 71), 0)
    up_weight = draw_up_weight(jax.random.fold_in(key_of[24], 71), 0)
    down_weight = draw_down_weight(jax.random.fold_in(key_of[24], 71), 0)
    head_weight = draw_head_weight(jax.random.fold_in(key_of[24], 71), 0)
    tables_moment = jnp.clip(jnp.exp(math.log(2.319336012135409e-08) - 1.3862944 * jax.random.uniform(key_of[15], (D,), jnp.float32) ** steps_of(key_of[15], (D,), ((0, 32),), -0.2, 0.2)), 5.798340030338522e-09, 2.319336012135409e-08)
    ada_moment = jnp.clip(jnp.exp(math.log(2.319336012135409e-08) - 1.3862944 * jax.random.uniform(key_of[16], (D,), jnp.float32) ** steps_of(key_of[16], (D,), ((0, 32),), -0.2, 0.2)), 5.798340030338522e-09, 2.319336012135409e-08)
    qkv_moment = jnp.clip(jnp.exp(math.log(2.319336012135409e-08) - 1.3862944 * jax.random.uniform(key_of[17], (D,), jnp.float32) ** steps_of(key_of[17], (D,), ((0, 32),), -0.2, 0.2)), 5.798340030338522e-09, 2.319336012135409e-08)
    out_moment = jnp.clip(jnp.exp(math.log(2.319336012135409e-08) - 1.3862944 * jax.random.uniform(key_of[18], (D,), jnp.float32) ** steps_of(key_of[18], (D,), ((0, 32),), -0.2, 0.2)), 5.798340030338522e-09, 2.319336012135409e-08)
    up_moment = jnp.clip(jnp.exp(math.log(2.319336012135409e-08) - 1.3862944 * jax.random.uniform(key_of[19], (D,), jnp.float32) ** steps_of(key_of[19], (D,), ((0, 32),), -0.2, 0.2)), 5.798340030338522e-09, 2.319336012135409e-08)
    down_moment = jnp.clip(jnp.exp(math.log(2.319336012135409e-08) - 1.3862944 * jax.random.uniform(key_of[20], (FF,), jnp.float32) ** steps_of(key_of[20], (FF,), ((0, 32),), -0.2, 0.2)), 5.798340030338522e-09, 2.319336012135409e-08)
    head_moment = jnp.clip(jnp.exp(math.log(2.319336012135409e-08) - 1.3862944 * jax.random.uniform(key_of[21], (D,), jnp.float32) ** steps_of(key_of[21], (D,), ((0, 32),), -0.2, 0.2)), 5.798340030338522e-09, 2.319336012135409e-08)
    vector_moment = jnp.clip(jnp.exp(math.log(2.319336012135409e-08) - 1.3862944 * jax.random.uniform(key_of[22], (D, 9), jnp.float32) ** steps_of(key_of[22], (D, 9), ((0, 32),), -0.2, 0.2)), 5.798340030338522e-09, 2.319336012135409e-08)
    column_moment = jnp.clip(jnp.exp(jax.random.uniform(key_of[23], (COLS,), jnp.float32, math.log(5.798340030338522e-09), math.log(2.319336012135409e-08))), 5.798340030338522e-09, 2.319336012135409e-08)
    return dict(code_vectors=code_vectors, scale_ids=scale_ids, segment_ids=segment_ids, real_mask=real_mask, labels=labels, targets=targets, loss_weight=loss_weight, tables=tables, vectors=vectors, ada_weight=ada_weight, qkv_weight=qkv_weight, out_weight=out_weight, up_weight=up_weight, down_weight=down_weight, head_weight=head_weight, tables_moment=tables_moment, ada_moment=ada_moment, qkv_moment=qkv_moment, out_moment=out_moment, up_moment=up_moment, down_moment=down_moment, head_moment=head_moment, vector_moment=vector_moment, column_moment=column_moment)


TINY_SQUARE = 1e-30
SCALE_FLOOR = 0.001
STEP_RATE = 1.0
CLIP_LIMIT = 1.0
NORM_EPSILON = 1e-06
MASK_VALUE = -1000000000.0

@jax.custom_vjp
def low(v):
    return lax.optimization_barrier(v.astype(jnp.bfloat16)).astype(jnp.float32)

@jax.custom_vjp
def low_back(v):
    return v

def low_keep(v):
    return (low(v), None)

def low_pass(kept, grad):
    return (grad,)

def back_keep(v):
    return (v, None)

def back_low(kept, grad):
    return (low(grad),)
low.defvjp(low_keep, low_pass)
low_back.defvjp(back_keep, back_low)

def matmul(left_side, right_side):
    return jnp.dot(left_side, right_side, precision=lax.Precision.HIGHEST, preferred_element_type=jnp.float32)

def layer_norm(values):
    center = values - lax.optimization_barrier(jnp.mean(values, axis=-1, keepdims=True))
    return center * lax.rsqrt(lax.optimization_barrier(jnp.mean(center * center, axis=-1, keepdims=True)) + NORM_EPSILON)

def head_norm(values, gain_vector):
    shaped = values.reshape(values.shape[0], HEADS, HEAD_DIM)
    normed = shaped * lax.rsqrt(lax.optimization_barrier(jnp.mean(shaped * shaped, axis=-1, keepdims=True)) + NORM_EPSILON)
    return normed * gain_vector.reshape(1, HEADS, HEAD_DIM)

def attention_mask(scale_row, segment_row, real_row):
    same_item = segment_row[:, None] == segment_row[None, :]
    earlier = scale_row[None, :] <= scale_row[:, None]
    places = jnp.arange(scale_row.shape[0])
    usable = (real_row[None, :] == 1) | (places[:, None] == places[None, :])
    return same_item & earlier & usable

def row_loss(params, row_inputs):
    tables, vectors, ada_weight, qkv_weight, out_weight, up_weight, down_weight, head_weight = params
    code_row, scale_row, segment_row, real_row, label_pair, target_row, weight_row = row_inputs
    level_hot = (scale_row[:, None] == jnp.arange(LEVELS)[None, :]).astype(jnp.float32)
    embedded = matmul(code_row, tables[:, CLASSES:CLASSES + CODE_DIM].T) + matmul(level_hot, tables[:, CLASSES + CODE_DIM:].T)
    label_hot = (label_pair[:, None] == jnp.arange(CLASSES)[None, :]).astype(jnp.float32)
    class_cond = matmul(label_hot, tables[:, :CLASSES].T)
    activated = low(jax.nn.silu(class_cond))
    modulation = low_back(matmul(activated, ada_weight)) + vectors[:, :6].T.reshape(1, 6 * D)
    segment_hot = (segment_row[:, None] == jnp.arange(2)[None, :]).astype(jnp.float32)
    token_mod = matmul(segment_hot, modulation)
    gamma_one, gamma_two, scale_one, scale_two, shift_one, shift_two = jnp.split(token_mod, 6, axis=1)
    normed = low(layer_norm(embedded) * (1.0 + scale_one) + shift_one)
    projected = low_back(matmul(normed, qkv_weight))
    queries = low(head_norm(projected[:, :D], vectors[:, 6]))
    keys_all = low(head_norm(projected[:, D:2 * D], vectors[:, 7]))
    values_all = low(projected[:, 2 * D:].reshape(-1, HEADS, HEAD_DIM))
    scores = low_back(jnp.einsum('qhd,khd->hqk', queries, keys_all, precision=lax.Precision.HIGHEST) * HEAD_DIM ** (-0.5))
    allowed = attention_mask(scale_row, segment_row, real_row)
    scores = jnp.where(allowed[None], scores, MASK_VALUE)
    exponent = jnp.exp(scores - lax.optimization_barrier(jnp.max(scores, axis=-1, keepdims=True)))
    probabilities = exponent / lax.optimization_barrier(jnp.sum(exponent, axis=-1, keepdims=True))
    mixed_heads = jnp.einsum('hqk,khd->qhd', low(probabilities), values_all, precision=lax.Precision.HIGHEST).reshape(-1, D)
    mixed_heads = low(low_back(mixed_heads))
    attended = low_back(matmul(mixed_heads, out_weight))
    residual_one = embedded + gamma_one * attended
    normed_two = low(layer_norm(residual_one) * (1.0 + scale_two) + shift_two)
    hidden_pre = low_back(matmul(normed_two, up_weight))
    hidden_act = low(jax.nn.gelu(hidden_pre, approximate=True))
    branch = low_back(matmul(hidden_act, down_weight))
    residual_two = residual_one + gamma_two * branch
    final_normed = low(layer_norm(residual_two) * vectors[:, 8])
    logits = low_back(matmul(final_normed, head_weight))
    logit_peak = lax.optimization_barrier(jnp.max(logits, axis=-1))
    log_total = logit_peak + jnp.log(lax.optimization_barrier(jnp.sum(jnp.exp(logits - logit_peak[:, None]), axis=-1)))
    picked = jnp.take_along_axis(logits, target_row[:, None].astype(jnp.int32), axis=1)[:, 0]
    return jnp.sum(weight_row.astype(jnp.float32) * (log_total - picked))

def reference(code_vectors, scale_ids, segment_ids, real_mask, labels, targets, loss_weight, tables, vectors, ada_weight, qkv_weight, out_weight, up_weight, down_weight, head_weight, tables_moment, ada_moment, qkv_moment, out_moment, up_moment, down_moment, head_moment, vector_moment, column_moment):
    rows_count = TOKENS // TOK_DEV
    batched = (code_vectors.astype(jnp.float32).reshape(rows_count, TOK_DEV, CODE_DIM), scale_ids.reshape(rows_count, TOK_DEV), segment_ids.reshape(rows_count, TOK_DEV), real_mask.reshape(rows_count, TOK_DEV), labels.reshape(rows_count, 2), targets.reshape(rows_count, TOK_DEV), loss_weight.reshape(rows_count, TOK_DEV))
    weight_total = jnp.sum(loss_weight.astype(jnp.float32))
    masters = (tables, vectors, ada_weight, qkv_weight, out_weight, up_weight, down_weight, head_weight)
    checked = jax.checkpoint(row_loss)

    def objective(parameters):
        rounded = tuple((low(parameter) for parameter in parameters))

        def scan_body(running, row_inputs):
            return (running + checked(rounded, row_inputs), None)
        summed, _ = lax.scan(scan_body, jnp.zeros((), jnp.float32), batched)
        return (summed / weight_total, summed)
    mean_loss, pullback, loss_sum = jax.vjp(objective, masters, has_aux=True)
    gradients = pullback(jnp.ones((), jnp.float32))[0]
    second_decay = 1.0 - STEP ** (-0.8)
    factored_index = (0, 2, 3, 4, 5, 6, 7)
    factored_moments = (tables_moment, ada_moment, qkv_moment, out_moment, up_moment, down_moment, head_moment)
    updates = [None] * 8
    moments_new = [None] * 8
    column_parts = []
    offset = 0
    for position, moment in zip(factored_index, factored_moments):
        gradient = gradients[position]
        squared = gradient * gradient + TINY_SQUARE
        rows_new = second_decay * moment + (1.0 - second_decay) * lax.optimization_barrier(jnp.mean(squared, axis=1))
        column_count = gradient.shape[1]
        cols_new = second_decay * column_moment[offset:offset + column_count] + (1.0 - second_decay) * lax.optimization_barrier(jnp.mean(squared, axis=0))
        offset += column_count
        estimate = rows_new[:, None] * cols_new[None, :] / jnp.mean(rows_new)
        updates[position] = gradient * lax.rsqrt(estimate)
        moments_new[position] = rows_new
        column_parts.append(cols_new)
    vector_new = second_decay * vector_moment + (1.0 - second_decay) * (gradients[1] * gradients[1] + TINY_SQUARE)
    updates[1] = gradients[1] * lax.rsqrt(vector_new)
    moments_new[1] = vector_new
    next_weights = []
    spreads = []
    for master, update in zip(masters, updates):
        spread = jnp.sqrt(jnp.mean(update * update))
        step_scale = jnp.maximum(SCALE_FLOOR, jnp.sqrt(jnp.mean(master * master)))
        next_weights.append(master - STEP_RATE * step_scale * (update / jnp.maximum(1.0, spread / CLIP_LIMIT)))
        spreads.append(spread)
    column_stat = jnp.concatenate(column_parts)
    clip_spread = jnp.stack(spreads)
    return (loss_sum, weight_total, gradients[0], moments_new[0], next_weights[0], gradients[1], moments_new[1], next_weights[1], gradients[2], moments_new[2], next_weights[2], gradients[3], moments_new[3], next_weights[3], gradients[4], moments_new[4], next_weights[4], gradients[5], moments_new[5], next_weights[5], gradients[6], moments_new[6], next_weights[6], gradients[7], moments_new[7], next_weights[7], column_stat, clip_spread)
```

```python
import math
from functools import partial

import jax
import jax.numpy as jnp
from jax import lax
from jax.experimental import pallas as pl
from jax.experimental.pallas import tpu as pltpu
from jax.sharding import PartitionSpec as P

D = 1024
HEADS = 16
HEAD_DIM = 64
CLASSES = 1000
CODES = 4096
CODE_DIM = 32
LEVELS = 10
STEP = 10


TINY_SQUARE = 1e-30
SCALE_FLOOR = 0.001
STEP_RATE = 1.0
CLIP_LIMIT = 1.0
NORM_EPSILON = 1e-06
MASK_VALUE = -1000000000.0

AXES = ("fsdp", "sub")
MESH = pl.DeviceIdType.MESH
ANY = pl.BlockSpec(memory_space=pl.ANY)
WHOLE = pl.BlockSpec(memory_space=pltpu.VMEM)
FIVE = (2, 2, 2, 2, 2)
DIMS = ("w", "u", "y", "x", "c")
SCATTER_ORDERS = (("c", "x", "y", "w", "u"), ("c", "y", "x", "w", "u"))
GATHER_ORDERS = (("u", "w", "y", "x", "c"), ("u", "w", "x", "y", "c"))
SCORE_SCALE = HEAD_DIM ** (-0.5)
EXP_SCALE = SCORE_SCALE * math.log2(math.e)
VMEM_GRANT = 58 * 1024 * 1024


def bfloat_product(left_side, right_side):
    return jnp.dot(left_side, right_side, preferred_element_type=jnp.float32)


class Place:
    def __init__(self):
        fsdp, sub = lax.axis_index("fsdp"), lax.axis_index("sub")
        self.bit = {
            "c": lax.rem(sub, 2),
            "x": lax.div(sub, 2),
            "y": lax.rem(fsdp, 2),
            "u": lax.rem(lax.div(fsdp, 2), 2),
            "w": lax.div(fsdp, 4),
        }
        bit = self.bit
        self.partner = {
            "c": (fsdp, sub + 1 - 2 * bit["c"]),
            "x": (fsdp, sub + 2 - 4 * bit["x"]),
            "y": (fsdp + 1 - 2 * bit["y"], sub),
            "u": (fsdp + 2 - 4 * bit["u"], sub),
            "w": (fsdp + 4 - 8 * bit["w"], sub),
        }

    def meet(self):
        barrier = pltpu.get_barrier_semaphore()
        for dim in DIMS:
            pl.semaphore_signal(
                barrier, inc=1, device_id=self.partner[dim], device_id_type=MESH
            )
        pl.semaphore_wait(barrier, 5)

    def send(self, src, dst, send_sem, recv_sem, dim):
        return pltpu.make_async_remote_copy(
            src_ref=src,
            dst_ref=dst,
            send_sem=send_sem,
            recv_sem=recv_sem,
            device_id=self.partner[dim],
            device_id_type=MESH,
        )


def when_in(index, low, high, body):
    if isinstance(index, int):
        if low <= index < high:
            body()
    else:
        pl.when((index >= low) & (index < high))(body)


class Gather:
    def __init__(self, place, groups, sends, recvs, local_sems):
        self.place, self.groups = place, groups
        self.sends, self.recvs, self.local_sems = sends, recvs, local_sems

    @staticmethod
    def scratch():
        dma = pltpu.SemaphoreType.DMA
        return [dma((5, 2, 2)), dma((5, 2, 2)), dma((2, 2))]

    def region(self, stage, parity):
        done = GATHER_ORDERS[parity][:stage]
        return tuple(slice(None) if d in done else self.place.bit[d] for d in DIMS)

    def copy(self, group, j, stage, parity, slot):
        _, _, own, full = group
        ref = full(j, parity, self.region(stage, parity))
        return self.place.send(
            own(j, parity) if stage == 0 else ref,
            ref,
            self.sends.at[stage, parity, slot],
            self.recvs.at[stage, parity, slot],
            GATHER_ORDERS[parity][stage],
        )

    def local(self, group, j, parity, slot):
        _, _, own, full = group
        return pltpu.make_async_copy(
            own(j, parity), full(j, parity, self.region(0, parity)), self.local_sems.at[parity, slot]
        )

    def step(self, t):
        for stage in reversed(range(6)):
            j = t - stage
            for group in self.groups:

                def body(group=group, stage=stage, j=j):
                    slot = lax.rem(j, 2)
                    for parity in range(2):
                        if stage == 0:
                            self.local(group, j, parity, slot).start()
                        if stage == 1:
                            self.local(group, j, parity, slot).wait()
                        if stage >= 1:
                            self.copy(group, j, stage - 1, parity, slot).wait()
                        if stage < 5:
                            self.copy(group, j, stage, parity, slot).start()

                when_in(j, group[0], group[1], body)


class Scatter:
    def __init__(self, place, groups, store, scratch):
        self.place, self.groups, self.store = place, groups, store
        self.keep = scratch[0]
        self.land = scratch[1:6]
        self.sums = (None,) + tuple(scratch[6:10])
        self.sends, self.recvs, self.keep_sems = scratch[10:13]
        self.first, self.end = groups[0][0], groups[-1][1]

    @staticmethod
    def scratch(piece, kind):
        dma = pltpu.SemaphoreType.DMA
        return (
            [pltpu.VMEM((2,) + (2,) * 4 + piece, kind)]
            + [pltpu.VMEM((2, 2) + (2,) * (4 - k) + piece, kind) for k in range(5)]
            + [pltpu.VMEM((2,) + (2,) * (5 - k) + piece, kind) for k in range(1, 5)]
            + [dma((5, 2, 2)), dma((5, 2, 2)), dma((2,))]
        )

    def half(self, stage, parity, other):
        order = SCATTER_ORDERS[parity]
        left = [d for d in DIMS if d not in order[:stage]]
        bit = self.place.bit[order[stage]]
        value = 1 - bit if other else bit
        return (parity,) + tuple(value if d == order[stage] else slice(None) for d in left)

    def copy(self, stage, parity, slot, source=None):
        if source is None:
            if stage == 0:
                source = self.keep.at[parity]
            else:
                source = self.sums[stage].at[self.half(stage, parity, True)]
        return self.place.send(
            source,
            self.land[stage].at[slot, parity],
            self.sends.at[stage, parity, slot],
            self.recvs.at[stage, parity, slot],
            SCATTER_ORDERS[parity][stage],
        )

    def step(self, t):
        for stage in reversed(range(6)):
            j = t - stage

            def body(stage=stage, j=j):
                slot = lax.rem(j, 2)
                for parity in range(2):
                    if stage >= 1:
                        before = stage - 1
                        if before == 0:
                            pltpu.make_async_copy(
                                self.keep.at[parity], self.keep.at[parity], self.keep_sems.at[parity]
                            ).wait()
                        self.copy(before, parity, slot).wait()
                        if before == 0:
                            mine = self.keep[parity]
                        else:
                            mine = self.sums[before][self.half(before, parity, False)]
                        total = mine.astype(jnp.float32) + self.land[before][slot, parity].astype(
                            jnp.float32
                        )
                        if stage < 5:
                            self.sums[stage][parity] = total.astype(self.keep.dtype)
                        else:
                            self.store(j, parity, total)
                    if 1 <= stage < 5:
                        self.copy(stage, parity, slot).start()

            if stage == 0:
                for low, high, source in self.groups:

                    def begin(source=source, j=j):
                        slot = lax.rem(j, 2)
                        core = self.place.bit["c"]
                        for parity in range(2):
                            self.copy(0, parity, slot, source(j, parity, 1 - core)).start()
                            pltpu.make_async_copy(
                                source(j, parity, core), self.keep.at[parity], self.keep_sems.at[parity]
                            ).start()

                    when_in(j, low, high, begin)
            else:
                when_in(j, self.first, self.end, body)


def params(collective_id, **more):
    return pltpu.CompilerParams(
        collective_id=collective_id, has_side_effects=True, vmem_limit_bytes=VMEM_GRANT, **more
    )


def columns(start, size):
    return pl.ds(pl.multiple_of(start, 128), size)


def small_gather_kernel(rows_ref, tags_ref, rows_full, tags_full, *sems):
    place = Place()
    place.meet()
    gather = Gather(
        place,
        [(0, 1, lambda j, p: (rows_ref, tags_ref)[p], lambda j, p, r: (rows_full, tags_full)[p].at[r])],
        *sems,
    )
    for t in range(6):
        gather.step(t)


def small_gather(rows, tags):
    return pl.pallas_call(
        small_gather_kernel,
        out_shape=(
            jax.ShapeDtypeStruct(FIVE + rows.shape, rows.dtype),
            jax.ShapeDtypeStruct(FIVE + tags.shape, tags.dtype),
        ),
        in_specs=[WHOLE, WHOLE],
        out_specs=(WHOLE, WHOLE),
        scratch_shapes=Gather.scratch(),
        compiler_params=params(0),
        name="small_gather",
    )(rows, tags)


def first_kernel(part_ref, own_ref, mod_ref, full_ref, *scratch):
    place = Place()
    place.meet()
    rows = part_ref.shape[5] // 2
    width = 256

    def store(j, parity, total):
        mod_ref[pl.ds(parity * rows, rows)] = total

    scatter = Scatter(
        place,
        [(0, 1, lambda j, p, core: part_ref.at[:, :, :, :, core, pl.ds(p * rows, rows)])],
        store,
        scratch[:13],
    )
    pairs = own_ref.shape[1] // (2 * width)
    gather = Gather(
        place,
        [
            (
                0,
                pairs,
                lambda j, p: own_ref.at[:, columns((2 * j + p) * width, width)],
                lambda j, p, r: full_ref.at[r + (slice(None), columns((2 * j + p) * width, width))],
            )
        ],
        *scratch[13:],
    )
    for t in range(pairs + 5):
        scatter.step(t)
        gather.step(t)


def first_exchange(part, own):
    return pl.pallas_call(
        first_kernel,
        out_shape=(
            jax.ShapeDtypeStruct(part.shape[5:], jnp.float32),
            jax.ShapeDtypeStruct(FIVE + own.shape, own.dtype),
        ),
        in_specs=[ANY, ANY],
        out_specs=(WHOLE, ANY),
        scratch_shapes=Scatter.scratch((part.shape[5] // 2, 128), jnp.float32) + Gather.scratch(),
        compiler_params=params(1),
        name="modulation_scatter_qkv_gather",
    )(part, own)


def head_mean(values):
    low_lane = lax.broadcasted_iota(jnp.int32, values.shape, 1) < HEAD_DIM
    low_sum = jnp.sum(jnp.where(low_lane, values, 0.0), axis=1, keepdims=True)
    high_sum = jnp.sum(jnp.where(low_lane, 0.0, values), axis=1, keepdims=True)
    return jnp.where(low_lane, low_sum, high_sum) * (1.0 / HEAD_DIM)


def of_head(values, head):
    low_lane = lax.broadcasted_iota(jnp.int32, values.shape, 1) < HEAD_DIM
    zero = jnp.zeros_like(values)
    return jnp.where(low_lane, values, zero) if head == 0 else jnp.where(low_lane, zero, values)


def dot_last(left, right):
    return lax.dot_general(left, right, (((1,), (1,)), ((), ())), preferred_element_type=jnp.float32)


def dot_first(left, right):
    return lax.dot_general(left, right, (((0,), (0,)), ((), ())), preferred_element_type=jnp.float32)


def dot_plain(left, right):
    return lax.dot_general(left, right, (((1,), (0,)), ((), ())), preferred_element_type=jnp.float32)


UNITS = 4


def normed_head(raw, gain):
    return (raw * lax.rsqrt(head_mean(raw * raw) + NORM_EPSILON) * gain).astype(jnp.bfloat16)


def attend_kernel(linked, q_ref, k_ref, v_ref, gain_ref, bias_ref, *refs):
    if linked:
        out_own, down_own, mixed_ref, out_full, down_full, qn, kn, vn = refs[:8]
        sems = refs[8:]
        place = Place()
        width = 128
        split = out_own.shape[1] // (2 * width)
        depth = out_own.shape[0]
        parts = down_own.shape[0] // depth

        def spread(j):
            return lax.div(j - split, split), lax.rem(j - split, split)

        def down_source(j, p):
            part, column = spread(j)
            return down_own.at[
                pl.ds(pl.multiple_of(part * depth, depth), depth), columns((2 * column + p) * width, width)
            ]

        def down_target(j, p, r):
            part, column = spread(j)
            return down_full.at[r + (part, slice(None), columns((2 * column + p) * width, width))]

        gather = Gather(
            place,
            [
                (
                    0,
                    split,
                    lambda j, p: out_own.at[:, columns((2 * j + p) * width, width)],
                    lambda j, p, r: out_full.at[r + (slice(None), columns((2 * j + p) * width, width))],
                ),
                (split, split + split * parts, down_source, down_target),
            ],
            *sems,
        )
        assert split + split * parts + 5 <= UNITS * (HEADS // 2)
        pl.when(pl.program_id(0) == 0)(place.meet)
    else:
        mixed_ref, qn, kn, vn = refs
    qn[...] = normed_head(q_ref[...], gain_ref[0:1])
    kn[...] = normed_head(k_ref[...], gain_ref[1:2])
    vn[...] = v_ref[...].astype(jnp.bfloat16)
    size = q_ref.shape[0] // UNITS

    @pl.loop(0, UNITS)
    def unit(u):
        if linked:
            gather.step(pl.program_id(0) * UNITS + u)
        rows = pl.ds(pl.multiple_of(u * size, size), size)
        both = []
        for head in range(2):
            scores = dot_last(of_head(qn[rows], head), kn[...]) * EXP_SCALE + bias_ref[rows]
            raised = jnp.exp2(scores)
            share = 1.0 / jnp.sum(raised, axis=1, keepdims=True)
            both.append(dot_plain((raised * share).astype(jnp.bfloat16), vn[...]))
        low_lane = lax.broadcasted_iota(jnp.int32, both[0].shape, 1) < HEAD_DIM
        mixed_ref[rows] = jnp.where(low_lane, both[0], both[1]).astype(jnp.bfloat16)


def attend(projected, gains, bias, out_own=None, down_own=None):
    tokens = projected.shape[0]
    pair = pl.BlockSpec((tokens, 128), lambda i: (0, i))
    specs = [
        pair,
        pl.BlockSpec((tokens, 128), lambda i: (0, i + 8)),
        pl.BlockSpec((tokens, 128), lambda i: (0, i + 16)),
        pl.BlockSpec((8, 128), lambda i: (0, i)),
        pl.BlockSpec((tokens, tokens), lambda i: (0, 0), pipeline_mode=pl.Buffered(1)),
    ]
    outs = [jax.ShapeDtypeStruct((tokens, D), jnp.bfloat16)]
    out_specs = [pair]
    scratch = [pltpu.VMEM((tokens, 128), jnp.bfloat16)] * 3
    operands = [projected, projected, projected, gains, bias]
    linked = out_own is not None
    if linked:
        depth = out_own.shape[0]
        specs += [ANY, ANY]
        operands += [out_own, down_own]
        outs += [
            jax.ShapeDtypeStruct(FIVE + out_own.shape, jnp.bfloat16),
            jax.ShapeDtypeStruct(FIVE + (down_own.shape[0] // depth, depth, D), jnp.bfloat16),
        ]
        out_specs += [ANY, ANY]
        scratch = scratch + Gather.scratch()
    return pl.pallas_call(
        partial(attend_kernel, linked),
        grid=(HEADS // 2,),
        out_shape=tuple(outs),
        in_specs=specs,
        out_specs=tuple(out_specs),
        scratch_shapes=scratch,
        compiler_params=params(2) if linked else pltpu.CompilerParams(vmem_limit_bytes=VMEM_GRANT),
        name="attention_forward",
    )(*operands)


def attend_back_kernel(linked, q_ref, k_ref, v_ref, m_ref, gain_ref, bias_ref, *refs):
    if linked:
        head_ref, up_ref, down_ref, grad_ref, gain_grad_ref, done_ref = refs[:6]
        qn, kn, vn, dq, dk, dv = refs[6:12]
        place = Place()
        width = 256
        wide = up_ref.shape[6] // (2 * width)
        narrow = down_ref.shape[7] // (2 * width)
        parts = down_ref.shape[5]

        def columns_of(ref, first):
            return lambda j, p, core: ref.at[
                :, :, :, :, core, :, columns((2 * (j - first) + p) * width, width)
            ]

        def down_source(j, p, core):
            spread = j - 2 * wide
            part, column = lax.div(spread, narrow), lax.rem(spread, narrow)
            return down_ref.at[:, :, :, :, core, part, :, columns((2 * column + p) * width, width)]

        def store(j, parity, total):
            done_ref[j, :, parity * width : (parity + 1) * width] = total

        pairs = 2 * wide + parts * narrow
        scatter = Scatter(
            place,
            [
                (0, wide, columns_of(head_ref, 0)),
                (wide, 2 * wide, columns_of(up_ref, wide)),
                (2 * wide, pairs, down_source),
            ],
            store,
            refs[12:],
        )
        assert pairs + 5 <= UNITS * (HEADS // 2)
        pl.when(pl.program_id(0) == 0)(place.meet)
    else:
        grad_ref, gain_grad_ref = refs[:2]
        qn, kn, vn, dq, dk, dv = refs[2:]
    qn[...] = normed_head(q_ref[...], gain_ref[0:1])
    kn[...] = normed_head(k_ref[...], gain_ref[1:2])
    vn[...] = v_ref[...].astype(jnp.bfloat16)
    dk[...] = jnp.zeros_like(dk)
    dv[...] = jnp.zeros_like(dv)
    size = q_ref.shape[0] // UNITS

    @pl.loop(0, UNITS)
    def unit(u):
        if linked:
            scatter.step(pl.program_id(0) * UNITS + u)
        rows = pl.ds(pl.multiple_of(u * size, size), size)
        query_sum = None
        for head in range(2):
            query = of_head(qn[rows], head)
            mixed = of_head(m_ref[rows], head)
            raised = jnp.exp2(dot_last(kn[...], query) * EXP_SCALE + bias_ref[:, rows])
            probs = raised * (1.0 / jnp.sum(raised, axis=0, keepdims=True))
            prob_grad = dot_last(vn[...], mixed)
            center = jnp.sum(probs * prob_grad, axis=0, keepdims=True)
            score_grad = (probs * (prob_grad - center)).astype(jnp.bfloat16)
            dk[...] += dot_plain(score_grad, query)
            dv[...] += dot_plain(probs.astype(jnp.bfloat16), mixed)
            part = dot_first(score_grad, of_head(kn[...], head))
            query_sum = part if query_sum is None else query_sum + part
        dq[rows] = query_sum

    gain_rows = []
    for place_at, raw_ref, grad in ((0, q_ref, dq), (1, k_ref, dk)):
        raw = raw_ref[...]
        normed_grad = grad[...] * SCORE_SCALE
        rate = lax.rsqrt(head_mean(raw * raw) + NORM_EPSILON)
        scaled = gain_ref[place_at : place_at + 1] * normed_grad
        back = rate * scaled - raw * (rate * rate * rate) * head_mean(raw * scaled)
        grad_ref[place_at] = back.astype(jnp.bfloat16)
        gain_rows.append(jnp.sum(normed_grad * raw * rate, axis=0, keepdims=True))
    grad_ref[2] = dv[...].astype(jnp.bfloat16)
    gain_grad_ref[...] = jnp.concatenate(gain_rows + [jnp.zeros((6, 128), jnp.float32)], axis=0)


def attend_back(projected, mixed_grad, gains, bias, head_grad=None, up_grad=None, down_grad=None):
    tokens = projected.shape[0]
    pair = pl.BlockSpec((tokens, 128), lambda i: (0, i))
    specs = [
        pair,
        pl.BlockSpec((tokens, 128), lambda i: (0, i + 8)),
        pl.BlockSpec((tokens, 128), lambda i: (0, i + 16)),
        pair,
        pl.BlockSpec((8, 128), lambda i: (0, i)),
        pl.BlockSpec((tokens, tokens), lambda i: (0, 0), pipeline_mode=pl.Buffered(1)),
    ]
    outs = [
        jax.ShapeDtypeStruct((3, tokens, D), jnp.bfloat16),
        jax.ShapeDtypeStruct((8, D), jnp.float32),
    ]
    out_specs = [
        pl.BlockSpec((3, tokens, 128), lambda i: (0, 0, i)),
        pl.BlockSpec((8, 128), lambda i: (0, i)),
    ]
    scratch = [pltpu.VMEM((tokens, 128), jnp.bfloat16)] * 3 + [
        pltpu.VMEM((tokens, 128), jnp.float32)
    ] * 3
    operands = [projected, projected, projected, mixed_grad, gains, bias]
    linked = head_grad is not None
    if linked:
        depth = head_grad.shape[5]
        specs += [ANY, ANY, ANY]
        operands += [head_grad, up_grad, down_grad]
        pairs = (head_grad.shape[6] + up_grad.shape[6] + down_grad.shape[5] * down_grad.shape[7]) // 512
        outs += [jax.ShapeDtypeStruct((pairs, depth, 512), jnp.float32)]
        out_specs += [WHOLE]
        scratch = scratch + Scatter.scratch((depth, 256), jnp.bfloat16)
    return pl.pallas_call(
        partial(attend_back_kernel, linked),
        grid=(HEADS // 2,),
        out_shape=tuple(outs),
        in_specs=specs,
        out_specs=tuple(out_specs),
        scratch_shapes=scratch,
        compiler_params=params(3) if linked else pltpu.CompilerParams(vmem_limit_bytes=VMEM_GRANT),
        name="attention_backward",
    )(*operands)


def last_kernel(qkv_ref, out_ref, small_ref, mod_ref, done_ref, small_done, mod_full, *scratch):
    place = Place()
    place.meet()
    width = 256
    wide = qkv_ref.shape[6] // (2 * width)
    narrow = out_ref.shape[6] // (2 * width)

    def columns_of(ref, first):
        return lambda j, p, core: ref.at[
            :, :, :, :, core, :, columns((2 * (j - first) + p) * width, width)
        ]

    def store(j, parity, total):
        done_ref[j, :, parity * width : (parity + 1) * width] = total

    pairs = wide + narrow
    scatter = Scatter(
        place,
        [(0, wide, columns_of(qkv_ref, 0)), (wide, pairs, columns_of(out_ref, wide))],
        store,
        scratch[:13],
    )
    half = small_ref.shape[5] // 2

    def small_store(j, parity, total):
        small_done[pl.ds(parity * half, half)] = total

    small = Scatter(
        place,
        [(0, 1, lambda j, p, core: small_ref.at[:, :, :, :, core, pl.ds(p * half, half)])],
        small_store,
        scratch[13:26],
    )
    rows = mod_ref.shape[0] // 2
    gather = Gather(
        place,
        [
            (
                0,
                1,
                lambda j, p: mod_ref.at[pl.ds(p * rows, rows)],
                lambda j, p, r: mod_full.at[r + (pl.ds(p * rows, rows),)],
            )
        ],
        *scratch[26:],
    )
    for t in range(6):
        gather.step(t)
        small.step(t)
        scatter.step(t)

    @pl.loop(6, pairs + 5)
    def later(t):
        scatter.step(t)


def last_exchange(qkv_grad, out_grad, small, modulation):
    depth = qkv_grad.shape[5]
    pairs = (qkv_grad.shape[6] + out_grad.shape[6]) // 512
    return pl.pallas_call(
        last_kernel,
        out_shape=(
            jax.ShapeDtypeStruct((pairs, depth, 512), jnp.float32),
            jax.ShapeDtypeStruct(small.shape[5:], jnp.float32),
            jax.ShapeDtypeStruct(FIVE + modulation.shape, modulation.dtype),
        ),
        in_specs=[ANY, ANY, ANY, ANY],
        out_specs=(WHOLE, WHOLE, ANY),
        scratch_shapes=Scatter.scratch((depth, 256), jnp.bfloat16)
        + Scatter.scratch((small.shape[5] // 2, 128), jnp.float32)
        + Gather.scratch(),
        compiler_params=params(4),
        name="last_scatter",
    )(qkv_grad, out_grad, small, modulation)


def total_kernel(in_ref, out_ref, sums, land, sends, recvs):
    place = Place()
    place.meet()
    sums[0] = in_ref[...]
    for stage, dim in enumerate(DIMS):
        copy = place.send(
            sums.at[stage], land.at[stage], sends.at[stage], recvs.at[stage], dim
        )
        copy.start()
        copy.wait()
        sums[stage + 1] = sums[stage] + land[stage]
    out_ref[...] = sums[5]


def total(values, collective_id):
    if not linked_mesh():
        return lax.psum(values, AXES)
    size = values.shape[0]
    rows = -(-size // 1024) * 8
    flat = jnp.pad(values, (0, rows * 128 - size)).reshape(rows, 128)
    summed = pl.pallas_call(
        total_kernel,
        out_shape=jax.ShapeDtypeStruct(flat.shape, jnp.float32),
        in_specs=[WHOLE],
        out_specs=WHOLE,
        scratch_shapes=[
            pltpu.VMEM((6, rows, 128), jnp.float32),
            pltpu.VMEM((5, rows, 128), jnp.float32),
            pltpu.SemaphoreType.DMA((5,)),
            pltpu.SemaphoreType.DMA((5,)),
        ],
        compiler_params=params(collective_id),
        name="total",
    )(flat)
    return summed.reshape(-1)[:size]


def linked_mesh():
    return lax.axis_size("fsdp") == 8 and lax.axis_size("sub") == 4


def gathered(values):
    return lax.all_gather(values, AXES, axis=0, tiled=True)


def scattered(values):
    return lax.psum_scatter(values, AXES, scatter_dimension=0, tiled=True)


def layer_norm(values):
    center = values - jnp.mean(values, axis=-1, keepdims=True)
    return center * lax.rsqrt(jnp.mean(center * center, axis=-1, keepdims=True) + NORM_EPSILON)


def modulate(values, scale_part, shift_part):
    return layer_norm(values) * (1.0 + scale_part) + shift_part


def final_norm(values, gain_vector):
    return layer_norm(values) * gain_vector


def attention_bias(scale_query, segment_query, scale_key, segment_key, real_key, same):
    usable = (segment_query == segment_key) & (scale_key <= scale_query) & ((real_key == 1) | same)
    return jnp.where(usable, 0.0, MASK_VALUE)


def split_product(left_side, right_low):
    high = left_side.astype(jnp.bfloat16)
    rest = (left_side - high.astype(jnp.float32)).astype(jnp.bfloat16)
    return bfloat_product(high, right_low) + bfloat_product(rest, right_low)


def on_device(
    code_vectors,
    scale_ids,
    segment_ids,
    real_mask,
    labels,
    targets,
    loss_weight,
    tables,
    vectors,
    ada_weight,
    qkv_weight,
    out_weight,
    up_weight,
    down_weight,
    head_weight,
    tables_moment,
    ada_moment,
    qkv_moment,
    out_moment,
    up_moment,
    down_moment,
    head_moment,
    vector_moment,
    column_moment,
):
    devices = lax.axis_size(AXES)
    linked = linked_mesh()
    depth = tables.shape[0]
    tokens = code_vectors.shape[0]
    masters = (
        tables,
        vectors,
        ada_weight,
        qkv_weight,
        out_weight,
        up_weight,
        down_weight,
        head_weight,
    )
    local_count = jnp.sum(loss_weight).astype(jnp.float32)
    local_squares = jnp.stack([jnp.sum(master * master) for master in masters])
    low = jnp.bfloat16
    part_kind = low if linked else jnp.float32
    tables_low = tables.astype(low)
    ada_low = ada_weight.astype(low)
    qkv_low = qkv_weight.astype(low)
    out_low = out_weight.astype(low)
    down_low = down_weight.astype(low)

    small_rows = jnp.concatenate(
        [
            tables_low[:, CLASSES:],
            vectors.astype(low),
            jnp.zeros((depth, 128 - CODE_DIM - LEVELS - 9), low),
        ],
        axis=1,
    )
    tags = jnp.zeros((8, 128), jnp.float32)
    tags = tags.at[0, :2].set(labels.astype(jnp.float32)).at[0, 2].set(local_count)
    if linked:
        small_full, tags_full = small_gather(small_rows, tags)
    else:
        small_full, tags_full = gathered(small_rows), gathered(tags)
    full_up = gathered(up_weight.astype(low))
    full_head = gathered(head_weight.astype(low))
    small_full = small_full.reshape(D, 128)
    tags_full = tags_full.reshape(devices, 8, 128)[:, 0]
    labels_all = tags_full[:, :2].reshape(2 * devices)
    weight_total = jnp.sum(tags_full[:, 2])
    code_tables = small_full[:, : CODE_DIM + LEVELS]
    gain_vector = small_full[:, CODE_DIM + LEVELS : CODE_DIM + LEVELS + 9].astype(jnp.float32)

    label_hot = (labels_all[:, None] == jnp.arange(CLASSES, dtype=jnp.float32)[None, :]).astype(low)
    class_cond = bfloat_product(label_hot, tables_low[:, :CLASSES].T)
    activated = jax.nn.silu(class_cond).astype(low)
    modulation_part = bfloat_product(activated, ada_low)
    if linked:
        own_modulation, full_qkv = first_exchange(
            modulation_part.reshape(FIVE + (12 * D // 128, 128)), qkv_low
        )
        own_modulation = own_modulation.reshape(2, 6 * D)
        full_qkv = full_qkv.reshape(D, 3 * D)
    else:
        own_modulation, full_qkv = scattered(modulation_part), gathered(qkv_low)
    modulation = own_modulation + gain_vector[:, :6].T.reshape(1, 6 * D)
    second = (segment_ids == 1)[:, None]

    def of_token(block):
        piece = modulation[:, block * D : (block + 1) * D]
        return jnp.where(second, piece[1:2], piece[0:1])

    gamma_one, gamma_two, scale_one, scale_two, shift_one, shift_two = (
        of_token(block) for block in range(6)
    )

    level_hot = (scale_ids[:, None] == jnp.arange(LEVELS)[None, :]).astype(low)
    code_levels = jnp.concatenate([code_vectors, level_hot], axis=1)
    embedded = bfloat_product(code_levels, code_tables.T)
    normed = modulate(embedded, scale_one, shift_one).astype(low)
    projected = bfloat_product(normed, full_qkv)
    gains = jnp.pad(gain_vector[:, 6:8].T, ((0, 6), (0, 0)))
    places = jnp.arange(tokens)
    same = places[:, None] == places[None, :]
    bias = attention_bias(
        scale_ids[:, None], segment_ids[:, None], scale_ids[None, :], segment_ids[None, :], real_mask[None, :], same
    )
    if linked:
        mixed_heads, full_out, full_down = attend(projected, gains, bias, out_low, down_low)
        full_out = full_out.reshape(D, D)
        full_down = full_down.reshape(-1, D)
    else:
        (mixed_heads,) = attend(projected, gains, bias)
        full_out, full_down = gathered(out_low), gathered(down_low)
    attended = bfloat_product(mixed_heads, full_out)
    residual_one = embedded + gamma_one * attended
    normed_two = modulate(residual_one, scale_two, shift_two).astype(low)
    hidden_pre = bfloat_product(normed_two, full_up)
    hidden_act = jax.nn.gelu(hidden_pre, approximate=True).astype(low)
    branch = bfloat_product(hidden_act, full_down)
    residual_two = residual_one + gamma_two * branch
    final_normed = final_norm(residual_two, gain_vector[:, 8]).astype(low)
    logits = bfloat_product(final_normed, full_head)
    logit_peak = jnp.max(logits, axis=-1, keepdims=True)
    log_total = logit_peak + jnp.log(jnp.sum(jnp.exp(logits - logit_peak), axis=-1, keepdims=True))
    target_hot = targets[:, None] == jnp.arange(CODES)[None, :]
    picked = jnp.sum(jnp.where(target_hot, logits, 0.0), axis=-1, keepdims=True)
    weight_column = loss_weight.astype(jnp.float32)[:, None]
    local_loss = jnp.sum(weight_column * (log_total - picked))
    logit_grad = (
        (jnp.exp(logits - log_total) - target_hot.astype(jnp.float32))
        * (weight_column / weight_total)
    ).astype(low)

    head_part = bfloat_product(final_normed.T, logit_grad).astype(part_kind)
    final_grad = bfloat_product(logit_grad, full_head.T)
    _, final_back = jax.vjp(final_norm, residual_two, gain_vector[:, 8])
    residual_grad, head_gain_grad = final_back(final_grad)
    branch_grad = (gamma_two * residual_grad).astype(low)

    def slot_sums(token_grad):
        other = jnp.sum(jnp.where(second, token_grad, 0.0), axis=0)
        first = jnp.sum(jnp.where(second, 0.0, token_grad), axis=0)
        return jnp.stack([first, other])

    gamma_two_grad = slot_sums(residual_grad * branch)
    down_part = bfloat_product(hidden_act.T, branch_grad).astype(part_kind)
    act_grad = bfloat_product(branch_grad, full_down.T)
    _, gelu_back = jax.vjp(partial(jax.nn.gelu, approximate=True), hidden_pre)
    pre_grad = gelu_back(act_grad)[0].astype(low)
    up_part = bfloat_product(normed_two.T, pre_grad).astype(part_kind)
    normed_two_grad = bfloat_product(pre_grad, full_up.T)
    _, modulate_two_back = jax.vjp(modulate, residual_one, scale_two, shift_two)
    norm_grad, scale_two_grad, shift_two_grad = modulate_two_back(normed_two_grad)
    scale_two_grad, shift_two_grad = slot_sums(scale_two_grad), slot_sums(shift_two_grad)
    residual_grad = residual_grad + norm_grad
    attended_grad = (gamma_one * residual_grad).astype(low)
    gamma_one_grad = slot_sums(residual_grad * attended)
    out_part = bfloat_product(mixed_heads.T, attended_grad).astype(part_kind)
    mixed_grad = bfloat_product(attended_grad, full_out.T).astype(low)
    turned_bias = attention_bias(
        scale_ids[None, :], segment_ids[None, :], scale_ids[:, None], segment_ids[:, None], real_mask[:, None], same
    )
    if linked:
        heads_grad, gain_grads, done = attend_back(
            projected,
            mixed_grad,
            gains,
            turned_bias,
            head_part.reshape(FIVE + (depth, CODES)),
            up_part.reshape(FIVE + (depth, up_part.shape[1])),
            down_part.reshape(FIVE + (down_part.shape[0] // D, depth, D)),
        )
        wide = CODES // 512
        wide_up = wide + up_part.shape[1] // 512
        head_grad = done[:wide].transpose(1, 0, 2).reshape(depth, CODES)
        up_grad = done[wide:wide_up].transpose(1, 0, 2).reshape(depth, -1)
        down_grad = done[wide_up:].reshape(-1, 2, depth, 512).transpose(0, 2, 1, 3).reshape(-1, D)
    else:
        heads_grad, gain_grads = attend_back(projected, mixed_grad, gains, turned_bias)
        head_grad, up_grad, down_grad = scattered(head_part), scattered(up_part), scattered(down_part)
    qkv_part = jnp.concatenate(
        [bfloat_product(normed.T, heads_grad[part]).astype(part_kind) for part in range(3)], axis=1
    )
    normed_grad = sum(
        bfloat_product(heads_grad[part], full_qkv[:, part * D : (part + 1) * D].T) for part in range(3)
    )
    _, modulate_one_back = jax.vjp(modulate, embedded, scale_one, shift_one)
    norm_grad, scale_one_grad, shift_one_grad = modulate_one_back(normed_grad)
    scale_one_grad, shift_one_grad = slot_sums(scale_one_grad), slot_sums(shift_one_grad)
    embedded_grad = residual_grad + norm_grad
    modulation_grad = jnp.concatenate(
        [
            gamma_one_grad,
            gamma_two_grad,
            scale_one_grad,
            scale_two_grad,
            shift_one_grad,
            shift_two_grad,
        ],
        axis=1,
    )
    bias_grad = jnp.sum(modulation_grad, axis=0).reshape(6, D)
    code_grad = split_product(embedded_grad.T, code_levels)
    small_part = jnp.concatenate(
        [
            code_grad,
            bias_grad.T,
            gain_grads[:2].T,
            head_gain_grad[:, None],
            jnp.zeros((D, 128 - CODE_DIM - LEVELS - 9), jnp.float32),
        ],
        axis=1,
    )
    modulation_low = modulation_grad.astype(low)
    if linked:
        done, small_grad, modulation_all = last_exchange(
            qkv_part.reshape(FIVE + (depth, 3 * D)),
            out_part.reshape(FIVE + (depth, D)),
            small_part.reshape(FIVE + (depth, 128)),
            modulation_low.reshape(12 * D // 128, 128),
        )
        modulation_all = modulation_all.reshape(2 * devices, 6 * D)
        wide = 3 * D // 512
        qkv_grad = done[:wide].transpose(1, 0, 2).reshape(depth, 3 * D)
        out_grad = done[wide:].transpose(1, 0, 2).reshape(depth, D)
    else:
        modulation_all = gathered(modulation_low)
        small_grad, qkv_grad, out_grad = scattered(small_part), scattered(qkv_part), scattered(out_part)
    ada_grad = bfloat_product(activated.T, modulation_all)
    activated_grad = bfloat_product(modulation_all, ada_low.T)
    _, silu_back = jax.vjp(jax.nn.silu, class_cond)
    cond_grad = silu_back(activated_grad)[0]
    class_grad = jnp.dot(
        cond_grad.T,
        label_hot.astype(jnp.float32),
        precision=lax.Precision.HIGHEST,
        preferred_element_type=jnp.float32,
    )
    tables_grad = jnp.concatenate([class_grad, small_grad[:, : CODE_DIM + LEVELS]], axis=1)
    vectors_grad = small_grad[:, CODE_DIM + LEVELS : CODE_DIM + LEVELS + 9]
    gradients = (
        tables_grad,
        vectors_grad,
        ada_grad,
        qkv_grad,
        out_grad,
        up_grad,
        down_grad,
        head_grad,
    )
    second_decay = 1.0 - STEP ** (-0.8)
    factored_index = (0, 2, 3, 4, 5, 6, 7)
    factored_moments = (
        tables_moment,
        ada_moment,
        qkv_moment,
        out_moment,
        up_moment,
        down_moment,
        head_moment,
    )
    rows_list = []
    column_parts = []
    row_parts = []
    for position, moment in zip(factored_index, factored_moments):
        gradient = gradients[position]
        squared = gradient * gradient + TINY_SQUARE
        rows_new = second_decay * moment + (1.0 - second_decay) * jnp.mean(squared, axis=1)
        rows_list.append(rows_new)
        column_parts.append(jnp.sum(squared, axis=0))
        row_parts.append(jnp.sum(rows_new))
    column_count = column_moment.shape[0]
    sums = total(
        jnp.concatenate(column_parts + [jnp.stack(row_parts), local_squares, local_loss[None]]), 5
    )
    column_total = sums[:column_count]
    row_total = sums[column_count : column_count + 7]
    weight_squares = sums[column_count + 7 : column_count + 15]
    loss_sum = sums[column_count + 15]
    updates = [None] * 8
    moments_new = [None] * 8
    column_new = []
    offset = 0
    for factor_slot, position in enumerate(factored_index):
        gradient = gradients[position]
        rows_all = gradient.shape[0] * devices
        column_count = gradient.shape[1]
        cols_new = second_decay * column_moment[offset : offset + column_count] + (
            1.0 - second_decay
        ) * (column_total[offset : offset + column_count] / rows_all)
        offset += column_count
        estimate = (
            rows_list[factor_slot][:, None]
            * cols_new[None, :]
            / (row_total[factor_slot] / rows_all)
        )
        updates[position] = gradient * lax.rsqrt(estimate)
        moments_new[position] = rows_list[factor_slot]
        column_new.append(cols_new)
    vector_new = second_decay * vector_moment + (1.0 - second_decay) * (
        gradients[1] * gradients[1] + TINY_SQUARE
    )
    updates[1] = gradients[1] * lax.rsqrt(vector_new)
    moments_new[1] = vector_new
    local_spread = jnp.stack([jnp.sum(update * update) for update in updates])
    spread_total = total(local_spread, 6)
    next_weights = []
    spreads = []
    for position in range(8):
        count_all = gradients[position].size * devices
        spread = jnp.sqrt(spread_total[position] / count_all)
        step_scale = jnp.maximum(SCALE_FLOOR, jnp.sqrt(weight_squares[position] / count_all))
        next_weights.append(
            masters[position]
            - STEP_RATE * step_scale * (updates[position] / jnp.maximum(1.0, spread / CLIP_LIMIT))
        )
        spreads.append(spread)
    column_stat = jnp.concatenate(column_new)
    clip_spread = jnp.stack(spreads)
    results = [loss_sum, weight_total]
    for position in range(8):
        results += [gradients[position], moments_new[position], next_weights[position]]
    return tuple(results + [column_stat, clip_spread])


def solution(mesh):
    in_specs = (
        P(("fsdp", "sub"), None),
        P(("fsdp", "sub")),
        P(("fsdp", "sub")),
        P(("fsdp", "sub")),
        P(("fsdp", "sub")),
        P(("fsdp", "sub")),
        P(("fsdp", "sub")),
        P(("fsdp", "sub"), None),
        P(("fsdp", "sub"), None),
        P(("fsdp", "sub"), None),
        P(("fsdp", "sub"), None),
        P(("fsdp", "sub"), None),
        P(("fsdp", "sub"), None),
        P(("fsdp", "sub"), None),
        P(("fsdp", "sub"), None),
        P(("fsdp", "sub")),
        P(("fsdp", "sub")),
        P(("fsdp", "sub")),
        P(("fsdp", "sub")),
        P(("fsdp", "sub")),
        P(("fsdp", "sub")),
        P(("fsdp", "sub")),
        P(("fsdp", "sub"), None),
        P(),
    )
    out_specs = (
        P(),
        P(),
        P(("fsdp", "sub"), None),
        P(("fsdp", "sub")),
        P(("fsdp", "sub"), None),
        P(("fsdp", "sub"), None),
        P(("fsdp", "sub"), None),
        P(("fsdp", "sub"), None),
        P(("fsdp", "sub"), None),
        P(("fsdp", "sub")),
        P(("fsdp", "sub"), None),
        P(("fsdp", "sub"), None),
        P(("fsdp", "sub")),
        P(("fsdp", "sub"), None),
        P(("fsdp", "sub"), None),
        P(("fsdp", "sub")),
        P(("fsdp", "sub"), None),
        P(("fsdp", "sub"), None),
        P(("fsdp", "sub")),
        P(("fsdp", "sub"), None),
        P(("fsdp", "sub"), None),
        P(("fsdp", "sub")),
        P(("fsdp", "sub"), None),
        P(("fsdp", "sub"), None),
        P(("fsdp", "sub")),
        P(("fsdp", "sub"), None),
        P(),
        P(),
    )
    return jax.shard_map(
        on_device, mesh=mesh, in_specs=in_specs, out_specs=out_specs, check_vma=False
    )
```

```python
import math
from functools import partial

import jax
import jax.numpy as jnp
from jax import lax
from jax.experimental import pallas as pl
from jax.experimental.pallas import tpu as pltpu
from jax.sharding import PartitionSpec as P

D = 1024
HEADS = 16
HEAD_DIM = 64
CLASSES = 1000
CODES = 4096
CODE_DIM = 32
LEVELS = 10
STEP = 10


TINY_SQUARE = 1e-30
SCALE_FLOOR = 0.001
STEP_RATE = 1.0
CLIP_LIMIT = 1.0
NORM_EPSILON = 1e-06
MASK_VALUE = -1000000000.0

AXES = ("fsdp", "sub")
MESH = pl.DeviceIdType.MESH
ANY = pl.BlockSpec(memory_space=pl.ANY)
WHOLE = pl.BlockSpec(memory_space=pltpu.VMEM)
FIVE = (2, 2, 2, 2, 2)
DIMS = ("w", "u", "y", "x", "c")
SCATTER_ORDERS = (("c", "x", "y", "w", "u"), ("c", "y", "x", "w", "u"))
GATHER_ORDERS = (("u", "w", "y", "x", "c"), ("u", "w", "x", "y", "c"))
SCORE_SCALE = HEAD_DIM ** (-0.5)
EXP_SCALE = SCORE_SCALE * math.log2(math.e)
VMEM_GRANT = 58 * 1024 * 1024
FIRST_WIDTH, FIRST_LAG = 256, 1
ATTEND_WIDTH, ATTEND_LAG = 128, 2
BACK_WIDTH, BACK_LAG = 256, 2
LAST_WIDTH, LAST_LAG = 256, 2


def bfloat_product(left_side, right_side):
    return jnp.dot(left_side, right_side, preferred_element_type=jnp.float32)


class Place:
    def __init__(self):
        fsdp, sub = lax.axis_index("fsdp"), lax.axis_index("sub")
        self.bit = {
            "c": lax.rem(sub, 2),
            "x": lax.div(sub, 2),
            "y": lax.rem(fsdp, 2),
            "u": lax.rem(lax.div(fsdp, 2), 2),
            "w": lax.div(fsdp, 4),
        }
        bit = self.bit
        self.partner = {
            "c": (fsdp, sub + 1 - 2 * bit["c"]),
            "x": (fsdp, sub + 2 - 4 * bit["x"]),
            "y": (fsdp + 1 - 2 * bit["y"], sub),
            "u": (fsdp + 2 - 4 * bit["u"], sub),
            "w": (fsdp + 4 - 8 * bit["w"], sub),
        }

    def meet(self):
        barrier = pltpu.get_barrier_semaphore()
        for dim in DIMS:
            pl.semaphore_signal(
                barrier, inc=1, device_id=self.partner[dim], device_id_type=MESH
            )
        pl.semaphore_wait(barrier, 5)

    def send(self, src, dst, send_sem, recv_sem, dim):
        return pltpu.make_async_remote_copy(
            src_ref=src,
            dst_ref=dst,
            send_sem=send_sem,
            recv_sem=recv_sem,
            device_id=self.partner[dim],
            device_id_type=MESH,
        )


def when_in(index, low, high, body):
    if isinstance(index, int):
        if low <= index < high:
            body()
    else:
        pl.when((index >= low) & (index < high))(body)


class Gather:
    def __init__(self, place, groups, sends, recvs, local_sems, lag=1):
        self.place, self.groups, self.lag = place, groups, lag
        self.sends, self.recvs, self.local_sems = sends, recvs, local_sems
        self.steps = groups[-1][1] + 5 * lag

    @staticmethod
    def scratch(lag=1):
        dma = pltpu.SemaphoreType.DMA
        return [dma((5, 2, 2 * lag)), dma((5, 2, 2 * lag)), dma((2, 2 * lag))]

    def region(self, stage, parity):
        done = GATHER_ORDERS[parity][:stage]
        return tuple(slice(None) if d in done else self.place.bit[d] for d in DIMS)

    def copy(self, group, j, stage, parity, slot):
        _, _, own, full = group
        ref = full(j, parity, self.region(stage, parity))
        return self.place.send(
            own(j, parity) if stage == 0 else ref,
            ref,
            self.sends.at[stage, parity, slot],
            self.recvs.at[stage, parity, slot],
            GATHER_ORDERS[parity][stage],
        )

    def local(self, group, j, parity, slot):
        _, _, own, full = group
        return pltpu.make_async_copy(
            own(j, parity), full(j, parity, self.region(0, parity)), self.local_sems.at[parity, slot]
        )

    def step(self, t):
        for stage in reversed(range(6)):
            j = t - stage * self.lag
            for group in self.groups:

                def body(group=group, stage=stage, j=j):
                    slot = lax.rem(j, 2 * self.lag)
                    for parity in range(2):
                        if stage == 0:
                            self.local(group, j, parity, slot).start()
                        if stage == 1:
                            self.local(group, j, parity, slot).wait()
                        if stage >= 1:
                            self.copy(group, j, stage - 1, parity, slot).wait()
                        if stage < 5:
                            self.copy(group, j, stage, parity, slot).start()

                when_in(j, group[0], group[1], body)


class Scatter:
    def __init__(self, place, groups, store, scratch, lag=1):
        self.place, self.groups, self.store, self.lag = place, groups, store, lag
        self.keep = scratch[0]
        self.land = scratch[1:6]
        self.sums = (None,) + tuple(scratch[6:10])
        self.sends, self.recvs, self.keep_sems = scratch[10:13]
        self.first, self.end = groups[0][0], groups[-1][1]
        self.steps = self.end + 5 * lag

    @staticmethod
    def scratch(piece, kind, lag=1):
        dma = pltpu.SemaphoreType.DMA
        return (
            [pltpu.VMEM((lag, 2) + (2,) * 4 + piece, kind)]
            + [pltpu.VMEM((2 * lag, 2) + (2,) * (4 - k) + piece, kind) for k in range(5)]
            + [pltpu.VMEM((lag, 2) + (2,) * (5 - k) + piece, kind) for k in range(1, 5)]
            + [dma((5, 2, 2 * lag)), dma((5, 2, 2 * lag)), dma((2, lag))]
        )

    def half(self, stage, parity, other):
        order = SCATTER_ORDERS[parity]
        left = [d for d in DIMS if d not in order[:stage]]
        bit = self.place.bit[order[stage]]
        value = 1 - bit if other else bit
        return (parity,) + tuple(value if d == order[stage] else slice(None) for d in left)

    def copy(self, stage, parity, j, source=None):
        slot = lax.rem(j, 2 * self.lag)
        if source is None:
            if stage == 0:
                source = self.keep.at[lax.rem(j, self.lag), parity]
            else:
                source = self.sums[stage].at[(lax.rem(j, self.lag),) + self.half(stage, parity, True)]
        return self.place.send(
            source,
            self.land[stage].at[slot, parity],
            self.sends.at[stage, parity, slot],
            self.recvs.at[stage, parity, slot],
            SCATTER_ORDERS[parity][stage],
        )

    def step(self, t):
        for stage in reversed(range(6)):
            j = t - stage * self.lag

            def body(stage=stage, j=j):
                slot, near = lax.rem(j, 2 * self.lag), lax.rem(j, self.lag)
                for parity in range(2):
                    before = stage - 1
                    if before == 0:
                        pltpu.make_async_copy(
                            self.keep.at[near, parity],
                            self.keep.at[near, parity],
                            self.keep_sems.at[parity, near],
                        ).wait()
                    self.copy(before, parity, j).wait()
                    if before == 0:
                        mine = self.keep[near, parity]
                    else:
                        mine = self.sums[before][(near,) + self.half(before, parity, False)]
                    total = mine.astype(jnp.float32) + self.land[before][slot, parity].astype(
                        jnp.float32
                    )
                    if stage < 5:
                        self.sums[stage][near, parity] = total.astype(self.keep.dtype)
                        self.copy(stage, parity, j).start()
                    else:
                        self.store(j, parity, total)

            if stage == 0:
                for low, high, source in self.groups:

                    def begin(source=source, j=j):
                        near = lax.rem(j, self.lag)
                        core = self.place.bit["c"]
                        for parity in range(2):
                            self.copy(0, parity, j, source(j, parity, 1 - core)).start()
                            pltpu.make_async_copy(
                                source(j, parity, core),
                                self.keep.at[near, parity],
                                self.keep_sems.at[parity, near],
                            ).start()

                    when_in(j, low, high, begin)
            else:
                when_in(j, self.first, self.end, body)


def finish(engine):
    done = UNITS * (HEADS // 2)

    @pl.when(pl.program_id(0) == HEADS // 2 - 1)
    def rest():
        for t in range(done, engine.steps):
            engine.step(t)


def params(collective_id, **more):
    return pltpu.CompilerParams(
        collective_id=collective_id, has_side_effects=True, vmem_limit_bytes=VMEM_GRANT, **more
    )


def columns(start, size):
    return pl.ds(pl.multiple_of(start, 128), size)


def small_gather_kernel(rows_ref, tags_ref, rows_full, tags_full, *sems):
    place = Place()
    place.meet()
    gather = Gather(
        place,
        [(0, 1, lambda j, p: (rows_ref, tags_ref)[p], lambda j, p, r: (rows_full, tags_full)[p].at[r])],
        *sems,
    )
    for t in range(6):
        gather.step(t)


def small_gather(rows, tags):
    return pl.pallas_call(
        small_gather_kernel,
        out_shape=(
            jax.ShapeDtypeStruct(FIVE + rows.shape, rows.dtype),
            jax.ShapeDtypeStruct(FIVE + tags.shape, tags.dtype),
        ),
        in_specs=[WHOLE, WHOLE],
        out_specs=(WHOLE, WHOLE),
        scratch_shapes=Gather.scratch(),
        compiler_params=params(0),
        name="small_gather",
    )(rows, tags)


def first_kernel(part_ref, own_ref, mod_ref, full_ref, *scratch):
    place = Place()
    place.meet()
    rows = part_ref.shape[5] // 2
    width = FIRST_WIDTH

    def store(j, parity, total):
        mod_ref[pl.ds(parity * rows, rows)] = total

    scatter = Scatter(
        place,
        [(0, 1, lambda j, p, core: part_ref.at[:, :, :, :, core, pl.ds(p * rows, rows)])],
        store,
        scratch[:13],
    )
    pairs = own_ref.shape[1] // (2 * width)
    gather = Gather(
        place,
        [
            (
                0,
                pairs,
                lambda j, p: own_ref.at[:, columns((2 * j + p) * width, width)],
                lambda j, p, r: full_ref.at[r + (slice(None), columns((2 * j + p) * width, width))],
            )
        ],
        *scratch[13:],
        lag=FIRST_LAG,
    )
    for t in range(6):
        scatter.step(t)
        gather.step(t)
    for t in range(6, gather.steps):
        gather.step(t)


def first_exchange(part, own):
    return pl.pallas_call(
        first_kernel,
        out_shape=(
            jax.ShapeDtypeStruct(part.shape[5:], jnp.float32),
            jax.ShapeDtypeStruct(FIVE + own.shape, own.dtype),
        ),
        in_specs=[ANY, ANY],
        out_specs=(WHOLE, ANY),
        scratch_shapes=Scatter.scratch((part.shape[5] // 2, 128), jnp.float32) + Gather.scratch(FIRST_LAG),
        compiler_params=params(1),
        name="modulation_scatter_qkv_gather",
    )(part, own)


def head_mean(values):
    low_lane = lax.broadcasted_iota(jnp.int32, values.shape, 1) < HEAD_DIM
    low_sum = jnp.sum(jnp.where(low_lane, values, 0.0), axis=1, keepdims=True)
    high_sum = jnp.sum(jnp.where(low_lane, 0.0, values), axis=1, keepdims=True)
    return jnp.where(low_lane, low_sum, high_sum) * (1.0 / HEAD_DIM)


def of_head(values, head):
    low_lane = lax.broadcasted_iota(jnp.int32, values.shape, 1) < HEAD_DIM
    zero = jnp.zeros_like(values)
    return jnp.where(low_lane, values, zero) if head == 0 else jnp.where(low_lane, zero, values)


def dot_last(left, right):
    return lax.dot_general(left, right, (((1,), (1,)), ((), ())), preferred_element_type=jnp.float32)


def dot_first(left, right):
    return lax.dot_general(left, right, (((0,), (0,)), ((), ())), preferred_element_type=jnp.float32)


def dot_plain(left, right):
    return lax.dot_general(left, right, (((1,), (0,)), ((), ())), preferred_element_type=jnp.float32)


UNITS = 4


def normed_head(raw, gain):
    return (raw * lax.rsqrt(head_mean(raw * raw) + NORM_EPSILON) * gain).astype(jnp.bfloat16)


def attend_kernel(linked, q_ref, k_ref, v_ref, gain_ref, bias_ref, *refs):
    if linked:
        out_own, down_own, mixed_ref, out_full, down_full, qn, kn, vn = refs[:8]
        sems = refs[8:]
        place = Place()
        width = ATTEND_WIDTH
        split = out_own.shape[1] // (2 * width)
        depth = out_own.shape[0]
        parts = down_own.shape[0] // depth

        def spread(j):
            return lax.div(j - split, split), lax.rem(j - split, split)

        def down_source(j, p):
            part, column = spread(j)
            return down_own.at[
                pl.ds(pl.multiple_of(part * depth, depth), depth), columns((2 * column + p) * width, width)
            ]

        def down_target(j, p, r):
            part, column = spread(j)
            return down_full.at[r + (part, slice(None), columns((2 * column + p) * width, width))]

        gather = Gather(
            place,
            [
                (
                    0,
                    split,
                    lambda j, p: out_own.at[:, columns((2 * j + p) * width, width)],
                    lambda j, p, r: out_full.at[r + (slice(None), columns((2 * j + p) * width, width))],
                ),
                (split, split + split * parts, down_source, down_target),
            ],
            *sems,
            lag=ATTEND_LAG,
        )
        pl.when(pl.program_id(0) == 0)(place.meet)
    else:
        mixed_ref, qn, kn, vn = refs
    qn[...] = normed_head(q_ref[...], gain_ref[0:1])
    kn[...] = normed_head(k_ref[...], gain_ref[1:2])
    vn[...] = v_ref[...].astype(jnp.bfloat16)
    size = q_ref.shape[0] // UNITS

    @pl.loop(0, UNITS)
    def unit(u):
        if linked:
            gather.step(pl.program_id(0) * UNITS + u)
        rows = pl.ds(pl.multiple_of(u * size, size), size)
        both = []
        for head in range(2):
            scores = dot_last(of_head(qn[rows], head), kn[...]) * EXP_SCALE + bias_ref[rows]
            raised = jnp.exp2(scores)
            share = 1.0 / jnp.sum(raised, axis=1, keepdims=True)
            both.append(dot_plain((raised * share).astype(jnp.bfloat16), vn[...]))
        low_lane = lax.broadcasted_iota(jnp.int32, both[0].shape, 1) < HEAD_DIM
        mixed_ref[rows] = jnp.where(low_lane, both[0], both[1]).astype(jnp.bfloat16)

    if linked:
        finish(gather)


def attend(projected, gains, bias, out_own=None, down_own=None):
    tokens = projected.shape[0]
    pair = pl.BlockSpec((tokens, 128), lambda i: (0, i))
    specs = [
        pair,
        pl.BlockSpec((tokens, 128), lambda i: (0, i + 8)),
        pl.BlockSpec((tokens, 128), lambda i: (0, i + 16)),
        pl.BlockSpec((8, 128), lambda i: (0, i)),
        pl.BlockSpec((tokens, tokens), lambda i: (0, 0), pipeline_mode=pl.Buffered(1)),
    ]
    outs = [jax.ShapeDtypeStruct((tokens, D), jnp.bfloat16)]
    out_specs = [pair]
    scratch = [pltpu.VMEM((tokens, 128), jnp.bfloat16)] * 3
    operands = [projected, projected, projected, gains, bias]
    linked = out_own is not None
    if linked:
        depth = out_own.shape[0]
        specs += [ANY, ANY]
        operands += [out_own, down_own]
        outs += [
            jax.ShapeDtypeStruct(FIVE + out_own.shape, jnp.bfloat16),
            jax.ShapeDtypeStruct(FIVE + (down_own.shape[0] // depth, depth, D), jnp.bfloat16),
        ]
        out_specs += [ANY, ANY]
        scratch = scratch + Gather.scratch(ATTEND_LAG)
    return pl.pallas_call(
        partial(attend_kernel, linked),
        grid=(HEADS // 2,),
        out_shape=tuple(outs),
        in_specs=specs,
        out_specs=tuple(out_specs),
        scratch_shapes=scratch,
        compiler_params=params(2) if linked else pltpu.CompilerParams(vmem_limit_bytes=VMEM_GRANT),
        name="attention_forward",
    )(*operands)


def attend_back_kernel(linked, q_ref, k_ref, v_ref, m_ref, gain_ref, bias_ref, *refs):
    if linked:
        head_ref, up_ref, down_ref, grad_ref, gain_grad_ref, done_ref = refs[:6]
        qn, kn, vn, dq, dk, dv = refs[6:12]
        place = Place()
        width = BACK_WIDTH
        wide = up_ref.shape[6] // (2 * width)
        narrow = down_ref.shape[7] // (2 * width)
        parts = down_ref.shape[5]

        def columns_of(ref, first):
            return lambda j, p, core: ref.at[
                :, :, :, :, core, :, columns((2 * (j - first) + p) * width, width)
            ]

        def down_source(j, p, core):
            spread = j - 2 * wide
            part, column = lax.div(spread, narrow), lax.rem(spread, narrow)
            return down_ref.at[:, :, :, :, core, part, :, columns((2 * column + p) * width, width)]

        def store(j, parity, total):
            done_ref[j, :, parity * width : (parity + 1) * width] = total

        pairs = 2 * wide + parts * narrow
        scatter = Scatter(
            place,
            [
                (0, wide, columns_of(head_ref, 0)),
                (wide, 2 * wide, columns_of(up_ref, wide)),
                (2 * wide, pairs, down_source),
            ],
            store,
            refs[12:],
            lag=BACK_LAG,
        )
        pl.when(pl.program_id(0) == 0)(place.meet)
    else:
        grad_ref, gain_grad_ref = refs[:2]
        qn, kn, vn, dq, dk, dv = refs[2:]
    qn[...] = normed_head(q_ref[...], gain_ref[0:1])
    kn[...] = normed_head(k_ref[...], gain_ref[1:2])
    vn[...] = v_ref[...].astype(jnp.bfloat16)
    dk[...] = jnp.zeros_like(dk)
    dv[...] = jnp.zeros_like(dv)
    size = q_ref.shape[0] // UNITS

    @pl.loop(0, UNITS)
    def unit(u):
        if linked:
            scatter.step(pl.program_id(0) * UNITS + u)
        rows = pl.ds(pl.multiple_of(u * size, size), size)
        query_sum = None
        for head in range(2):
            query = of_head(qn[rows], head)
            mixed = of_head(m_ref[rows], head)
            raised = jnp.exp2(dot_last(kn[...], query) * EXP_SCALE + bias_ref[:, rows])
            probs = raised * (1.0 / jnp.sum(raised, axis=0, keepdims=True))
            prob_grad = dot_last(vn[...], mixed)
            center = jnp.sum(probs * prob_grad, axis=0, keepdims=True)
            score_grad = (probs * (prob_grad - center)).astype(jnp.bfloat16)
            dk[...] += dot_plain(score_grad, query)
            dv[...] += dot_plain(probs.astype(jnp.bfloat16), mixed)
            part = dot_first(score_grad, of_head(kn[...], head))
            query_sum = part if query_sum is None else query_sum + part
        dq[rows] = query_sum

    gain_rows = []
    for place_at, raw_ref, grad in ((0, q_ref, dq), (1, k_ref, dk)):
        raw = raw_ref[...]
        normed_grad = grad[...] * SCORE_SCALE
        rate = lax.rsqrt(head_mean(raw * raw) + NORM_EPSILON)
        scaled = gain_ref[place_at : place_at + 1] * normed_grad
        back = rate * scaled - raw * (rate * rate * rate) * head_mean(raw * scaled)
        grad_ref[place_at] = back.astype(jnp.bfloat16)
        gain_rows.append(jnp.sum(normed_grad * raw * rate, axis=0, keepdims=True))
    grad_ref[2] = dv[...].astype(jnp.bfloat16)
    gain_grad_ref[...] = jnp.concatenate(gain_rows + [jnp.zeros((6, 128), jnp.float32)], axis=0)
    if linked:
        finish(scatter)


def attend_back(projected, mixed_grad, gains, bias, head_grad=None, up_grad=None, down_grad=None):
    tokens = projected.shape[0]
    pair = pl.BlockSpec((tokens, 128), lambda i: (0, i))
    specs = [
        pair,
        pl.BlockSpec((tokens, 128), lambda i: (0, i + 8)),
        pl.BlockSpec((tokens, 128), lambda i: (0, i + 16)),
        pair,
        pl.BlockSpec((8, 128), lambda i: (0, i)),
        pl.BlockSpec((tokens, tokens), lambda i: (0, 0), pipeline_mode=pl.Buffered(1)),
    ]
    outs = [
        jax.ShapeDtypeStruct((3, tokens, D), jnp.bfloat16),
        jax.ShapeDtypeStruct((8, D), jnp.float32),
    ]
    out_specs = [
        pl.BlockSpec((3, tokens, 128), lambda i: (0, 0, i)),
        pl.BlockSpec((8, 128), lambda i: (0, i)),
    ]
    scratch = [pltpu.VMEM((tokens, 128), jnp.bfloat16)] * 3 + [
        pltpu.VMEM((tokens, 128), jnp.float32)
    ] * 3
    operands = [projected, projected, projected, mixed_grad, gains, bias]
    linked = head_grad is not None
    if linked:
        depth = head_grad.shape[5]
        specs += [ANY, ANY, ANY]
        operands += [head_grad, up_grad, down_grad]
        pairs = (head_grad.shape[6] + up_grad.shape[6] + down_grad.shape[5] * down_grad.shape[7]) // (2 * BACK_WIDTH)
        outs += [jax.ShapeDtypeStruct((pairs, depth, 2 * BACK_WIDTH), jnp.float32)]
        out_specs += [WHOLE]
        scratch = scratch + Scatter.scratch((depth, BACK_WIDTH), jnp.bfloat16, BACK_LAG)
    return pl.pallas_call(
        partial(attend_back_kernel, linked),
        grid=(HEADS // 2,),
        out_shape=tuple(outs),
        in_specs=specs,
        out_specs=tuple(out_specs),
        scratch_shapes=scratch,
        compiler_params=params(3) if linked else pltpu.CompilerParams(vmem_limit_bytes=VMEM_GRANT),
        name="attention_backward",
    )(*operands)


WEIGHT_COLUMNS = (CLASSES + CODE_DIM + LEVELS, 9, 6 * D, 3 * D, D, 4 * D, D, CODES)
SUM_STARTS = (0, None, 1152, 1152 + 6144, 1152 + 9216, 1152 + 10240, 1152 + 14336, 1152 + 15360)
SCALARS = 1152 + 19456
SUM_LANES = SCALARS + 128
SMALL_LANES = CODE_DIM + LEVELS + 9
DECAY = 1.0 - STEP ** (-0.8)


def three_terms(values):
    high = values.astype(jnp.bfloat16)
    rest = values - high.astype(jnp.float32)
    middle = rest.astype(jnp.bfloat16)
    return high, middle, (rest - middle.astype(jnp.float32)).astype(jnp.bfloat16)


def lane_row(scalars):
    lanes = lax.broadcasted_iota(jnp.int32, (1, 128), 1)
    row = jnp.zeros((1, 128), jnp.float32)
    for lane, value in scalars:
        row = jnp.where(lanes == lane, value, row)
    return row


def whole_sum(values):
    return jnp.sum(jnp.sum(values, axis=0, keepdims=True), axis=1, keepdims=True)


def weight_tiles(tables_grad, ada_grad, done_attention, done_last, depth):
    def blocks(ref, first, count, width):
        return [(lambda at=first + i: ref[at], i * width, width) for i in range(count)]

    near, far = 2 * LAST_WIDTH, 2 * BACK_WIDTH
    tables_columns = WEIGHT_COLUMNS[0]
    wide = CODES // far
    return {
        0: [(0, [(lambda: tables_grad[:, :tables_columns], 0, tables_columns)])],
        2: [(1, [(lambda: ada_grad[...], 0, 6 * D)])],
        3: [(2, blocks(done_last, D // near, 3 * D // near, near))],
        4: [(3, blocks(done_last, 0, D // near, near))],
        5: [(4, blocks(done_attention, wide, wide, far))],
        6: [(6 + part, blocks(done_attention, 2 * wide + part * (D // far), D // far, far)) for part in range(4)],
        7: [(5, blocks(done_attention, 0, wide, far))],
    }


class Total:
    def __init__(self, place, sums, land, sends, recvs):
        self.place, self.sums, self.land = place, sums, land
        self.sends, self.recvs = sends, recvs

    @staticmethod
    def scratch(lanes):
        dma = pltpu.SemaphoreType.DMA
        return [
            pltpu.VMEM((6, 1, lanes), jnp.float32),
            pltpu.VMEM((5, 1, lanes), jnp.float32),
            dma((5,)),
            dma((5,)),
        ]

    def run(self):
        for stage, dim in enumerate(DIMS):
            copy = self.place.send(
                self.sums.at[stage], self.land.at[stage], self.sends.at[stage], self.recvs.at[stage], dim
            )
            copy.start()
            copy.wait()
            self.sums[stage + 1] = self.sums[stage] + self.land[stage]


def last_kernel(
    out_ref,
    qkv_low,
    embedded_ref,
    grad_ref,
    heads_grad,
    normed_ref,
    codes_ref,
    second_ref,
    scale_ref,
    known_ref,
    gains_ref,
    act_ref,
    cond_ref,
    hot_ref,
    loss_ref,
    attention_ref,
    tables_ref,
    vectors_ref,
    ada_ref,
    qkv_master,
    out_master,
    up_master,
    down_master,
    head_master,
    moments_ref,
    vector_moment_ref,
    column_moment_ref,
    done_ref,
    small_done,
    tables_grad,
    ada_grad,
    rows_ref,
    columns_ref,
    facts_ref,
    *scratch,
):
    place = Place()
    place.meet()
    devices = lax.axis_size(AXES)
    depth = tables_ref.shape[0]
    width = LAST_WIDTH
    narrow = D // (2 * width)
    part_grads, qkv_full, embedded, grad, code_sums, mod_ref, small_ref, load_sems = scratch[40:48]
    loads = [
        pltpu.make_async_copy(source, target, load_sems.at[i])
        for i, (source, target) in enumerate(
            ((qkv_low, qkv_full), (embedded_ref, embedded), (grad_ref, grad))
        )
    ]
    for load in loads:
        load.start()

    def columns_of(ref, first):
        return lambda j, p, core: ref.at[
            :, :, :, :, core, :, columns((2 * (j - first) + p) * width, width)
        ]

    def store(j, parity, total):
        done_ref[j, :, parity * width : (parity + 1) * width] = total

    pairs = 4 * narrow
    scatter = Scatter(
        place,
        [(0, narrow, columns_of(out_ref, 0))]
        + [
            ((1 + part) * narrow, (2 + part) * narrow, columns_of(part_grads.at[part], (1 + part) * narrow))
            for part in range(3)
        ],
        store,
        scratch[:13],
        lag=LAST_LAG,
    )
    half = depth // 2

    def small_store(j, parity, total):
        small_done[pl.ds(parity * half, half)] = total

    small = Scatter(
        place,
        [(0, 1, lambda j, p, core: small_ref.at[:, :, :, :, core, pl.ds(p * half, half)])],
        small_store,
        scratch[13:26],
    )
    mod_sums, mod_land, mod_all, mod_sends, mod_recvs = scratch[26:31]
    bit = place.bit

    def mod_copy(stage):
        dim = ("c", "x", "y", "u", "w")[stage]
        if stage < 3:
            source, target = (mod_ref, mod_sums.at[0], mod_sums.at[1])[stage], mod_land.at[stage]
        elif stage == 3:
            source = target = mod_all.at[bit["w"], bit["u"]]
        else:
            source = target = mod_all.at[bit["w"]]
        return place.send(source, target, mod_sends.at[stage], mod_recvs.at[stage], dim)

    def mod_step(stage):
        if stage:
            mod_copy(stage - 1).wait()
        if stage == 1:
            mod_sums[0] = mod_ref[...] + mod_land[0]
        elif stage == 2:
            mod_sums[1] = mod_sums[0] + mod_land[1]
        elif stage == 3:
            mod_all[bit["w"], bit["u"]] = mod_sums[1] + mod_land[2]
        if stage < 5:
            mod_copy(stage).start()

    first_total = Total(place, *scratch[31:35])
    second_total = Total(place, *scratch[35:39])
    sums, facts = first_total.sums, scratch[39]
    tiles = weight_tiles(tables_grad, ada_grad, attention_ref, done_ref, depth)
    masters = (
        tables_ref,
        vectors_ref,
        ada_ref,
        qkv_master,
        out_master,
        up_master,
        down_master,
        head_master,
    )

    def ada_part():
        slots = mod_all[...].reshape(2 * devices, 6 * D)
        ada_grad[...] = dot_first(act_ref[...], slots)
        activated_grad = dot_last(slots, ada_ref[...].astype(jnp.bfloat16))
        cond = cond_ref[...]
        gate = 1.0 / (1.0 + jnp.exp(-cond))
        cond_grad = activated_grad * (gate * (1.0 + cond * (1.0 - gate)))
        shape = (128, hot_ref.shape[1])
        source = lax.broadcasted_iota(jnp.int32, shape, 0)
        target = lax.broadcasted_iota(jnp.int32, shape, 1)
        moved = (target == source + (CLASSES - 9)) & (source >= 9) & (source < SMALL_LANES)
        shift = jnp.where(moved, 1.0, 0.0).astype(jnp.bfloat16)
        total = jnp.zeros((depth, hot_ref.shape[1]), jnp.float32)
        for term in three_terms(cond_grad)[::-1]:
            total = total + dot_first(term, hot_ref[...])
        for term in three_terms(small_done[...])[::-1]:
            total = total + dot_plain(term, shift)
        tables_grad[...] = total

    def stats(position):
        row_total = jnp.zeros((1, 1), jnp.float32)
        for index, group in tiles[position]:
            row_sum = jnp.zeros((depth, 1), jnp.float32)
            for load, first, size in group:
                gradient = load()
                squared = gradient * gradient + TINY_SQUARE
                row_sum = row_sum + jnp.sum(squared, axis=1, keepdims=True)
                at = SUM_STARTS[position] + first
                sums[0, :, at : at + size] += jnp.sum(squared, axis=0, keepdims=True)
            rows_new = DECAY * moments_ref[index] + (1.0 - DECAY) * (
                row_sum * (1.0 / WEIGHT_COLUMNS[position])
            )
            rows_ref[index] = rows_new
            row_total = row_total + jnp.sum(rows_new, axis=0, keepdims=True)
        facts[...] += lane_row([(position, row_total)])

    def squares(first, end):
        for position in range(first, end):
            master = masters[position][...]
            facts[...] += lane_row([(8 + position, whole_sum(master * master))])

    def part_grad(part):
        @pl.loop(0, D // 256)
        def tile(i):
            at = columns(i * 256, 256)
            product = dot_first(normed_ref[...], heads_grad[part, :, at])
            part_grads[part, :, :, :, :, :, :, at] = product.astype(jnp.bfloat16).reshape(
                FIVE + (depth, 256)
            )

    tokens = normed_ref.shape[0]
    block = tokens // 4
    slot_rows = [jnp.zeros((1, D), jnp.float32)] * 4

    def norm_back(index):
        rows = slice(index * block, (index + 1) * block)
        back = jnp.zeros((block, D), jnp.float32)
        for part in range(3):
            back = back + dot_last(heads_grad[part, rows], qkv_full[:, part * D : (part + 1) * D])
        values = embedded[rows]
        center = values - jnp.sum(values, axis=1, keepdims=True) * (1.0 / D)
        rate = lax.rsqrt(jnp.sum(center * center, axis=1, keepdims=True) * (1.0 / D) + NORM_EPSILON)
        unit = center * rate
        other = second_ref[rows] > 0.5
        scale_back = back * unit
        for at, value in enumerate((scale_back, back)):
            everything = jnp.sum(value, axis=0, keepdims=True)
            second = jnp.sum(jnp.where(other, value, 0.0), axis=0, keepdims=True)
            slot_rows[2 * at] = slot_rows[2 * at] + (everything - second)
            slot_rows[2 * at + 1] = slot_rows[2 * at + 1] + second
        unit_back = back * (1.0 + jnp.where(other, scale_ref[1:2], scale_ref[0:1]))
        mean_back = jnp.sum(unit_back, axis=1, keepdims=True) * (1.0 / D)
        mean_along = jnp.sum(unit_back * unit, axis=1, keepdims=True) * (1.0 / D)
        total = grad[rows] + rate * (unit_back - mean_back - unit * mean_along)
        high = total.astype(jnp.bfloat16)
        rest = (total - high.astype(jnp.float32)).astype(jnp.bfloat16)
        product = dot_first(codes_ref[rows], high) + dot_first(codes_ref[rows], rest)
        code_sums[...] = product if index == 0 else code_sums[...] + product

    def gather_rows():
        spot = 2 * (4 * bit["y"] + 2 * bit["x"] + bit["c"])
        row_ids = lax.broadcasted_iota(jnp.int32, (16, D), 0)
        for kind in range(6):
            if kind in (2, 4):
                first, other = slot_rows[kind - 2 : kind]
            else:
                at = slice(kind * D, (kind + 1) * D)
                first, other = known_ref[0:1, at], known_ref[1:2, at]
            placed = jnp.where(row_ids == spot, first, jnp.where(row_ids == spot + 1, other, 0.0))
            mod_ref[:, kind * D : (kind + 1) * D] = placed.astype(jnp.bfloat16)
            code_sums[kind : kind + 1] = first + other
        code_sums[6:9] = gains_ref[0:3]
        small_ref[...] = code_sums[...].T.reshape(FIVE + (depth, 128))

    sums[0] = jnp.zeros_like(sums[0])
    facts[...] = lane_row([(16, loss_ref[...])])
    steps = iter(range(scatter.steps))
    for _ in range(narrow):
        scatter.step(next(steps))
    for part in range(3):
        part_grad(part)
        for _ in range(narrow):
            scatter.step(next(steps))
    for load in loads:
        load.wait()
    for index in range(4):
        norm_back(index)
        scatter.step(next(steps))
    gather_rows()
    beside = [
        partial(stats, 5),
        partial(stats, 6),
        partial(stats, 7),
        partial(squares, 0, 5),
        partial(squares, 5, 8),
    ]
    for t in range(6):
        mod_step(t)
        small.step(t)
        if t < len(beside):
            beside[t]()
        for step in steps:
            scatter.step(step)
            break
    for step in steps:
        scatter.step(step)
    ada_part()
    stats(0)
    stats(2)
    stats(3)
    stats(4)
    sums[0, :, SCALARS:] = facts[...]
    first_total.run()
    columns_ref[...] = DECAY * column_moment_ref[...] + (1.0 - DECAY) * sums[5] * (1.0 / D)
    start, end = SUM_STARTS[6], SUM_STARTS[6] + D
    columns_ref[:, start:end] = DECAY * column_moment_ref[:, start:end] + (1.0 - DECAY) * sums[
        5, :, start:end
    ] * (1.0 / (4 * D))

    def rows_all(position):
        return 4.0 * D if position == 6 else 1.0 * D

    scalars = []
    for position, groups in tiles.items():
        at = SCALARS + position
        row_mean = sums[5, :, at : at + 1] * (1.0 / rows_all(position))
        spread = jnp.zeros((1, 1), jnp.float32)
        for index, group in groups:
            for load, first, size in group:
                lane = SUM_STARTS[position] + first
                estimate = rows_ref[index] * columns_ref[:, lane : lane + size] / row_mean
                update = load() * lax.rsqrt(estimate)
                spread = spread + whole_sum(update * update)
        scalars.append((position, spread))
    gradient = small_done[:, :9]
    moment = DECAY * vector_moment_ref[...] + (1.0 - DECAY) * (gradient * gradient + TINY_SQUARE)
    update = gradient * lax.rsqrt(moment)
    scalars.append((1, whole_sum(update * update)))
    second_total.sums[0] = lane_row(scalars)
    second_total.run()
    spread_row, factor_row = [], []
    for position in range(8):
        count = rows_all(position) * WEIGHT_COLUMNS[position]
        spread = jnp.sqrt(second_total.sums[5, :, position : position + 1] * (1.0 / count))
        at = SCALARS + 8 + position
        scale = jnp.maximum(SCALE_FLOOR, jnp.sqrt(sums[5, :, at : at + 1] * (1.0 / count)))
        spread_row.append((position, spread))
        factor_row.append((position, STEP_RATE * scale / jnp.maximum(1.0, spread / CLIP_LIMIT)))
    facts_ref[0] = lane_row(spread_row)
    facts_ref[1] = lane_row(factor_row)
    facts_ref[2] = sums[5, :, SCALARS:]


def last_exchange(far, near, attention_done, masters, moments):
    depth = far[0].shape[5]
    pairs = 4 * D // (2 * LAST_WIDTH)
    dma = pltpu.SemaphoreType.DMA
    f32, low = jnp.float32, jnp.bfloat16
    tokens = far[2].shape[0]
    operands = list(far) + list(near) + [attention_done] + list(masters) + list(moments)
    return pl.pallas_call(
        last_kernel,
        out_shape=(
            jax.ShapeDtypeStruct((pairs, depth, 2 * LAST_WIDTH), f32),
            jax.ShapeDtypeStruct((depth, 128), f32),
            jax.ShapeDtypeStruct((depth, 1152), f32),
            jax.ShapeDtypeStruct((depth, 6 * D), f32),
            jax.ShapeDtypeStruct((10, depth, 1), f32),
            jax.ShapeDtypeStruct((1, SUM_LANES), f32),
            jax.ShapeDtypeStruct((3, 1, 128), f32),
        ),
        in_specs=[ANY] * 4 + [WHOLE] * (len(operands) - 4),
        out_specs=(WHOLE,) * 7,
        scratch_shapes=Scatter.scratch((depth, LAST_WIDTH), low, LAST_LAG)
        + Scatter.scratch((depth // 2, 128), f32)
        + [
            pltpu.VMEM((2, 16, 6 * D), low),
            pltpu.VMEM((3, 16, 6 * D), low),
            pltpu.VMEM((2, 2, 16, 6 * D), low),
            dma((5,)),
            dma((5,)),
        ]
        + Total.scratch(SUM_LANES)
        + Total.scratch(128)
        + [pltpu.VMEM((1, 128), f32)]
        + [
            pltpu.VMEM((3,) + FIVE + (depth, D), low),
            pltpu.VMEM((D, 3 * D), low),
            pltpu.VMEM((tokens, D), f32),
            pltpu.VMEM((tokens, D), f32),
            pltpu.VMEM((128, D), f32),
            pltpu.VMEM((16, 6 * D), low),
            pltpu.VMEM(FIVE + (depth, 128), f32),
            dma((3,)),
        ],
        compiler_params=params(4),
        name="last_scatter",
    )(*operands)


def step_kernel(
    done_ref,
    small_ref,
    tables_grad,
    ada_grad,
    rows_ref,
    columns_ref,
    facts_ref,
    attention_ref,
    vector_moment_ref,
    tables_ref,
    vectors_ref,
    ada_ref,
    qkv_master,
    out_master,
    up_master,
    down_master,
    head_master,
    *outs,
):
    depth = tables_ref.shape[0]
    masters = (
        tables_ref,
        vectors_ref,
        ada_ref,
        qkv_master,
        out_master,
        up_master,
        down_master,
        head_master,
    )
    vector_stat = outs[16]
    tiles = weight_tiles(tables_grad, ada_grad, attention_ref, done_ref, depth)
    for position, groups in tiles.items():
        grad_ref, next_ref, master = outs[2 * position], outs[2 * position + 1], masters[position]
        factor = facts_ref[1, :, position : position + 1]
        mean_scale = 1.0 / (4 * D) if position == 6 else 1.0 / D
        row_mean = facts_ref[2, :, position : position + 1] * mean_scale
        for order, (index, group) in enumerate(groups):
            at = slice(order * depth, (order + 1) * depth)
            for load, first, size in group:
                gradient = load()
                lane = SUM_STARTS[position] + first
                estimate = rows_ref[index] * columns_ref[:, lane : lane + size] / row_mean
                grad_ref[at, first : first + size] = gradient
                next_ref[at, first : first + size] = master[at, first : first + size] - factor * (
                    gradient * lax.rsqrt(estimate)
                )
    gradient = small_ref[:, :9]
    moment = DECAY * vector_moment_ref[...] + (1.0 - DECAY) * (gradient * gradient + TINY_SQUARE)
    vector_stat[...] = moment
    outs[2][...] = gradient
    outs[3][...] = vectors_ref[...] - facts_ref[1, :, 1:2] * (gradient * lax.rsqrt(moment))


def take_step(last, attention_done, vector_moment, masters):
    operands = list(last) + [attention_done, vector_moment] + list(masters)
    shapes = []
    for master in masters:
        shapes += [jax.ShapeDtypeStruct(master.shape, jnp.float32)] * 2
    shapes.append(jax.ShapeDtypeStruct(vector_moment.shape, jnp.float32))
    return pl.pallas_call(
        step_kernel,
        out_shape=tuple(shapes),
        in_specs=[WHOLE] * len(operands),
        out_specs=(WHOLE,) * len(shapes),
        compiler_params=pltpu.CompilerParams(vmem_limit_bytes=VMEM_GRANT),
        name="weight_step",
    )(*operands)


def linked_mesh():
    return lax.axis_size("fsdp") == 8 and lax.axis_size("sub") == 4


def gathered(values):
    return lax.all_gather(values, AXES, axis=0, tiled=True)


def scattered(values):
    return lax.psum_scatter(values, AXES, scatter_dimension=0, tiled=True)


def layer_norm(values):
    center = values - jnp.mean(values, axis=-1, keepdims=True)
    return center * lax.rsqrt(jnp.mean(center * center, axis=-1, keepdims=True) + NORM_EPSILON)


def modulate(values, scale_part, shift_part):
    return layer_norm(values) * (1.0 + scale_part) + shift_part


def final_norm(values, gain_vector):
    return layer_norm(values) * gain_vector


def attention_bias(scale_query, segment_query, scale_key, segment_key, real_key, same):
    usable = (segment_query == segment_key) & (scale_key <= scale_query) & ((real_key == 1) | same)
    return jnp.where(usable, 0.0, MASK_VALUE)


def split_product(left_side, right_low):
    high = left_side.astype(jnp.bfloat16)
    rest = (left_side - high.astype(jnp.float32)).astype(jnp.bfloat16)
    return bfloat_product(high, right_low) + bfloat_product(rest, right_low)


def on_device(
    code_vectors,
    scale_ids,
    segment_ids,
    real_mask,
    labels,
    targets,
    loss_weight,
    tables,
    vectors,
    ada_weight,
    qkv_weight,
    out_weight,
    up_weight,
    down_weight,
    head_weight,
    tables_moment,
    ada_moment,
    qkv_moment,
    out_moment,
    up_moment,
    down_moment,
    head_moment,
    vector_moment,
    column_moment,
):
    devices = lax.axis_size(AXES)
    linked = linked_mesh()
    depth = tables.shape[0]
    tokens = code_vectors.shape[0]
    masters = (
        tables,
        vectors,
        ada_weight,
        qkv_weight,
        out_weight,
        up_weight,
        down_weight,
        head_weight,
    )
    local_count = jnp.sum(loss_weight).astype(jnp.float32)
    low = jnp.bfloat16
    part_kind = low if linked else jnp.float32
    tables_low = tables.astype(low)
    ada_low = ada_weight.astype(low)
    qkv_low = qkv_weight.astype(low)
    out_low = out_weight.astype(low)
    down_low = down_weight.astype(low)

    small_rows = jnp.concatenate(
        [
            tables_low[:, CLASSES:],
            vectors.astype(low),
            jnp.zeros((depth, 128 - CODE_DIM - LEVELS - 9), low),
        ],
        axis=1,
    )
    tags = jnp.zeros((8, 128), jnp.float32)
    tags = tags.at[0, :2].set(labels.astype(jnp.float32)).at[0, 2].set(local_count)
    if linked:
        small_full, tags_full = small_gather(small_rows, tags)
    else:
        small_full, tags_full = gathered(small_rows), gathered(tags)
    full_up = gathered(up_weight.astype(low))
    full_head = gathered(head_weight.astype(low))
    small_full = small_full.reshape(D, 128)
    tags_full = tags_full.reshape(devices, 8, 128)[:, 0]
    labels_all = tags_full[:, :2].reshape(2 * devices)
    weight_total = jnp.sum(tags_full[:, 2])
    code_tables = small_full[:, : CODE_DIM + LEVELS]
    gain_vector = small_full[:, CODE_DIM + LEVELS : CODE_DIM + LEVELS + 9].astype(jnp.float32)

    label_hot = (labels_all[:, None] == jnp.arange(1152, dtype=jnp.float32)[None, :]).astype(low)
    class_cond = bfloat_product(label_hot[:, :CLASSES], tables_low[:, :CLASSES].T)
    activated = jax.nn.silu(class_cond).astype(low)
    modulation_part = bfloat_product(activated, ada_low)
    if linked:
        own_modulation, full_qkv = first_exchange(
            modulation_part.reshape(FIVE + (12 * D // 128, 128)), qkv_low
        )
        own_modulation = own_modulation.reshape(2, 6 * D)
        full_qkv = full_qkv.reshape(D, 3 * D)
    else:
        own_modulation, full_qkv = scattered(modulation_part), gathered(qkv_low)
    modulation = own_modulation + gain_vector[:, :6].T.reshape(1, 6 * D)
    second = (segment_ids == 1)[:, None]

    def of_token(block):
        piece = modulation[:, block * D : (block + 1) * D]
        return jnp.where(second, piece[1:2], piece[0:1])

    gamma_one, gamma_two, scale_one, scale_two, shift_one, shift_two = (
        of_token(block) for block in range(6)
    )

    level_hot = (scale_ids[:, None] == jnp.arange(LEVELS)[None, :]).astype(low)
    code_levels = jnp.concatenate([code_vectors, level_hot], axis=1)
    embedded = bfloat_product(code_levels, code_tables.T)
    normed = modulate(embedded, scale_one, shift_one).astype(low)
    projected = bfloat_product(normed, full_qkv)
    gains = jnp.pad(gain_vector[:, 6:8].T, ((0, 6), (0, 0)))
    places = jnp.arange(tokens)
    same = places[:, None] == places[None, :]
    bias = attention_bias(
        scale_ids[:, None], segment_ids[:, None], scale_ids[None, :], segment_ids[None, :], real_mask[None, :], same
    )
    if linked:
        mixed_heads, full_out, full_down = attend(projected, gains, bias, out_low, down_low)
        full_out = full_out.reshape(D, D)
        full_down = full_down.reshape(-1, D)
    else:
        (mixed_heads,) = attend(projected, gains, bias)
        full_out, full_down = gathered(out_low), gathered(down_low)
    attended = bfloat_product(mixed_heads, full_out)
    residual_one = embedded + gamma_one * attended
    normed_two = modulate(residual_one, scale_two, shift_two).astype(low)
    hidden_pre = bfloat_product(normed_two, full_up)
    hidden_act = jax.nn.gelu(hidden_pre, approximate=True).astype(low)
    branch = bfloat_product(hidden_act, full_down)
    residual_two = residual_one + gamma_two * branch
    final_normed = final_norm(residual_two, gain_vector[:, 8]).astype(low)
    logits = bfloat_product(final_normed, full_head)
    logit_peak = jnp.max(logits, axis=-1, keepdims=True)
    log_total = logit_peak + jnp.log(jnp.sum(jnp.exp(logits - logit_peak), axis=-1, keepdims=True))
    target_hot = targets[:, None] == jnp.arange(CODES)[None, :]
    picked = jnp.sum(jnp.where(target_hot, logits, 0.0), axis=-1, keepdims=True)
    weight_column = loss_weight.astype(jnp.float32)[:, None]
    local_loss = jnp.sum(weight_column * (log_total - picked))
    logit_grad = (
        (jnp.exp(logits - log_total) - target_hot.astype(jnp.float32))
        * (weight_column / weight_total)
    ).astype(low)

    head_part = bfloat_product(final_normed.T, logit_grad).astype(part_kind)
    final_grad = bfloat_product(logit_grad, full_head.T)
    _, final_back = jax.vjp(final_norm, residual_two, gain_vector[:, 8])
    residual_grad, head_gain_grad = final_back(final_grad)
    branch_grad = (gamma_two * residual_grad).astype(low)

    def slot_sums(token_grad):
        other = jnp.sum(jnp.where(second, token_grad, 0.0), axis=0)
        first = jnp.sum(jnp.where(second, 0.0, token_grad), axis=0)
        return jnp.stack([first, other])

    gamma_two_grad = slot_sums(residual_grad * branch)
    down_part = bfloat_product(hidden_act.T, branch_grad).astype(part_kind)
    act_grad = bfloat_product(branch_grad, full_down.T)
    _, gelu_back = jax.vjp(partial(jax.nn.gelu, approximate=True), hidden_pre)
    pre_grad = gelu_back(act_grad)[0].astype(low)
    up_part = bfloat_product(normed_two.T, pre_grad).astype(part_kind)
    normed_two_grad = bfloat_product(pre_grad, full_up.T)
    _, modulate_two_back = jax.vjp(modulate, residual_one, scale_two, shift_two)
    norm_grad, scale_two_grad, shift_two_grad = modulate_two_back(normed_two_grad)
    scale_two_grad, shift_two_grad = slot_sums(scale_two_grad), slot_sums(shift_two_grad)
    residual_grad = residual_grad + norm_grad
    attended_grad = (gamma_one * residual_grad).astype(low)
    gamma_one_grad = slot_sums(residual_grad * attended)
    out_part = bfloat_product(mixed_heads.T, attended_grad).astype(part_kind)
    mixed_grad = bfloat_product(attended_grad, full_out.T).astype(low)
    turned_bias = attention_bias(
        scale_ids[None, :], segment_ids[None, :], scale_ids[:, None], segment_ids[:, None], real_mask[:, None], same
    )
    if linked:
        heads_grad, gain_grads, attention_done = attend_back(
            projected,
            mixed_grad,
            gains,
            turned_bias,
            head_part.reshape(FIVE + (depth, CODES)),
            up_part.reshape(FIVE + (depth, up_part.shape[1])),
            down_part.reshape(FIVE + (down_part.shape[0] // D, depth, D)),
        )
    else:
        heads_grad, gain_grads = attend_back(projected, mixed_grad, gains, turned_bias)
        head_grad, up_grad, down_grad = scattered(head_part), scattered(up_part), scattered(down_part)
    if linked:
        unknown = jnp.zeros((2, D), jnp.float32)
        factored_rows = [tables_moment, ada_moment, qkv_moment, out_moment, up_moment, head_moment]
        row_moments = jnp.concatenate(factored_rows + [down_moment]).reshape(10, depth, 1)
        padding = jnp.zeros((110,), jnp.float32)
        column_moments = jnp.concatenate(
            [column_moment[:1042], padding, column_moment[1042:], jnp.zeros((128,), jnp.float32)]
        )[None]
        known = jnp.concatenate(
            [gamma_one_grad, gamma_two_grad, unknown, scale_two_grad, unknown, shift_two_grad], axis=1
        )
        gain_rows = jnp.concatenate([gain_grads[:2], head_gain_grad[None], jnp.zeros((5, D), jnp.float32)])
        codes = jnp.pad(code_levels, ((0, 0), (9, 128 - SMALL_LANES)))
        last = last_exchange(
            (out_part.reshape(FIVE + (depth, D)), full_qkv, embedded, residual_grad),
            (
                heads_grad,
                normed,
                codes,
                second.astype(jnp.float32),
                modulation[:, 2 * D : 3 * D],
                known,
                gain_rows,
                activated,
                class_cond,
                label_hot,
                local_loss[None, None],
            ),
            attention_done,
            masters,
            (row_moments, vector_moment, column_moments),
        )
        stepped = take_step(last, attention_done, vector_moment, masters)
        rows_new, cols_new, facts = last[4].reshape(10 * depth), last[5][0], last[6][:, 0]
        stats = [rows_new[i * depth : (i + 1) * depth] for i in range(6)] + [rows_new[6 * depth :]]
        moment_of = (stats[0], stepped[16], stats[1], stats[2], stats[3], stats[4], stats[6], stats[5])
        results = [facts[2, 16], weight_total]
        for position in range(8):
            results += [stepped[2 * position], moment_of[position], stepped[2 * position + 1]]
        column_stat = jnp.concatenate([cols_new[:1042], cols_new[1152:SCALARS]])
        return tuple(results + [column_stat, facts[0, :8]])

    qkv_part = jnp.concatenate(
        [bfloat_product(normed.T, heads_grad[part]).astype(part_kind) for part in range(3)], axis=1
    )
    normed_grad = sum(
        bfloat_product(heads_grad[part], full_qkv[:, part * D : (part + 1) * D].T) for part in range(3)
    )
    _, modulate_one_back = jax.vjp(modulate, embedded, scale_one, shift_one)
    norm_grad, scale_one_grad, shift_one_grad = modulate_one_back(normed_grad)
    scale_one_grad, shift_one_grad = slot_sums(scale_one_grad), slot_sums(shift_one_grad)
    embedded_grad = residual_grad + norm_grad
    modulation_grad = jnp.concatenate(
        [
            gamma_one_grad,
            gamma_two_grad,
            scale_one_grad,
            scale_two_grad,
            shift_one_grad,
            shift_two_grad,
        ],
        axis=1,
    )
    bias_grad = jnp.sum(modulation_grad, axis=0).reshape(6, D)
    code_grad = split_product(embedded_grad.T, code_levels)
    small_part = jnp.concatenate(
        [
            bias_grad.T,
            gain_grads[:2].T,
            head_gain_grad[:, None],
            code_grad,
            jnp.zeros((D, 128 - CODE_DIM - LEVELS - 9), jnp.float32),
        ],
        axis=1,
    )
    modulation_low = modulation_grad.astype(low)
    modulation_all = gathered(modulation_low)
    small_grad, qkv_grad, out_grad = scattered(small_part), scattered(qkv_part), scattered(out_part)
    ada_grad = bfloat_product(activated.T, modulation_all)
    activated_grad = bfloat_product(modulation_all, ada_low.T)
    _, silu_back = jax.vjp(jax.nn.silu, class_cond)
    cond_grad = silu_back(activated_grad)[0]
    class_grad = jnp.dot(
        cond_grad.T,
        label_hot[:, :CLASSES].astype(jnp.float32),
        precision=lax.Precision.HIGHEST,
        preferred_element_type=jnp.float32,
    )
    tables_grad = jnp.concatenate([class_grad, small_grad[:, 9:SMALL_LANES]], axis=1)
    vectors_grad = small_grad[:, :9]
    gradients = (
        tables_grad,
        vectors_grad,
        ada_grad,
        qkv_grad,
        out_grad,
        up_grad,
        down_grad,
        head_grad,
    )
    second_decay = DECAY
    factored_index = (0, 2, 3, 4, 5, 6, 7)
    factored_moments = (
        tables_moment,
        ada_moment,
        qkv_moment,
        out_moment,
        up_moment,
        down_moment,
        head_moment,
    )
    local_squares = jnp.stack([jnp.sum(master * master) for master in masters])
    rows_list = []
    column_parts = []
    row_parts = []
    for position, moment in zip(factored_index, factored_moments):
        gradient = gradients[position]
        squared = gradient * gradient + TINY_SQUARE
        rows_new = second_decay * moment + (1.0 - second_decay) * jnp.mean(squared, axis=1)
        rows_list.append(rows_new)
        column_parts.append(jnp.sum(squared, axis=0))
        row_parts.append(jnp.sum(rows_new))
    column_count = column_moment.shape[0]
    sums = lax.psum(
        jnp.concatenate(column_parts + [jnp.stack(row_parts), local_squares, local_loss[None]]), AXES
    )
    column_total = sums[:column_count]
    row_total = sums[column_count : column_count + 7]
    weight_squares = sums[column_count + 7 : column_count + 15]
    loss_sum = sums[column_count + 15]
    updates = [None] * 8
    moments_new = [None] * 8
    column_new = []
    offset = 0
    for factor_slot, position in enumerate(factored_index):
        gradient = gradients[position]
        rows_all = gradient.shape[0] * devices
        column_count = gradient.shape[1]
        cols_new = second_decay * column_moment[offset : offset + column_count] + (
            1.0 - second_decay
        ) * (column_total[offset : offset + column_count] / rows_all)
        offset += column_count
        estimate = (
            rows_list[factor_slot][:, None]
            * cols_new[None, :]
            / (row_total[factor_slot] / rows_all)
        )
        updates[position] = gradient * lax.rsqrt(estimate)
        moments_new[position] = rows_list[factor_slot]
        column_new.append(cols_new)
    vector_new = second_decay * vector_moment + (1.0 - second_decay) * (
        gradients[1] * gradients[1] + TINY_SQUARE
    )
    updates[1] = gradients[1] * lax.rsqrt(vector_new)
    moments_new[1] = vector_new
    local_spread = jnp.stack([jnp.sum(update * update) for update in updates])
    spread_total = lax.psum(local_spread, AXES)
    next_weights = []
    spreads = []
    for position in range(8):
        count_all = gradients[position].size * devices
        spread = jnp.sqrt(spread_total[position] / count_all)
        step_scale = jnp.maximum(SCALE_FLOOR, jnp.sqrt(weight_squares[position] / count_all))
        next_weights.append(
            masters[position]
            - STEP_RATE * step_scale * (updates[position] / jnp.maximum(1.0, spread / CLIP_LIMIT))
        )
        spreads.append(spread)
    column_stat = jnp.concatenate(column_new)
    clip_spread = jnp.stack(spreads)
    results = [loss_sum, weight_total]
    for position in range(8):
        results += [gradients[position], moments_new[position], next_weights[position]]
    return tuple(results + [column_stat, clip_spread])


def solution(mesh):
    in_specs = (
        P(("fsdp", "sub"), None),
        P(("fsdp", "sub")),
        P(("fsdp", "sub")),
        P(("fsdp", "sub")),
        P(("fsdp", "sub")),
        P(("fsdp", "sub")),
        P(("fsdp", "sub")),
        P(("fsdp", "sub"), None),
        P(("fsdp", "sub"), None),
        P(("fsdp", "sub"), None),
        P(("fsdp", "sub"), None),
        P(("fsdp", "sub"), None),
        P(("fsdp", "sub"), None),
        P(("fsdp", "sub"), None),
        P(("fsdp", "sub"), None),
        P(("fsdp", "sub")),
        P(("fsdp", "sub")),
        P(("fsdp", "sub")),
        P(("fsdp", "sub")),
        P(("fsdp", "sub")),
        P(("fsdp", "sub")),
        P(("fsdp", "sub")),
        P(("fsdp", "sub"), None),
        P(),
    )
    out_specs = (
        P(),
        P(),
        P(("fsdp", "sub"), None),
        P(("fsdp", "sub")),
        P(("fsdp", "sub"), None),
        P(("fsdp", "sub"), None),
        P(("fsdp", "sub"), None),
        P(("fsdp", "sub"), None),
        P(("fsdp", "sub"), None),
        P(("fsdp", "sub")),
        P(("fsdp", "sub"), None),
        P(("fsdp", "sub"), None),
        P(("fsdp", "sub")),
        P(("fsdp", "sub"), None),
        P(("fsdp", "sub"), None),
        P(("fsdp", "sub")),
        P(("fsdp", "sub"), None),
        P(("fsdp", "sub"), None),
        P(("fsdp", "sub")),
        P(("fsdp", "sub"), None),
        P(("fsdp", "sub"), None),
        P(("fsdp", "sub")),
        P(("fsdp", "sub"), None),
        P(("fsdp", "sub"), None),
        P(("fsdp", "sub")),
        P(("fsdp", "sub"), None),
        P(),
        P(),
    )
    return jax.shard_map(
        on_device, mesh=mesh, in_specs=in_specs, out_specs=out_specs, check_vma=False
    )
```

```python
import math
from functools import partial

import jax
import jax.numpy as jnp
from jax import lax
from jax.experimental import pallas as pl
from jax.experimental.pallas import tpu as pltpu
from jax.sharding import PartitionSpec as P

D = 1024
HEADS = 16
HEAD_DIM = 64
CLASSES = 1000
CODES = 4096
CODE_DIM = 32
LEVELS = 10
STEP = 10


TINY_SQUARE = 1e-30
SCALE_FLOOR = 0.001
STEP_RATE = 1.0
CLIP_LIMIT = 1.0
NORM_EPSILON = 1e-06
MASK_VALUE = -1000000000.0

AXES = ("fsdp", "sub")
MESH = pl.DeviceIdType.MESH
ANY = pl.BlockSpec(memory_space=pl.ANY)
WHOLE = pl.BlockSpec(memory_space=pltpu.VMEM)
FIVE = (2, 2, 2, 2, 2)
DIMS = ("w", "u", "y", "x", "c")
SCATTER_ORDERS = (("c", "x", "y", "w", "u"), ("c", "y", "x", "w", "u"))
GATHER_ORDERS = tuple(order[::-1] for order in SCATTER_ORDERS)
SCORE_SCALE = HEAD_DIM ** (-0.5)
EXP_SCALE = SCORE_SCALE * math.log2(math.e)
VMEM_GRANT = 58 * 1024 * 1024
FIRST_WIDTH, FIRST_LAG = 256, 1
ATTEND_WIDTH, ATTEND_LAG = 128, 3
BACK_WIDTH, BACK_LAG = 256, 2
LAST_WIDTH, LAST_LAG = 256, 2


def bfloat_product(left_side, right_side):
    return jnp.dot(left_side, right_side, preferred_element_type=jnp.float32)


class Place:
    def __init__(self):
        fsdp, sub = lax.axis_index("fsdp"), lax.axis_index("sub")
        self.bit = {
            "c": lax.rem(sub, 2),
            "x": lax.div(sub, 2),
            "y": lax.rem(fsdp, 2),
            "u": lax.rem(lax.div(fsdp, 2), 2),
            "w": lax.div(fsdp, 4),
        }
        bit = self.bit
        self.partner = {
            "c": (fsdp, sub + 1 - 2 * bit["c"]),
            "x": (fsdp, sub + 2 - 4 * bit["x"]),
            "y": (fsdp + 1 - 2 * bit["y"], sub),
            "u": (fsdp + 2 - 4 * bit["u"], sub),
            "w": (fsdp + 4 - 8 * bit["w"], sub),
        }

    def meet(self):
        barrier = pltpu.get_barrier_semaphore()
        for dim in DIMS:
            pl.semaphore_signal(
                barrier, inc=1, device_id=self.partner[dim], device_id_type=MESH
            )
        pl.semaphore_wait(barrier, 5)

    def send(self, src, dst, send_sem, recv_sem, dim):
        return pltpu.make_async_remote_copy(
            src_ref=src,
            dst_ref=dst,
            send_sem=send_sem,
            recv_sem=recv_sem,
            device_id=self.partner[dim],
            device_id_type=MESH,
        )


def when_in(index, low, high, body):
    if isinstance(index, int):
        if low <= index < high:
            body()
    else:
        pl.when((index >= low) & (index < high))(body)


class Gather:
    def __init__(self, place, groups, sends, recvs, local_sems, lag=1):
        self.place, self.groups, self.lag = place, groups, lag
        self.sends, self.recvs, self.local_sems = sends, recvs, local_sems
        self.steps = groups[-1][1] + 5 * lag

    @staticmethod
    def scratch(lag=1):
        dma = pltpu.SemaphoreType.DMA
        return [dma((5, 2, 2 * lag)), dma((5, 2, 2 * lag)), dma((2, 2 * lag))]

    def region(self, stage, parity):
        done = GATHER_ORDERS[parity][:stage]
        return tuple(slice(None) if d in done else self.place.bit[d] for d in DIMS)

    def copy(self, group, j, stage, parity, slot):
        _, _, own, full = group
        ref = full(j, parity, self.region(stage, parity))
        return self.place.send(
            own(j, parity) if stage == 0 else ref,
            ref,
            self.sends.at[stage, parity, slot],
            self.recvs.at[stage, parity, slot],
            GATHER_ORDERS[parity][stage],
        )

    def local(self, group, j, parity, slot):
        _, _, own, full = group
        return pltpu.make_async_copy(
            own(j, parity), full(j, parity, self.region(0, parity)), self.local_sems.at[parity, slot]
        )

    def step(self, t):
        for stage in reversed(range(6)):
            j = t - stage * self.lag
            for group in self.groups:

                def body(group=group, stage=stage, j=j):
                    slot = lax.rem(j, 2 * self.lag)
                    for parity in range(2):
                        if stage == 0:
                            self.local(group, j, parity, slot).start()
                        if stage == 1:
                            self.local(group, j, parity, slot).wait()
                        if stage >= 1:
                            self.copy(group, j, stage - 1, parity, slot).wait()
                        if stage < 5:
                            self.copy(group, j, stage, parity, slot).start()

                when_in(j, group[0], group[1], body)


class Scatter:
    def __init__(self, place, groups, store, scratch, lag=1):
        self.place, self.groups, self.store, self.lag = place, groups, store, lag
        self.keep = scratch[0]
        self.land = scratch[1:6]
        self.sums = (None,) + tuple(scratch[6:10])
        self.sends, self.recvs, self.keep_sems = scratch[10:13]
        self.first, self.end = groups[0][0], groups[-1][1]
        self.steps = self.end + 5 * lag

    @staticmethod
    def scratch(piece, kind, lag=1):
        dma = pltpu.SemaphoreType.DMA
        return (
            [pltpu.VMEM((lag, 2) + (2,) * 4 + piece, kind)]
            + [pltpu.VMEM((2 * lag, 2) + (2,) * (4 - k) + piece, kind) for k in range(5)]
            + [pltpu.VMEM((lag, 2) + (2,) * (5 - k) + piece, kind) for k in range(1, 5)]
            + [dma((5, 2, 2 * lag)), dma((5, 2, 2 * lag)), dma((2, lag))]
        )

    def half(self, stage, parity, other):
        order = SCATTER_ORDERS[parity]
        left = [d for d in DIMS if d not in order[:stage]]
        bit = self.place.bit[order[stage]]
        value = 1 - bit if other else bit
        return (parity,) + tuple(value if d == order[stage] else slice(None) for d in left)

    def copy(self, stage, parity, j, source=None):
        slot = lax.rem(j, 2 * self.lag)
        if source is None:
            if stage == 0:
                source = self.keep.at[lax.rem(j, self.lag), parity]
            else:
                source = self.sums[stage].at[(lax.rem(j, self.lag),) + self.half(stage, parity, True)]
        return self.place.send(
            source,
            self.land[stage].at[slot, parity],
            self.sends.at[stage, parity, slot],
            self.recvs.at[stage, parity, slot],
            SCATTER_ORDERS[parity][stage],
        )

    def step(self, t):
        for stage in reversed(range(6)):
            j = t - stage * self.lag

            def body(stage=stage, j=j):
                slot, near = lax.rem(j, 2 * self.lag), lax.rem(j, self.lag)
                for parity in range(2):
                    before = stage - 1
                    if before == 0:
                        pltpu.make_async_copy(
                            self.keep.at[near, parity],
                            self.keep.at[near, parity],
                            self.keep_sems.at[parity, near],
                        ).wait()
                    self.copy(before, parity, j).wait()
                    if before == 0:
                        mine = self.keep[near, parity]
                    else:
                        mine = self.sums[before][(near,) + self.half(before, parity, False)]
                    total = mine.astype(jnp.float32) + self.land[before][slot, parity].astype(
                        jnp.float32
                    )
                    if stage < 5:
                        self.sums[stage][near, parity] = total.astype(self.keep.dtype)
                        self.copy(stage, parity, j).start()
                    else:
                        self.store(j, parity, total)

            if stage == 0:
                for low, high, source in self.groups:

                    def begin(source=source, j=j):
                        near = lax.rem(j, self.lag)
                        core = self.place.bit["c"]
                        for parity in range(2):
                            self.copy(0, parity, j, source(j, parity, 1 - core)).start()
                            pltpu.make_async_copy(
                                source(j, parity, core),
                                self.keep.at[near, parity],
                                self.keep_sems.at[parity, near],
                            ).start()

                    when_in(j, low, high, begin)
            else:
                when_in(j, self.first, self.end, body)


def finish(engine):
    done = UNITS * (HEADS // 2)

    @pl.when(pl.program_id(0) == HEADS // 2 - 1)
    def rest():
        for t in range(done, engine.steps):
            engine.step(t)


def params(collective_id, **more):
    return pltpu.CompilerParams(
        collective_id=collective_id, has_side_effects=True, vmem_limit_bytes=VMEM_GRANT, **more
    )


def columns(start, size):
    return pl.ds(pl.multiple_of(start, 128), size)


def slot_labels(tags_full, order):
    pieces = []
    for number in range(32):
        bits = {dim: (number >> (4 - at)) & 1 for at, dim in enumerate(order)}
        pieces.append(tags_full[bits["w"], bits["u"], bits["y"], bits["x"], bits["c"], 0:2])
    return jnp.concatenate(pieces, axis=0)


def hot_of(labels):
    lanes = lax.broadcasted_iota(jnp.int32, labels.shape, 1).astype(jnp.float32)
    blocks = [jnp.where(labels == lanes + 128.0 * at, 1.0, 0.0) for at in range(9)]
    return jnp.concatenate(blocks, axis=1).astype(jnp.bfloat16)


def begin_kernel(
    rows_ref,
    tags_ref,
    tables_ref,
    ada_ref,
    qkv_ref,
    out_own_ref,
    codes_ref,
    token_columns,
    token_rows,
    projected_ref,
    qkv_out,
    out_full,
    embedded_ref,
    normed_ref,
    modulation_ref,
    vectors_ref,
    hot_ref,
    cond_ref,
    act_ref,
    tag_sums,
    bias_ref,
    turned_ref,
    *scratch,
):
    place = Place()
    place.meet()
    bit = place.bit
    (
        rows_full,
        tags_full,
        own_qkv,
        own_out,
        qkv_full,
        part,
        unit,
        staged,
        copy_sems,
        mod_sends,
        mod_recvs,
    ) = scratch[:11]
    mod_land, mod_sums = scratch[11:16], scratch[16:21]
    own_qkv[...] = qkv_ref[...].astype(jnp.bfloat16)
    own_out[...] = out_own_ref[...].astype(jnp.bfloat16)
    small = Gather(
        place,
        [(0, 1, lambda j, p: (rows_ref, tags_ref)[p], lambda j, p, r: (rows_full, tags_full)[p].at[r])],
        *scratch[21:24],
    )
    width = FIRST_WIDTH
    pairs = 3 * D // (2 * width)

    def of_weight(own, full, first):
        return (
            lambda j, p: own.at[:, columns((2 * (j - first) + p) * width, width)],
            lambda j, p, r: full.at[r + (slice(None), columns((2 * (j - first) + p) * width, width))],
        )

    gather = Gather(
        place,
        [
            (0, pairs) + of_weight(own_qkv, qkv_full, 0),
            (pairs, pairs + D // (2 * width)) + of_weight(own_out, out_full, pairs),
        ],
        *scratch[24:27],
        lag=FIRST_LAG,
    )
    lanes = 3 * D
    orders = (("x", "y", "w", "u", "c"), ("y", "x", "w", "u", "c"))

    def mod_half(stage, parity, other):
        dim = orders[parity][stage]
        value = 1 - bit[dim] if other else bit[dim]
        left = [d for d in ("x", "y", "w") if d not in orders[parity][:stage]]
        return tuple(value if d == dim else slice(None) for d in left)

    def mod_view(stage, parity, other):
        if stage == 0:
            at = pl.ds(parity * lanes, lanes)
            return part, mod_half(0, parity, other) + (slice(None), at)
        if stage < 3:
            return mod_sums[stage - 1], (parity,) + mod_half(stage, parity, other)
        return mod_sums[stage - 1], (parity,)

    def mod_copy(stage, parity):
        ref, at = mod_view(stage, parity, True)
        return place.send(
            ref.at[at],
            mod_land[stage].at[parity],
            mod_sends.at[stage, parity],
            mod_recvs.at[stage, parity],
            orders[parity][stage],
        )

    def mod_step(stage):
        for parity in range(2):
            if stage:
                mod_copy(stage - 1, parity).wait()
                ref, at = mod_view(stage - 1, parity, False)
                mod_sums[stage - 1][parity] = ref[at] + mod_land[stage - 1][parity]
            if stage < 5:
                mod_copy(stage, parity).start()

    def mask(query, key, same):
        usable = (query[0] == key[0]) & (key[1] <= query[1]) & ((key[2] > 0.5) | same)
        return jnp.where(usable, 0.0, MASK_VALUE)

    tokens = codes_ref.shape[0]
    block = tokens // 4

    def masks(index, size):
        at = slice(index * size, (index + 1) * size)
        shape = (size, tokens)
        same = lax.broadcasted_iota(jnp.int32, shape, 0) + index * size == lax.broadcasted_iota(
            jnp.int32, shape, 1
        )
        down = [token_columns[at, i : i + 1] for i in range(3)]
        across = [token_rows[i : i + 1] for i in range(3)]
        bias_ref[at] = mask(down, across, same)
        turned_ref[at] = mask(across, down, same)

    def embed(index):
        at = slice(index * block, (index + 1) * block)
        values = dot_last(codes_ref[at], rows_full[...].reshape(D, 128))
        embedded_ref[at] = values
        center = values - jnp.sum(values, axis=1, keepdims=True) * (1.0 / D)
        rate = lax.rsqrt(jnp.sum(center * center, axis=1, keepdims=True) * (1.0 / D) + NORM_EPSILON)
        unit[at] = center * rate

    masking = iter(range(8))
    steps = iter(range(gather.steps))
    for t in range(6):
        small.step(t)
        gather.step(next(steps))
        if t < 5:
            masks(next(masking), tokens // 8)
    tag_sums[...] = jnp.sum(tags_full[...].reshape(32, 8, 128), axis=0)
    low = jnp.bfloat16
    class_tables = tables_ref[:, :D].astype(low)
    for order, target in ((DIMS, None), (("x", "y", "w", "u", "c"), part)):
        hot = hot_of(slot_labels(tags_full, order))
        cond = dot_last(hot[:, :D], class_tables)
        act = (cond / (1.0 + jnp.exp(-cond))).astype(low)
        if target is None:
            hot_ref[...], cond_ref[...], act_ref[...] = hot, cond, act
        else:
            target[...] = dot_plain(act, ada_ref[...].astype(low)).reshape(2, 2, 2, 8, 6 * D)
    vectors_ref[...] = rows_full[...].reshape(D, 128).astype(jnp.float32).T[0:16]
    for stage in range(6):
        mod_step(stage)
        for step in steps:
            gather.step(step)
            break
        if stage < 4:
            embed(stage)
        for index in masking:
            masks(index, tokens // 8)
            break
    for step in steps:
        gather.step(step)
    store_qkv = pltpu.make_async_copy(qkv_full, qkv_out, copy_sems.at[2])
    store_qkv.start()
    spot = 4 * bit["u"] + 2 * bit["c"]
    row_ids = lax.broadcasted_iota(jnp.int32, (8, D), 0)
    for kind in range(6):
        at = (kind % 3) * D
        group = mod_sums[4][kind // 3, :, at : at + D]
        for slot in range(2):
            row = jnp.sum(jnp.where(row_ids == spot + slot, group, 0.0), axis=0, keepdims=True)
            modulation_ref[slot : slot + 1, kind * D : (kind + 1) * D] = row + vectors_ref[kind : kind + 1]
    stores = []
    for index in range(4):
        at = slice(index * block, (index + 1) * block)
        other = token_columns[at, 0:1] > 0.5
        scale = jnp.where(other, modulation_ref[1:2, 2 * D : 3 * D], modulation_ref[0:1, 2 * D : 3 * D])
        shift = jnp.where(other, modulation_ref[1:2, 4 * D : 5 * D], modulation_ref[0:1, 4 * D : 5 * D])
        normed = (unit[at] * (1.0 + scale) + shift).astype(low)
        normed_ref[at] = normed
        if index >= 2:
            stores[index - 2].wait()
        for column in range(0, 3 * D, 512):
            weight = qkv_full[:, :, :, :, :, :, column : column + 512].reshape(D, 512)
            staged[index % 2, :, column : column + 512] = dot_plain(normed, weight)
        stores.append(
            pltpu.make_async_copy(
                staged.at[index % 2], projected_ref.at[pl.ds(index * block, block)], copy_sems.at[index % 2]
            )
        )
        stores[index].start()
    stores[2].wait()
    stores[3].wait()
    store_qkv.wait()


def begin(rows, tags, tables, ada_weight, qkv_weight, out_weight, codes, token_columns, token_rows):
    depth = rows.shape[0]
    tokens = codes.shape[0]
    f32, low = jnp.float32, jnp.bfloat16
    dma = pltpu.SemaphoreType.DMA
    lanes = 3 * D
    lands = [
        pltpu.VMEM((2, 2, 2, 8, lanes), f32),
        pltpu.VMEM((2, 2, 8, lanes), f32),
    ] + [pltpu.VMEM((2, 8, lanes), f32)] * 3
    shape = jax.ShapeDtypeStruct
    return pl.pallas_call(
        begin_kernel,
        out_shape=(
            shape((tokens, 3 * D), f32),
            shape(FIVE + (depth, 3 * D), low),
            shape(FIVE + (depth, D), low),
            shape((tokens, D), f32),
            shape((tokens, D), low),
            shape((2, 6 * D), f32),
            shape((16, D), f32),
            shape((64, 1152), low),
            shape((64, depth), f32),
            shape((64, depth), low),
            shape((8, 128), f32),
            shape((tokens, tokens), f32),
            shape((tokens, tokens), f32),
        ),
        in_specs=[WHOLE] * 9,
        out_specs=(ANY, ANY, ANY) + (WHOLE,) * 10,
        scratch_shapes=[
            pltpu.VMEM(FIVE + (depth, 128), low),
            pltpu.VMEM(FIVE + (8, 128), f32),
            pltpu.VMEM((depth, 3 * D), low),
            pltpu.VMEM((depth, D), low),
            pltpu.VMEM(FIVE + (depth, 3 * D), low),
            pltpu.VMEM((2, 2, 2, 8, 6 * D), f32),
            pltpu.VMEM((tokens, D), f32),
            pltpu.VMEM((2, tokens // 4, 3 * D), f32),
            dma((3,)),
            dma((5, 2)),
            dma((5, 2)),
        ]
        + lands
        + lands
        + Gather.scratch()
        + Gather.scratch(FIRST_LAG),
        compiler_params=params(0),
        name="begin",
    )(rows, tags, tables, ada_weight, qkv_weight, out_weight, codes, token_columns, token_rows)


def head_mean(values):
    low_lane = lax.broadcasted_iota(jnp.int32, values.shape, 1) < HEAD_DIM
    low_sum = jnp.sum(jnp.where(low_lane, values, 0.0), axis=1, keepdims=True)
    high_sum = jnp.sum(jnp.where(low_lane, 0.0, values), axis=1, keepdims=True)
    return jnp.where(low_lane, low_sum, high_sum) * (1.0 / HEAD_DIM)


def of_head(values, head):
    low_lane = lax.broadcasted_iota(jnp.int32, values.shape, 1) < HEAD_DIM
    zero = jnp.zeros_like(values)
    return jnp.where(low_lane, values, zero) if head == 0 else jnp.where(low_lane, zero, values)


def dot_last(left, right):
    return lax.dot_general(left, right, (((1,), (1,)), ((), ())), preferred_element_type=jnp.float32)


def dot_first(left, right):
    return lax.dot_general(left, right, (((0,), (0,)), ((), ())), preferred_element_type=jnp.float32)


def dot_plain(left, right):
    return lax.dot_general(left, right, (((1,), (0,)), ((), ())), preferred_element_type=jnp.float32)


UNITS = 4


def normed_head(raw, gain):
    return (raw * lax.rsqrt(head_mean(raw * raw) + NORM_EPSILON) * gain).astype(jnp.bfloat16)


def attend_kernel(linked, q_ref, k_ref, v_ref, gain_ref, bias_ref, *refs):
    if linked:
        down_own, mixed_ref, exact_ref, total_ref, down_full, qn, kn, vn = refs[:8]
        sems = refs[8:]
        place = Place()
        width = ATTEND_WIDTH
        split = D // (2 * width)
        depth = down_full.shape[6]
        parts = down_full.shape[5]

        def down_source(j, p):
            part, column = lax.div(j, split), lax.rem(j, split)
            return down_own.at[
                pl.ds(pl.multiple_of(part * depth, depth), depth), columns((2 * column + p) * width, width)
            ]

        def down_target(j, p, r):
            part, column = lax.div(j, split), lax.rem(j, split)
            return down_full.at[r + (part, slice(None), columns((2 * column + p) * width, width))]

        gather = Gather(place, [(0, split * parts, down_source, down_target)], *sems, lag=ATTEND_LAG)
        pl.when(pl.program_id(0) == 0)(place.meet)
    else:
        mixed_ref, exact_ref, total_ref, qn, kn, vn = refs
    qn[...] = normed_head(q_ref[...], gain_ref[0:1])
    kn[...] = normed_head(k_ref[...], gain_ref[1:2])
    vn[...] = v_ref[...].astype(jnp.bfloat16)
    tokens = q_ref.shape[0]
    both, sums = [], []
    for head in range(2):
        query = of_head(qn[...], head)
        mixed = jnp.zeros((tokens, 128), jnp.float32)
        lanes = jnp.zeros((tokens, 128), jnp.float32)
        for order in range(UNITS // 2):
            if linked:
                gather.step(pl.program_id(0) * UNITS + head * (UNITS // 2) + order)
            size = tokens // (UNITS // 2)
            keys = slice(order * size, (order + 1) * size)
            raised = jnp.exp2(dot_last(query, kn[keys]) * EXP_SCALE + bias_ref[:, keys])
            for lane in range(0, size, 128):
                lanes = lanes + raised[:, lane : lane + 128]
            mixed = mixed + dot_plain(raised.astype(jnp.bfloat16), vn[keys])
        total = jnp.sum(lanes, axis=1, keepdims=True)
        both.append(mixed * (1.0 / total))
        sums.append(total)
    low_lane = lax.broadcasted_iota(jnp.int32, both[0].shape, 1) < HEAD_DIM
    exact = jnp.where(low_lane, both[0], both[1])
    mixed_ref[...] = exact.astype(jnp.bfloat16)
    exact_ref[...] = exact
    total_ref[...] = jnp.log2(jnp.where(low_lane, sums[0], sums[1]))

    if linked:
        finish(gather)


def attend(projected, gains, bias, down_own=None, depth=None):
    tokens = projected.shape[0]
    pair = pl.BlockSpec((tokens, 128), lambda i: (0, i))
    specs = [
        pair,
        pl.BlockSpec((tokens, 128), lambda i: (0, i + 8)),
        pl.BlockSpec((tokens, 128), lambda i: (0, i + 16)),
        pl.BlockSpec((8, 128), lambda i: (0, i)),
        pl.BlockSpec((tokens, tokens), lambda i: (0, 0), pipeline_mode=pl.Buffered(1)),
    ]
    outs = [jax.ShapeDtypeStruct((tokens, D), kind) for kind in (jnp.bfloat16, jnp.float32, jnp.float32)]
    out_specs = [pair] * 3
    scratch = [pltpu.VMEM((tokens, 128), jnp.bfloat16)] * 3
    operands = [projected, projected, projected, gains, bias]
    linked = down_own is not None
    if linked:
        specs += [ANY]
        operands += [down_own]
        outs += [jax.ShapeDtypeStruct(FIVE + (down_own.shape[0] // depth, depth, D), jnp.bfloat16)]
        out_specs += [ANY]
        scratch = scratch + Gather.scratch(ATTEND_LAG)
    return pl.pallas_call(
        partial(attend_kernel, linked),
        grid=(HEADS // 2,),
        out_shape=tuple(outs),
        in_specs=specs,
        out_specs=tuple(out_specs),
        scratch_shapes=scratch,
        compiler_params=params(2) if linked else pltpu.CompilerParams(vmem_limit_bytes=VMEM_GRANT),
        name="attention_forward",
    )(*operands)


def attend_back_kernel(linked, q_ref, k_ref, v_ref, m_ref, exact_ref, total_ref, gain_ref, bias_ref, *refs):
    if linked:
        head_ref, up_ref, down_ref, grad_ref, gain_grad_ref, done_ref = refs[:6]
        qn, kn, vn, dk, dv, turned, dq_turned, key_turned = refs[6:14]
        place = Place()
        width = BACK_WIDTH
        wide = up_ref.shape[6] // (2 * width)
        narrow = down_ref.shape[7] // (2 * width)
        parts = down_ref.shape[5]

        def columns_of(ref, first):
            return lambda j, p, core: ref.at[
                :, :, :, :, core, :, columns((2 * (j - first) + p) * width, width)
            ]

        def down_source(j, p, core):
            spread = j - 2 * wide
            part, column = lax.div(spread, narrow), lax.rem(spread, narrow)
            return down_ref.at[:, :, :, :, core, part, :, columns((2 * column + p) * width, width)]

        def store(j, parity, total):
            done_ref[j, :, parity * width : (parity + 1) * width] = total

        pairs = 2 * wide + parts * narrow
        scatter = Scatter(
            place,
            [
                (0, wide, columns_of(head_ref, 0)),
                (wide, 2 * wide, columns_of(up_ref, wide)),
                (2 * wide, pairs, down_source),
            ],
            store,
            refs[14:],
            lag=BACK_LAG,
        )
        pl.when(pl.program_id(0) == 0)(place.meet)
    else:
        grad_ref, gain_grad_ref = refs[:2]
        qn, kn, vn, dk, dv, turned, dq_turned, key_turned = refs[2:]
    qn[...] = normed_head(q_ref[...], gain_ref[0:1])
    kn[...] = normed_head(k_ref[...], gain_ref[1:2])
    vn[...] = v_ref[...].astype(jnp.bfloat16)
    for head in range(2):
        key_turned[head] = of_head(kn[...], head).T
    turned[0] = total_ref[...].T
    turned[1] = (head_mean(m_ref[...].astype(jnp.float32) * exact_ref[...]) * HEAD_DIM).T
    tokens = q_ref.shape[0]
    size = tokens // (UNITS // 2)
    for head in range(2):
        query = of_head(qn[...], head)
        mixed = of_head(m_ref[...], head)
        at = head * HEAD_DIM
        total = turned[0, at : at + 1]
        center = turned[1, at : at + 1]
        for order in range(UNITS // 2):
            if linked:
                scatter.step(pl.program_id(0) * UNITS + head * (UNITS // 2) + order)
            keys = slice(order * size, (order + 1) * size)
            scores = dot_last(kn[keys], query) * EXP_SCALE + (bias_ref[keys] - total)
            probs = jnp.exp2(scores)
            prob_grad = dot_last(vn[keys], mixed)
            score_grad = (probs * (prob_grad - center)).astype(jnp.bfloat16)
            key_part = dot_plain(score_grad, query)
            value_part = dot_plain(probs.astype(jnp.bfloat16), mixed)
            query_part = dot_plain(key_turned[head, :, keys], score_grad)
            dk[keys] = key_part if head == 0 else dk[keys] + key_part
            dv[keys] = value_part if head == 0 else dv[keys] + value_part
            dq_turned[...] = query_part if head == 0 and order == 0 else dq_turned[...] + query_part

    gain_rows = []
    for place_at, raw_ref, grad in ((0, q_ref, dq_turned[...].T), (1, k_ref, dk[...])):
        raw = raw_ref[...]
        normed_grad = grad * SCORE_SCALE
        rate = lax.rsqrt(head_mean(raw * raw) + NORM_EPSILON)
        scaled = gain_ref[place_at : place_at + 1] * normed_grad
        back = rate * scaled - raw * (rate * rate * rate) * head_mean(raw * scaled)
        grad_ref[place_at] = back.astype(jnp.bfloat16)
        gain_rows.append(jnp.sum(normed_grad * raw * rate, axis=0, keepdims=True))
    grad_ref[2] = dv[...].astype(jnp.bfloat16)
    gain_grad_ref[...] = jnp.concatenate(gain_rows + [jnp.zeros((6, 128), jnp.float32)], axis=0)
    if linked:
        finish(scatter)


def attend_back(projected, mixed_grad, exact, totals, gains, bias, head_grad=None, up_grad=None, down_grad=None):
    tokens = projected.shape[0]
    pair = pl.BlockSpec((tokens, 128), lambda i: (0, i))
    specs = [
        pair,
        pl.BlockSpec((tokens, 128), lambda i: (0, i + 8)),
        pl.BlockSpec((tokens, 128), lambda i: (0, i + 16)),
        pair,
        pair,
        pair,
        pl.BlockSpec((8, 128), lambda i: (0, i)),
        pl.BlockSpec((tokens, tokens), lambda i: (0, 0), pipeline_mode=pl.Buffered(1)),
    ]
    outs = [
        jax.ShapeDtypeStruct((3, tokens, D), jnp.bfloat16),
        jax.ShapeDtypeStruct((8, D), jnp.float32),
    ]
    out_specs = [
        pl.BlockSpec((3, tokens, 128), lambda i: (0, 0, i)),
        pl.BlockSpec((8, 128), lambda i: (0, i)),
    ]
    scratch = [pltpu.VMEM((tokens, 128), jnp.bfloat16)] * 3 + [
        pltpu.VMEM((tokens, 128), jnp.float32)
    ] * 2
    scratch += [
        pltpu.VMEM((2, 128, tokens), jnp.float32),
        pltpu.VMEM((128, tokens), jnp.float32),
        pltpu.VMEM((2, 128, tokens), jnp.bfloat16),
    ]
    operands = [projected, projected, projected, mixed_grad, exact, totals, gains, bias]
    linked = head_grad is not None
    if linked:
        depth = head_grad.shape[5]
        specs += [ANY, ANY, ANY]
        operands += [head_grad, up_grad, down_grad]
        pairs = (head_grad.shape[6] + up_grad.shape[6] + down_grad.shape[5] * down_grad.shape[7]) // (2 * BACK_WIDTH)
        outs += [jax.ShapeDtypeStruct((pairs, depth, 2 * BACK_WIDTH), jnp.float32)]
        out_specs += [WHOLE]
        scratch = scratch + Scatter.scratch((depth, BACK_WIDTH), jnp.bfloat16, BACK_LAG)
    return pl.pallas_call(
        partial(attend_back_kernel, linked),
        grid=(HEADS // 2,),
        out_shape=tuple(outs),
        in_specs=specs,
        out_specs=tuple(out_specs),
        scratch_shapes=scratch,
        compiler_params=params(3) if linked else pltpu.CompilerParams(vmem_limit_bytes=VMEM_GRANT),
        name="attention_backward",
    )(*operands)


WEIGHT_COLUMNS = (CLASSES + CODE_DIM + LEVELS, 9, 6 * D, 3 * D, D, 4 * D, D, CODES)
SUM_STARTS = (0, None, 1152, 1152 + 6144, 1152 + 9216, 1152 + 10240, 1152 + 14336, 1152 + 15360)
SCALARS = 1152 + 19456
SUM_LANES = SCALARS + 128
SMALL_LANES = CODE_DIM + LEVELS + 9
DECAY = 1.0 - STEP ** (-0.8)


def three_terms(values):
    high = values.astype(jnp.bfloat16)
    rest = values - high.astype(jnp.float32)
    middle = rest.astype(jnp.bfloat16)
    return high, middle, (rest - middle.astype(jnp.float32)).astype(jnp.bfloat16)


def lane_row(scalars):
    lanes = lax.broadcasted_iota(jnp.int32, (1, 128), 1)
    row = jnp.zeros((1, 128), jnp.float32)
    for lane, value in scalars:
        row = jnp.where(lanes == lane, value, row)
    return row


def whole_sum(values):
    return jnp.sum(jnp.sum(values, axis=0, keepdims=True), axis=1, keepdims=True)


def weight_tiles(tables_grad, ada_grad, done_attention, done_last, depth):
    def blocks(ref, first, count, width):
        return [(lambda at=first + i: ref[at], i * width, width) for i in range(count)]

    near, far = 2 * LAST_WIDTH, 2 * BACK_WIDTH
    tables_columns = WEIGHT_COLUMNS[0]
    wide = CODES // far
    return {
        0: [(0, [(lambda: tables_grad[:, :tables_columns], 0, tables_columns)])],
        2: [(1, [(lambda: ada_grad[...], 0, 6 * D)])],
        3: [(2, blocks(done_last, D // near, 3 * D // near, near))],
        4: [(3, blocks(done_last, 0, D // near, near))],
        5: [(4, blocks(done_attention, wide, wide, far))],
        6: [(6 + part, blocks(done_attention, 2 * wide + part * (D // far), D // far, far)) for part in range(4)],
        7: [(5, blocks(done_attention, 0, wide, far))],
    }


class Total:
    def __init__(self, place, sums, land, sends, recvs):
        self.place, self.sums, self.land = place, sums, land
        self.sends, self.recvs = sends, recvs

    @staticmethod
    def scratch(lanes):
        dma = pltpu.SemaphoreType.DMA
        return [
            pltpu.VMEM((6, 1, lanes), jnp.float32),
            pltpu.VMEM((5, 1, lanes), jnp.float32),
            dma((5,)),
            dma((5,)),
        ]

    def run(self):
        for stage, dim in enumerate(DIMS):
            copy = self.place.send(
                self.sums.at[stage], self.land.at[stage], self.sends.at[stage], self.recvs.at[stage], dim
            )
            copy.start()
            copy.wait()
            self.sums[stage + 1] = self.sums[stage] + self.land[stage]


def last_kernel(
    out_ref,
    qkv_low,
    embedded_ref,
    grad_ref,
    heads_grad,
    normed_ref,
    codes_ref,
    second_ref,
    scale_ref,
    known_ref,
    gains_ref,
    act_ref,
    cond_ref,
    hot_ref,
    loss_ref,
    attention_ref,
    tables_ref,
    vectors_ref,
    ada_ref,
    qkv_master,
    out_master,
    up_master,
    down_master,
    head_master,
    moments_ref,
    vector_moment_ref,
    column_moment_ref,
    done_ref,
    small_done,
    tables_grad,
    ada_grad,
    rows_ref,
    columns_ref,
    facts_ref,
    *scratch,
):
    place = Place()
    place.meet()
    devices = lax.axis_size(AXES)
    depth = tables_ref.shape[0]
    width = LAST_WIDTH
    narrow = D // (2 * width)
    part_grads, qkv_full, embedded, grad, code_sums, mod_ref, small_ref, load_sems = scratch[40:48]
    loads = [
        pltpu.make_async_copy(source, target, load_sems.at[i])
        for i, (source, target) in enumerate(
            ((qkv_low, qkv_full), (embedded_ref, embedded), (grad_ref, grad))
        )
    ]
    for load in loads:
        load.start()

    def columns_of(ref, first):
        return lambda j, p, core: ref.at[
            :, :, :, :, core, :, columns((2 * (j - first) + p) * width, width)
        ]

    def store(j, parity, total):
        done_ref[j, :, parity * width : (parity + 1) * width] = total

    pairs = 4 * narrow
    scatter = Scatter(
        place,
        [(0, narrow, columns_of(out_ref, 0))]
        + [
            ((1 + part) * narrow, (2 + part) * narrow, columns_of(part_grads.at[part], (1 + part) * narrow))
            for part in range(3)
        ],
        store,
        scratch[:13],
        lag=LAST_LAG,
    )
    half = depth // 2

    def small_store(j, parity, total):
        small_done[pl.ds(parity * half, half)] = total

    small = Scatter(
        place,
        [(0, 1, lambda j, p, core: small_ref.at[:, :, :, :, core, pl.ds(p * half, half)])],
        small_store,
        scratch[13:26],
    )
    mod_sums, mod_land, mod_all, mod_sends, mod_recvs = scratch[26:31]
    bit = place.bit

    def mod_copy(stage):
        dim = ("c", "x", "y", "u", "w")[stage]
        if stage < 3:
            source, target = (mod_ref, mod_sums.at[0], mod_sums.at[1])[stage], mod_land.at[stage]
        elif stage == 3:
            source = target = mod_all.at[bit["w"], bit["u"]]
        else:
            source = target = mod_all.at[bit["w"]]
        return place.send(source, target, mod_sends.at[stage], mod_recvs.at[stage], dim)

    def mod_step(stage):
        if stage:
            mod_copy(stage - 1).wait()
        if stage == 1:
            mod_sums[0] = mod_ref[...] + mod_land[0]
        elif stage == 2:
            mod_sums[1] = mod_sums[0] + mod_land[1]
        elif stage == 3:
            mod_all[bit["w"], bit["u"]] = mod_sums[1] + mod_land[2]
        if stage < 5:
            mod_copy(stage).start()

    first_total = Total(place, *scratch[31:35])
    second_total = Total(place, *scratch[35:39])
    sums, facts = first_total.sums, scratch[39]
    tiles = weight_tiles(tables_grad, ada_grad, attention_ref, done_ref, depth)
    masters = (
        tables_ref,
        vectors_ref,
        ada_ref,
        qkv_master,
        out_master,
        up_master,
        down_master,
        head_master,
    )

    def ada_part():
        slots = mod_all[...].reshape(2 * devices, 6 * D)
        ada_grad[...] = dot_first(act_ref[...], slots)
        activated_grad = dot_last(slots, ada_ref[...].astype(jnp.bfloat16))
        cond = cond_ref[...]
        gate = 1.0 / (1.0 + jnp.exp(-cond))
        cond_grad = activated_grad * (gate * (1.0 + cond * (1.0 - gate)))
        shape = (128, hot_ref.shape[1])
        source = lax.broadcasted_iota(jnp.int32, shape, 0)
        target = lax.broadcasted_iota(jnp.int32, shape, 1)
        moved = (target == source + (CLASSES - 9)) & (source >= 9) & (source < SMALL_LANES)
        shift = jnp.where(moved, 1.0, 0.0).astype(jnp.bfloat16)
        total = jnp.zeros((depth, hot_ref.shape[1]), jnp.float32)
        for term in three_terms(cond_grad)[::-1]:
            total = total + dot_first(term, hot_ref[...])
        for term in three_terms(small_done[...])[::-1]:
            total = total + dot_plain(term, shift)
        tables_grad[...] = total

    def stats(position):
        row_total = jnp.zeros((1, 1), jnp.float32)
        for index, group in tiles[position]:
            row_sum = jnp.zeros((depth, 1), jnp.float32)
            for load, first, size in group:
                gradient = load()
                squared = gradient * gradient + TINY_SQUARE
                row_sum = row_sum + jnp.sum(squared, axis=1, keepdims=True)
                at = SUM_STARTS[position] + first
                sums[0, :, at : at + size] += jnp.sum(squared, axis=0, keepdims=True)
            rows_new = DECAY * moments_ref[index] + (1.0 - DECAY) * (
                row_sum * (1.0 / WEIGHT_COLUMNS[position])
            )
            rows_ref[index] = rows_new
            row_total = row_total + jnp.sum(rows_new, axis=0, keepdims=True)
        facts[...] += lane_row([(position, row_total)])

    def squares(first, end):
        for position in range(first, end):
            master = masters[position][...]
            facts[...] += lane_row([(8 + position, whole_sum(master * master))])

    def part_grad(part):
        @pl.loop(0, D // 256)
        def tile(i):
            at = columns(i * 256, 256)
            product = dot_first(normed_ref[...], heads_grad[part, :, at])
            part_grads[part, :, :, :, :, :, :, at] = product.astype(jnp.bfloat16).reshape(
                FIVE + (depth, 256)
            )

    tokens = normed_ref.shape[0]
    block = tokens // 4
    slot_rows = [jnp.zeros((1, D), jnp.float32)] * 4

    def norm_back(index):
        rows = slice(index * block, (index + 1) * block)
        back = jnp.zeros((block, D), jnp.float32)
        for part in range(3):
            back = back + dot_last(heads_grad[part, rows], qkv_full[:, part * D : (part + 1) * D])
        values = embedded[rows]
        center = values - jnp.sum(values, axis=1, keepdims=True) * (1.0 / D)
        rate = lax.rsqrt(jnp.sum(center * center, axis=1, keepdims=True) * (1.0 / D) + NORM_EPSILON)
        unit = center * rate
        other = second_ref[rows] > 0.5
        scale_back = back * unit
        for at, value in enumerate((scale_back, back)):
            everything = jnp.sum(value, axis=0, keepdims=True)
            second = jnp.sum(jnp.where(other, value, 0.0), axis=0, keepdims=True)
            slot_rows[2 * at] = slot_rows[2 * at] + (everything - second)
            slot_rows[2 * at + 1] = slot_rows[2 * at + 1] + second
        unit_back = back * (1.0 + jnp.where(other, scale_ref[1:2], scale_ref[0:1]))
        mean_back = jnp.sum(unit_back, axis=1, keepdims=True) * (1.0 / D)
        mean_along = jnp.sum(unit_back * unit, axis=1, keepdims=True) * (1.0 / D)
        total = grad[rows] + rate * (unit_back - mean_back - unit * mean_along)
        high = total.astype(jnp.bfloat16)
        rest = (total - high.astype(jnp.float32)).astype(jnp.bfloat16)
        product = dot_first(codes_ref[rows], high) + dot_first(codes_ref[rows], rest)
        code_sums[...] = product if index == 0 else code_sums[...] + product

    def gather_rows():
        spot = 2 * (4 * bit["y"] + 2 * bit["x"] + bit["c"])
        row_ids = lax.broadcasted_iota(jnp.int32, (16, D), 0)
        for kind in range(6):
            if kind in (2, 4):
                first, other = slot_rows[kind - 2 : kind]
            else:
                at = slice(kind * D, (kind + 1) * D)
                first, other = known_ref[0:1, at], known_ref[1:2, at]
            placed = jnp.where(row_ids == spot, first, jnp.where(row_ids == spot + 1, other, 0.0))
            mod_ref[:, kind * D : (kind + 1) * D] = placed.astype(jnp.bfloat16)
            code_sums[kind : kind + 1] = first + other
        code_sums[6:9] = gains_ref[0:3]
        small_ref[...] = code_sums[...].T.reshape(FIVE + (depth, 128))

    sums[0] = jnp.zeros_like(sums[0])
    facts[...] = lane_row([(16, loss_ref[...])])
    steps = iter(range(scatter.steps))
    for _ in range(narrow):
        scatter.step(next(steps))
    for part in range(3):
        part_grad(part)
        for _ in range(narrow):
            scatter.step(next(steps))
    for load in loads:
        load.wait()
    for index in range(4):
        norm_back(index)
        scatter.step(next(steps))
    gather_rows()
    beside = [
        partial(stats, 5),
        partial(stats, 6),
        partial(stats, 7),
        partial(squares, 0, 5),
        partial(squares, 5, 8),
    ]
    for t in range(6):
        mod_step(t)
        small.step(t)
        if t < len(beside):
            beside[t]()
        for step in steps:
            scatter.step(step)
            break
    for step in steps:
        scatter.step(step)
    ada_part()
    stats(0)
    stats(2)
    stats(3)
    stats(4)
    sums[0, :, SCALARS:] = facts[...]
    first_total.run()
    columns_ref[...] = DECAY * column_moment_ref[...] + (1.0 - DECAY) * sums[5] * (1.0 / D)
    start, end = SUM_STARTS[6], SUM_STARTS[6] + D
    columns_ref[:, start:end] = DECAY * column_moment_ref[:, start:end] + (1.0 - DECAY) * sums[
        5, :, start:end
    ] * (1.0 / (4 * D))

    def rows_all(position):
        return 4.0 * D if position == 6 else 1.0 * D

    scalars = []
    for position, groups in tiles.items():
        at = SCALARS + position
        row_mean = sums[5, :, at : at + 1] * (1.0 / rows_all(position))
        spread = jnp.zeros((1, 1), jnp.float32)
        for index, group in groups:
            for load, first, size in group:
                lane = SUM_STARTS[position] + first
                estimate = rows_ref[index] * columns_ref[:, lane : lane + size] / row_mean
                update = load() * lax.rsqrt(estimate)
                spread = spread + whole_sum(update * update)
        scalars.append((position, spread))
    gradient = small_done[:, :9]
    moment = DECAY * vector_moment_ref[...] + (1.0 - DECAY) * (gradient * gradient + TINY_SQUARE)
    update = gradient * lax.rsqrt(moment)
    scalars.append((1, whole_sum(update * update)))
    second_total.sums[0] = lane_row(scalars)
    second_total.run()
    spread_row, factor_row = [], []
    for position in range(8):
        count = rows_all(position) * WEIGHT_COLUMNS[position]
        spread = jnp.sqrt(second_total.sums[5, :, position : position + 1] * (1.0 / count))
        at = SCALARS + 8 + position
        scale = jnp.maximum(SCALE_FLOOR, jnp.sqrt(sums[5, :, at : at + 1] * (1.0 / count)))
        spread_row.append((position, spread))
        factor_row.append((position, STEP_RATE * scale / jnp.maximum(1.0, spread / CLIP_LIMIT)))
    facts_ref[0] = lane_row(spread_row)
    facts_ref[1] = lane_row(factor_row)
    facts_ref[2] = sums[5, :, SCALARS:]


def last_exchange(far, near, attention_done, masters, moments):
    depth = far[0].shape[5]
    pairs = 4 * D // (2 * LAST_WIDTH)
    dma = pltpu.SemaphoreType.DMA
    f32, low = jnp.float32, jnp.bfloat16
    tokens = far[2].shape[0]
    operands = list(far) + list(near) + [attention_done] + list(masters) + list(moments)
    return pl.pallas_call(
        last_kernel,
        out_shape=(
            jax.ShapeDtypeStruct((pairs, depth, 2 * LAST_WIDTH), f32),
            jax.ShapeDtypeStruct((depth, 128), f32),
            jax.ShapeDtypeStruct((depth, 1152), f32),
            jax.ShapeDtypeStruct((depth, 6 * D), f32),
            jax.ShapeDtypeStruct((10, depth, 1), f32),
            jax.ShapeDtypeStruct((1, SUM_LANES), f32),
            jax.ShapeDtypeStruct((3, 1, 128), f32),
        ),
        in_specs=[ANY] * 4 + [WHOLE] * (len(operands) - 4),
        out_specs=(WHOLE,) * 7,
        scratch_shapes=Scatter.scratch((depth, LAST_WIDTH), low, LAST_LAG)
        + Scatter.scratch((depth // 2, 128), f32)
        + [
            pltpu.VMEM((2, 16, 6 * D), low),
            pltpu.VMEM((3, 16, 6 * D), low),
            pltpu.VMEM((2, 2, 16, 6 * D), low),
            dma((5,)),
            dma((5,)),
        ]
        + Total.scratch(SUM_LANES)
        + Total.scratch(128)
        + [pltpu.VMEM((1, 128), f32)]
        + [
            pltpu.VMEM((3,) + FIVE + (depth, D), low),
            pltpu.VMEM((D, 3 * D), low),
            pltpu.VMEM((tokens, D), f32),
            pltpu.VMEM((tokens, D), f32),
            pltpu.VMEM((128, D), f32),
            pltpu.VMEM((16, 6 * D), low),
            pltpu.VMEM(FIVE + (depth, 128), f32),
            dma((3,)),
        ],
        compiler_params=params(4),
        name="last_scatter",
    )(*operands)


def step_kernel(
    done_ref,
    small_ref,
    tables_grad,
    ada_grad,
    rows_ref,
    columns_ref,
    facts_ref,
    attention_ref,
    vector_moment_ref,
    tables_ref,
    vectors_ref,
    ada_ref,
    qkv_master,
    out_master,
    up_master,
    down_master,
    head_master,
    *outs,
):
    depth = tables_ref.shape[0]
    masters = (
        tables_ref,
        vectors_ref,
        ada_ref,
        qkv_master,
        out_master,
        up_master,
        down_master,
        head_master,
    )
    vector_stat = outs[16]
    tiles = weight_tiles(tables_grad, ada_grad, attention_ref, done_ref, depth)
    for position, groups in tiles.items():
        grad_ref, next_ref, master = outs[2 * position], outs[2 * position + 1], masters[position]
        factor = facts_ref[1, :, position : position + 1]
        mean_scale = 1.0 / (4 * D) if position == 6 else 1.0 / D
        row_mean = facts_ref[2, :, position : position + 1] * mean_scale
        for order, (index, group) in enumerate(groups):
            at = slice(order * depth, (order + 1) * depth)
            for load, first, size in group:
                gradient = load()
                lane = SUM_STARTS[position] + first
                estimate = rows_ref[index] * columns_ref[:, lane : lane + size] / row_mean
                grad_ref[at, first : first + size] = gradient
                next_ref[at, first : first + size] = master[at, first : first + size] - factor * (
                    gradient * lax.rsqrt(estimate)
                )
    gradient = small_ref[:, :9]
    moment = DECAY * vector_moment_ref[...] + (1.0 - DECAY) * (gradient * gradient + TINY_SQUARE)
    vector_stat[...] = moment
    outs[2][...] = gradient
    outs[3][...] = vectors_ref[...] - facts_ref[1, :, 1:2] * (gradient * lax.rsqrt(moment))


def take_step(last, attention_done, vector_moment, masters):
    operands = list(last) + [attention_done, vector_moment] + list(masters)
    shapes = []
    for master in masters:
        shapes += [jax.ShapeDtypeStruct(master.shape, jnp.float32)] * 2
    shapes.append(jax.ShapeDtypeStruct(vector_moment.shape, jnp.float32))
    return pl.pallas_call(
        step_kernel,
        out_shape=tuple(shapes),
        in_specs=[WHOLE] * len(operands),
        out_specs=(WHOLE,) * len(shapes),
        compiler_params=pltpu.CompilerParams(vmem_limit_bytes=VMEM_GRANT),
        name="weight_step",
    )(*operands)


def linked_mesh():
    return lax.axis_size("fsdp") == 8 and lax.axis_size("sub") == 4


def gathered(values):
    return lax.all_gather(values, AXES, axis=0, tiled=True)


def scattered(values):
    return lax.psum_scatter(values, AXES, scatter_dimension=0, tiled=True)


def layer_norm(values):
    center = values - jnp.mean(values, axis=-1, keepdims=True)
    return center * lax.rsqrt(jnp.mean(center * center, axis=-1, keepdims=True) + NORM_EPSILON)


def modulate(values, scale_part, shift_part):
    return layer_norm(values) * (1.0 + scale_part) + shift_part


def final_norm(values, gain_vector):
    return layer_norm(values) * gain_vector


def attention_bias(query, key):
    usable = (query[1] == key[1]) & (key[0] <= query[0]) & ((key[2] == 1) | (query[3] == key[3]))
    return jnp.where(usable, 0.0, MASK_VALUE)


def split_product(left_side, right_low):
    high = left_side.astype(jnp.bfloat16)
    rest = (left_side - high.astype(jnp.float32)).astype(jnp.bfloat16)
    return bfloat_product(high, right_low) + bfloat_product(rest, right_low)


def on_device(
    code_vectors,
    scale_ids,
    segment_ids,
    real_mask,
    labels,
    targets,
    loss_weight,
    tables,
    vectors,
    ada_weight,
    qkv_weight,
    out_weight,
    up_weight,
    down_weight,
    head_weight,
    tables_moment,
    ada_moment,
    qkv_moment,
    out_moment,
    up_moment,
    down_moment,
    head_moment,
    vector_moment,
    column_moment,
):
    devices = lax.axis_size(AXES)
    linked = linked_mesh()
    depth = tables.shape[0]
    tokens = code_vectors.shape[0]
    masters = (
        tables,
        vectors,
        ada_weight,
        qkv_weight,
        out_weight,
        up_weight,
        down_weight,
        head_weight,
    )
    local_count = jnp.sum(loss_weight).astype(jnp.float32)
    low = jnp.bfloat16
    part_kind = low if linked else jnp.float32
    tables_low = tables.astype(low)
    ada_low = ada_weight.astype(low)
    qkv_low = qkv_weight.astype(low)
    out_low = out_weight.astype(low)
    down_low = down_weight.astype(low)

    full_up = gathered(up_weight.astype(low))
    full_head = gathered(head_weight.astype(low))
    small_rows = jnp.concatenate(
        [vectors.astype(low), tables_low[:, CLASSES:], jnp.zeros((depth, 128 - SMALL_LANES), low)], axis=1
    )
    tag_row = jnp.concatenate([labels.astype(jnp.float32), local_count[None], jnp.zeros((5,), jnp.float32)])
    tags = jnp.broadcast_to(tag_row[:, None], (8, 128))
    level_hot = (scale_ids[:, None] == jnp.arange(LEVELS)[None, :]).astype(low)
    code_levels = jnp.concatenate([code_vectors, level_hot], axis=1)
    codes = jnp.pad(code_levels, ((0, 0), (9, 128 - SMALL_LANES)))
    second = (segment_ids == 1)[:, None]
    if linked:
        token_rows = jnp.stack([segment_ids, scale_ids, real_mask] + [real_mask] * 5).astype(jnp.float32)
        token_columns = jnp.pad(token_rows[:3].T, ((0, 0), (0, 125)))
        (
            projected,
            full_qkv,
            full_out,
            embedded,
            normed,
            modulation,
            vector_rows,
            label_hot,
            class_cond,
            activated,
            tag_sums,
            bias,
            turned_bias,
        ) = begin(
            small_rows, tags, tables, ada_weight, qkv_weight, out_weight, codes, token_columns, token_rows
        )
        full_qkv, full_out = full_qkv.reshape(D, 3 * D), full_out.reshape(D, D)
        weight_total = tag_sums[2, 0]
        gains = vector_rows[6:14]
        head_gain = vector_rows[8]
    else:
        small_full = gathered(small_rows)
        tags_full = gathered(tags).reshape(devices, 8, 128)[:, :, 0]
        labels_all = tags_full[:, :2].reshape(2 * devices)
        weight_total = jnp.sum(tags_full[:, 2])
        gain_vector = small_full[:, :9].astype(jnp.float32)
        label_hot = (labels_all[:, None] == jnp.arange(1152, dtype=jnp.float32)[None, :]).astype(low)
        class_cond = bfloat_product(label_hot[:, :CLASSES], tables_low[:, :CLASSES].T)
        activated = jax.nn.silu(class_cond).astype(low)
        own_modulation, full_qkv = scattered(bfloat_product(activated, ada_low)), gathered(qkv_low)
        modulation = own_modulation + gain_vector[:, :6].T.reshape(1, 6 * D)
        embedded = bfloat_product(codes, small_full.T)
        gains = jnp.pad(gain_vector[:, 6:8].T, ((0, 6), (0, 0)))
        head_gain = gain_vector[:, 8]

    def of_token(block):
        piece = modulation[:, block * D : (block + 1) * D]
        return jnp.where(second, piece[1:2], piece[0:1])

    gamma_one, gamma_two, scale_one, scale_two, shift_one, shift_two = (
        of_token(block) for block in range(6)
    )
    if linked:
        mixed_heads, exact, totals, full_down = attend(projected, gains, bias, down_low, depth)
        full_down = full_down.reshape(-1, D)
    else:
        normed = modulate(embedded, scale_one, shift_one).astype(low)
        projected = bfloat_product(normed, full_qkv)
        places = jnp.arange(tokens)
        masks = (scale_ids, segment_ids, real_mask, places)
        bias = attention_bias([m[:, None] for m in masks], [m[None, :] for m in masks])
        turned_bias = attention_bias([m[None, :] for m in masks], [m[:, None] for m in masks])
        mixed_heads, exact, totals = attend(projected, gains, bias)
        full_out, full_down = gathered(out_low), gathered(down_low)
    attended = bfloat_product(mixed_heads, full_out)
    residual_one = embedded + gamma_one * attended
    normed_two = modulate(residual_one, scale_two, shift_two).astype(low)
    hidden_pre = bfloat_product(normed_two, full_up)
    hidden_act = jax.nn.gelu(hidden_pre, approximate=True).astype(low)
    branch = bfloat_product(hidden_act, full_down)
    residual_two = residual_one + gamma_two * branch
    final_normed = final_norm(residual_two, head_gain).astype(low)
    logits = bfloat_product(final_normed, full_head)
    logit_peak = jnp.max(logits, axis=-1, keepdims=True)
    log_total = logit_peak + jnp.log(jnp.sum(jnp.exp(logits - logit_peak), axis=-1, keepdims=True))
    target_hot = targets[:, None] == jnp.arange(CODES)[None, :]
    picked = jnp.sum(jnp.where(target_hot, logits, 0.0), axis=-1, keepdims=True)
    weight_column = loss_weight.astype(jnp.float32)[:, None]
    local_loss = jnp.sum(weight_column * (log_total - picked))
    logit_grad = (
        (jnp.exp(logits - log_total) - target_hot.astype(jnp.float32))
        * (weight_column / weight_total)
    ).astype(low)

    head_part = bfloat_product(final_normed.T, logit_grad).astype(part_kind)
    final_grad = bfloat_product(logit_grad, full_head.T)
    _, final_back = jax.vjp(final_norm, residual_two, head_gain)
    residual_grad, head_gain_grad = final_back(final_grad)
    branch_grad = (gamma_two * residual_grad).astype(low)

    def slot_sums(token_grad):
        other = jnp.sum(jnp.where(second, token_grad, 0.0), axis=0)
        first = jnp.sum(jnp.where(second, 0.0, token_grad), axis=0)
        return jnp.stack([first, other])

    gamma_two_grad = slot_sums(residual_grad * branch)
    down_part = bfloat_product(hidden_act.T, branch_grad).astype(part_kind)
    act_grad = bfloat_product(branch_grad, full_down.T)
    _, gelu_back = jax.vjp(partial(jax.nn.gelu, approximate=True), hidden_pre)
    pre_grad = gelu_back(act_grad)[0].astype(low)
    up_part = bfloat_product(normed_two.T, pre_grad).astype(part_kind)
    normed_two_grad = bfloat_product(pre_grad, full_up.T)
    _, modulate_two_back = jax.vjp(modulate, residual_one, scale_two, shift_two)
    norm_grad, scale_two_grad, shift_two_grad = modulate_two_back(normed_two_grad)
    scale_two_grad, shift_two_grad = slot_sums(scale_two_grad), slot_sums(shift_two_grad)
    residual_grad = residual_grad + norm_grad
    attended_grad = (gamma_one * residual_grad).astype(low)
    gamma_one_grad = slot_sums(residual_grad * attended)
    out_part = bfloat_product(mixed_heads.T, attended_grad).astype(part_kind)
    mixed_grad = bfloat_product(attended_grad, full_out.T).astype(low)
    if linked:
        heads_grad, gain_grads, attention_done = attend_back(
            projected,
            mixed_grad,
            exact,
            totals,
            gains,
            turned_bias,
            head_part.reshape(FIVE + (depth, CODES)),
            up_part.reshape(FIVE + (depth, up_part.shape[1])),
            down_part.reshape(FIVE + (down_part.shape[0] // D, depth, D)),
        )
    else:
        heads_grad, gain_grads = attend_back(projected, mixed_grad, exact, totals, gains, turned_bias)
        head_grad, up_grad, down_grad = scattered(head_part), scattered(up_part), scattered(down_part)
    if linked:
        unknown = jnp.zeros((2, D), jnp.float32)
        factored_rows = [tables_moment, ada_moment, qkv_moment, out_moment, up_moment, head_moment]
        row_moments = jnp.concatenate(factored_rows + [down_moment]).reshape(10, depth, 1)
        padding = jnp.zeros((110,), jnp.float32)
        column_moments = jnp.concatenate(
            [column_moment[:1042], padding, column_moment[1042:], jnp.zeros((128,), jnp.float32)]
        )[None]
        known = jnp.concatenate(
            [gamma_one_grad, gamma_two_grad, unknown, scale_two_grad, unknown, shift_two_grad], axis=1
        )
        gain_rows = jnp.concatenate([gain_grads[:2], head_gain_grad[None], jnp.zeros((5, D), jnp.float32)])
        last = last_exchange(
            (out_part.reshape(FIVE + (depth, D)), full_qkv, embedded, residual_grad),
            (
                heads_grad,
                normed,
                codes,
                second.astype(jnp.float32),
                modulation[:, 2 * D : 3 * D],
                known,
                gain_rows,
                activated,
                class_cond,
                label_hot,
                local_loss[None, None],
            ),
            attention_done,
            masters,
            (row_moments, vector_moment, column_moments),
        )
        stepped = take_step(last, attention_done, vector_moment, masters)
        rows_new, cols_new, facts = last[4].reshape(10 * depth), last[5][0], last[6][:, 0]
        stats = [rows_new[i * depth : (i + 1) * depth] for i in range(6)] + [rows_new[6 * depth :]]
        moment_of = (stats[0], stepped[16], stats[1], stats[2], stats[3], stats[4], stats[6], stats[5])
        results = [facts[2, 16], weight_total]
        for position in range(8):
            results += [stepped[2 * position], moment_of[position], stepped[2 * position + 1]]
        column_stat = jnp.concatenate([cols_new[:1042], cols_new[1152:SCALARS]])
        return tuple(results + [column_stat, facts[0, :8]])

    qkv_part = jnp.concatenate(
        [bfloat_product(normed.T, heads_grad[part]).astype(part_kind) for part in range(3)], axis=1
    )
    normed_grad = sum(
        bfloat_product(heads_grad[part], full_qkv[:, part * D : (part + 1) * D].T) for part in range(3)
    )
    _, modulate_one_back = jax.vjp(modulate, embedded, scale_one, shift_one)
    norm_grad, scale_one_grad, shift_one_grad = modulate_one_back(normed_grad)
    scale_one_grad, shift_one_grad = slot_sums(scale_one_grad), slot_sums(shift_one_grad)
    embedded_grad = residual_grad + norm_grad
    modulation_grad = jnp.concatenate(
        [
            gamma_one_grad,
            gamma_two_grad,
            scale_one_grad,
            scale_two_grad,
            shift_one_grad,
            shift_two_grad,
        ],
        axis=1,
    )
    bias_grad = jnp.sum(modulation_grad, axis=0).reshape(6, D)
    code_grad = split_product(embedded_grad.T, code_levels)
    small_part = jnp.concatenate(
        [
            bias_grad.T,
            gain_grads[:2].T,
            head_gain_grad[:, None],
            code_grad,
            jnp.zeros((D, 128 - CODE_DIM - LEVELS - 9), jnp.float32),
        ],
        axis=1,
    )
    modulation_low = modulation_grad.astype(low)
    modulation_all = gathered(modulation_low)
    small_grad, qkv_grad, out_grad = scattered(small_part), scattered(qkv_part), scattered(out_part)
    ada_grad = bfloat_product(activated.T, modulation_all)
    activated_grad = bfloat_product(modulation_all, ada_low.T)
    _, silu_back = jax.vjp(jax.nn.silu, class_cond)
    cond_grad = silu_back(activated_grad)[0]
    class_grad = jnp.dot(
        cond_grad.T,
        label_hot[:, :CLASSES].astype(jnp.float32),
        precision=lax.Precision.HIGHEST,
        preferred_element_type=jnp.float32,
    )
    tables_grad = jnp.concatenate([class_grad, small_grad[:, 9:SMALL_LANES]], axis=1)
    vectors_grad = small_grad[:, :9]
    gradients = (
        tables_grad,
        vectors_grad,
        ada_grad,
        qkv_grad,
        out_grad,
        up_grad,
        down_grad,
        head_grad,
    )
    second_decay = DECAY
    factored_index = (0, 2, 3, 4, 5, 6, 7)
    factored_moments = (
        tables_moment,
        ada_moment,
        qkv_moment,
        out_moment,
        up_moment,
        down_moment,
        head_moment,
    )
    local_squares = jnp.stack([jnp.sum(master * master) for master in masters])
    rows_list = []
    column_parts = []
    row_parts = []
    for position, moment in zip(factored_index, factored_moments):
        gradient = gradients[position]
        squared = gradient * gradient + TINY_SQUARE
        rows_new = second_decay * moment + (1.0 - second_decay) * jnp.mean(squared, axis=1)
        rows_list.append(rows_new)
        column_parts.append(jnp.sum(squared, axis=0))
        row_parts.append(jnp.sum(rows_new))
    column_count = column_moment.shape[0]
    sums = lax.psum(
        jnp.concatenate(column_parts + [jnp.stack(row_parts), local_squares, local_loss[None]]), AXES
    )
    column_total = sums[:column_count]
    row_total = sums[column_count : column_count + 7]
    weight_squares = sums[column_count + 7 : column_count + 15]
    loss_sum = sums[column_count + 15]
    updates = [None] * 8
    moments_new = [None] * 8
    column_new = []
    offset = 0
    for factor_slot, position in enumerate(factored_index):
        gradient = gradients[position]
        rows_all = gradient.shape[0] * devices
        column_count = gradient.shape[1]
        cols_new = second_decay * column_moment[offset : offset + column_count] + (
            1.0 - second_decay
        ) * (column_total[offset : offset + column_count] / rows_all)
        offset += column_count
        estimate = (
            rows_list[factor_slot][:, None]
            * cols_new[None, :]
            / (row_total[factor_slot] / rows_all)
        )
        updates[position] = gradient * lax.rsqrt(estimate)
        moments_new[position] = rows_list[factor_slot]
        column_new.append(cols_new)
    vector_new = second_decay * vector_moment + (1.0 - second_decay) * (
        gradients[1] * gradients[1] + TINY_SQUARE
    )
    updates[1] = gradients[1] * lax.rsqrt(vector_new)
    moments_new[1] = vector_new
    local_spread = jnp.stack([jnp.sum(update * update) for update in updates])
    spread_total = lax.psum(local_spread, AXES)
    next_weights = []
    spreads = []
    for position in range(8):
        count_all = gradients[position].size * devices
        spread = jnp.sqrt(spread_total[position] / count_all)
        step_scale = jnp.maximum(SCALE_FLOOR, jnp.sqrt(weight_squares[position] / count_all))
        next_weights.append(
            masters[position]
            - STEP_RATE * step_scale * (updates[position] / jnp.maximum(1.0, spread / CLIP_LIMIT))
        )
        spreads.append(spread)
    column_stat = jnp.concatenate(column_new)
    clip_spread = jnp.stack(spreads)
    results = [loss_sum, weight_total]
    for position in range(8):
        results += [gradients[position], moments_new[position], next_weights[position]]
    return tuple(results + [column_stat, clip_spread])


def solution(mesh):
    in_specs = (
        P(("fsdp", "sub"), None),
        P(("fsdp", "sub")),
        P(("fsdp", "sub")),
        P(("fsdp", "sub")),
        P(("fsdp", "sub")),
        P(("fsdp", "sub")),
        P(("fsdp", "sub")),
        P(("fsdp", "sub"), None),
        P(("fsdp", "sub"), None),
        P(("fsdp", "sub"), None),
        P(("fsdp", "sub"), None),
        P(("fsdp", "sub"), None),
        P(("fsdp", "sub"), None),
        P(("fsdp", "sub"), None),
        P(("fsdp", "sub"), None),
        P(("fsdp", "sub")),
        P(("fsdp", "sub")),
        P(("fsdp", "sub")),
        P(("fsdp", "sub")),
        P(("fsdp", "sub")),
        P(("fsdp", "sub")),
        P(("fsdp", "sub")),
        P(("fsdp", "sub"), None),
        P(),
    )
    out_specs = (
        P(),
        P(),
        P(("fsdp", "sub"), None),
        P(("fsdp", "sub")),
        P(("fsdp", "sub"), None),
        P(("fsdp", "sub"), None),
        P(("fsdp", "sub"), None),
        P(("fsdp", "sub"), None),
        P(("fsdp", "sub"), None),
        P(("fsdp", "sub")),
        P(("fsdp", "sub"), None),
        P(("fsdp", "sub"), None),
        P(("fsdp", "sub")),
        P(("fsdp", "sub"), None),
        P(("fsdp", "sub"), None),
        P(("fsdp", "sub")),
        P(("fsdp", "sub"), None),
        P(("fsdp", "sub"), None),
        P(("fsdp", "sub")),
        P(("fsdp", "sub"), None),
        P(("fsdp", "sub"), None),
        P(("fsdp", "sub")),
        P(("fsdp", "sub"), None),
        P(("fsdp", "sub"), None),
        P(("fsdp", "sub")),
        P(("fsdp", "sub"), None),
        P(),
        P(),
    )
    return jax.shard_map(
        on_device, mesh=mesh, in_specs=in_specs, out_specs=out_specs, check_vma=False
    )
```

```python
import math
from functools import partial

import jax
import jax.numpy as jnp
from jax import lax
from jax.experimental import pallas as pl
from jax.experimental.pallas import tpu as pltpu
from jax.sharding import PartitionSpec as P

D = 1024
HEADS = 16
HEAD_DIM = 64
CLASSES = 1000
CODES = 4096
CODE_DIM = 32
LEVELS = 10
STEP = 10


TINY_SQUARE = 1e-30
SCALE_FLOOR = 0.001
STEP_RATE = 1.0
CLIP_LIMIT = 1.0
NORM_EPSILON = 1e-06
MASK_VALUE = -1000000000.0

AXES = ("fsdp", "sub")
MESH = pl.DeviceIdType.MESH
ANY = pl.BlockSpec(memory_space=pl.ANY)
WHOLE = pl.BlockSpec(memory_space=pltpu.VMEM)
FIVE = (2, 2, 2, 2, 2)
DIMS = ("w", "u", "y", "x", "c")
SCATTER_ORDERS = (("c", "x", "y", "w", "u"), ("c", "y", "x", "w", "u"))
GATHER_ORDERS = tuple(order[::-1] for order in SCATTER_ORDERS)
SCORE_SCALE = HEAD_DIM ** (-0.5)
EXP_SCALE = SCORE_SCALE * math.log2(math.e)
VMEM_GRANT = 58 * 1024 * 1024
FIRST_WIDTH, FIRST_LAG = 256, 2
ATTEND_WIDTH, ATTEND_LAG = 128, 3
BACK_WIDTH, BACK_LAG = 256, 2
LAST_WIDTH, LAST_LAG = 256, 2


def bfloat_product(left_side, right_side):
    return jnp.dot(left_side, right_side, preferred_element_type=jnp.float32)


class Place:
    def __init__(self):
        fsdp, sub = lax.axis_index("fsdp"), lax.axis_index("sub")
        self.bit = {
            "c": lax.rem(sub, 2),
            "x": lax.div(sub, 2),
            "y": lax.rem(fsdp, 2),
            "u": lax.rem(lax.div(fsdp, 2), 2),
            "w": lax.div(fsdp, 4),
        }
        bit = self.bit
        self.partner = {
            "c": (fsdp, sub + 1 - 2 * bit["c"]),
            "x": (fsdp, sub + 2 - 4 * bit["x"]),
            "y": (fsdp + 1 - 2 * bit["y"], sub),
            "u": (fsdp + 2 - 4 * bit["u"], sub),
            "w": (fsdp + 4 - 8 * bit["w"], sub),
        }

    def meet(self):
        barrier = pltpu.get_barrier_semaphore()
        for dim in DIMS:
            pl.semaphore_signal(
                barrier, inc=1, device_id=self.partner[dim], device_id_type=MESH
            )
        pl.semaphore_wait(barrier, 5)

    def send(self, src, dst, send_sem, recv_sem, dim):
        return pltpu.make_async_remote_copy(
            src_ref=src,
            dst_ref=dst,
            send_sem=send_sem,
            recv_sem=recv_sem,
            device_id=self.partner[dim],
            device_id_type=MESH,
        )


def when_in(index, low, high, body):
    if isinstance(index, int):
        if low <= index < high:
            body()
    else:
        pl.when((index >= low) & (index < high))(body)


class Gather:
    def __init__(self, place, groups, sends, recvs, local_sems, lag=1):
        self.place, self.groups, self.lag = place, groups, lag
        self.sends, self.recvs, self.local_sems = sends, recvs, local_sems
        self.steps = groups[-1][1] + 5 * lag

    @staticmethod
    def scratch(lag=1):
        dma = pltpu.SemaphoreType.DMA
        return [dma((5, 2, 2 * lag)), dma((5, 2, 2 * lag)), dma((2, 2 * lag))]

    def region(self, stage, parity):
        done = GATHER_ORDERS[parity][:stage]
        return tuple(slice(None) if d in done else self.place.bit[d] for d in DIMS)

    def copy(self, group, j, stage, parity, slot):
        _, _, own, full = group
        ref = full(j, parity, self.region(stage, parity))
        return self.place.send(
            own(j, parity) if stage == 0 else ref,
            ref,
            self.sends.at[stage, parity, slot],
            self.recvs.at[stage, parity, slot],
            GATHER_ORDERS[parity][stage],
        )

    def local(self, group, j, parity, slot):
        _, _, own, full = group
        return pltpu.make_async_copy(
            own(j, parity), full(j, parity, self.region(0, parity)), self.local_sems.at[parity, slot]
        )

    def step(self, t):
        for stage in reversed(range(6)):
            j = t - stage * self.lag
            for group in self.groups:

                def body(group=group, stage=stage, j=j):
                    slot = lax.rem(j, 2 * self.lag)
                    for parity in range(2):
                        if stage == 0:
                            self.local(group, j, parity, slot).start()
                        if stage == 1:
                            self.local(group, j, parity, slot).wait()
                        if stage >= 1:
                            self.copy(group, j, stage - 1, parity, slot).wait()
                        if stage < 5:
                            self.copy(group, j, stage, parity, slot).start()

                when_in(j, group[0], group[1], body)


class Scatter:
    def __init__(self, place, groups, store, scratch, lag=1):
        self.place, self.groups, self.store, self.lag = place, groups, store, lag
        self.keep = scratch[0]
        self.land = scratch[1:6]
        self.sums = (None,) + tuple(scratch[6:10])
        self.sends, self.recvs, self.keep_sems = scratch[10:13]
        self.first, self.end = groups[0][0], groups[-1][1]
        self.steps = self.end + 5 * lag

    @staticmethod
    def scratch(piece, kind, lag=1):
        dma = pltpu.SemaphoreType.DMA
        return (
            [pltpu.VMEM((lag, 2) + (2,) * 4 + piece, kind)]
            + [pltpu.VMEM((2 * lag, 2) + (2,) * (4 - k) + piece, kind) for k in range(5)]
            + [pltpu.VMEM((lag, 2) + (2,) * (5 - k) + piece, kind) for k in range(1, 5)]
            + [dma((5, 2, 2 * lag)), dma((5, 2, 2 * lag)), dma((2, lag))]
        )

    def half(self, stage, parity, other):
        order = SCATTER_ORDERS[parity]
        left = [d for d in DIMS if d not in order[:stage]]
        bit = self.place.bit[order[stage]]
        value = 1 - bit if other else bit
        return (parity,) + tuple(value if d == order[stage] else slice(None) for d in left)

    def copy(self, stage, parity, j, source=None):
        slot = lax.rem(j, 2 * self.lag)
        if source is None:
            if stage == 0:
                source = self.keep.at[lax.rem(j, self.lag), parity]
            else:
                source = self.sums[stage].at[(lax.rem(j, self.lag),) + self.half(stage, parity, True)]
        return self.place.send(
            source,
            self.land[stage].at[slot, parity],
            self.sends.at[stage, parity, slot],
            self.recvs.at[stage, parity, slot],
            SCATTER_ORDERS[parity][stage],
        )

    def step(self, t):
        for stage in reversed(range(6)):
            j = t - stage * self.lag

            def body(stage=stage, j=j):
                slot, near = lax.rem(j, 2 * self.lag), lax.rem(j, self.lag)
                for parity in range(2):
                    before = stage - 1
                    if before == 0:
                        pltpu.make_async_copy(
                            self.keep.at[near, parity],
                            self.keep.at[near, parity],
                            self.keep_sems.at[parity, near],
                        ).wait()
                    self.copy(before, parity, j).wait()
                    if before == 0:
                        mine = self.keep[near, parity]
                    else:
                        mine = self.sums[before][(near,) + self.half(before, parity, False)]
                    landed = self.land[before][slot, parity]
                    if stage < 5:
                        self.sums[stage][near, parity] = mine + landed
                        self.copy(stage, parity, j).start()
                    else:
                        self.store(j, parity, mine.astype(jnp.float32) + landed.astype(jnp.float32))

            if stage == 0:
                for low, high, source in self.groups:

                    def begin(source=source, j=j):
                        near = lax.rem(j, self.lag)
                        core = self.place.bit["c"]
                        for parity in range(2):
                            self.copy(0, parity, j, source(j, parity, 1 - core)).start()
                            pltpu.make_async_copy(
                                source(j, parity, core),
                                self.keep.at[near, parity],
                                self.keep_sems.at[parity, near],
                            ).start()

                    when_in(j, low, high, begin)
            else:
                when_in(j, self.first, self.end, body)


def finish(engine):
    done = UNITS * (HEADS // 2)

    @pl.when(pl.program_id(0) == HEADS // 2 - 1)
    def rest():
        for t in range(done, engine.steps):
            engine.step(t)


def params(collective_id, **more):
    return pltpu.CompilerParams(
        collective_id=collective_id, has_side_effects=True, vmem_limit_bytes=VMEM_GRANT, **more
    )


def columns(start, size):
    return pl.ds(pl.multiple_of(start, 128), size)


def slot_labels(tags_full, order):
    pieces = []
    for number in range(32):
        bits = {dim: (number >> (4 - at)) & 1 for at, dim in enumerate(order)}
        pieces.append(tags_full[bits["w"], bits["u"], bits["y"], bits["x"], bits["c"], 0:2])
    return jnp.concatenate(pieces, axis=0)


def hot_of(labels):
    lanes = lax.broadcasted_iota(jnp.int32, labels.shape, 1).astype(jnp.float32)
    blocks = [jnp.where(labels == lanes + 128.0 * at, 1.0, 0.0) for at in range(9)]
    return jnp.concatenate(blocks, axis=1).astype(jnp.bfloat16)


def begin_kernel(
    rows_ref,
    tags_ref,
    tables_ref,
    ada_ref,
    qkv_ref,
    out_own_ref,
    codes_ref,
    token_columns,
    token_rows,
    projected_ref,
    qkv_out,
    out_full,
    embedded_ref,
    normed_ref,
    modulation_ref,
    vectors_ref,
    hot_ref,
    cond_ref,
    act_ref,
    tag_sums,
    bias_ref,
    turned_ref,
    *scratch,
):
    place = Place()
    place.meet()
    bit = place.bit
    (
        rows_full,
        tags_full,
        own_qkv,
        own_out,
        qkv_full,
        part,
        unit,
        staged,
        copy_sems,
        mod_sends,
        mod_recvs,
    ) = scratch[:11]
    mod_land, mod_sums = scratch[11:16], scratch[16:21]
    own_qkv[...] = qkv_ref[...].astype(jnp.bfloat16)
    own_out[...] = out_own_ref[...].astype(jnp.bfloat16)
    small = Gather(
        place,
        [(0, 1, lambda j, p: (rows_ref, tags_ref)[p], lambda j, p, r: (rows_full, tags_full)[p].at[r])],
        *scratch[21:24],
    )
    width = FIRST_WIDTH
    pairs = 3 * D // (2 * width)

    def of_weight(own, full, first):
        return (
            lambda j, p: own.at[:, columns((2 * (j - first) + p) * width, width)],
            lambda j, p, r: full.at[r + (slice(None), columns((2 * (j - first) + p) * width, width))],
        )

    gather = Gather(
        place,
        [
            (0, pairs) + of_weight(own_qkv, qkv_full, 0),
            (pairs, pairs + D // (2 * width)) + of_weight(own_out, out_full, pairs),
        ],
        *scratch[24:27],
        lag=FIRST_LAG,
    )
    lanes = 3 * D
    orders = (("x", "y", "w", "u", "c"), ("y", "x", "w", "u", "c"))

    def mod_half(stage, parity, other):
        dim = orders[parity][stage]
        value = 1 - bit[dim] if other else bit[dim]
        left = [d for d in ("x", "y", "w") if d not in orders[parity][:stage]]
        return tuple(value if d == dim else slice(None) for d in left)

    def mod_view(stage, parity, other):
        if stage == 0:
            at = pl.ds(parity * lanes, lanes)
            return part, mod_half(0, parity, other) + (slice(None), at)
        if stage < 3:
            return mod_sums[stage - 1], (parity,) + mod_half(stage, parity, other)
        return mod_sums[stage - 1], (parity,)

    def mod_copy(stage, parity):
        ref, at = mod_view(stage, parity, True)
        return place.send(
            ref.at[at],
            mod_land[stage].at[parity],
            mod_sends.at[stage, parity],
            mod_recvs.at[stage, parity],
            orders[parity][stage],
        )

    def mod_step(stage):
        for parity in range(2):
            if stage:
                mod_copy(stage - 1, parity).wait()
                ref, at = mod_view(stage - 1, parity, False)
                mod_sums[stage - 1][parity] = ref[at] + mod_land[stage - 1][parity]
            if stage < 5:
                mod_copy(stage, parity).start()

    def mask(query, key, same):
        usable = (query[0] == key[0]) & (key[1] <= query[1]) & ((key[2] > 0.5) | same)
        return jnp.where(usable, 0.0, MASK_VALUE)

    tokens = codes_ref.shape[0]
    block = tokens // 4

    def masks(index, size):
        at = slice(index * size, (index + 1) * size)
        shape = (size, tokens)
        same = lax.broadcasted_iota(jnp.int32, shape, 0) + index * size == lax.broadcasted_iota(
            jnp.int32, shape, 1
        )
        down = [token_columns[at, i : i + 1] for i in range(3)]
        across = [token_rows[i : i + 1] for i in range(3)]
        bias_ref[at] = mask(down, across, same)
        turned_ref[at] = mask(across, down, same)

    def embed(index):
        at = slice(index * block, (index + 1) * block)
        values = dot_last(codes_ref[at], rows_full[...].reshape(D, 128))
        embedded_ref[at] = values
        center = values - jnp.sum(values, axis=1, keepdims=True) * (1.0 / D)
        rate = lax.rsqrt(jnp.sum(center * center, axis=1, keepdims=True) * (1.0 / D) + NORM_EPSILON)
        unit[at] = center * rate

    masking = iter(range(8))
    steps = iter(range(gather.steps))
    for t in range(6):
        small.step(t)
        gather.step(next(steps))
        if t < 5:
            masks(next(masking), tokens // 8)
    tag_sums[...] = jnp.sum(tags_full[...].reshape(32, 8, 128), axis=0)
    low = jnp.bfloat16
    class_tables = tables_ref[:, :D].astype(low)
    for order, target in ((DIMS, None), (("x", "y", "w", "u", "c"), part)):
        hot = hot_of(slot_labels(tags_full, order))
        cond = dot_last(hot[:, :D], class_tables)
        act = (cond / (1.0 + jnp.exp(-cond))).astype(low)
        if target is None:
            hot_ref[...], cond_ref[...], act_ref[...] = hot, cond, act
        else:
            target[...] = dot_plain(act, ada_ref[...].astype(low)).reshape(2, 2, 2, 8, 6 * D)
    vectors_ref[...] = rows_full[...].reshape(D, 128).astype(jnp.float32).T[0:16]
    for stage in range(6):
        mod_step(stage)
        for step in steps:
            gather.step(step)
            break
        if stage < 4:
            embed(stage)
        for index in masking:
            masks(index, tokens // 8)
            break
    for step in steps:
        gather.step(step)
    store_qkv = pltpu.make_async_copy(qkv_full, qkv_out, copy_sems.at[2])
    store_qkv.start()
    spot = 4 * bit["u"] + 2 * bit["c"]
    row_ids = lax.broadcasted_iota(jnp.int32, (8, D), 0)
    for kind in range(6):
        at = (kind % 3) * D
        group = mod_sums[4][kind // 3, :, at : at + D]
        for slot in range(2):
            row = jnp.sum(jnp.where(row_ids == spot + slot, group, 0.0), axis=0, keepdims=True)
            modulation_ref[slot : slot + 1, kind * D : (kind + 1) * D] = row + vectors_ref[kind : kind + 1]
    stores = []
    for index in range(4):
        at = slice(index * block, (index + 1) * block)
        other = token_columns[at, 0:1] > 0.5
        scale = jnp.where(other, modulation_ref[1:2, 2 * D : 3 * D], modulation_ref[0:1, 2 * D : 3 * D])
        shift = jnp.where(other, modulation_ref[1:2, 4 * D : 5 * D], modulation_ref[0:1, 4 * D : 5 * D])
        normed = (unit[at] * (1.0 + scale) + shift).astype(low)
        normed_ref[at] = normed
        if index >= 2:
            stores[index - 2].wait()
        for column in range(0, 3 * D, 512):
            weight = qkv_full[:, :, :, :, :, :, column : column + 512].reshape(D, 512)
            staged[index % 2, :, column : column + 512] = dot_plain(normed, weight)
        stores.append(
            pltpu.make_async_copy(
                staged.at[index % 2], projected_ref.at[pl.ds(index * block, block)], copy_sems.at[index % 2]
            )
        )
        stores[index].start()
    stores[2].wait()
    stores[3].wait()
    store_qkv.wait()


def begin(rows, tags, tables, ada_weight, qkv_weight, out_weight, codes, token_columns, token_rows):
    depth = rows.shape[0]
    tokens = codes.shape[0]
    f32, low = jnp.float32, jnp.bfloat16
    dma = pltpu.SemaphoreType.DMA
    lanes = 3 * D
    lands = [
        pltpu.VMEM((2, 2, 2, 8, lanes), f32),
        pltpu.VMEM((2, 2, 8, lanes), f32),
    ] + [pltpu.VMEM((2, 8, lanes), f32)] * 3
    shape = jax.ShapeDtypeStruct
    return pl.pallas_call(
        begin_kernel,
        out_shape=(
            shape((tokens, 3 * D), f32),
            shape(FIVE + (depth, 3 * D), low),
            shape(FIVE + (depth, D), low),
            shape((tokens, D), f32),
            shape((tokens, D), low),
            shape((2, 6 * D), f32),
            shape((16, D), f32),
            shape((64, 1152), low),
            shape((64, depth), f32),
            shape((64, depth), low),
            shape((8, 128), f32),
            shape((tokens, tokens), f32),
            shape((tokens, tokens), f32),
        ),
        in_specs=[WHOLE] * 9,
        out_specs=(ANY, ANY, ANY) + (WHOLE,) * 10,
        scratch_shapes=[
            pltpu.VMEM(FIVE + (depth, 128), low),
            pltpu.VMEM(FIVE + (8, 128), f32),
            pltpu.VMEM((depth, 3 * D), low),
            pltpu.VMEM((depth, D), low),
            pltpu.VMEM(FIVE + (depth, 3 * D), low),
            pltpu.VMEM((2, 2, 2, 8, 6 * D), f32),
            pltpu.VMEM((tokens, D), f32),
            pltpu.VMEM((2, tokens // 4, 3 * D), f32),
            dma((3,)),
            dma((5, 2)),
            dma((5, 2)),
        ]
        + lands
        + lands
        + Gather.scratch()
        + Gather.scratch(FIRST_LAG),
        compiler_params=params(0),
        name="begin",
    )(rows, tags, tables, ada_weight, qkv_weight, out_weight, codes, token_columns, token_rows)


def head_mean(values):
    low_lane = lax.broadcasted_iota(jnp.int32, values.shape, 1) < HEAD_DIM
    low_sum = jnp.sum(jnp.where(low_lane, values, 0.0), axis=1, keepdims=True)
    high_sum = jnp.sum(jnp.where(low_lane, 0.0, values), axis=1, keepdims=True)
    return jnp.where(low_lane, low_sum, high_sum) * (1.0 / HEAD_DIM)


def of_head(values, head):
    low_lane = lax.broadcasted_iota(jnp.int32, values.shape, 1) < HEAD_DIM
    zero = jnp.zeros_like(values)
    return jnp.where(low_lane, values, zero) if head == 0 else jnp.where(low_lane, zero, values)


def dot_last(left, right):
    return lax.dot_general(left, right, (((1,), (1,)), ((), ())), preferred_element_type=jnp.float32)


def dot_first(left, right):
    return lax.dot_general(left, right, (((0,), (0,)), ((), ())), preferred_element_type=jnp.float32)


def dot_plain(left, right):
    return lax.dot_general(left, right, (((1,), (0,)), ((), ())), preferred_element_type=jnp.float32)


UNITS = 4


def normed_head(raw, gain):
    return (raw * lax.rsqrt(head_mean(raw * raw) + NORM_EPSILON) * gain).astype(jnp.bfloat16)


def attend_kernel(linked, q_ref, k_ref, v_ref, gain_ref, bias_ref, *refs):
    if linked:
        down_own, half_ref, mixed_ref, exact_ref, total_ref, down_full, up_full, head_full = refs[:8]
        qn, kn, vn, pair_sems, passing, pass_sems = refs[8:14]
        sems = refs[14:]
        place = Place()
        core = place.bit["c"]

        def pair_copies():
            start = 0
            for order, full in enumerate((up_full, head_full)):
                size = full.shape[6]
                source = half_ref.at[:, :, :, :, :, start : start + size]
                target = full.at[:, :, :, :, core]
                yield place.send(source, target, pair_sems.at[0, order], pair_sems.at[1, order], "c")
                start += size

        chunks = HEADS // 2
        piece = passing.shape[6]

        def load(i):
            return pltpu.make_async_copy(
                half_ref.at[:, :, :, :, :, i * piece : (i + 1) * piece], passing.at[i % 2], pass_sems.at[0, i % 2]
            )

        def save(i):
            full = (up_full, head_full)[i // (chunks // 2)]
            at = (i % (chunks // 2)) * piece
            return pltpu.make_async_copy(
                passing.at[i % 2], full.at[:, :, :, :, core, :, at : at + piece], pass_sems.at[1, i % 2]
            )

        def each_chunk(body):
            for i in range(chunks):
                pl.when(pl.program_id(0) == i)(partial(body, i))

        def begin_chunk(i):
            if i >= 2:
                save(i - 2).wait()
            load(i).start()

        def end_chunk(i):
            load(i).wait()
            save(i).start()
            if i == chunks - 1:
                save(i - 1).wait()
                save(i).wait()

        width = ATTEND_WIDTH
        split = D // (2 * width)
        depth = down_full.shape[6]
        parts = down_full.shape[5]

        def down_source(j, p):
            part, column = lax.div(j, split), lax.rem(j, split)
            return down_own.at[
                pl.ds(pl.multiple_of(part * depth, depth), depth), columns((2 * column + p) * width, width)
            ]

        def down_target(j, p, r):
            part, column = lax.div(j, split), lax.rem(j, split)
            return down_full.at[r + (part, slice(None), columns((2 * column + p) * width, width))]

        gather = Gather(place, [(0, split * parts, down_source, down_target)], *sems, lag=ATTEND_LAG)

        @pl.when(pl.program_id(0) == 0)
        def first():
            place.meet()
            for copy in pair_copies():
                copy.start()

        each_chunk(begin_chunk)
    else:
        mixed_ref, exact_ref, total_ref, qn, kn, vn = refs
    qn[...] = normed_head(q_ref[...], gain_ref[0:1])
    kn[...] = normed_head(k_ref[...], gain_ref[1:2])
    vn[...] = v_ref[...].astype(jnp.bfloat16)
    tokens = q_ref.shape[0]
    both, sums = [], []
    for head in range(2):
        query = of_head(qn[...], head)
        mixed = jnp.zeros((tokens, 128), jnp.float32)
        lanes = jnp.zeros((tokens, 128), jnp.float32)
        for order in range(UNITS // 2):
            if linked:
                gather.step(pl.program_id(0) * UNITS + head * (UNITS // 2) + order)
            size = tokens // (UNITS // 2)
            keys = slice(order * size, (order + 1) * size)
            raised = jnp.exp2(dot_last(query, kn[keys]) * EXP_SCALE + bias_ref[:, keys])
            for lane in range(0, size, 128):
                lanes = lanes + raised[:, lane : lane + 128]
            mixed = mixed + dot_plain(raised.astype(jnp.bfloat16), vn[keys])
        total = jnp.sum(lanes, axis=1, keepdims=True)
        both.append(mixed * (1.0 / total))
        sums.append(total)
    low_lane = lax.broadcasted_iota(jnp.int32, both[0].shape, 1) < HEAD_DIM
    exact = jnp.where(low_lane, both[0], both[1])
    mixed_ref[...] = exact.astype(jnp.bfloat16)
    exact_ref[...] = exact
    total_ref[...] = jnp.log2(jnp.where(low_lane, sums[0], sums[1]))

    if linked:
        finish(gather)
        each_chunk(end_chunk)

        @pl.when(pl.program_id(0) == HEADS // 2 - 1)
        def pair_done():
            for copy in pair_copies():
                copy.wait()


def attend(projected, gains, bias, down_own=None, half=None):
    tokens = projected.shape[0]
    pair = pl.BlockSpec((tokens, 128), lambda i: (0, i))
    specs = [
        pair,
        pl.BlockSpec((tokens, 128), lambda i: (0, i + 8)),
        pl.BlockSpec((tokens, 128), lambda i: (0, i + 16)),
        pl.BlockSpec((8, 128), lambda i: (0, i)),
        pl.BlockSpec((tokens, tokens), lambda i: (0, 0), pipeline_mode=pl.Buffered(1)),
    ]
    outs = [jax.ShapeDtypeStruct((tokens, D), kind) for kind in (jnp.bfloat16, jnp.float32, jnp.float32)]
    out_specs = [pair] * 3
    scratch = [pltpu.VMEM((tokens, 128), jnp.bfloat16)] * 3
    operands = [projected, projected, projected, gains, bias]
    linked = down_own is not None
    if linked:
        depth = half.shape[4]
        specs += [ANY, ANY]
        operands += [down_own, half]
        outs += [jax.ShapeDtypeStruct(FIVE + (down_own.shape[0] // depth, depth, D), jnp.bfloat16)]
        outs += [jax.ShapeDtypeStruct(FIVE + (depth, half.shape[5] // 2), jnp.bfloat16)] * 2
        out_specs += [ANY] * 3
        scratch = scratch + [pltpu.SemaphoreType.DMA((2, 2))]
        scratch += [pltpu.VMEM((2,) + half.shape[:5] + (half.shape[5] // (HEADS // 2),), jnp.bfloat16)]
        scratch += [pltpu.SemaphoreType.DMA((2, 2))] + Gather.scratch(ATTEND_LAG)
    return pl.pallas_call(
        partial(attend_kernel, linked),
        grid=(HEADS // 2,),
        out_shape=tuple(outs),
        in_specs=specs,
        out_specs=tuple(out_specs),
        scratch_shapes=scratch,
        compiler_params=params(2) if linked else pltpu.CompilerParams(vmem_limit_bytes=VMEM_GRANT),
        name="attention_forward",
    )(*operands)


def attend_back_kernel(linked, q_ref, k_ref, v_ref, m_ref, exact_ref, total_ref, gain_ref, bias_ref, *refs):
    if linked:
        up_ref, down_ref, grad_ref, gain_grad_ref, done_ref = refs[:5]
        qn, kn, vn, dk, dv, turned, dq_turned, key_turned = refs[5:13]
        place = Place()
        width = BACK_WIDTH
        wide = up_ref.shape[6] // (2 * width)
        narrow = down_ref.shape[7] // (2 * width)
        parts = down_ref.shape[5]

        def columns_of(ref, first):
            return lambda j, p, core: ref.at[
                :, :, :, :, core, :, columns((2 * (j - first) + p) * width, width)
            ]

        def down_source(j, p, core):
            spread = j - wide
            part, column = lax.div(spread, narrow), lax.rem(spread, narrow)
            return down_ref.at[:, :, :, :, core, part, :, columns((2 * column + p) * width, width)]

        def store(j, parity, total):
            done_ref[j, :, parity * width : (parity + 1) * width] = total

        pairs = wide + parts * narrow
        scatter = Scatter(
            place,
            [
                (0, wide, columns_of(up_ref, 0)),
                (wide, pairs, down_source),
            ],
            store,
            refs[13:],
            lag=BACK_LAG,
        )
        pl.when(pl.program_id(0) == 0)(place.meet)
    else:
        grad_ref, gain_grad_ref = refs[:2]
        qn, kn, vn, dk, dv, turned, dq_turned, key_turned = refs[2:]
    qn[...] = normed_head(q_ref[...], gain_ref[0:1])
    kn[...] = normed_head(k_ref[...], gain_ref[1:2])
    vn[...] = v_ref[...].astype(jnp.bfloat16)
    for head in range(2):
        key_turned[head] = of_head(kn[...], head).T
    turned[0] = total_ref[...].T
    turned[1] = (head_mean(m_ref[...].astype(jnp.float32) * exact_ref[...]) * HEAD_DIM).T
    tokens = q_ref.shape[0]
    size = tokens // (UNITS // 2)
    for head in range(2):
        query = of_head(qn[...], head)
        mixed = of_head(m_ref[...], head)
        at = head * HEAD_DIM
        total = turned[0, at : at + 1]
        center = turned[1, at : at + 1]
        for order in range(UNITS // 2):
            if linked:
                scatter.step(pl.program_id(0) * UNITS + head * (UNITS // 2) + order)
            keys = slice(order * size, (order + 1) * size)
            scores = dot_last(kn[keys], query) * EXP_SCALE + (bias_ref[keys] - total)
            probs = jnp.exp2(scores)
            prob_grad = dot_last(vn[keys], mixed)
            score_grad = (probs * (prob_grad - center)).astype(jnp.bfloat16)
            key_part = dot_plain(score_grad, query)
            value_part = dot_plain(probs.astype(jnp.bfloat16), mixed)
            query_part = dot_plain(key_turned[head, :, keys], score_grad)
            dk[keys] = key_part if head == 0 else dk[keys] + key_part
            dv[keys] = value_part if head == 0 else dv[keys] + value_part
            dq_turned[...] = query_part if head == 0 and order == 0 else dq_turned[...] + query_part

    gain_rows = []
    for place_at, raw_ref, grad in ((0, q_ref, dq_turned[...].T), (1, k_ref, dk[...])):
        raw = raw_ref[...]
        normed_grad = grad * SCORE_SCALE
        rate = lax.rsqrt(head_mean(raw * raw) + NORM_EPSILON)
        scaled = gain_ref[place_at : place_at + 1] * normed_grad
        back = rate * scaled - raw * (rate * rate * rate) * head_mean(raw * scaled)
        grad_ref[place_at] = back.astype(jnp.bfloat16)
        gain_rows.append(jnp.sum(normed_grad * raw * rate, axis=0, keepdims=True))
    grad_ref[2] = dv[...].astype(jnp.bfloat16)
    gain_grad_ref[...] = jnp.concatenate(gain_rows + [jnp.zeros((6, 128), jnp.float32)], axis=0)
    if linked:
        finish(scatter)


def attend_back(projected, mixed_grad, exact, totals, gains, bias, up_grad=None, down_grad=None):
    tokens = projected.shape[0]
    pair = pl.BlockSpec((tokens, 128), lambda i: (0, i))
    specs = [
        pair,
        pl.BlockSpec((tokens, 128), lambda i: (0, i + 8)),
        pl.BlockSpec((tokens, 128), lambda i: (0, i + 16)),
        pair,
        pair,
        pair,
        pl.BlockSpec((8, 128), lambda i: (0, i)),
        pl.BlockSpec((tokens, tokens), lambda i: (0, 0), pipeline_mode=pl.Buffered(1)),
    ]
    outs = [
        jax.ShapeDtypeStruct((3, tokens, D), jnp.bfloat16),
        jax.ShapeDtypeStruct((8, D), jnp.float32),
    ]
    out_specs = [
        pl.BlockSpec((3, tokens, 128), lambda i: (0, 0, i)),
        pl.BlockSpec((8, 128), lambda i: (0, i)),
    ]
    scratch = [pltpu.VMEM((tokens, 128), jnp.bfloat16)] * 3 + [
        pltpu.VMEM((tokens, 128), jnp.float32)
    ] * 2
    scratch += [
        pltpu.VMEM((2, 128, tokens), jnp.float32),
        pltpu.VMEM((128, tokens), jnp.float32),
        pltpu.VMEM((2, 128, tokens), jnp.bfloat16),
    ]
    operands = [projected, projected, projected, mixed_grad, exact, totals, gains, bias]
    linked = up_grad is not None
    if linked:
        depth = up_grad.shape[5]
        specs += [ANY, ANY]
        operands += [up_grad, down_grad]
        pairs = (up_grad.shape[6] + down_grad.shape[5] * down_grad.shape[7]) // (2 * BACK_WIDTH)
        outs += [jax.ShapeDtypeStruct((pairs, depth, 2 * BACK_WIDTH), jnp.float32)]
        out_specs += [WHOLE]
        scratch = scratch + Scatter.scratch((depth, BACK_WIDTH), jnp.bfloat16, BACK_LAG)
    return pl.pallas_call(
        partial(attend_back_kernel, linked),
        grid=(HEADS // 2,),
        out_shape=tuple(outs),
        in_specs=specs,
        out_specs=tuple(out_specs),
        scratch_shapes=scratch,
        compiler_params=params(3) if linked else pltpu.CompilerParams(vmem_limit_bytes=VMEM_GRANT),
        name="attention_backward",
    )(*operands)


TANH_RATE = math.sqrt(2.0 / math.pi)
DENSE_WIDTH = 512


def dense_back_kernel(
    branch_ref,
    normed_ref,
    pre_ref,
    down_ref,
    up_ref,
    residual_ref,
    grad_ref,
    attended_ref,
    token_columns,
    mods_ref,
    head_ref,
    up_grad,
    down_grad,
    residual_grad,
    attended_grad,
    rows_ref,
    done_ref,
    normed_turned,
    pre_grad,
    hidden,
    back,
    *scratch,
):
    place = Place()
    index = pl.program_id(0)
    width = BACK_WIDTH

    def store(j, parity, total):
        done_ref[j, :, parity * width : (parity + 1) * width] = total

    pairs = head_ref.shape[6] // (2 * width)
    scatter = Scatter(
        place,
        [
            (
                0,
                pairs,
                lambda j, p, core: head_ref.at[:, :, :, :, core, :, columns((2 * j + p) * width, width)],
            )
        ],
        store,
        scratch,
        lag=BACK_LAG,
    )

    @pl.when(index == 0)
    def first():
        place.meet()
        normed_turned[...] = normed_ref[...].T
        back[...] = jnp.zeros_like(back)

    tokens = branch_ref.shape[0]
    block = tokens // 4
    blocks = [slice(i * block, (i + 1) * block) for i in range(4)]
    scatter.step(index * 3)
    for rows in blocks:
        act_grad = dot_last(branch_ref[rows], down_ref[...])
        value = pre_ref[rows]
        square = value * value
        bent = jnp.tanh(TANH_RATE * value * (1.0 + 0.044715 * square))
        half = 0.5 * (1.0 + bent)
        slope = half + 0.5 * value * (1.0 - bent * bent) * (TANH_RATE * (1.0 + 3 * 0.044715 * square))
        pre_grad[rows] = (slope * act_grad).astype(jnp.bfloat16)
        hidden[rows] = (value * half).astype(jnp.bfloat16)
    scatter.step(index * 3 + 1)
    down_grad[...] = dot_first(hidden[...], branch_ref[...]).astype(jnp.bfloat16)
    up_grad[...] = dot_plain(normed_turned[...], pre_grad[...]).astype(jnp.bfloat16)
    scatter.step(index * 3 + 2)
    for rows in blocks:
        back[rows] += dot_last(pre_grad[rows], up_ref[...])

    @pl.when(index == pl.num_programs(0) - 1)
    def last():
        sums = [jnp.zeros((1, D), jnp.float32)] * 6
        for rows in blocks:
            values, slope = residual_ref[rows], back[rows]
            center = values - jnp.sum(values, axis=1, keepdims=True) * (1.0 / D)
            rate = lax.rsqrt(
                jnp.sum(center * center, axis=1, keepdims=True) * (1.0 / D) + NORM_EPSILON
            )
            unit = center * rate
            other = token_columns[rows, 0:1] > 0.5
            unit_back = slope * (1.0 + jnp.where(other, mods_ref[1:2], mods_ref[0:1]))
            mean_back = jnp.sum(unit_back, axis=1, keepdims=True) * (1.0 / D)
            mean_along = jnp.sum(unit_back * unit, axis=1, keepdims=True) * (1.0 / D)
            total = grad_ref[rows] + rate * (unit_back - mean_back - unit * mean_along)
            residual_grad[rows] = total
            attended_grad[rows] = (total * jnp.where(other, mods_ref[3:4], mods_ref[2:3])).astype(
                jnp.bfloat16
            )
            for at, value in enumerate((slope * unit, slope, total * attended_ref[rows])):
                second = jnp.sum(jnp.where(other, value, 0.0), axis=0, keepdims=True)
                first_slot = jnp.sum(jnp.where(other, 0.0, value), axis=0, keepdims=True)
                sums[2 * at] = sums[2 * at] + first_slot
                sums[2 * at + 1] = sums[2 * at + 1] + second
        for at in range(6):
            rows_ref[at : at + 1] = sums[at]


def dense_back(branch_grad, normed, pre, down, up, residual, grad, attended, token_columns, mods, head):
    tokens, wide = pre.shape
    depth = head.shape[5]
    pairs = head.shape[6] // (2 * BACK_WIDTH)
    f32, low = jnp.float32, jnp.bfloat16
    width = DENSE_WIDTH

    def fixed(*shape):
        return pl.BlockSpec(shape, lambda i: (0,) * len(shape), pipeline_mode=pl.Buffered(1))

    across = pl.BlockSpec((D, width), lambda i: (0, i))
    along = pl.BlockSpec((width, D), lambda i: (i, 0))
    shape = jax.ShapeDtypeStruct
    return pl.pallas_call(
        dense_back_kernel,
        grid=(wide // width,),
        out_shape=(
            shape((D, wide), low),
            shape((wide, D), low),
            shape((tokens, D), f32),
            shape((tokens, D), low),
            shape((8, D), f32),
            shape((pairs, depth, 2 * BACK_WIDTH), f32),
        ),
        in_specs=[
            fixed(tokens, D),
            fixed(tokens, D),
            pl.BlockSpec((tokens, width), lambda i: (0, i)),
            along,
            across,
            fixed(tokens, D),
            fixed(tokens, D),
            fixed(tokens, D),
            fixed(tokens, 128),
            fixed(8, D),
            ANY,
        ],
        out_specs=(across, along, fixed(tokens, D), fixed(tokens, D), fixed(8, D), WHOLE),
        scratch_shapes=[
            pltpu.VMEM((D, tokens), low),
            pltpu.VMEM((tokens, width), low),
            pltpu.VMEM((tokens, width), low),
            pltpu.VMEM((tokens, D), f32),
        ]
        + Scatter.scratch((depth, BACK_WIDTH), low, BACK_LAG),
        compiler_params=params(5),
        name="dense_backward",
    )(branch_grad, normed, pre, down, up, residual, grad, attended, token_columns, mods, head)


WEIGHT_COLUMNS = (CLASSES + CODE_DIM + LEVELS, 9, 6 * D, 3 * D, D, 4 * D, D, CODES)
SUM_STARTS = (0, None, 1152, 1152 + 6144, 1152 + 9216, 1152 + 10240, 1152 + 14336, 1152 + 15360)
SCALARS = 1152 + 19456
SUM_LANES = SCALARS + 128
SMALL_LANES = CODE_DIM + LEVELS + 9
DECAY = 1.0 - STEP ** (-0.8)


def three_terms(values):
    high = values.astype(jnp.bfloat16)
    rest = values - high.astype(jnp.float32)
    middle = rest.astype(jnp.bfloat16)
    return high, middle, (rest - middle.astype(jnp.float32)).astype(jnp.bfloat16)


def lane_row(scalars):
    lanes = lax.broadcasted_iota(jnp.int32, (1, 128), 1)
    row = jnp.zeros((1, 128), jnp.float32)
    for lane, value in scalars:
        row = jnp.where(lanes == lane, value, row)
    return row


def whole_sum(values):
    return jnp.sum(jnp.sum(values, axis=0, keepdims=True), axis=1, keepdims=True)


def weight_tiles(tables_grad, ada_grad, done_head, done_attention, done_last):
    def blocks(ref, first, count, width):
        return [(lambda at=first + i: ref[at], i * width, width) for i in range(count)]

    near, far = 2 * LAST_WIDTH, 2 * BACK_WIDTH
    tables_columns = WEIGHT_COLUMNS[0]
    wide = CODES // far
    return {
        0: [(0, [(lambda: tables_grad[:, :tables_columns], 0, tables_columns)])],
        2: [(1, [(lambda: ada_grad[...], 0, 6 * D)])],
        3: [(2, blocks(done_last, D // near, 3 * D // near, near))],
        4: [(3, blocks(done_last, 0, D // near, near))],
        5: [(4, blocks(done_attention, 0, wide, far))],
        6: [(6 + part, blocks(done_attention, wide + part * (D // far), D // far, far)) for part in range(4)],
        7: [(5, blocks(done_head, 0, wide, far))],
    }


class Total:
    def __init__(self, place, sums, land, sends, recvs):
        self.place, self.sums, self.land = place, sums, land
        self.sends, self.recvs = sends, recvs

    @staticmethod
    def scratch(lanes):
        dma = pltpu.SemaphoreType.DMA
        return [
            pltpu.VMEM((6, 1, lanes), jnp.float32),
            pltpu.VMEM((5, 1, lanes), jnp.float32),
            dma((5,)),
            dma((5,)),
        ]

    def run(self):
        for stage, dim in enumerate(DIMS):
            copy = self.place.send(
                self.sums.at[stage], self.land.at[stage], self.sends.at[stage], self.recvs.at[stage], dim
            )
            copy.start()
            copy.wait()
            self.sums[stage + 1] = self.sums[stage] + self.land[stage]


def last_kernel(
    out_ref,
    qkv_low,
    embedded_ref,
    grad_ref,
    heads_grad,
    normed_ref,
    codes_ref,
    second_ref,
    scale_ref,
    known_ref,
    gains_ref,
    act_ref,
    cond_ref,
    hot_ref,
    loss_ref,
    done_head,
    attention_ref,
    tables_ref,
    vectors_ref,
    ada_ref,
    qkv_master,
    out_master,
    up_master,
    down_master,
    head_master,
    moments_ref,
    vector_moment_ref,
    column_moment_ref,
    done_ref,
    small_done,
    tables_grad,
    ada_grad,
    rows_ref,
    columns_ref,
    facts_ref,
    *scratch,
):
    place = Place()
    place.meet()
    devices = lax.axis_size(AXES)
    depth = tables_ref.shape[0]
    width = LAST_WIDTH
    narrow = D // (2 * width)
    part_grads, qkv_full, embedded, grad, code_sums, mod_ref, small_ref, load_sems = scratch[40:48]
    loads = [
        pltpu.make_async_copy(source, target, load_sems.at[i])
        for i, (source, target) in enumerate(
            ((qkv_low, qkv_full), (embedded_ref, embedded), (grad_ref, grad))
        )
    ]
    for load in loads:
        load.start()

    def columns_of(ref, first):
        return lambda j, p, core: ref.at[
            :, :, :, :, core, :, columns((2 * (j - first) + p) * width, width)
        ]

    def store(j, parity, total):
        done_ref[j, :, parity * width : (parity + 1) * width] = total

    pairs = 4 * narrow
    scatter = Scatter(
        place,
        [(0, narrow, columns_of(out_ref, 0))]
        + [
            ((1 + part) * narrow, (2 + part) * narrow, columns_of(part_grads.at[part], (1 + part) * narrow))
            for part in range(3)
        ],
        store,
        scratch[:13],
        lag=LAST_LAG,
    )
    half = depth // 2

    def small_store(j, parity, total):
        small_done[pl.ds(parity * half, half)] = total

    small = Scatter(
        place,
        [(0, 1, lambda j, p, core: small_ref.at[:, :, :, :, core, pl.ds(p * half, half)])],
        small_store,
        scratch[13:26],
    )
    mod_sums, mod_land, mod_all, mod_sends, mod_recvs = scratch[26:31]
    bit = place.bit

    def mod_copy(stage):
        dim = ("c", "x", "y", "u", "w")[stage]
        if stage < 3:
            source, target = (mod_ref, mod_sums.at[0], mod_sums.at[1])[stage], mod_land.at[stage]
        elif stage == 3:
            source = target = mod_all.at[bit["w"], bit["u"]]
        else:
            source = target = mod_all.at[bit["w"]]
        return place.send(source, target, mod_sends.at[stage], mod_recvs.at[stage], dim)

    def mod_step(stage):
        if stage:
            mod_copy(stage - 1).wait()
        if stage == 1:
            mod_sums[0] = mod_ref[...] + mod_land[0]
        elif stage == 2:
            mod_sums[1] = mod_sums[0] + mod_land[1]
        elif stage == 3:
            mod_all[bit["w"], bit["u"]] = mod_sums[1] + mod_land[2]
        if stage < 5:
            mod_copy(stage).start()

    first_total = Total(place, *scratch[31:35])
    second_total = Total(place, *scratch[35:39])
    sums, facts = first_total.sums, scratch[39]
    tiles = weight_tiles(tables_grad, ada_grad, done_head, attention_ref, done_ref)
    masters = (
        tables_ref,
        vectors_ref,
        ada_ref,
        qkv_master,
        out_master,
        up_master,
        down_master,
        head_master,
    )

    def ada_part():
        slots = mod_all[...].reshape(2 * devices, 6 * D)
        ada_grad[...] = dot_first(act_ref[...], slots)
        activated_grad = dot_last(slots, ada_ref[...].astype(jnp.bfloat16))
        cond = cond_ref[...]
        gate = 1.0 / (1.0 + jnp.exp(-cond))
        cond_grad = activated_grad * (gate * (1.0 + cond * (1.0 - gate)))
        shape = (128, hot_ref.shape[1])
        source = lax.broadcasted_iota(jnp.int32, shape, 0)
        target = lax.broadcasted_iota(jnp.int32, shape, 1)
        moved = (target == source + (CLASSES - 9)) & (source >= 9) & (source < SMALL_LANES)
        shift = jnp.where(moved, 1.0, 0.0).astype(jnp.bfloat16)
        total = jnp.zeros((depth, hot_ref.shape[1]), jnp.float32)
        for term in three_terms(cond_grad)[::-1]:
            total = total + dot_first(term, hot_ref[...])
        for term in three_terms(small_done[...])[::-1]:
            total = total + dot_plain(term, shift)
        tables_grad[...] = total

    def stats(position):
        row_total = jnp.zeros((1, 1), jnp.float32)
        for index, group in tiles[position]:
            row_sum = jnp.zeros((depth, 1), jnp.float32)
            for load, first, size in group:
                gradient = load()
                squared = gradient * gradient + TINY_SQUARE
                row_sum = row_sum + jnp.sum(squared, axis=1, keepdims=True)
                at = SUM_STARTS[position] + first
                sums[0, :, at : at + size] += jnp.sum(squared, axis=0, keepdims=True)
            rows_new = DECAY * moments_ref[index] + (1.0 - DECAY) * (
                row_sum * (1.0 / WEIGHT_COLUMNS[position])
            )
            rows_ref[index] = rows_new
            row_total = row_total + jnp.sum(rows_new, axis=0, keepdims=True)
        facts[...] += lane_row([(position, row_total)])

    def squares(first, end):
        for position in range(first, end):
            master = masters[position][...]
            facts[...] += lane_row([(8 + position, whole_sum(master * master))])

    def part_grad(part):
        @pl.loop(0, D // 256)
        def tile(i):
            at = columns(i * 256, 256)
            product = dot_first(normed_ref[...], heads_grad[part, :, at])
            part_grads[part, :, :, :, :, :, :, at] = product.astype(jnp.bfloat16).reshape(
                FIVE + (depth, 256)
            )

    tokens = normed_ref.shape[0]
    block = tokens // 4
    slot_rows = [jnp.zeros((1, D), jnp.float32)] * 4

    def norm_back(index):
        rows = slice(index * block, (index + 1) * block)
        back = jnp.zeros((block, D), jnp.float32)
        for part in range(3):
            back = back + dot_last(heads_grad[part, rows], qkv_full[:, part * D : (part + 1) * D])
        values = embedded[rows]
        center = values - jnp.sum(values, axis=1, keepdims=True) * (1.0 / D)
        rate = lax.rsqrt(jnp.sum(center * center, axis=1, keepdims=True) * (1.0 / D) + NORM_EPSILON)
        unit = center * rate
        other = second_ref[rows] > 0.5
        scale_back = back * unit
        for at, value in enumerate((scale_back, back)):
            everything = jnp.sum(value, axis=0, keepdims=True)
            second = jnp.sum(jnp.where(other, value, 0.0), axis=0, keepdims=True)
            slot_rows[2 * at] = slot_rows[2 * at] + (everything - second)
            slot_rows[2 * at + 1] = slot_rows[2 * at + 1] + second
        unit_back = back * (1.0 + jnp.where(other, scale_ref[1:2], scale_ref[0:1]))
        mean_back = jnp.sum(unit_back, axis=1, keepdims=True) * (1.0 / D)
        mean_along = jnp.sum(unit_back * unit, axis=1, keepdims=True) * (1.0 / D)
        total = grad[rows] + rate * (unit_back - mean_back - unit * mean_along)
        high = total.astype(jnp.bfloat16)
        rest = (total - high.astype(jnp.float32)).astype(jnp.bfloat16)
        product = dot_first(codes_ref[rows], high) + dot_first(codes_ref[rows], rest)
        code_sums[...] = product if index == 0 else code_sums[...] + product

    def gather_rows():
        spot = 2 * (4 * bit["y"] + 2 * bit["x"] + bit["c"])
        row_ids = lax.broadcasted_iota(jnp.int32, (16, D), 0)
        for kind in range(6):
            if kind in (2, 4):
                first, other = slot_rows[kind - 2 : kind]
            else:
                at = slice(kind * D, (kind + 1) * D)
                first, other = known_ref[0:1, at], known_ref[1:2, at]
            placed = jnp.where(row_ids == spot, first, jnp.where(row_ids == spot + 1, other, 0.0))
            mod_ref[:, kind * D : (kind + 1) * D] = placed.astype(jnp.bfloat16)
            code_sums[kind : kind + 1] = first + other
        code_sums[6:9] = gains_ref[0:3]
        small_ref[...] = code_sums[...].T.reshape(FIVE + (depth, 128))

    sums[0] = jnp.zeros_like(sums[0])
    facts[...] = lane_row([(16, loss_ref[...])])
    steps = iter(range(scatter.steps))
    for _ in range(narrow):
        scatter.step(next(steps))
    for part in range(3):
        part_grad(part)
        for _ in range(narrow):
            scatter.step(next(steps))
    for load in loads:
        load.wait()
    for index in range(4):
        norm_back(index)
        if index % 2:
            scatter.step(next(steps))
    gather_rows()
    beside = [
        partial(stats, 5),
        partial(stats, 6),
        partial(stats, 7),
        partial(squares, 0, 5),
        partial(squares, 5, 8),
    ]
    for t in range(6):
        mod_step(t)
        small.step(t)
        if t < len(beside):
            beside[t]()
        for step in steps:
            scatter.step(step)
            break
    ada_part()
    for step in steps:
        scatter.step(step)
    stats(0)
    stats(2)
    stats(3)
    stats(4)
    sums[0, :, SCALARS:] = facts[...]
    first_total.run()
    columns_ref[...] = DECAY * column_moment_ref[...] + (1.0 - DECAY) * sums[5] * (1.0 / D)
    start, end = SUM_STARTS[6], SUM_STARTS[6] + D
    columns_ref[:, start:end] = DECAY * column_moment_ref[:, start:end] + (1.0 - DECAY) * sums[
        5, :, start:end
    ] * (1.0 / (4 * D))

    def rows_all(position):
        return 4.0 * D if position == 6 else 1.0 * D

    scalars = []
    for position, groups in tiles.items():
        at = SCALARS + position
        row_mean = sums[5, :, at : at + 1] * (1.0 / rows_all(position))
        spread = jnp.zeros((1, 1), jnp.float32)
        for index, group in groups:
            for load, first, size in group:
                lane = SUM_STARTS[position] + first
                estimate = rows_ref[index] * columns_ref[:, lane : lane + size] / row_mean
                update = load() * lax.rsqrt(estimate)
                spread = spread + whole_sum(update * update)
        scalars.append((position, spread))
    gradient = small_done[:, :9]
    moment = DECAY * vector_moment_ref[...] + (1.0 - DECAY) * (gradient * gradient + TINY_SQUARE)
    update = gradient * lax.rsqrt(moment)
    scalars.append((1, whole_sum(update * update)))
    second_total.sums[0] = lane_row(scalars)
    second_total.run()
    spread_row, factor_row = [], []
    for position in range(8):
        count = rows_all(position) * WEIGHT_COLUMNS[position]
        spread = jnp.sqrt(second_total.sums[5, :, position : position + 1] * (1.0 / count))
        at = SCALARS + 8 + position
        scale = jnp.maximum(SCALE_FLOOR, jnp.sqrt(sums[5, :, at : at + 1] * (1.0 / count)))
        spread_row.append((position, spread))
        factor_row.append((position, STEP_RATE * scale / jnp.maximum(1.0, spread / CLIP_LIMIT)))
    facts_ref[0] = lane_row(spread_row)
    facts_ref[1] = lane_row(factor_row)
    facts_ref[2] = sums[5, :, SCALARS:]


def last_exchange(far, near, done, masters, moments):
    depth = far[0].shape[5]
    pairs = 4 * D // (2 * LAST_WIDTH)
    dma = pltpu.SemaphoreType.DMA
    f32, low = jnp.float32, jnp.bfloat16
    tokens = far[2].shape[0]
    operands = list(far) + list(near) + list(done) + list(masters) + list(moments)
    return pl.pallas_call(
        last_kernel,
        out_shape=(
            jax.ShapeDtypeStruct((pairs, depth, 2 * LAST_WIDTH), f32),
            jax.ShapeDtypeStruct((depth, 128), f32),
            jax.ShapeDtypeStruct((depth, 1152), f32),
            jax.ShapeDtypeStruct((depth, 6 * D), f32),
            jax.ShapeDtypeStruct((10, depth, 1), f32),
            jax.ShapeDtypeStruct((1, SUM_LANES), f32),
            jax.ShapeDtypeStruct((3, 1, 128), f32),
        ),
        in_specs=[ANY] * 4 + [WHOLE] * (len(operands) - 4),
        out_specs=(WHOLE,) * 7,
        scratch_shapes=Scatter.scratch((depth, LAST_WIDTH), low, LAST_LAG)
        + Scatter.scratch((depth // 2, 128), f32)
        + [
            pltpu.VMEM((2, 16, 6 * D), low),
            pltpu.VMEM((3, 16, 6 * D), low),
            pltpu.VMEM((2, 2, 16, 6 * D), low),
            dma((5,)),
            dma((5,)),
        ]
        + Total.scratch(SUM_LANES)
        + Total.scratch(128)
        + [pltpu.VMEM((1, 128), f32)]
        + [
            pltpu.VMEM((3,) + FIVE + (depth, D), low),
            pltpu.VMEM((D, 3 * D), low),
            pltpu.VMEM((tokens, D), f32),
            pltpu.VMEM((tokens, D), f32),
            pltpu.VMEM((128, D), f32),
            pltpu.VMEM((16, 6 * D), low),
            pltpu.VMEM(FIVE + (depth, 128), f32),
            dma((3,)),
        ],
        compiler_params=params(4),
        name="last_scatter",
    )(*operands)


def step_kernel(
    done_ref,
    small_ref,
    tables_grad,
    ada_grad,
    rows_ref,
    columns_ref,
    facts_ref,
    done_head,
    attention_ref,
    vector_moment_ref,
    tables_ref,
    vectors_ref,
    ada_ref,
    qkv_master,
    out_master,
    up_master,
    down_master,
    head_master,
    *outs,
):
    depth = tables_ref.shape[0]
    masters = (
        tables_ref,
        vectors_ref,
        ada_ref,
        qkv_master,
        out_master,
        up_master,
        down_master,
        head_master,
    )
    vector_stat = outs[16]
    tiles = weight_tiles(tables_grad, ada_grad, done_head, attention_ref, done_ref)
    for position, groups in tiles.items():
        grad_ref, next_ref, master = outs[2 * position], outs[2 * position + 1], masters[position]
        factor = facts_ref[1, :, position : position + 1]
        mean_scale = 1.0 / (4 * D) if position == 6 else 1.0 / D
        row_mean = facts_ref[2, :, position : position + 1] * mean_scale
        for order, (index, group) in enumerate(groups):
            at = slice(order * depth, (order + 1) * depth)
            for load, first, size in group:
                gradient = load()
                lane = SUM_STARTS[position] + first
                estimate = rows_ref[index] * columns_ref[:, lane : lane + size] / row_mean
                grad_ref[at, first : first + size] = gradient
                next_ref[at, first : first + size] = master[at, first : first + size] - factor * (
                    gradient * lax.rsqrt(estimate)
                )
    gradient = small_ref[:, :9]
    moment = DECAY * vector_moment_ref[...] + (1.0 - DECAY) * (gradient * gradient + TINY_SQUARE)
    vector_stat[...] = moment
    outs[2][...] = gradient
    outs[3][...] = vectors_ref[...] - facts_ref[1, :, 1:2] * (gradient * lax.rsqrt(moment))


def take_step(last, done, vector_moment, masters):
    operands = list(last) + list(done) + [vector_moment] + list(masters)
    shapes = []
    for master in masters:
        shapes += [jax.ShapeDtypeStruct(master.shape, jnp.float32)] * 2
    shapes.append(jax.ShapeDtypeStruct(vector_moment.shape, jnp.float32))
    return pl.pallas_call(
        step_kernel,
        out_shape=tuple(shapes),
        in_specs=[WHOLE] * len(operands),
        out_specs=(WHOLE,) * len(shapes),
        compiler_params=pltpu.CompilerParams(vmem_limit_bytes=VMEM_GRANT),
        name="weight_step",
    )(*operands)


def linked_mesh():
    return lax.axis_size("fsdp") == 8 and lax.axis_size("sub") == 4


def gathered(values):
    return lax.all_gather(values, AXES, axis=0, tiled=True)


def scattered(values):
    return lax.psum_scatter(values, AXES, scatter_dimension=0, tiled=True)


def layer_norm(values):
    center = values - jnp.mean(values, axis=-1, keepdims=True)
    return center * lax.rsqrt(jnp.mean(center * center, axis=-1, keepdims=True) + NORM_EPSILON)


def modulate(values, scale_part, shift_part):
    return layer_norm(values) * (1.0 + scale_part) + shift_part


def final_norm(values, gain_vector):
    return layer_norm(values) * gain_vector


def attention_bias(query, key):
    usable = (query[1] == key[1]) & (key[0] <= query[0]) & ((key[2] == 1) | (query[3] == key[3]))
    return jnp.where(usable, 0.0, MASK_VALUE)


def split_product(left_side, right_low):
    high = left_side.astype(jnp.bfloat16)
    rest = (left_side - high.astype(jnp.float32)).astype(jnp.bfloat16)
    return bfloat_product(high, right_low) + bfloat_product(rest, right_low)


def on_device(
    code_vectors,
    scale_ids,
    segment_ids,
    real_mask,
    labels,
    targets,
    loss_weight,
    tables,
    vectors,
    ada_weight,
    qkv_weight,
    out_weight,
    up_weight,
    down_weight,
    head_weight,
    tables_moment,
    ada_moment,
    qkv_moment,
    out_moment,
    up_moment,
    down_moment,
    head_moment,
    vector_moment,
    column_moment,
):
    devices = lax.axis_size(AXES)
    linked = linked_mesh()
    depth = tables.shape[0]
    tokens = code_vectors.shape[0]
    masters = (
        tables,
        vectors,
        ada_weight,
        qkv_weight,
        out_weight,
        up_weight,
        down_weight,
        head_weight,
    )
    local_count = jnp.sum(loss_weight).astype(jnp.float32)
    low = jnp.bfloat16
    part_kind = low if linked else jnp.float32
    tables_low = tables.astype(low)
    ada_low = ada_weight.astype(low)
    qkv_low = qkv_weight.astype(low)
    out_low = out_weight.astype(low)
    down_low = down_weight.astype(low)

    if linked:
        cores = [[core + 2 * chip for chip in range(devices // 2)] for core in range(2)]
        up_head = lax.all_gather(
            jnp.concatenate([up_weight, head_weight], axis=1).astype(low),
            AXES,
            axis_index_groups=cores,
            axis=0,
            tiled=True,
        ).reshape(2, 2, 2, 2, depth, -1)
    else:
        full_up = gathered(up_weight.astype(low))
        full_head = gathered(head_weight.astype(low))
    small_rows = jnp.concatenate(
        [vectors.astype(low), tables_low[:, CLASSES:], jnp.zeros((depth, 128 - SMALL_LANES), low)], axis=1
    )
    tag_row = jnp.concatenate([labels.astype(jnp.float32), local_count[None], jnp.zeros((5,), jnp.float32)])
    tags = jnp.broadcast_to(tag_row[:, None], (8, 128))
    level_hot = (scale_ids[:, None] == jnp.arange(LEVELS)[None, :]).astype(low)
    code_levels = jnp.concatenate([code_vectors, level_hot], axis=1)
    codes = jnp.pad(code_levels, ((0, 0), (9, 128 - SMALL_LANES)))
    second = (segment_ids == 1)[:, None]
    if linked:
        token_rows = jnp.stack([segment_ids, scale_ids, real_mask] + [real_mask] * 5).astype(jnp.float32)
        token_columns = jnp.pad(token_rows[:3].T, ((0, 0), (0, 125)))
        (
            projected,
            full_qkv,
            full_out,
            embedded,
            normed,
            modulation,
            vector_rows,
            label_hot,
            class_cond,
            activated,
            tag_sums,
            bias,
            turned_bias,
        ) = begin(
            small_rows, tags, tables, ada_weight, qkv_weight, out_weight, codes, token_columns, token_rows
        )
        full_qkv, full_out = full_qkv.reshape(D, 3 * D), full_out.reshape(D, D)
        weight_total = tag_sums[2, 0]
        gains = vector_rows[6:14]
        head_gain = vector_rows[8]
    else:
        small_full = gathered(small_rows)
        tags_full = gathered(tags).reshape(devices, 8, 128)[:, :, 0]
        labels_all = tags_full[:, :2].reshape(2 * devices)
        weight_total = jnp.sum(tags_full[:, 2])
        gain_vector = small_full[:, :9].astype(jnp.float32)
        label_hot = (labels_all[:, None] == jnp.arange(1152, dtype=jnp.float32)[None, :]).astype(low)
        class_cond = bfloat_product(label_hot[:, :CLASSES], tables_low[:, :CLASSES].T)
        activated = jax.nn.silu(class_cond).astype(low)
        own_modulation, full_qkv = scattered(bfloat_product(activated, ada_low)), gathered(qkv_low)
        modulation = own_modulation + gain_vector[:, :6].T.reshape(1, 6 * D)
        embedded = bfloat_product(codes, small_full.T)
        gains = jnp.pad(gain_vector[:, 6:8].T, ((0, 6), (0, 0)))
        head_gain = gain_vector[:, 8]

    def of_token(block):
        piece = modulation[:, block * D : (block + 1) * D]
        return jnp.where(second, piece[1:2], piece[0:1])

    gamma_one, gamma_two, scale_one, scale_two, shift_one, shift_two = (
        of_token(block) for block in range(6)
    )
    if linked:
        mixed_heads, exact, totals, full_down, full_up, full_head = attend(
            projected, gains, bias, down_low, up_head
        )
        full_down = full_down.reshape(-1, D)
        full_up, full_head = full_up.reshape(D, -1), full_head.reshape(D, -1)
    else:
        normed = modulate(embedded, scale_one, shift_one).astype(low)
        projected = bfloat_product(normed, full_qkv)
        places = jnp.arange(tokens)
        masks = (scale_ids, segment_ids, real_mask, places)
        bias = attention_bias([m[:, None] for m in masks], [m[None, :] for m in masks])
        turned_bias = attention_bias([m[None, :] for m in masks], [m[:, None] for m in masks])
        mixed_heads, exact, totals = attend(projected, gains, bias)
        full_out, full_down = gathered(out_low), gathered(down_low)
    attended = bfloat_product(mixed_heads, full_out)
    residual_one = embedded + gamma_one * attended
    normed_two = modulate(residual_one, scale_two, shift_two).astype(low)
    hidden_pre = bfloat_product(normed_two, full_up)
    hidden_act = jax.nn.gelu(hidden_pre, approximate=True).astype(low)
    branch = bfloat_product(hidden_act, full_down)
    residual_two = residual_one + gamma_two * branch
    final_normed = final_norm(residual_two, head_gain).astype(low)
    logits = bfloat_product(final_normed, full_head)
    logit_peak = jnp.max(logits, axis=-1, keepdims=True)
    log_total = logit_peak + jnp.log(jnp.sum(jnp.exp(logits - logit_peak), axis=-1, keepdims=True))
    target_hot = targets[:, None] == jnp.arange(CODES)[None, :]
    picked = jnp.sum(jnp.where(target_hot, logits, 0.0), axis=-1, keepdims=True)
    weight_column = loss_weight.astype(jnp.float32)[:, None]
    local_loss = jnp.sum(weight_column * (log_total - picked))
    logit_grad = (
        (jnp.exp(logits - log_total) - target_hot.astype(jnp.float32))
        * (weight_column / weight_total)
    ).astype(low)

    head_part = bfloat_product(final_normed.T, logit_grad).astype(part_kind)
    final_grad = bfloat_product(logit_grad, full_head.T)
    _, final_back = jax.vjp(final_norm, residual_two, head_gain)
    residual_grad, head_gain_grad = final_back(final_grad)
    branch_grad = (gamma_two * residual_grad).astype(low)

    def slot_sums(token_grad):
        other = jnp.sum(jnp.where(second, token_grad, 0.0), axis=0)
        first = jnp.sum(jnp.where(second, 0.0, token_grad), axis=0)
        return jnp.stack([first, other])

    gamma_two_grad = slot_sums(residual_grad * branch)
    if linked:
        mods = jnp.concatenate([modulation[:, 3 * D : 4 * D], modulation[:, :D], jnp.zeros((4, D), jnp.float32)])
        up_part, down_part, residual_grad, attended_grad, slot_rows, head_done = dense_back(
            branch_grad,
            normed_two,
            hidden_pre,
            full_down,
            full_up,
            residual_one,
            residual_grad,
            attended,
            token_columns,
            mods,
            head_part.reshape(FIVE + (depth, CODES)),
        )
        scale_two_grad, shift_two_grad, gamma_one_grad = slot_rows[0:2], slot_rows[2:4], slot_rows[4:6]
    else:
        down_part = bfloat_product(hidden_act.T, branch_grad).astype(part_kind)
        act_grad = bfloat_product(branch_grad, full_down.T)
        _, gelu_back = jax.vjp(partial(jax.nn.gelu, approximate=True), hidden_pre)
        pre_grad = gelu_back(act_grad)[0].astype(low)
        up_part = bfloat_product(normed_two.T, pre_grad).astype(part_kind)
        normed_two_grad = bfloat_product(pre_grad, full_up.T)
        _, modulate_two_back = jax.vjp(modulate, residual_one, scale_two, shift_two)
        norm_grad, scale_two_grad, shift_two_grad = modulate_two_back(normed_two_grad)
        scale_two_grad, shift_two_grad = slot_sums(scale_two_grad), slot_sums(shift_two_grad)
        residual_grad = residual_grad + norm_grad
        attended_grad = (gamma_one * residual_grad).astype(low)
        gamma_one_grad = slot_sums(residual_grad * attended)
    out_part = bfloat_product(mixed_heads.T, attended_grad).astype(part_kind)
    mixed_grad = bfloat_product(attended_grad, full_out.T).astype(low)
    if linked:
        heads_grad, gain_grads, attention_done = attend_back(
            projected,
            mixed_grad,
            exact,
            totals,
            gains,
            turned_bias,
            up_part.reshape(FIVE + (depth, up_part.shape[1])),
            down_part.reshape(FIVE + (down_part.shape[0] // D, depth, D)),
        )
    else:
        heads_grad, gain_grads = attend_back(projected, mixed_grad, exact, totals, gains, turned_bias)
        head_grad, up_grad, down_grad = scattered(head_part), scattered(up_part), scattered(down_part)
    if linked:
        unknown = jnp.zeros((2, D), jnp.float32)
        factored_rows = [tables_moment, ada_moment, qkv_moment, out_moment, up_moment, head_moment]
        row_moments = jnp.concatenate(factored_rows + [down_moment]).reshape(10, depth, 1)
        padding = jnp.zeros((110,), jnp.float32)
        column_moments = jnp.concatenate(
            [column_moment[:1042], padding, column_moment[1042:], jnp.zeros((128,), jnp.float32)]
        )[None]
        known = jnp.concatenate(
            [gamma_one_grad, gamma_two_grad, unknown, scale_two_grad, unknown, shift_two_grad], axis=1
        )
        gain_rows = jnp.concatenate([gain_grads[:2], head_gain_grad[None], jnp.zeros((5, D), jnp.float32)])
        last = last_exchange(
            (out_part.reshape(FIVE + (depth, D)), full_qkv, embedded, residual_grad),
            (
                heads_grad,
                normed,
                codes,
                second.astype(jnp.float32),
                modulation[:, 2 * D : 3 * D],
                known,
                gain_rows,
                activated,
                class_cond,
                label_hot,
                local_loss[None, None],
            ),
            (head_done, attention_done),
            masters,
            (row_moments, vector_moment, column_moments),
        )
        stepped = take_step(last, (head_done, attention_done), vector_moment, masters)
        rows_new, cols_new, facts = last[4].reshape(10 * depth), last[5][0], last[6][:, 0]
        stats = [rows_new[i * depth : (i + 1) * depth] for i in range(6)] + [rows_new[6 * depth :]]
        moment_of = (stats[0], stepped[16], stats[1], stats[2], stats[3], stats[4], stats[6], stats[5])
        results = [facts[2, 16], weight_total]
        for position in range(8):
            results += [stepped[2 * position], moment_of[position], stepped[2 * position + 1]]
        column_stat = jnp.concatenate([cols_new[:1042], cols_new[1152:SCALARS]])
        return tuple(results + [column_stat, facts[0, :8]])

    qkv_part = jnp.concatenate(
        [bfloat_product(normed.T, heads_grad[part]).astype(part_kind) for part in range(3)], axis=1
    )
    normed_grad = sum(
        bfloat_product(heads_grad[part], full_qkv[:, part * D : (part + 1) * D].T) for part in range(3)
    )
    _, modulate_one_back = jax.vjp(modulate, embedded, scale_one, shift_one)
    norm_grad, scale_one_grad, shift_one_grad = modulate_one_back(normed_grad)
    scale_one_grad, shift_one_grad = slot_sums(scale_one_grad), slot_sums(shift_one_grad)
    embedded_grad = residual_grad + norm_grad
    modulation_grad = jnp.concatenate(
        [
            gamma_one_grad,
            gamma_two_grad,
            scale_one_grad,
            scale_two_grad,
            shift_one_grad,
            shift_two_grad,
        ],
        axis=1,
    )
    bias_grad = jnp.sum(modulation_grad, axis=0).reshape(6, D)
    code_grad = split_product(embedded_grad.T, code_levels)
    small_part = jnp.concatenate(
        [
            bias_grad.T,
            gain_grads[:2].T,
            head_gain_grad[:, None],
            code_grad,
            jnp.zeros((D, 128 - CODE_DIM - LEVELS - 9), jnp.float32),
        ],
        axis=1,
    )
    modulation_low = modulation_grad.astype(low)
    modulation_all = gathered(modulation_low)
    small_grad, qkv_grad, out_grad = scattered(small_part), scattered(qkv_part), scattered(out_part)
    ada_grad = bfloat_product(activated.T, modulation_all)
    activated_grad = bfloat_product(modulation_all, ada_low.T)
    _, silu_back = jax.vjp(jax.nn.silu, class_cond)
    cond_grad = silu_back(activated_grad)[0]
    class_grad = jnp.dot(
        cond_grad.T,
        label_hot[:, :CLASSES].astype(jnp.float32),
        precision=lax.Precision.HIGHEST,
        preferred_element_type=jnp.float32,
    )
    tables_grad = jnp.concatenate([class_grad, small_grad[:, 9:SMALL_LANES]], axis=1)
    vectors_grad = small_grad[:, :9]
    gradients = (
        tables_grad,
        vectors_grad,
        ada_grad,
        qkv_grad,
        out_grad,
        up_grad,
        down_grad,
        head_grad,
    )
    second_decay = DECAY
    factored_index = (0, 2, 3, 4, 5, 6, 7)
    factored_moments = (
        tables_moment,
        ada_moment,
        qkv_moment,
        out_moment,
        up_moment,
        down_moment,
        head_moment,
    )
    local_squares = jnp.stack([jnp.sum(master * master) for master in masters])
    rows_list = []
    column_parts = []
    row_parts = []
    for position, moment in zip(factored_index, factored_moments):
        gradient = gradients[position]
        squared = gradient * gradient + TINY_SQUARE
        rows_new = second_decay * moment + (1.0 - second_decay) * jnp.mean(squared, axis=1)
        rows_list.append(rows_new)
        column_parts.append(jnp.sum(squared, axis=0))
        row_parts.append(jnp.sum(rows_new))
    column_count = column_moment.shape[0]
    sums = lax.psum(
        jnp.concatenate(column_parts + [jnp.stack(row_parts), local_squares, local_loss[None]]), AXES
    )
    column_total = sums[:column_count]
    row_total = sums[column_count : column_count + 7]
    weight_squares = sums[column_count + 7 : column_count + 15]
    loss_sum = sums[column_count + 15]
    updates = [None] * 8
    moments_new = [None] * 8
    column_new = []
    offset = 0
    for factor_slot, position in enumerate(factored_index):
        gradient = gradients[position]
        rows_all = gradient.shape[0] * devices
        column_count = gradient.shape[1]
        cols_new = second_decay * column_moment[offset : offset + column_count] + (
            1.0 - second_decay
        ) * (column_total[offset : offset + column_count] / rows_all)
        offset += column_count
        estimate = (
            rows_list[factor_slot][:, None]
            * cols_new[None, :]
            / (row_total[factor_slot] / rows_all)
        )
        updates[position] = gradient * lax.rsqrt(estimate)
        moments_new[position] = rows_list[factor_slot]
        column_new.append(cols_new)
    vector_new = second_decay * vector_moment + (1.0 - second_decay) * (
        gradients[1] * gradients[1] + TINY_SQUARE
    )
    updates[1] = gradients[1] * lax.rsqrt(vector_new)
    moments_new[1] = vector_new
    local_spread = jnp.stack([jnp.sum(update * update) for update in updates])
    spread_total = lax.psum(local_spread, AXES)
    next_weights = []
    spreads = []
    for position in range(8):
        count_all = gradients[position].size * devices
        spread = jnp.sqrt(spread_total[position] / count_all)
        step_scale = jnp.maximum(SCALE_FLOOR, jnp.sqrt(weight_squares[position] / count_all))
        next_weights.append(
            masters[position]
            - STEP_RATE * step_scale * (updates[position] / jnp.maximum(1.0, spread / CLIP_LIMIT))
        )
        spreads.append(spread)
    column_stat = jnp.concatenate(column_new)
    clip_spread = jnp.stack(spreads)
    results = [loss_sum, weight_total]
    for position in range(8):
        results += [gradients[position], moments_new[position], next_weights[position]]
    return tuple(results + [column_stat, clip_spread])


def solution(mesh):
    in_specs = (
        P(("fsdp", "sub"), None),
        P(("fsdp", "sub")),
        P(("fsdp", "sub")),
        P(("fsdp", "sub")),
        P(("fsdp", "sub")),
        P(("fsdp", "sub")),
        P(("fsdp", "sub")),
        P(("fsdp", "sub"), None),
        P(("fsdp", "sub"), None),
        P(("fsdp", "sub"), None),
        P(("fsdp", "sub"), None),
        P(("fsdp", "sub"), None),
        P(("fsdp", "sub"), None),
        P(("fsdp", "sub"), None),
        P(("fsdp", "sub"), None),
        P(("fsdp", "sub")),
        P(("fsdp", "sub")),
        P(("fsdp", "sub")),
        P(("fsdp", "sub")),
        P(("fsdp", "sub")),
        P(("fsdp", "sub")),
        P(("fsdp", "sub")),
        P(("fsdp", "sub"), None),
        P(),
    )
    out_specs = (
        P(),
        P(),
        P(("fsdp", "sub"), None),
        P(("fsdp", "sub")),
        P(("fsdp", "sub"), None),
        P(("fsdp", "sub"), None),
        P(("fsdp", "sub"), None),
        P(("fsdp", "sub"), None),
        P(("fsdp", "sub"), None),
        P(("fsdp", "sub")),
        P(("fsdp", "sub"), None),
        P(("fsdp", "sub"), None),
        P(("fsdp", "sub")),
        P(("fsdp", "sub"), None),
        P(("fsdp", "sub"), None),
        P(("fsdp", "sub")),
        P(("fsdp", "sub"), None),
        P(("fsdp", "sub"), None),
        P(("fsdp", "sub")),
        P(("fsdp", "sub"), None),
        P(("fsdp", "sub"), None),
        P(("fsdp", "sub")),
        P(("fsdp", "sub"), None),
        P(("fsdp", "sub"), None),
        P(("fsdp", "sub")),
        P(("fsdp", "sub"), None),
        P(),
        P(),
    )
    return jax.shard_map(
        on_device, mesh=mesh, in_specs=in_specs, out_specs=out_specs, check_vma=False
    )
```

```python
import math
from functools import partial

import jax
import jax.numpy as jnp
from jax import lax
from jax.experimental import pallas as pl
from jax.experimental.pallas import tpu as pltpu
from jax.sharding import PartitionSpec as P

D = 1024
HEADS = 16
HEAD_DIM = 64
CLASSES = 1000
CODES = 4096
CODE_DIM = 32
LEVELS = 10
STEP = 10


TINY_SQUARE = 1e-30
SCALE_FLOOR = 0.001
STEP_RATE = 1.0
CLIP_LIMIT = 1.0
NORM_EPSILON = 1e-06
MASK_VALUE = -1000000000.0

AXES = ("fsdp", "sub")
MESH = pl.DeviceIdType.MESH
ANY = pl.BlockSpec(memory_space=pl.ANY)
WHOLE = pl.BlockSpec(memory_space=pltpu.VMEM)
FIVE = (2, 2, 2, 2, 2)
DIMS = ("w", "u", "y", "x", "c")
SCATTER_ORDERS = (("c", "x", "y", "w", "u"), ("c", "y", "x", "w", "u"))
GATHER_ORDERS = tuple(order[::-1] for order in SCATTER_ORDERS)
SCORE_SCALE = HEAD_DIM ** (-0.5)
EXP_SCALE = SCORE_SCALE * math.log2(math.e)
VMEM_GRANT = 58 * 1024 * 1024
FIRST_WIDTH, FIRST_LAG = 256, 2
ATTEND_WIDTH, ATTEND_LAG = 128, 3
BACK_WIDTH, BACK_LAG = 256, 3
LAST_WIDTH, LAST_LAG = 256, 2


def bfloat_product(left_side, right_side):
    return jnp.dot(left_side, right_side, preferred_element_type=jnp.float32)


class Place:
    def __init__(self):
        fsdp, sub = lax.axis_index("fsdp"), lax.axis_index("sub")
        self.bit = {
            "c": lax.rem(sub, 2),
            "x": lax.div(sub, 2),
            "y": lax.rem(fsdp, 2),
            "u": lax.rem(lax.div(fsdp, 2), 2),
            "w": lax.div(fsdp, 4),
        }
        bit = self.bit
        self.partner = {
            "c": (fsdp, sub + 1 - 2 * bit["c"]),
            "x": (fsdp, sub + 2 - 4 * bit["x"]),
            "y": (fsdp + 1 - 2 * bit["y"], sub),
            "u": (fsdp + 2 - 4 * bit["u"], sub),
            "w": (fsdp + 4 - 8 * bit["w"], sub),
        }

    def meet(self):
        barrier = pltpu.get_barrier_semaphore()
        for dim in DIMS:
            pl.semaphore_signal(
                barrier, inc=1, device_id=self.partner[dim], device_id_type=MESH
            )
        pl.semaphore_wait(barrier, 5)

    def send(self, src, dst, send_sem, recv_sem, dim):
        return pltpu.make_async_remote_copy(
            src_ref=src,
            dst_ref=dst,
            send_sem=send_sem,
            recv_sem=recv_sem,
            device_id=self.partner[dim],
            device_id_type=MESH,
        )


def when_in(index, low, high, body):
    if isinstance(index, int):
        if low <= index < high:
            body()
    else:
        pl.when((index >= low) & (index < high))(body)


class Gather:
    def __init__(self, place, groups, sends, recvs, local_sems, lag=1):
        self.place, self.groups, self.lag = place, groups, lag
        self.sends, self.recvs, self.local_sems = sends, recvs, local_sems
        self.steps = groups[-1][1] + 5 * lag

    @staticmethod
    def scratch(lag=1):
        dma = pltpu.SemaphoreType.DMA
        return [dma((5, 2, 2 * lag)), dma((5, 2, 2 * lag)), dma((2, 2 * lag))]

    def region(self, stage, parity):
        done = GATHER_ORDERS[parity][:stage]
        return tuple(slice(None) if d in done else self.place.bit[d] for d in DIMS)

    def copy(self, group, j, stage, parity, slot):
        _, _, own, full = group
        ref = full(j, parity, self.region(stage, parity))
        return self.place.send(
            own(j, parity) if stage == 0 else ref,
            ref,
            self.sends.at[stage, parity, slot],
            self.recvs.at[stage, parity, slot],
            GATHER_ORDERS[parity][stage],
        )

    def local(self, group, j, parity, slot):
        _, _, own, full = group
        return pltpu.make_async_copy(
            own(j, parity), full(j, parity, self.region(0, parity)), self.local_sems.at[parity, slot]
        )

    def step(self, t):
        for stage in reversed(range(6)):
            j = t - stage * self.lag
            for group in self.groups:

                def body(group=group, stage=stage, j=j):
                    slot = lax.rem(j, 2 * self.lag)
                    for parity in range(2):
                        if stage == 0:
                            self.local(group, j, parity, slot).start()
                        if stage == 1:
                            self.local(group, j, parity, slot).wait()
                        if stage >= 1:
                            self.copy(group, j, stage - 1, parity, slot).wait()
                        if stage < 5:
                            self.copy(group, j, stage, parity, slot).start()

                when_in(j, group[0], group[1], body)


class Scatter:
    def __init__(self, place, groups, store, scratch, lag=1):
        self.place, self.groups, self.store, self.lag = place, groups, store, lag
        self.keep = scratch[0]
        self.land = scratch[1:6]
        self.sums = (None,) + tuple(scratch[6:10])
        self.sends, self.recvs, self.keep_sems = scratch[10:13]
        self.first, self.end = groups[0][0], groups[-1][1]
        self.steps = self.end + 5 * lag
        rows, lanes = self.land[4].shape[2:]
        by_rows = self.keep.shape[5] != rows
        self.parts = [
            (slice(None),) * 4
            + (
                (slice(p * rows, (p + 1) * rows), slice(None))
                if by_rows
                else (slice(None), slice(p * lanes, (p + 1) * lanes))
            )
            for p in range(2)
        ]

    @staticmethod
    def scratch(piece, kind, lag=1, by_rows=False):
        dma = pltpu.SemaphoreType.DMA
        whole = (2 * piece[0], piece[1]) if by_rows else (piece[0], 2 * piece[1])
        return (
            [pltpu.VMEM((lag,) + (2,) * 4 + whole, kind), pltpu.VMEM((2 * lag,) + (2,) * 4 + whole, kind)]
            + [pltpu.VMEM((2 * lag, 2) + (2,) * (4 - k) + piece, kind) for k in range(1, 5)]
            + [pltpu.VMEM((lag, 2) + (2,) * (5 - k) + piece, kind) for k in range(1, 5)]
            + [dma((5, 2, 2 * lag)), dma((5, 2, 2 * lag)), dma((lag,))]
        )

    def half(self, stage, parity, other):
        order = SCATTER_ORDERS[parity]
        left = [d for d in DIMS if d not in order[:stage]]
        bit = self.place.bit[order[stage]]
        value = 1 - bit if other else bit
        return tuple(value if d == order[stage] else slice(None) for d in left)

    def copies(self, stage, j, source=None):
        slot, near = lax.rem(j, 2 * self.lag), lax.rem(j, self.lag)
        if stage == 0:
            pieces = [(self.keep.at[near] if source is None else source, self.land[0].at[slot])]
        elif stage < 3:
            pieces = [
                (
                    self.sums[stage].at[(near, parity) + self.half(stage, parity, True)],
                    self.land[stage].at[slot, parity],
                )
                for parity in range(2)
            ]
        else:
            at = (near, slice(None)) + self.half(stage, 0, True)
            pieces = [(self.sums[stage].at[at], self.land[stage].at[slot])]
        return [
            self.place.send(
                piece,
                target,
                self.sends.at[stage, parity, slot],
                self.recvs.at[stage, parity, slot],
                SCATTER_ORDERS[parity][stage],
            )
            for parity, (piece, target) in enumerate(pieces)
        ]

    def kept(self, j):
        near = lax.rem(j, self.lag)
        return self.keep.at[near], self.keep_sems.at[near]

    def step(self, t):
        for stage in reversed(range(6)):
            j = t - stage * self.lag

            def body(stage=stage, j=j):
                slot, near = lax.rem(j, 2 * self.lag), lax.rem(j, self.lag)
                before = stage - 1
                if before == 0:
                    keep, sem = self.kept(j)
                    pltpu.make_async_copy(keep, keep, sem).wait()
                for copy in self.copies(before, j):
                    copy.wait()
                if before < 3:
                    for parity in range(2):
                        if before == 0:
                            mine = self.keep[(near,) + self.parts[parity]]
                            landed = self.land[0][(slot,) + self.parts[parity]]
                        else:
                            mine = self.sums[before][(near, parity) + self.half(before, parity, False)]
                            landed = self.land[before][slot, parity]
                        self.sums[stage][near, parity] = mine + landed
                else:
                    mine = self.sums[before][(near, slice(None)) + self.half(before, 0, False)]
                    landed = self.land[before][slot]
                    if stage < 5:
                        self.sums[stage][near] = mine + landed
                    else:
                        total = mine.astype(jnp.float32) + landed.astype(jnp.float32)
                        for parity in range(2):
                            self.store(j, parity, total[parity])
                if stage < 5:
                    for copy in self.copies(stage, j):
                        copy.start()

            if stage == 0:
                for low, high, source in self.groups:

                    def begin(source=source, j=j):
                        core = self.place.bit["c"]
                        for copy in self.copies(0, j, source(j, 1 - core)):
                            copy.start()
                        pltpu.make_async_copy(source(j, core), *self.kept(j)).start()

                    when_in(j, low, high, begin)
            else:
                when_in(j, self.first, self.end, body)


def finish(engine):
    done = UNITS * (HEADS // 2)

    @pl.when(pl.program_id(0) == HEADS // 2 - 1)
    def rest():
        for t in range(done, engine.steps):
            engine.step(t)


def params(collective_id, **more):
    return pltpu.CompilerParams(
        collective_id=collective_id, has_side_effects=True, vmem_limit_bytes=VMEM_GRANT, **more
    )


def columns(start, size):
    return pl.ds(pl.multiple_of(start, 128), size)


def slot_labels(tags_full, order):
    pieces = []
    for number in range(32):
        bits = {dim: (number >> (4 - at)) & 1 for at, dim in enumerate(order)}
        pieces.append(tags_full[bits["w"], bits["u"], bits["y"], bits["x"], bits["c"], 0:2])
    return jnp.concatenate(pieces, axis=0)


def hot_of(labels):
    lanes = lax.broadcasted_iota(jnp.int32, labels.shape, 1).astype(jnp.float32)
    blocks = [jnp.where(labels == lanes + 128.0 * at, 1.0, 0.0) for at in range(9)]
    return jnp.concatenate(blocks, axis=1).astype(jnp.bfloat16)


def begin_kernel(
    rows_ref,
    tags_ref,
    tables_ref,
    ada_ref,
    qkv_ref,
    out_own_ref,
    codes_ref,
    token_columns,
    token_rows,
    projected_ref,
    qkv_out,
    out_full,
    embedded_ref,
    normed_ref,
    modulation_ref,
    vectors_ref,
    hot_ref,
    cond_ref,
    act_ref,
    tag_sums,
    bias_ref,
    turned_ref,
    *scratch,
):
    place = Place()
    place.meet()
    bit = place.bit
    (
        rows_full,
        tags_full,
        own_qkv,
        own_out,
        qkv_full,
        part,
        unit,
        staged,
        copy_sems,
        mod_sends,
        mod_recvs,
    ) = scratch[:11]
    mod_land, mod_sums = scratch[11:16], scratch[16:21]
    own_qkv[...] = qkv_ref[...].astype(jnp.bfloat16)
    own_out[...] = out_own_ref[...].astype(jnp.bfloat16)
    small = Gather(
        place,
        [(0, 1, lambda j, p: (rows_ref, tags_ref)[p], lambda j, p, r: (rows_full, tags_full)[p].at[r])],
        *scratch[21:24],
    )
    width = FIRST_WIDTH
    pairs = 3 * D // (2 * width)

    def of_weight(own, full, first):
        return (
            lambda j, p: own.at[:, columns((2 * (j - first) + p) * width, width)],
            lambda j, p, r: full.at[r + (slice(None), columns((2 * (j - first) + p) * width, width))],
        )

    gather = Gather(
        place,
        [
            (0, pairs) + of_weight(own_qkv, qkv_full, 0),
            (pairs, pairs + D // (2 * width)) + of_weight(own_out, out_full, pairs),
        ],
        *scratch[24:27],
        lag=FIRST_LAG,
    )
    lanes = 3 * D
    orders = (("x", "y", "w", "u", "c"), ("y", "x", "w", "u", "c"))

    def mod_half(stage, parity, other):
        dim = orders[parity][stage]
        value = 1 - bit[dim] if other else bit[dim]
        left = [d for d in ("x", "y", "w") if d not in orders[parity][:stage]]
        return tuple(value if d == dim else slice(None) for d in left)

    def mod_view(stage, parity, other):
        if stage == 0:
            at = pl.ds(parity * lanes, lanes)
            return part, mod_half(0, parity, other) + (slice(None), at)
        if stage < 3:
            return mod_sums[stage - 1], (parity,) + mod_half(stage, parity, other)
        return mod_sums[stage - 1], (parity,)

    def mod_copy(stage, parity):
        ref, at = mod_view(stage, parity, True)
        return place.send(
            ref.at[at],
            mod_land[stage].at[parity],
            mod_sends.at[stage, parity],
            mod_recvs.at[stage, parity],
            orders[parity][stage],
        )

    def mod_step(stage):
        for parity in range(2):
            if stage:
                mod_copy(stage - 1, parity).wait()
                ref, at = mod_view(stage - 1, parity, False)
                mod_sums[stage - 1][parity] = ref[at] + mod_land[stage - 1][parity]
            if stage < 5:
                mod_copy(stage, parity).start()

    def mask(query, key, same):
        usable = (query[0] == key[0]) & (key[1] <= query[1]) & ((key[2] > 0.5) | same)
        return jnp.where(usable, 0.0, MASK_VALUE)

    tokens = codes_ref.shape[0]
    block = tokens // 4

    def masks(index, size):
        at = slice(index * size, (index + 1) * size)
        shape = (size, tokens)
        same = lax.broadcasted_iota(jnp.int32, shape, 0) + index * size == lax.broadcasted_iota(
            jnp.int32, shape, 1
        )
        down = [token_columns[at, i : i + 1] for i in range(3)]
        across = [token_rows[i : i + 1] for i in range(3)]
        bias_ref[at] = mask(down, across, same)
        turned_ref[at] = mask(across, down, same)

    def embed(index):
        at = slice(index * block, (index + 1) * block)
        values = dot_last(codes_ref[at], rows_full[...].reshape(D, 128))
        embedded_ref[at] = values
        center = values - jnp.sum(values, axis=1, keepdims=True) * (1.0 / D)
        rate = lax.rsqrt(jnp.sum(center * center, axis=1, keepdims=True) * (1.0 / D) + NORM_EPSILON)
        unit[at] = center * rate

    masking = iter(range(8))
    steps = iter(range(gather.steps))
    for t in range(6):
        small.step(t)
        gather.step(next(steps))
        if t < 5:
            masks(next(masking), tokens // 8)
    tag_sums[...] = jnp.sum(tags_full[...].reshape(32, 8, 128), axis=0)
    low = jnp.bfloat16
    class_tables = tables_ref[:, :D].astype(low)
    for order, target in ((DIMS, None), (("x", "y", "w", "u", "c"), part)):
        hot = hot_of(slot_labels(tags_full, order))
        cond = dot_last(hot[:, :D], class_tables)
        act = (cond / (1.0 + jnp.exp(-cond))).astype(low)
        if target is None:
            hot_ref[...], cond_ref[...], act_ref[...] = hot, cond, act
        else:
            target[...] = dot_plain(act, ada_ref[...].astype(low)).reshape(2, 2, 2, 8, 6 * D)
    vectors_ref[...] = rows_full[...].reshape(D, 128).astype(jnp.float32).T[0:16]
    for stage in range(6):
        mod_step(stage)
        for step in steps:
            gather.step(step)
            break
        if stage < 4:
            embed(stage)
        for index in masking:
            masks(index, tokens // 8)
            break
    for step in steps:
        gather.step(step)
    store_qkv = pltpu.make_async_copy(qkv_full, qkv_out, copy_sems.at[2])
    store_qkv.start()
    spot = 4 * bit["u"] + 2 * bit["c"]
    row_ids = lax.broadcasted_iota(jnp.int32, (8, D), 0)
    for kind in range(6):
        at = (kind % 3) * D
        group = mod_sums[4][kind // 3, :, at : at + D]
        for slot in range(2):
            row = jnp.sum(jnp.where(row_ids == spot + slot, group, 0.0), axis=0, keepdims=True)
            modulation_ref[slot : slot + 1, kind * D : (kind + 1) * D] = row + vectors_ref[kind : kind + 1]
    stores = []
    for index in range(4):
        at = slice(index * block, (index + 1) * block)
        other = token_columns[at, 0:1] > 0.5
        scale = jnp.where(other, modulation_ref[1:2, 2 * D : 3 * D], modulation_ref[0:1, 2 * D : 3 * D])
        shift = jnp.where(other, modulation_ref[1:2, 4 * D : 5 * D], modulation_ref[0:1, 4 * D : 5 * D])
        normed = (unit[at] * (1.0 + scale) + shift).astype(low)
        normed_ref[at] = normed
        if index >= 2:
            stores[index - 2].wait()
        for column in range(0, 3 * D, 512):
            weight = qkv_full[:, :, :, :, :, :, column : column + 512].reshape(D, 512)
            staged[index % 2, :, column : column + 512] = dot_plain(normed, weight)
        stores.append(
            pltpu.make_async_copy(
                staged.at[index % 2], projected_ref.at[pl.ds(index * block, block)], copy_sems.at[index % 2]
            )
        )
        stores[index].start()
    stores[2].wait()
    stores[3].wait()
    store_qkv.wait()


def begin(rows, tags, tables, ada_weight, qkv_weight, out_weight, codes, token_columns, token_rows):
    depth = rows.shape[0]
    tokens = codes.shape[0]
    f32, low = jnp.float32, jnp.bfloat16
    dma = pltpu.SemaphoreType.DMA
    lanes = 3 * D
    lands = [
        pltpu.VMEM((2, 2, 2, 8, lanes), f32),
        pltpu.VMEM((2, 2, 8, lanes), f32),
    ] + [pltpu.VMEM((2, 8, lanes), f32)] * 3
    shape = jax.ShapeDtypeStruct
    return pl.pallas_call(
        begin_kernel,
        out_shape=(
            shape((tokens, 3 * D), f32),
            shape(FIVE + (depth, 3 * D), low),
            shape(FIVE + (depth, D), low),
            shape((tokens, D), f32),
            shape((tokens, D), low),
            shape((2, 6 * D), f32),
            shape((16, D), f32),
            shape((64, 1152), low),
            shape((64, depth), f32),
            shape((64, depth), low),
            shape((8, 128), f32),
            shape((tokens, tokens), f32),
            shape((tokens, tokens), f32),
        ),
        in_specs=[WHOLE] * 9,
        out_specs=(ANY, ANY, ANY) + (WHOLE,) * 10,
        scratch_shapes=[
            pltpu.VMEM(FIVE + (depth, 128), low),
            pltpu.VMEM(FIVE + (8, 128), f32),
            pltpu.VMEM((depth, 3 * D), low),
            pltpu.VMEM((depth, D), low),
            pltpu.VMEM(FIVE + (depth, 3 * D), low),
            pltpu.VMEM((2, 2, 2, 8, 6 * D), f32),
            pltpu.VMEM((tokens, D), f32),
            pltpu.VMEM((2, tokens // 4, 3 * D), f32),
            dma((3,)),
            dma((5, 2)),
            dma((5, 2)),
        ]
        + lands
        + lands
        + Gather.scratch()
        + Gather.scratch(FIRST_LAG),
        compiler_params=params(0),
        name="begin",
    )(rows, tags, tables, ada_weight, qkv_weight, out_weight, codes, token_columns, token_rows)


def head_mean(values):
    low_lane = lax.broadcasted_iota(jnp.int32, values.shape, 1) < HEAD_DIM
    low_sum = jnp.sum(jnp.where(low_lane, values, 0.0), axis=1, keepdims=True)
    high_sum = jnp.sum(jnp.where(low_lane, 0.0, values), axis=1, keepdims=True)
    return jnp.where(low_lane, low_sum, high_sum) * (1.0 / HEAD_DIM)


def of_head(values, head):
    low_lane = lax.broadcasted_iota(jnp.int32, values.shape, 1) < HEAD_DIM
    zero = jnp.zeros_like(values)
    return jnp.where(low_lane, values, zero) if head == 0 else jnp.where(low_lane, zero, values)


def dot_last(left, right):
    return lax.dot_general(left, right, (((1,), (1,)), ((), ())), preferred_element_type=jnp.float32)


def dot_first(left, right):
    return lax.dot_general(left, right, (((0,), (0,)), ((), ())), preferred_element_type=jnp.float32)


def dot_plain(left, right):
    return lax.dot_general(left, right, (((1,), (0,)), ((), ())), preferred_element_type=jnp.float32)


UNITS = 4


def normed_head(raw, gain):
    return (raw * lax.rsqrt(head_mean(raw * raw) + NORM_EPSILON) * gain).astype(jnp.bfloat16)


def attend_kernel(linked, q_ref, k_ref, v_ref, gain_ref, bias_ref, *refs):
    if linked:
        down_own, half_ref, mixed_ref, exact_ref, total_ref, down_full, up_full, head_full = refs[:8]
        qn, kn, vn, pair_sems, passing, pass_sems = refs[8:14]
        sems = refs[14:]
        place = Place()
        core = place.bit["c"]

        def pair_copies():
            start = 0
            for order, full in enumerate((up_full, head_full)):
                size = full.shape[6]
                source = half_ref.at[:, :, :, :, :, start : start + size]
                target = full.at[:, :, :, :, core]
                yield place.send(source, target, pair_sems.at[0, order], pair_sems.at[1, order], "c")
                start += size

        chunks = HEADS // 2
        piece = passing.shape[6]

        def load(i):
            return pltpu.make_async_copy(
                half_ref.at[:, :, :, :, :, i * piece : (i + 1) * piece], passing.at[i % 2], pass_sems.at[0, i % 2]
            )

        def save(i):
            full = (up_full, head_full)[i // (chunks // 2)]
            at = (i % (chunks // 2)) * piece
            return pltpu.make_async_copy(
                passing.at[i % 2], full.at[:, :, :, :, core, :, at : at + piece], pass_sems.at[1, i % 2]
            )

        def each_chunk(body):
            for i in range(chunks):
                pl.when(pl.program_id(0) == i)(partial(body, i))

        def begin_chunk(i):
            if i >= 2:
                save(i - 2).wait()
            load(i).start()

        def end_chunk(i):
            load(i).wait()
            save(i).start()
            if i == chunks - 1:
                save(i - 1).wait()
                save(i).wait()

        width = ATTEND_WIDTH
        split = D // (2 * width)
        depth = down_full.shape[6]
        parts = down_full.shape[5]

        def down_source(j, p):
            part, column = lax.div(j, split), lax.rem(j, split)
            return down_own.at[
                pl.ds(pl.multiple_of(part * depth, depth), depth), columns((2 * column + p) * width, width)
            ]

        def down_target(j, p, r):
            part, column = lax.div(j, split), lax.rem(j, split)
            return down_full.at[r + (part, slice(None), columns((2 * column + p) * width, width))]

        gather = Gather(place, [(0, split * parts, down_source, down_target)], *sems, lag=ATTEND_LAG)

        @pl.when(pl.program_id(0) == 0)
        def first():
            place.meet()
            for copy in pair_copies():
                copy.start()

        each_chunk(begin_chunk)
    else:
        mixed_ref, exact_ref, total_ref, qn, kn, vn = refs
    qn[...] = normed_head(q_ref[...], gain_ref[0:1])
    kn[...] = normed_head(k_ref[...], gain_ref[1:2])
    vn[...] = v_ref[...].astype(jnp.bfloat16)
    tokens = q_ref.shape[0]
    both, sums = [], []
    for head in range(2):
        query = of_head(qn[...], head)
        mixed = jnp.zeros((tokens, 128), jnp.float32)
        lanes = jnp.zeros((tokens, 128), jnp.float32)
        for order in range(UNITS // 2):
            if linked:
                gather.step(pl.program_id(0) * UNITS + head * (UNITS // 2) + order)
            size = tokens // (UNITS // 2)
            keys = slice(order * size, (order + 1) * size)
            raised = jnp.exp2(dot_last(query, kn[keys]) * EXP_SCALE + bias_ref[:, keys])
            for lane in range(0, size, 128):
                lanes = lanes + raised[:, lane : lane + 128]
            mixed = mixed + dot_plain(raised.astype(jnp.bfloat16), vn[keys])
        total = jnp.sum(lanes, axis=1, keepdims=True)
        both.append(mixed * (1.0 / total))
        sums.append(total)
    low_lane = lax.broadcasted_iota(jnp.int32, both[0].shape, 1) < HEAD_DIM
    exact = jnp.where(low_lane, both[0], both[1])
    mixed_ref[...] = exact.astype(jnp.bfloat16)
    exact_ref[...] = exact
    total_ref[...] = jnp.log2(jnp.where(low_lane, sums[0], sums[1]))

    if linked:
        finish(gather)
        each_chunk(end_chunk)

        @pl.when(pl.program_id(0) == HEADS // 2 - 1)
        def pair_done():
            for copy in pair_copies():
                copy.wait()


def attend(projected, gains, bias, down_own=None, half=None):
    tokens = projected.shape[0]
    pair = pl.BlockSpec((tokens, 128), lambda i: (0, i))
    specs = [
        pair,
        pl.BlockSpec((tokens, 128), lambda i: (0, i + 8)),
        pl.BlockSpec((tokens, 128), lambda i: (0, i + 16)),
        pl.BlockSpec((8, 128), lambda i: (0, i)),
        pl.BlockSpec((tokens, tokens), lambda i: (0, 0), pipeline_mode=pl.Buffered(1)),
    ]
    outs = [jax.ShapeDtypeStruct((tokens, D), kind) for kind in (jnp.bfloat16, jnp.float32, jnp.float32)]
    out_specs = [pair] * 3
    scratch = [pltpu.VMEM((tokens, 128), jnp.bfloat16)] * 3
    operands = [projected, projected, projected, gains, bias]
    linked = down_own is not None
    if linked:
        depth = half.shape[4]
        specs += [ANY, ANY]
        operands += [down_own, half]
        outs += [jax.ShapeDtypeStruct(FIVE + (down_own.shape[0] // depth, depth, D), jnp.bfloat16)]
        outs += [jax.ShapeDtypeStruct(FIVE + (depth, half.shape[5] // 2), jnp.bfloat16)] * 2
        out_specs += [ANY] * 3
        scratch = scratch + [pltpu.SemaphoreType.DMA((2, 2))]
        scratch += [pltpu.VMEM((2,) + half.shape[:5] + (half.shape[5] // (HEADS // 2),), jnp.bfloat16)]
        scratch += [pltpu.SemaphoreType.DMA((2, 2))] + Gather.scratch(ATTEND_LAG)
    return pl.pallas_call(
        partial(attend_kernel, linked),
        grid=(HEADS // 2,),
        out_shape=tuple(outs),
        in_specs=specs,
        out_specs=tuple(out_specs),
        scratch_shapes=scratch,
        compiler_params=params(2) if linked else pltpu.CompilerParams(vmem_limit_bytes=VMEM_GRANT),
        name="attention_forward",
    )(*operands)


def attend_back_kernel(linked, q_ref, k_ref, v_ref, m_ref, exact_ref, total_ref, gain_ref, bias_ref, *refs):
    if linked:
        up_ref, down_ref, grad_ref, gain_grad_ref, done_ref = refs[:5]
        qn, kn, vn, dk, dv, turned, dq_turned, key_turned = refs[5:13]
        place = Place()
        width = BACK_WIDTH
        wide = up_ref.shape[6] // (2 * width)
        narrow = down_ref.shape[7] // (2 * width)
        parts = down_ref.shape[5]

        def columns_of(ref, first):
            return lambda j, core: ref.at[
                :, :, :, :, core, :, columns(2 * (j - first) * width, 2 * width)
            ]

        def down_source(j, core):
            spread = j - wide
            part, column = lax.div(spread, narrow), lax.rem(spread, narrow)
            return down_ref.at[:, :, :, :, core, part, :, columns(2 * column * width, 2 * width)]

        def store(j, parity, total):
            done_ref[j, :, parity * width : (parity + 1) * width] = total

        pairs = wide + parts * narrow
        scatter = Scatter(
            place,
            [
                (0, wide, columns_of(up_ref, 0)),
                (wide, pairs, down_source),
            ],
            store,
            refs[13:],
            lag=BACK_LAG,
        )
        pl.when(pl.program_id(0) == 0)(place.meet)
    else:
        grad_ref, gain_grad_ref = refs[:2]
        qn, kn, vn, dk, dv, turned, dq_turned, key_turned = refs[2:]
    qn[...] = normed_head(q_ref[...], gain_ref[0:1])
    kn[...] = normed_head(k_ref[...], gain_ref[1:2])
    vn[...] = v_ref[...].astype(jnp.bfloat16)
    for head in range(2):
        key_turned[head] = of_head(kn[...], head).T
    turned[0] = total_ref[...].T
    turned[1] = (head_mean(m_ref[...].astype(jnp.float32) * exact_ref[...]) * HEAD_DIM).T
    tokens = q_ref.shape[0]
    size = tokens // (UNITS // 2)
    for head in range(2):
        query = of_head(qn[...], head)
        mixed = of_head(m_ref[...], head)
        at = head * HEAD_DIM
        total = turned[0, at : at + 1]
        center = turned[1, at : at + 1]
        for order in range(UNITS // 2):
            if linked:
                scatter.step(pl.program_id(0) * UNITS + head * (UNITS // 2) + order)
            keys = slice(order * size, (order + 1) * size)
            scores = dot_last(kn[keys], query) * EXP_SCALE + (bias_ref[keys] - total)
            probs = jnp.exp2(scores)
            prob_grad = dot_last(vn[keys], mixed)
            score_grad = (probs * (prob_grad - center)).astype(jnp.bfloat16)
            key_part = dot_plain(score_grad, query)
            value_part = dot_plain(probs.astype(jnp.bfloat16), mixed)
            query_part = dot_plain(key_turned[head, :, keys], score_grad)
            dk[keys] = key_part if head == 0 else dk[keys] + key_part
            dv[keys] = value_part if head == 0 else dv[keys] + value_part
            dq_turned[...] = query_part if head == 0 and order == 0 else dq_turned[...] + query_part

    gain_rows = []
    for place_at, raw_ref, grad in ((0, q_ref, dq_turned[...].T), (1, k_ref, dk[...])):
        raw = raw_ref[...]
        normed_grad = grad * SCORE_SCALE
        rate = lax.rsqrt(head_mean(raw * raw) + NORM_EPSILON)
        scaled = gain_ref[place_at : place_at + 1] * normed_grad
        back = rate * scaled - raw * (rate * rate * rate) * head_mean(raw * scaled)
        grad_ref[place_at] = back.astype(jnp.bfloat16)
        gain_rows.append(jnp.sum(normed_grad * raw * rate, axis=0, keepdims=True))
    grad_ref[2] = dv[...].astype(jnp.bfloat16)
    gain_grad_ref[...] = jnp.concatenate(gain_rows + [jnp.zeros((6, 128), jnp.float32)], axis=0)
    if linked:
        finish(scatter)


def attend_back(projected, mixed_grad, exact, totals, gains, bias, up_grad=None, down_grad=None):
    tokens = projected.shape[0]
    pair = pl.BlockSpec((tokens, 128), lambda i: (0, i))
    specs = [
        pair,
        pl.BlockSpec((tokens, 128), lambda i: (0, i + 8)),
        pl.BlockSpec((tokens, 128), lambda i: (0, i + 16)),
        pair,
        pair,
        pair,
        pl.BlockSpec((8, 128), lambda i: (0, i)),
        pl.BlockSpec((tokens, tokens), lambda i: (0, 0), pipeline_mode=pl.Buffered(1)),
    ]
    outs = [
        jax.ShapeDtypeStruct((3, tokens, D), jnp.bfloat16),
        jax.ShapeDtypeStruct((8, D), jnp.float32),
    ]
    out_specs = [
        pl.BlockSpec((3, tokens, 128), lambda i: (0, 0, i)),
        pl.BlockSpec((8, 128), lambda i: (0, i)),
    ]
    scratch = [pltpu.VMEM((tokens, 128), jnp.bfloat16)] * 3 + [
        pltpu.VMEM((tokens, 128), jnp.float32)
    ] * 2
    scratch += [
        pltpu.VMEM((2, 128, tokens), jnp.float32),
        pltpu.VMEM((128, tokens), jnp.float32),
        pltpu.VMEM((2, 128, tokens), jnp.bfloat16),
    ]
    operands = [projected, projected, projected, mixed_grad, exact, totals, gains, bias]
    linked = up_grad is not None
    if linked:
        depth = up_grad.shape[5]
        specs += [ANY, ANY]
        operands += [up_grad, down_grad]
        pairs = (up_grad.shape[6] + down_grad.shape[5] * down_grad.shape[7]) // (2 * BACK_WIDTH)
        outs += [jax.ShapeDtypeStruct((pairs, depth, 2 * BACK_WIDTH), jnp.float32)]
        out_specs += [WHOLE]
        scratch = scratch + Scatter.scratch((depth, BACK_WIDTH), jnp.bfloat16, BACK_LAG)
    return pl.pallas_call(
        partial(attend_back_kernel, linked),
        grid=(HEADS // 2,),
        out_shape=tuple(outs),
        in_specs=specs,
        out_specs=tuple(out_specs),
        scratch_shapes=scratch,
        compiler_params=params(3) if linked else pltpu.CompilerParams(vmem_limit_bytes=VMEM_GRANT),
        name="attention_backward",
    )(*operands)


TANH_RATE = math.sqrt(2.0 / math.pi)
DENSE_WIDTH = 512


def dense_back_kernel(
    branch_ref,
    normed_ref,
    pre_ref,
    down_ref,
    up_ref,
    residual_ref,
    grad_ref,
    attended_ref,
    token_columns,
    mods_ref,
    head_ref,
    up_grad,
    down_grad,
    residual_grad,
    attended_grad,
    rows_ref,
    done_ref,
    normed_turned,
    pre_grad,
    hidden,
    back,
    *scratch,
):
    place = Place()
    index = pl.program_id(0)
    width = BACK_WIDTH

    def store(j, parity, total):
        done_ref[j, :, parity * width : (parity + 1) * width] = total

    pairs = head_ref.shape[6] // (2 * width)
    scatter = Scatter(
        place,
        [
            (
                0,
                pairs,
                lambda j, core: head_ref.at[:, :, :, :, core, :, columns(2 * j * width, 2 * width)],
            )
        ],
        store,
        scratch,
        lag=BACK_LAG,
    )

    @pl.when(index == 0)
    def first():
        place.meet()
        normed_turned[...] = normed_ref[...].T
        back[...] = jnp.zeros_like(back)

    tokens = branch_ref.shape[0]
    block = tokens // 4
    blocks = [slice(i * block, (i + 1) * block) for i in range(4)]
    scatter.step(index * 3)
    for rows in blocks:
        act_grad = dot_last(branch_ref[rows], down_ref[...])
        value = pre_ref[rows]
        square = value * value
        bent = jnp.tanh(TANH_RATE * value * (1.0 + 0.044715 * square))
        half = 0.5 * (1.0 + bent)
        slope = half + 0.5 * value * (1.0 - bent * bent) * (TANH_RATE * (1.0 + 3 * 0.044715 * square))
        pre_grad[rows] = (slope * act_grad).astype(jnp.bfloat16)
        hidden[rows] = (value * half).astype(jnp.bfloat16)
    scatter.step(index * 3 + 1)
    down_grad[...] = dot_first(hidden[...], branch_ref[...]).astype(jnp.bfloat16)
    up_grad[...] = dot_plain(normed_turned[...], pre_grad[...]).astype(jnp.bfloat16)
    scatter.step(index * 3 + 2)
    for rows in blocks:
        back[rows] += dot_last(pre_grad[rows], up_ref[...])

    @pl.when(index == pl.num_programs(0) - 1)
    def last():
        sums = [jnp.zeros((1, D), jnp.float32)] * 6
        for rows in blocks:
            values, slope = residual_ref[rows], back[rows]
            center = values - jnp.sum(values, axis=1, keepdims=True) * (1.0 / D)
            rate = lax.rsqrt(
                jnp.sum(center * center, axis=1, keepdims=True) * (1.0 / D) + NORM_EPSILON
            )
            unit = center * rate
            other = token_columns[rows, 0:1] > 0.5
            unit_back = slope * (1.0 + jnp.where(other, mods_ref[1:2], mods_ref[0:1]))
            mean_back = jnp.sum(unit_back, axis=1, keepdims=True) * (1.0 / D)
            mean_along = jnp.sum(unit_back * unit, axis=1, keepdims=True) * (1.0 / D)
            total = grad_ref[rows] + rate * (unit_back - mean_back - unit * mean_along)
            residual_grad[rows] = total
            attended_grad[rows] = (total * jnp.where(other, mods_ref[3:4], mods_ref[2:3])).astype(
                jnp.bfloat16
            )
            for at, value in enumerate((slope * unit, slope, total * attended_ref[rows])):
                second = jnp.sum(jnp.where(other, value, 0.0), axis=0, keepdims=True)
                first_slot = jnp.sum(jnp.where(other, 0.0, value), axis=0, keepdims=True)
                sums[2 * at] = sums[2 * at] + first_slot
                sums[2 * at + 1] = sums[2 * at + 1] + second
        for at in range(6):
            rows_ref[at : at + 1] = sums[at]


def dense_back(branch_grad, normed, pre, down, up, residual, grad, attended, token_columns, mods, head):
    tokens, wide = pre.shape
    depth = head.shape[5]
    pairs = head.shape[6] // (2 * BACK_WIDTH)
    f32, low = jnp.float32, jnp.bfloat16
    width = DENSE_WIDTH

    def fixed(*shape):
        return pl.BlockSpec(shape, lambda i: (0,) * len(shape), pipeline_mode=pl.Buffered(1))

    across = pl.BlockSpec((D, width), lambda i: (0, i))
    along = pl.BlockSpec((width, D), lambda i: (i, 0))
    shape = jax.ShapeDtypeStruct
    return pl.pallas_call(
        dense_back_kernel,
        grid=(wide // width,),
        out_shape=(
            shape((D, wide), low),
            shape((wide, D), low),
            shape((tokens, D), f32),
            shape((tokens, D), low),
            shape((8, D), f32),
            shape((pairs, depth, 2 * BACK_WIDTH), f32),
        ),
        in_specs=[
            fixed(tokens, D),
            fixed(tokens, D),
            pl.BlockSpec((tokens, width), lambda i: (0, i)),
            along,
            across,
            fixed(tokens, D),
            fixed(tokens, D),
            fixed(tokens, D),
            fixed(tokens, 128),
            fixed(8, D),
            ANY,
        ],
        out_specs=(across, along, fixed(tokens, D), fixed(tokens, D), fixed(8, D), WHOLE),
        scratch_shapes=[
            pltpu.VMEM((D, tokens), low),
            pltpu.VMEM((tokens, width), low),
            pltpu.VMEM((tokens, width), low),
            pltpu.VMEM((tokens, D), f32),
        ]
        + Scatter.scratch((depth, BACK_WIDTH), low, BACK_LAG),
        compiler_params=params(5),
        name="dense_backward",
    )(branch_grad, normed, pre, down, up, residual, grad, attended, token_columns, mods, head)


WEIGHT_COLUMNS = (CLASSES + CODE_DIM + LEVELS, 9, 6 * D, 3 * D, D, 4 * D, D, CODES)
SUM_STARTS = (0, None, 1152, 1152 + 6144, 1152 + 9216, 1152 + 10240, 1152 + 14336, 1152 + 15360)
SCALARS = 1152 + 19456
SUM_LANES = SCALARS + 128
SMALL_LANES = CODE_DIM + LEVELS + 9
DECAY = 1.0 - STEP ** (-0.8)


def three_terms(values):
    high = values.astype(jnp.bfloat16)
    rest = values - high.astype(jnp.float32)
    middle = rest.astype(jnp.bfloat16)
    return high, middle, (rest - middle.astype(jnp.float32)).astype(jnp.bfloat16)


def lane_row(scalars):
    lanes = lax.broadcasted_iota(jnp.int32, (1, 128), 1)
    row = jnp.zeros((1, 128), jnp.float32)
    for lane, value in scalars:
        row = jnp.where(lanes == lane, value, row)
    return row


def whole_sum(values):
    return jnp.sum(jnp.sum(values, axis=0, keepdims=True), axis=1, keepdims=True)


def weight_tiles(tables_grad, ada_grad, done_head, done_attention, done_last):
    def blocks(ref, first, count, width):
        return [(lambda at=first + i: ref[at], i * width, width) for i in range(count)]

    near, far = 2 * LAST_WIDTH, 2 * BACK_WIDTH
    tables_columns = WEIGHT_COLUMNS[0]
    wide = CODES // far
    return {
        0: [(0, [(lambda: tables_grad[:, :tables_columns], 0, tables_columns)])],
        2: [(1, [(lambda: ada_grad[...], 0, 6 * D)])],
        3: [(2, blocks(done_last, D // near, 3 * D // near, near))],
        4: [(3, blocks(done_last, 0, D // near, near))],
        5: [(4, blocks(done_attention, 0, wide, far))],
        6: [(6 + part, blocks(done_attention, wide + part * (D // far), D // far, far)) for part in range(4)],
        7: [(5, blocks(done_head, 0, wide, far))],
    }


class Total:
    def __init__(self, place, sums, land, sends, recvs):
        self.place, self.sums, self.land = place, sums, land
        self.sends, self.recvs = sends, recvs

    @staticmethod
    def scratch(lanes):
        dma = pltpu.SemaphoreType.DMA
        return [
            pltpu.VMEM((6, 1, lanes), jnp.float32),
            pltpu.VMEM((5, 1, lanes), jnp.float32),
            dma((5,)),
            dma((5,)),
        ]

    def run(self):
        for stage, dim in enumerate(DIMS):
            copy = self.place.send(
                self.sums.at[stage], self.land.at[stage], self.sends.at[stage], self.recvs.at[stage], dim
            )
            copy.start()
            copy.wait()
            self.sums[stage + 1] = self.sums[stage] + self.land[stage]


def last_kernel(
    out_ref,
    qkv_low,
    embedded_ref,
    grad_ref,
    heads_grad,
    normed_ref,
    codes_ref,
    second_ref,
    scale_ref,
    known_ref,
    gains_ref,
    act_ref,
    cond_ref,
    hot_ref,
    loss_ref,
    done_head,
    attention_ref,
    tables_ref,
    vectors_ref,
    ada_ref,
    qkv_master,
    out_master,
    up_master,
    down_master,
    head_master,
    moments_ref,
    vector_moment_ref,
    column_moment_ref,
    done_ref,
    small_done,
    tables_grad,
    ada_grad,
    rows_ref,
    columns_ref,
    facts_ref,
    *scratch,
):
    place = Place()
    place.meet()
    devices = lax.axis_size(AXES)
    depth = tables_ref.shape[0]
    width = LAST_WIDTH
    narrow = D // (2 * width)
    part_grads, qkv_full, embedded, grad, code_sums, mod_ref, small_ref, load_sems = scratch[40:48]
    loads = [
        pltpu.make_async_copy(source, target, load_sems.at[i])
        for i, (source, target) in enumerate(
            ((qkv_low, qkv_full), (embedded_ref, embedded), (grad_ref, grad))
        )
    ]
    for load in loads:
        load.start()

    def columns_of(ref, first):
        return lambda j, core: ref.at[
            :, :, :, :, core, :, columns(2 * (j - first) * width, 2 * width)
        ]

    def store(j, parity, total):
        done_ref[j, :, parity * width : (parity + 1) * width] = total

    pairs = 4 * narrow
    scatter = Scatter(
        place,
        [(0, narrow, columns_of(out_ref, 0))]
        + [
            ((1 + part) * narrow, (2 + part) * narrow, columns_of(part_grads.at[part], (1 + part) * narrow))
            for part in range(3)
        ],
        store,
        scratch[:13],
        lag=LAST_LAG,
    )
    half = depth // 2

    def small_store(j, parity, total):
        small_done[pl.ds(parity * half, half)] = total

    small = Scatter(
        place,
        [(0, 1, lambda j, core: small_ref.at[:, :, :, :, core])],
        small_store,
        scratch[13:26],
    )
    mod_sums, mod_land, mod_all, mod_sends, mod_recvs = scratch[26:31]
    bit = place.bit

    def mod_copy(stage):
        dim = ("c", "x", "y", "u", "w")[stage]
        if stage < 3:
            source, target = (mod_ref, mod_sums.at[0], mod_sums.at[1])[stage], mod_land.at[stage]
        elif stage == 3:
            source = target = mod_all.at[bit["w"], bit["u"]]
        else:
            source = target = mod_all.at[bit["w"]]
        return place.send(source, target, mod_sends.at[stage], mod_recvs.at[stage], dim)

    def mod_step(stage):
        if stage:
            mod_copy(stage - 1).wait()
        if stage == 1:
            mod_sums[0] = mod_ref[...] + mod_land[0]
        elif stage == 2:
            mod_sums[1] = mod_sums[0] + mod_land[1]
        elif stage == 3:
            mod_all[bit["w"], bit["u"]] = mod_sums[1] + mod_land[2]
        if stage < 5:
            mod_copy(stage).start()

    first_total = Total(place, *scratch[31:35])
    second_total = Total(place, *scratch[35:39])
    sums, facts = first_total.sums, scratch[39]
    tiles = weight_tiles(tables_grad, ada_grad, done_head, attention_ref, done_ref)
    masters = (
        tables_ref,
        vectors_ref,
        ada_ref,
        qkv_master,
        out_master,
        up_master,
        down_master,
        head_master,
    )

    def ada_part():
        slots = mod_all[...].reshape(2 * devices, 6 * D)
        ada_grad[...] = dot_first(act_ref[...], slots)
        activated_grad = dot_last(slots, ada_ref[...].astype(jnp.bfloat16))
        cond = cond_ref[...]
        gate = 1.0 / (1.0 + jnp.exp(-cond))
        cond_grad = activated_grad * (gate * (1.0 + cond * (1.0 - gate)))
        shape = (128, hot_ref.shape[1])
        source = lax.broadcasted_iota(jnp.int32, shape, 0)
        target = lax.broadcasted_iota(jnp.int32, shape, 1)
        moved = (target == source + (CLASSES - 9)) & (source >= 9) & (source < SMALL_LANES)
        shift = jnp.where(moved, 1.0, 0.0).astype(jnp.bfloat16)
        total = jnp.zeros((depth, hot_ref.shape[1]), jnp.float32)
        for term in three_terms(cond_grad)[::-1]:
            total = total + dot_first(term, hot_ref[...])
        for term in three_terms(small_done[...])[::-1]:
            total = total + dot_plain(term, shift)
        tables_grad[...] = total

    def stats(position):
        row_total = jnp.zeros((1, 1), jnp.float32)
        for index, group in tiles[position]:
            row_sum = jnp.zeros((depth, 1), jnp.float32)
            for load, first, size in group:
                gradient = load()
                squared = gradient * gradient + TINY_SQUARE
                row_sum = row_sum + jnp.sum(squared, axis=1, keepdims=True)
                at = SUM_STARTS[position] + first
                sums[0, :, at : at + size] += jnp.sum(squared, axis=0, keepdims=True)
            rows_new = DECAY * moments_ref[index] + (1.0 - DECAY) * (
                row_sum * (1.0 / WEIGHT_COLUMNS[position])
            )
            rows_ref[index] = rows_new
            row_total = row_total + jnp.sum(rows_new, axis=0, keepdims=True)
        facts[...] += lane_row([(position, row_total)])

    def squares(first, end):
        for position in range(first, end):
            master = masters[position][...]
            facts[...] += lane_row([(8 + position, whole_sum(master * master))])

    def part_grad(part):
        @pl.loop(0, D // 256)
        def tile(i):
            at = columns(i * 256, 256)
            product = dot_first(normed_ref[...], heads_grad[part, :, at])
            part_grads[part, :, :, :, :, :, :, at] = product.astype(jnp.bfloat16).reshape(
                FIVE + (depth, 256)
            )

    tokens = normed_ref.shape[0]
    block = tokens // 4
    slot_rows = [jnp.zeros((1, D), jnp.float32)] * 4

    def norm_back(index):
        rows = slice(index * block, (index + 1) * block)
        back = jnp.zeros((block, D), jnp.float32)
        for part in range(3):
            back = back + dot_last(heads_grad[part, rows], qkv_full[:, part * D : (part + 1) * D])
        values = embedded[rows]
        center = values - jnp.sum(values, axis=1, keepdims=True) * (1.0 / D)
        rate = lax.rsqrt(jnp.sum(center * center, axis=1, keepdims=True) * (1.0 / D) + NORM_EPSILON)
        unit = center * rate
        other = second_ref[rows] > 0.5
        scale_back = back * unit
        for at, value in enumerate((scale_back, back)):
            everything = jnp.sum(value, axis=0, keepdims=True)
            second = jnp.sum(jnp.where(other, value, 0.0), axis=0, keepdims=True)
            slot_rows[2 * at] = slot_rows[2 * at] + (everything - second)
            slot_rows[2 * at + 1] = slot_rows[2 * at + 1] + second
        unit_back = back * (1.0 + jnp.where(other, scale_ref[1:2], scale_ref[0:1]))
        mean_back = jnp.sum(unit_back, axis=1, keepdims=True) * (1.0 / D)
        mean_along = jnp.sum(unit_back * unit, axis=1, keepdims=True) * (1.0 / D)
        total = grad[rows] + rate * (unit_back - mean_back - unit * mean_along)
        high = total.astype(jnp.bfloat16)
        rest = (total - high.astype(jnp.float32)).astype(jnp.bfloat16)
        product = dot_first(codes_ref[rows], high) + dot_first(codes_ref[rows], rest)
        code_sums[...] = product if index == 0 else code_sums[...] + product

    def gather_rows():
        spot = 2 * (4 * bit["y"] + 2 * bit["x"] + bit["c"])
        row_ids = lax.broadcasted_iota(jnp.int32, (16, D), 0)
        for kind in range(6):
            if kind in (2, 4):
                first, other = slot_rows[kind - 2 : kind]
            else:
                at = slice(kind * D, (kind + 1) * D)
                first, other = known_ref[0:1, at], known_ref[1:2, at]
            placed = jnp.where(row_ids == spot, first, jnp.where(row_ids == spot + 1, other, 0.0))
            mod_ref[:, kind * D : (kind + 1) * D] = placed.astype(jnp.bfloat16)
            code_sums[kind : kind + 1] = first + other
        code_sums[6:9] = gains_ref[0:3]
        small_ref[...] = code_sums[...].T.reshape(FIVE + (depth, 128))

    sums[0] = jnp.zeros_like(sums[0])
    facts[...] = lane_row([(16, loss_ref[...])])
    steps = iter(range(scatter.steps))
    for _ in range(narrow):
        scatter.step(next(steps))
    for part in range(3):
        part_grad(part)
        for _ in range(narrow):
            scatter.step(next(steps))
    for load in loads:
        load.wait()
    for index in range(4):
        norm_back(index)
        if index % 2:
            scatter.step(next(steps))
    gather_rows()
    beside = [
        partial(stats, 5),
        partial(stats, 6),
        partial(stats, 7),
        partial(squares, 0, 5),
        partial(squares, 5, 8),
    ]
    for t in range(6):
        mod_step(t)
        small.step(t)
        if t < len(beside):
            beside[t]()
        for step in steps:
            scatter.step(step)
            break
    ada_part()
    for step in steps:
        scatter.step(step)
    stats(0)
    stats(2)
    stats(3)
    stats(4)
    sums[0, :, SCALARS:] = facts[...]
    first_total.run()
    columns_ref[...] = DECAY * column_moment_ref[...] + (1.0 - DECAY) * sums[5] * (1.0 / D)
    start, end = SUM_STARTS[6], SUM_STARTS[6] + D
    columns_ref[:, start:end] = DECAY * column_moment_ref[:, start:end] + (1.0 - DECAY) * sums[
        5, :, start:end
    ] * (1.0 / (4 * D))

    def rows_all(position):
        return 4.0 * D if position == 6 else 1.0 * D

    scalars = []
    for position, groups in tiles.items():
        at = SCALARS + position
        row_mean = sums[5, :, at : at + 1] * (1.0 / rows_all(position))
        spread = jnp.zeros((1, 1), jnp.float32)
        for index, group in groups:
            for load, first, size in group:
                lane = SUM_STARTS[position] + first
                estimate = rows_ref[index] * columns_ref[:, lane : lane + size] / row_mean
                update = load() * lax.rsqrt(estimate)
                spread = spread + whole_sum(update * update)
        scalars.append((position, spread))
    gradient = small_done[:, :9]
    moment = DECAY * vector_moment_ref[...] + (1.0 - DECAY) * (gradient * gradient + TINY_SQUARE)
    update = gradient * lax.rsqrt(moment)
    scalars.append((1, whole_sum(update * update)))
    second_total.sums[0] = lane_row(scalars)
    second_total.run()
    spread_row, factor_row = [], []
    for position in range(8):
        count = rows_all(position) * WEIGHT_COLUMNS[position]
        spread = jnp.sqrt(second_total.sums[5, :, position : position + 1] * (1.0 / count))
        at = SCALARS + 8 + position
        scale = jnp.maximum(SCALE_FLOOR, jnp.sqrt(sums[5, :, at : at + 1] * (1.0 / count)))
        spread_row.append((position, spread))
        factor_row.append((position, STEP_RATE * scale / jnp.maximum(1.0, spread / CLIP_LIMIT)))
    facts_ref[0] = lane_row(spread_row)
    facts_ref[1] = lane_row(factor_row)
    facts_ref[2] = sums[5, :, SCALARS:]


def last_exchange(far, near, done, masters, moments):
    depth = far[0].shape[5]
    pairs = 4 * D // (2 * LAST_WIDTH)
    dma = pltpu.SemaphoreType.DMA
    f32, low = jnp.float32, jnp.bfloat16
    tokens = far[2].shape[0]
    operands = list(far) + list(near) + list(done) + list(masters) + list(moments)
    return pl.pallas_call(
        last_kernel,
        out_shape=(
            jax.ShapeDtypeStruct((pairs, depth, 2 * LAST_WIDTH), f32),
            jax.ShapeDtypeStruct((depth, 128), f32),
            jax.ShapeDtypeStruct((depth, 1152), f32),
            jax.ShapeDtypeStruct((depth, 6 * D), f32),
            jax.ShapeDtypeStruct((10, depth, 1), f32),
            jax.ShapeDtypeStruct((1, SUM_LANES), f32),
            jax.ShapeDtypeStruct((3, 1, 128), f32),
        ),
        in_specs=[ANY] * 4 + [WHOLE] * (len(operands) - 4),
        out_specs=(WHOLE,) * 7,
        scratch_shapes=Scatter.scratch((depth, LAST_WIDTH), low, LAST_LAG)
        + Scatter.scratch((depth // 2, 128), f32, 1, True)
        + [
            pltpu.VMEM((2, 16, 6 * D), low),
            pltpu.VMEM((3, 16, 6 * D), low),
            pltpu.VMEM((2, 2, 16, 6 * D), low),
            dma((5,)),
            dma((5,)),
        ]
        + Total.scratch(SUM_LANES)
        + Total.scratch(128)
        + [pltpu.VMEM((1, 128), f32)]
        + [
            pltpu.VMEM((3,) + FIVE + (depth, D), low),
            pltpu.VMEM((D, 3 * D), low),
            pltpu.VMEM((tokens, D), f32),
            pltpu.VMEM((tokens, D), f32),
            pltpu.VMEM((128, D), f32),
            pltpu.VMEM((16, 6 * D), low),
            pltpu.VMEM(FIVE + (depth, 128), f32),
            dma((3,)),
        ],
        compiler_params=params(4),
        name="last_scatter",
    )(*operands)


def step_kernel(
    done_ref,
    small_ref,
    tables_grad,
    ada_grad,
    rows_ref,
    columns_ref,
    facts_ref,
    done_head,
    attention_ref,
    vector_moment_ref,
    tables_ref,
    vectors_ref,
    ada_ref,
    qkv_master,
    out_master,
    up_master,
    down_master,
    head_master,
    *outs,
):
    depth = tables_ref.shape[0]
    masters = (
        tables_ref,
        vectors_ref,
        ada_ref,
        qkv_master,
        out_master,
        up_master,
        down_master,
        head_master,
    )
    vector_stat = outs[16]
    tiles = weight_tiles(tables_grad, ada_grad, done_head, attention_ref, done_ref)
    for position, groups in tiles.items():
        grad_ref, next_ref, master = outs[2 * position], outs[2 * position + 1], masters[position]
        factor = facts_ref[1, :, position : position + 1]
        mean_scale = 1.0 / (4 * D) if position == 6 else 1.0 / D
        row_mean = facts_ref[2, :, position : position + 1] * mean_scale
        for order, (index, group) in enumerate(groups):
            at = slice(order * depth, (order + 1) * depth)
            for load, first, size in group:
                gradient = load()
                lane = SUM_STARTS[position] + first
                estimate = rows_ref[index] * columns_ref[:, lane : lane + size] / row_mean
                grad_ref[at, first : first + size] = gradient
                next_ref[at, first : first + size] = master[at, first : first + size] - factor * (
                    gradient * lax.rsqrt(estimate)
                )
    gradient = small_ref[:, :9]
    moment = DECAY * vector_moment_ref[...] + (1.0 - DECAY) * (gradient * gradient + TINY_SQUARE)
    vector_stat[...] = moment
    outs[2][...] = gradient
    outs[3][...] = vectors_ref[...] - facts_ref[1, :, 1:2] * (gradient * lax.rsqrt(moment))


def take_step(last, done, vector_moment, masters):
    operands = list(last) + list(done) + [vector_moment] + list(masters)
    shapes = []
    for master in masters:
        shapes += [jax.ShapeDtypeStruct(master.shape, jnp.float32)] * 2
    shapes.append(jax.ShapeDtypeStruct(vector_moment.shape, jnp.float32))
    return pl.pallas_call(
        step_kernel,
        out_shape=tuple(shapes),
        in_specs=[WHOLE] * len(operands),
        out_specs=(WHOLE,) * len(shapes),
        compiler_params=pltpu.CompilerParams(vmem_limit_bytes=VMEM_GRANT),
        name="weight_step",
    )(*operands)


def linked_mesh():
    return lax.axis_size("fsdp") == 8 and lax.axis_size("sub") == 4


def gathered(values):
    return lax.all_gather(values, AXES, axis=0, tiled=True)


def scattered(values):
    return lax.psum_scatter(values, AXES, scatter_dimension=0, tiled=True)


def layer_norm(values):
    center = values - jnp.mean(values, axis=-1, keepdims=True)
    return center * lax.rsqrt(jnp.mean(center * center, axis=-1, keepdims=True) + NORM_EPSILON)


def modulate(values, scale_part, shift_part):
    return layer_norm(values) * (1.0 + scale_part) + shift_part


def final_norm(values, gain_vector):
    return layer_norm(values) * gain_vector


def attention_bias(query, key):
    usable = (query[1] == key[1]) & (key[0] <= query[0]) & ((key[2] == 1) | (query[3] == key[3]))
    return jnp.where(usable, 0.0, MASK_VALUE)


def split_product(left_side, right_low):
    high = left_side.astype(jnp.bfloat16)
    rest = (left_side - high.astype(jnp.float32)).astype(jnp.bfloat16)
    return bfloat_product(high, right_low) + bfloat_product(rest, right_low)


def on_device(
    code_vectors,
    scale_ids,
    segment_ids,
    real_mask,
    labels,
    targets,
    loss_weight,
    tables,
    vectors,
    ada_weight,
    qkv_weight,
    out_weight,
    up_weight,
    down_weight,
    head_weight,
    tables_moment,
    ada_moment,
    qkv_moment,
    out_moment,
    up_moment,
    down_moment,
    head_moment,
    vector_moment,
    column_moment,
):
    devices = lax.axis_size(AXES)
    linked = linked_mesh()
    depth = tables.shape[0]
    tokens = code_vectors.shape[0]
    masters = (
        tables,
        vectors,
        ada_weight,
        qkv_weight,
        out_weight,
        up_weight,
        down_weight,
        head_weight,
    )
    local_count = jnp.sum(loss_weight).astype(jnp.float32)
    low = jnp.bfloat16
    part_kind = low if linked else jnp.float32
    tables_low = tables.astype(low)
    ada_low = ada_weight.astype(low)
    qkv_low = qkv_weight.astype(low)
    out_low = out_weight.astype(low)
    down_low = down_weight.astype(low)

    if linked:
        cores = [[core + 2 * chip for chip in range(devices // 2)] for core in range(2)]
        up_head = lax.all_gather(
            jnp.concatenate([up_weight, head_weight], axis=1).astype(low),
            AXES,
            axis_index_groups=cores,
            axis=0,
            tiled=True,
        ).reshape(2, 2, 2, 2, depth, -1)
    else:
        full_up = gathered(up_weight.astype(low))
        full_head = gathered(head_weight.astype(low))
    small_rows = jnp.concatenate(
        [vectors.astype(low), tables_low[:, CLASSES:], jnp.zeros((depth, 128 - SMALL_LANES), low)], axis=1
    )
    tag_row = jnp.concatenate([labels.astype(jnp.float32), local_count[None], jnp.zeros((5,), jnp.float32)])
    tags = jnp.broadcast_to(tag_row[:, None], (8, 128))
    level_hot = (scale_ids[:, None] == jnp.arange(LEVELS)[None, :]).astype(low)
    code_levels = jnp.concatenate([code_vectors, level_hot], axis=1)
    codes = jnp.pad(code_levels, ((0, 0), (9, 128 - SMALL_LANES)))
    second = (segment_ids == 1)[:, None]
    if linked:
        token_rows = jnp.stack([segment_ids, scale_ids, real_mask] + [real_mask] * 5).astype(jnp.float32)
        token_columns = jnp.pad(token_rows[:3].T, ((0, 0), (0, 125)))
        (
            projected,
            full_qkv,
            full_out,
            embedded,
            normed,
            modulation,
            vector_rows,
            label_hot,
            class_cond,
            activated,
            tag_sums,
            bias,
            turned_bias,
        ) = begin(
            small_rows, tags, tables, ada_weight, qkv_weight, out_weight, codes, token_columns, token_rows
        )
        full_qkv, full_out = full_qkv.reshape(D, 3 * D), full_out.reshape(D, D)
        weight_total = tag_sums[2, 0]
        gains = vector_rows[6:14]
        head_gain = vector_rows[8]
    else:
        small_full = gathered(small_rows)
        tags_full = gathered(tags).reshape(devices, 8, 128)[:, :, 0]
        labels_all = tags_full[:, :2].reshape(2 * devices)
        weight_total = jnp.sum(tags_full[:, 2])
        gain_vector = small_full[:, :9].astype(jnp.float32)
        label_hot = (labels_all[:, None] == jnp.arange(1152, dtype=jnp.float32)[None, :]).astype(low)
        class_cond = bfloat_product(label_hot[:, :CLASSES], tables_low[:, :CLASSES].T)
        activated = jax.nn.silu(class_cond).astype(low)
        own_modulation, full_qkv = scattered(bfloat_product(activated, ada_low)), gathered(qkv_low)
        modulation = own_modulation + gain_vector[:, :6].T.reshape(1, 6 * D)
        embedded = bfloat_product(codes, small_full.T)
        gains = jnp.pad(gain_vector[:, 6:8].T, ((0, 6), (0, 0)))
        head_gain = gain_vector[:, 8]

    def of_token(block):
        piece = modulation[:, block * D : (block + 1) * D]
        return jnp.where(second, piece[1:2], piece[0:1])

    gamma_one, gamma_two, scale_one, scale_two, shift_one, shift_two = (
        of_token(block) for block in range(6)
    )
    if linked:
        mixed_heads, exact, totals, full_down, full_up, full_head = attend(
            projected, gains, bias, down_low, up_head
        )
        full_down = full_down.reshape(-1, D)
        full_up, full_head = full_up.reshape(D, -1), full_head.reshape(D, -1)
    else:
        normed = modulate(embedded, scale_one, shift_one).astype(low)
        projected = bfloat_product(normed, full_qkv)
        places = jnp.arange(tokens)
        masks = (scale_ids, segment_ids, real_mask, places)
        bias = attention_bias([m[:, None] for m in masks], [m[None, :] for m in masks])
        turned_bias = attention_bias([m[None, :] for m in masks], [m[:, None] for m in masks])
        mixed_heads, exact, totals = attend(projected, gains, bias)
        full_out, full_down = gathered(out_low), gathered(down_low)
    attended = bfloat_product(mixed_heads, full_out)
    residual_one = embedded + gamma_one * attended
    normed_two = modulate(residual_one, scale_two, shift_two).astype(low)
    hidden_pre = bfloat_product(normed_two, full_up)
    hidden_act = jax.nn.gelu(hidden_pre, approximate=True).astype(low)
    branch = bfloat_product(hidden_act, full_down)
    residual_two = residual_one + gamma_two * branch
    final_normed = final_norm(residual_two, head_gain).astype(low)
    logits = bfloat_product(final_normed, full_head)
    logit_peak = jnp.max(logits, axis=-1, keepdims=True)
    log_total = logit_peak + jnp.log(jnp.sum(jnp.exp(logits - logit_peak), axis=-1, keepdims=True))
    target_hot = targets[:, None] == jnp.arange(CODES)[None, :]
    picked = jnp.sum(jnp.where(target_hot, logits, 0.0), axis=-1, keepdims=True)
    weight_column = loss_weight.astype(jnp.float32)[:, None]
    local_loss = jnp.sum(weight_column * (log_total - picked))
    logit_grad = (
        (jnp.exp(logits - log_total) - target_hot.astype(jnp.float32))
        * (weight_column / weight_total)
    ).astype(low)

    head_part = bfloat_product(final_normed.T, logit_grad).astype(part_kind)
    final_grad = bfloat_product(logit_grad, full_head.T)
    _, final_back = jax.vjp(final_norm, residual_two, head_gain)
    residual_grad, head_gain_grad = final_back(final_grad)
    branch_grad = (gamma_two * residual_grad).astype(low)

    def slot_sums(token_grad):
        other = jnp.sum(jnp.where(second, token_grad, 0.0), axis=0)
        first = jnp.sum(jnp.where(second, 0.0, token_grad), axis=0)
        return jnp.stack([first, other])

    gamma_two_grad = slot_sums(residual_grad * branch)
    if linked:
        mods = jnp.concatenate([modulation[:, 3 * D : 4 * D], modulation[:, :D], jnp.zeros((4, D), jnp.float32)])
        up_part, down_part, residual_grad, attended_grad, slot_rows, head_done = dense_back(
            branch_grad,
            normed_two,
            hidden_pre,
            full_down,
            full_up,
            residual_one,
            residual_grad,
            attended,
            token_columns,
            mods,
            head_part.reshape(FIVE + (depth, CODES)),
        )
        scale_two_grad, shift_two_grad, gamma_one_grad = slot_rows[0:2], slot_rows[2:4], slot_rows[4:6]
    else:
        down_part = bfloat_product(hidden_act.T, branch_grad).astype(part_kind)
        act_grad = bfloat_product(branch_grad, full_down.T)
        _, gelu_back = jax.vjp(partial(jax.nn.gelu, approximate=True), hidden_pre)
        pre_grad = gelu_back(act_grad)[0].astype(low)
        up_part = bfloat_product(normed_two.T, pre_grad).astype(part_kind)
        normed_two_grad = bfloat_product(pre_grad, full_up.T)
        _, modulate_two_back = jax.vjp(modulate, residual_one, scale_two, shift_two)
        norm_grad, scale_two_grad, shift_two_grad = modulate_two_back(normed_two_grad)
        scale_two_grad, shift_two_grad = slot_sums(scale_two_grad), slot_sums(shift_two_grad)
        residual_grad = residual_grad + norm_grad
        attended_grad = (gamma_one * residual_grad).astype(low)
        gamma_one_grad = slot_sums(residual_grad * attended)
    out_part = bfloat_product(mixed_heads.T, attended_grad).astype(part_kind)
    mixed_grad = bfloat_product(attended_grad, full_out.T).astype(low)
    if linked:
        heads_grad, gain_grads, attention_done = attend_back(
            projected,
            mixed_grad,
            exact,
            totals,
            gains,
            turned_bias,
            up_part.reshape(FIVE + (depth, up_part.shape[1])),
            down_part.reshape(FIVE + (down_part.shape[0] // D, depth, D)),
        )
    else:
        heads_grad, gain_grads = attend_back(projected, mixed_grad, exact, totals, gains, turned_bias)
        head_grad, up_grad, down_grad = scattered(head_part), scattered(up_part), scattered(down_part)
    if linked:
        unknown = jnp.zeros((2, D), jnp.float32)
        factored_rows = [tables_moment, ada_moment, qkv_moment, out_moment, up_moment, head_moment]
        row_moments = jnp.concatenate(factored_rows + [down_moment]).reshape(10, depth, 1)
        padding = jnp.zeros((110,), jnp.float32)
        column_moments = jnp.concatenate(
            [column_moment[:1042], padding, column_moment[1042:], jnp.zeros((128,), jnp.float32)]
        )[None]
        known = jnp.concatenate(
            [gamma_one_grad, gamma_two_grad, unknown, scale_two_grad, unknown, shift_two_grad], axis=1
        )
        gain_rows = jnp.concatenate([gain_grads[:2], head_gain_grad[None], jnp.zeros((5, D), jnp.float32)])
        last = last_exchange(
            (out_part.reshape(FIVE + (depth, D)), full_qkv, embedded, residual_grad),
            (
                heads_grad,
                normed,
                codes,
                second.astype(jnp.float32),
                modulation[:, 2 * D : 3 * D],
                known,
                gain_rows,
                activated,
                class_cond,
                label_hot,
                local_loss[None, None],
            ),
            (head_done, attention_done),
            masters,
            (row_moments, vector_moment, column_moments),
        )
        stepped = take_step(last, (head_done, attention_done), vector_moment, masters)
        rows_new, cols_new, facts = last[4].reshape(10 * depth), last[5][0], last[6][:, 0]
        stats = [rows_new[i * depth : (i + 1) * depth] for i in range(6)] + [rows_new[6 * depth :]]
        moment_of = (stats[0], stepped[16], stats[1], stats[2], stats[3], stats[4], stats[6], stats[5])
        results = [facts[2, 16], weight_total]
        for position in range(8):
            results += [stepped[2 * position], moment_of[position], stepped[2 * position + 1]]
        column_stat = jnp.concatenate([cols_new[:1042], cols_new[1152:SCALARS]])
        return tuple(results + [column_stat, facts[0, :8]])

    qkv_part = jnp.concatenate(
        [bfloat_product(normed.T, heads_grad[part]).astype(part_kind) for part in range(3)], axis=1
    )
    normed_grad = sum(
        bfloat_product(heads_grad[part], full_qkv[:, part * D : (part + 1) * D].T) for part in range(3)
    )
    _, modulate_one_back = jax.vjp(modulate, embedded, scale_one, shift_one)
    norm_grad, scale_one_grad, shift_one_grad = modulate_one_back(normed_grad)
    scale_one_grad, shift_one_grad = slot_sums(scale_one_grad), slot_sums(shift_one_grad)
    embedded_grad = residual_grad + norm_grad
    modulation_grad = jnp.concatenate(
        [
            gamma_one_grad,
            gamma_two_grad,
            scale_one_grad,
            scale_two_grad,
            shift_one_grad,
            shift_two_grad,
        ],
        axis=1,
    )
    bias_grad = jnp.sum(modulation_grad, axis=0).reshape(6, D)
    code_grad = split_product(embedded_grad.T, code_levels)
    small_part = jnp.concatenate(
        [
            bias_grad.T,
            gain_grads[:2].T,
            head_gain_grad[:, None],
            code_grad,
            jnp.zeros((D, 128 - CODE_DIM - LEVELS - 9), jnp.float32),
        ],
        axis=1,
    )
    modulation_low = modulation_grad.astype(low)
    modulation_all = gathered(modulation_low)
    small_grad, qkv_grad, out_grad = scattered(small_part), scattered(qkv_part), scattered(out_part)
    ada_grad = bfloat_product(activated.T, modulation_all)
    activated_grad = bfloat_product(modulation_all, ada_low.T)
    _, silu_back = jax.vjp(jax.nn.silu, class_cond)
    cond_grad = silu_back(activated_grad)[0]
    class_grad = jnp.dot(
        cond_grad.T,
        label_hot[:, :CLASSES].astype(jnp.float32),
        precision=lax.Precision.HIGHEST,
        preferred_element_type=jnp.float32,
    )
    tables_grad = jnp.concatenate([class_grad, small_grad[:, 9:SMALL_LANES]], axis=1)
    vectors_grad = small_grad[:, :9]
    gradients = (
        tables_grad,
        vectors_grad,
        ada_grad,
        qkv_grad,
        out_grad,
        up_grad,
        down_grad,
        head_grad,
    )
    second_decay = DECAY
    factored_index = (0, 2, 3, 4, 5, 6, 7)
    factored_moments = (
        tables_moment,
        ada_moment,
        qkv_moment,
        out_moment,
        up_moment,
        down_moment,
        head_moment,
    )
    local_squares = jnp.stack([jnp.sum(master * master) for master in masters])
    rows_list = []
    column_parts = []
    row_parts = []
    for position, moment in zip(factored_index, factored_moments):
        gradient = gradients[position]
        squared = gradient * gradient + TINY_SQUARE
        rows_new = second_decay * moment + (1.0 - second_decay) * jnp.mean(squared, axis=1)
        rows_list.append(rows_new)
        column_parts.append(jnp.sum(squared, axis=0))
        row_parts.append(jnp.sum(rows_new))
    column_count = column_moment.shape[0]
    sums = lax.psum(
        jnp.concatenate(column_parts + [jnp.stack(row_parts), local_squares, local_loss[None]]), AXES
    )
    column_total = sums[:column_count]
    row_total = sums[column_count : column_count + 7]
    weight_squares = sums[column_count + 7 : column_count + 15]
    loss_sum = sums[column_count + 15]
    updates = [None] * 8
    moments_new = [None] * 8
    column_new = []
    offset = 0
    for factor_slot, position in enumerate(factored_index):
        gradient = gradients[position]
        rows_all = gradient.shape[0] * devices
        column_count = gradient.shape[1]
        cols_new = second_decay * column_moment[offset : offset + column_count] + (
            1.0 - second_decay
        ) * (column_total[offset : offset + column_count] / rows_all)
        offset += column_count
        estimate = (
            rows_list[factor_slot][:, None]
            * cols_new[None, :]
            / (row_total[factor_slot] / rows_all)
        )
        updates[position] = gradient * lax.rsqrt(estimate)
        moments_new[position] = rows_list[factor_slot]
        column_new.append(cols_new)
    vector_new = second_decay * vector_moment + (1.0 - second_decay) * (
        gradients[1] * gradients[1] + TINY_SQUARE
    )
    updates[1] = gradients[1] * lax.rsqrt(vector_new)
    moments_new[1] = vector_new
    local_spread = jnp.stack([jnp.sum(update * update) for update in updates])
    spread_total = lax.psum(local_spread, AXES)
    next_weights = []
    spreads = []
    for position in range(8):
        count_all = gradients[position].size * devices
        spread = jnp.sqrt(spread_total[position] / count_all)
        step_scale = jnp.maximum(SCALE_FLOOR, jnp.sqrt(weight_squares[position] / count_all))
        next_weights.append(
            masters[position]
            - STEP_RATE * step_scale * (updates[position] / jnp.maximum(1.0, spread / CLIP_LIMIT))
        )
        spreads.append(spread)
    column_stat = jnp.concatenate(column_new)
    clip_spread = jnp.stack(spreads)
    results = [loss_sum, weight_total]
    for position in range(8):
        results += [gradients[position], moments_new[position], next_weights[position]]
    return tuple(results + [column_stat, clip_spread])


def solution(mesh):
    in_specs = (
        P(("fsdp", "sub"), None),
        P(("fsdp", "sub")),
        P(("fsdp", "sub")),
        P(("fsdp", "sub")),
        P(("fsdp", "sub")),
        P(("fsdp", "sub")),
        P(("fsdp", "sub")),
        P(("fsdp", "sub"), None),
        P(("fsdp", "sub"), None),
        P(("fsdp", "sub"), None),
        P(("fsdp", "sub"), None),
        P(("fsdp", "sub"), None),
        P(("fsdp", "sub"), None),
        P(("fsdp", "sub"), None),
        P(("fsdp", "sub"), None),
        P(("fsdp", "sub")),
        P(("fsdp", "sub")),
        P(("fsdp", "sub")),
        P(("fsdp", "sub")),
        P(("fsdp", "sub")),
        P(("fsdp", "sub")),
        P(("fsdp", "sub")),
        P(("fsdp", "sub"), None),
        P(),
    )
    out_specs = (
        P(),
        P(),
        P(("fsdp", "sub"), None),
        P(("fsdp", "sub")),
        P(("fsdp", "sub"), None),
        P(("fsdp", "sub"), None),
        P(("fsdp", "sub"), None),
        P(("fsdp", "sub"), None),
        P(("fsdp", "sub"), None),
        P(("fsdp", "sub")),
        P(("fsdp", "sub"), None),
        P(("fsdp", "sub"), None),
        P(("fsdp", "sub")),
        P(("fsdp", "sub"), None),
        P(("fsdp", "sub"), None),
        P(("fsdp", "sub")),
        P(("fsdp", "sub"), None),
        P(("fsdp", "sub"), None),
        P(("fsdp", "sub")),
        P(("fsdp", "sub"), None),
        P(("fsdp", "sub"), None),
        P(("fsdp", "sub")),
        P(("fsdp", "sub"), None),
        P(("fsdp", "sub"), None),
        P(("fsdp", "sub")),
        P(("fsdp", "sub"), None),
        P(),
        P(),
    )
    return jax.shard_map(
        on_device, mesh=mesh, in_specs=in_specs, out_specs=out_specs, check_vma=False
    )
```

```python
import math
from functools import partial

import jax
import jax.numpy as jnp
from jax import lax
from jax.experimental import pallas as pl
from jax.experimental.pallas import tpu as pltpu
from jax.sharding import PartitionSpec as P

D = 1024
HEADS = 16
HEAD_DIM = 64
CLASSES = 1000
CODES = 4096
CODE_DIM = 32
LEVELS = 10
STEP = 10


TINY_SQUARE = 1e-30
SCALE_FLOOR = 0.001
STEP_RATE = 1.0
CLIP_LIMIT = 1.0
NORM_EPSILON = 1e-06
MASK_VALUE = -1000000000.0

AXES = ("fsdp", "sub")
MESH = pl.DeviceIdType.MESH
ANY = pl.BlockSpec(memory_space=pl.ANY)
WHOLE = pl.BlockSpec(memory_space=pltpu.VMEM)
FIVE = (2, 2, 2, 2, 2)
DIMS = ("w", "u", "y", "x", "c")
SCATTER_ORDERS = (("c", "x", "y", "w", "u"), ("c", "y", "x", "w", "u"))
GATHER_ORDERS = tuple(order[::-1] for order in SCATTER_ORDERS)
SCORE_SCALE = HEAD_DIM ** (-0.5)
EXP_SCALE = SCORE_SCALE * math.log2(math.e)
VMEM_GRANT = 58 * 1024 * 1024
FIRST_WIDTH, FIRST_LAG = 256, 2
ATTEND_WIDTH, ATTEND_LAG = 128, 3
BACK_WIDTH, BACK_LAG = 256, 3
LAST_WIDTH, LAST_LAG = 256, 2


def bfloat_product(left_side, right_side):
    return jnp.dot(left_side, right_side, preferred_element_type=jnp.float32)


class Place:
    def __init__(self):
        fsdp, sub = lax.axis_index("fsdp"), lax.axis_index("sub")
        self.bit = {
            "c": lax.rem(sub, 2),
            "x": lax.div(sub, 2),
            "y": lax.rem(fsdp, 2),
            "u": lax.rem(lax.div(fsdp, 2), 2),
            "w": lax.div(fsdp, 4),
        }
        bit = self.bit
        self.partner = {
            "c": (fsdp, sub + 1 - 2 * bit["c"]),
            "x": (fsdp, sub + 2 - 4 * bit["x"]),
            "y": (fsdp + 1 - 2 * bit["y"], sub),
            "u": (fsdp + 2 - 4 * bit["u"], sub),
            "w": (fsdp + 4 - 8 * bit["w"], sub),
        }

    def meet(self):
        barrier = pltpu.get_barrier_semaphore()
        for dim in DIMS:
            pl.semaphore_signal(
                barrier, inc=1, device_id=self.partner[dim], device_id_type=MESH
            )
        pl.semaphore_wait(barrier, 5)

    def send(self, src, dst, send_sem, recv_sem, dim):
        return pltpu.make_async_remote_copy(
            src_ref=src,
            dst_ref=dst,
            send_sem=send_sem,
            recv_sem=recv_sem,
            device_id=self.partner[dim],
            device_id_type=MESH,
        )


def when_in(index, low, high, body):
    if isinstance(index, int):
        if low <= index < high:
            body()
    else:
        pl.when((index >= low) & (index < high))(body)


class Gather:
    def __init__(self, place, groups, sends, recvs, local_sems, lag=1):
        self.place, self.groups, self.lag = place, groups, lag
        self.sends, self.recvs, self.local_sems = sends, recvs, local_sems
        self.steps = groups[-1][1] + 5 * lag

    @staticmethod
    def scratch(lag=1):
        dma = pltpu.SemaphoreType.DMA
        return [dma((5, 2, 2 * lag)), dma((5, 2, 2 * lag)), dma((2, 2 * lag))]

    def region(self, stage, parity):
        done = GATHER_ORDERS[parity][:stage]
        return tuple(slice(None) if d in done else self.place.bit[d] for d in DIMS)

    def copy(self, group, j, stage, parity, slot):
        _, _, own, full = group
        ref = full(j, parity, self.region(stage, parity))
        return self.place.send(
            own(j, parity) if stage == 0 else ref,
            ref,
            self.sends.at[stage, parity, slot],
            self.recvs.at[stage, parity, slot],
            GATHER_ORDERS[parity][stage],
        )

    def local(self, group, j, parity, slot):
        _, _, own, full = group
        return pltpu.make_async_copy(
            own(j, parity), full(j, parity, self.region(0, parity)), self.local_sems.at[parity, slot]
        )

    def step(self, t):
        for stage in reversed(range(6)):
            j = t - stage * self.lag
            for group in self.groups:

                def body(group=group, stage=stage, j=j):
                    slot = lax.rem(j, 2 * self.lag)
                    for parity in range(2):
                        if stage == 0:
                            self.local(group, j, parity, slot).start()
                        if stage == 1:
                            self.local(group, j, parity, slot).wait()
                        if stage >= 1:
                            self.copy(group, j, stage - 1, parity, slot).wait()
                        if stage < 5:
                            self.copy(group, j, stage, parity, slot).start()

                when_in(j, group[0], group[1], body)


class Scatter:
    def __init__(self, place, groups, store, scratch, lag=1):
        self.place, self.groups, self.store, self.lag = place, groups, store, lag
        self.keep = scratch[0]
        self.land = scratch[1:6]
        self.sums = (None,) + tuple(scratch[6:10])
        self.sends, self.recvs, self.keep_sems = scratch[10:13]
        self.first, self.end = groups[0][0], groups[-1][1]
        self.steps = self.end + 5 * lag
        rows, lanes = self.land[4].shape[2:]
        by_rows = self.keep.shape[5] != rows
        self.parts = [
            (slice(None),) * 4
            + (
                (slice(p * rows, (p + 1) * rows), slice(None))
                if by_rows
                else (slice(None), slice(p * lanes, (p + 1) * lanes))
            )
            for p in range(2)
        ]

    @staticmethod
    def scratch(piece, kind, lag=1, by_rows=False):
        dma = pltpu.SemaphoreType.DMA
        whole = (2 * piece[0], piece[1]) if by_rows else (piece[0], 2 * piece[1])
        return (
            [pltpu.VMEM((lag,) + (2,) * 4 + whole, kind), pltpu.VMEM((2 * lag,) + (2,) * 4 + whole, kind)]
            + [pltpu.VMEM((2 * lag, 2) + (2,) * (4 - k) + piece, kind) for k in range(1, 5)]
            + [pltpu.VMEM((lag, 2) + (2,) * (5 - k) + piece, kind) for k in range(1, 5)]
            + [dma((5, 2, 2 * lag)), dma((5, 2, 2 * lag)), dma((lag,))]
        )

    def half(self, stage, parity, other):
        order = SCATTER_ORDERS[parity]
        left = [d for d in DIMS if d not in order[:stage]]
        bit = self.place.bit[order[stage]]
        value = 1 - bit if other else bit
        return tuple(value if d == order[stage] else slice(None) for d in left)

    def copies(self, stage, j, source=None):
        slot, near = lax.rem(j, 2 * self.lag), lax.rem(j, self.lag)
        if stage == 0:
            pieces = [(self.keep.at[near] if source is None else source, self.land[0].at[slot])]
        elif stage < 3:
            pieces = [
                (
                    self.sums[stage].at[(near, parity) + self.half(stage, parity, True)],
                    self.land[stage].at[slot, parity],
                )
                for parity in range(2)
            ]
        else:
            at = (near, slice(None)) + self.half(stage, 0, True)
            pieces = [(self.sums[stage].at[at], self.land[stage].at[slot])]
        return [
            self.place.send(
                piece,
                target,
                self.sends.at[stage, parity, slot],
                self.recvs.at[stage, parity, slot],
                SCATTER_ORDERS[parity][stage],
            )
            for parity, (piece, target) in enumerate(pieces)
        ]

    def kept(self, j):
        near = lax.rem(j, self.lag)
        return self.keep.at[near], self.keep_sems.at[near]

    def step(self, t):
        for stage in reversed(range(6)):
            j = t - stage * self.lag

            def body(stage=stage, j=j):
                slot, near = lax.rem(j, 2 * self.lag), lax.rem(j, self.lag)
                before = stage - 1
                if before == 0:
                    keep, sem = self.kept(j)
                    pltpu.make_async_copy(keep, keep, sem).wait()
                for copy in self.copies(before, j):
                    copy.wait()
                if before < 3:
                    for parity in range(2):
                        if before == 0:
                            mine = self.keep[(near,) + self.parts[parity]]
                            landed = self.land[0][(slot,) + self.parts[parity]]
                        else:
                            mine = self.sums[before][(near, parity) + self.half(before, parity, False)]
                            landed = self.land[before][slot, parity]
                        self.sums[stage][near, parity] = mine + landed
                else:
                    mine = self.sums[before][(near, slice(None)) + self.half(before, 0, False)]
                    landed = self.land[before][slot]
                    if stage < 5:
                        self.sums[stage][near] = mine + landed
                    else:
                        total = mine.astype(jnp.float32) + landed.astype(jnp.float32)
                        for parity in range(2):
                            self.store(j, parity, total[parity])
                if stage < 5:
                    for copy in self.copies(stage, j):
                        copy.start()

            if stage == 0:
                for low, high, source in self.groups:

                    def begin(source=source, j=j):
                        core = self.place.bit["c"]
                        for copy in self.copies(0, j, source(j, 1 - core)):
                            copy.start()
                        pltpu.make_async_copy(source(j, core), *self.kept(j)).start()

                    when_in(j, low, high, begin)
            else:
                when_in(j, self.first, self.end, body)


def finish(engine):
    done = UNITS * (HEADS // 2)

    @pl.when(pl.program_id(0) == HEADS // 2 - 1)
    def rest():
        for t in range(done, engine.steps):
            engine.step(t)


def params(collective_id, **more):
    return pltpu.CompilerParams(
        collective_id=collective_id, has_side_effects=True, vmem_limit_bytes=VMEM_GRANT, **more
    )


def columns(start, size):
    return pl.ds(pl.multiple_of(start, 128), size)


def slot_labels(tags_full, order):
    pieces = []
    for number in range(32):
        bits = {dim: (number >> (4 - at)) & 1 for at, dim in enumerate(order)}
        pieces.append(tags_full[bits["w"], bits["u"], bits["y"], bits["x"], bits["c"], 0:2])
    return jnp.concatenate(pieces, axis=0)


def hot_of(labels):
    lanes = lax.broadcasted_iota(jnp.int32, labels.shape, 1).astype(jnp.float32)
    blocks = [jnp.where(labels == lanes + 128.0 * at, 1.0, 0.0) for at in range(9)]
    return jnp.concatenate(blocks, axis=1).astype(jnp.bfloat16)


def begin_kernel(
    rows_ref,
    tags_ref,
    tables_ref,
    ada_ref,
    qkv_ref,
    out_own_ref,
    codes_ref,
    token_columns,
    token_rows,
    projected_ref,
    qkv_out,
    out_full,
    embedded_ref,
    normed_ref,
    modulation_ref,
    vectors_ref,
    hot_ref,
    cond_ref,
    act_ref,
    tag_sums,
    bias_ref,
    turned_ref,
    *scratch,
):
    place = Place()
    place.meet()
    bit = place.bit
    (
        rows_full,
        tags_full,
        own_qkv,
        own_out,
        qkv_full,
        part,
        unit,
        staged,
        copy_sems,
        mod_sends,
        mod_recvs,
    ) = scratch[:11]
    mod_land, mod_sums = scratch[11:16], scratch[16:21]
    own_qkv[...] = qkv_ref[...].astype(jnp.bfloat16)
    own_out[...] = out_own_ref[...].astype(jnp.bfloat16)
    small = Gather(
        place,
        [(0, 1, lambda j, p: (rows_ref, tags_ref)[p], lambda j, p, r: (rows_full, tags_full)[p].at[r])],
        *scratch[21:24],
    )
    width = FIRST_WIDTH
    pairs = 3 * D // (2 * width)

    def of_weight(own, full, first):
        return (
            lambda j, p: own.at[:, columns((2 * (j - first) + p) * width, width)],
            lambda j, p, r: full.at[r + (slice(None), columns((2 * (j - first) + p) * width, width))],
        )

    gather = Gather(
        place,
        [
            (0, pairs) + of_weight(own_qkv, qkv_full, 0),
            (pairs, pairs + D // (2 * width)) + of_weight(own_out, out_full, pairs),
        ],
        *scratch[24:27],
        lag=FIRST_LAG,
    )
    lanes = 3 * D
    orders = (("x", "y", "w", "u", "c"), ("y", "x", "w", "u", "c"))

    def mod_half(stage, parity, other):
        dim = orders[parity][stage]
        value = 1 - bit[dim] if other else bit[dim]
        left = [d for d in ("x", "y", "w") if d not in orders[parity][:stage]]
        return tuple(value if d == dim else slice(None) for d in left)

    def mod_view(stage, parity, other):
        if stage == 0:
            at = pl.ds(parity * lanes, lanes)
            return part, mod_half(0, parity, other) + (slice(None), at)
        if stage < 3:
            return mod_sums[stage - 1], (parity,) + mod_half(stage, parity, other)
        return mod_sums[stage - 1], (parity,)

    def mod_copy(stage, parity):
        ref, at = mod_view(stage, parity, True)
        return place.send(
            ref.at[at],
            mod_land[stage].at[parity],
            mod_sends.at[stage, parity],
            mod_recvs.at[stage, parity],
            orders[parity][stage],
        )

    def mod_step(stage):
        for parity in range(2):
            if stage:
                mod_copy(stage - 1, parity).wait()
                ref, at = mod_view(stage - 1, parity, False)
                mod_sums[stage - 1][parity] = ref[at] + mod_land[stage - 1][parity]
            if stage < 5:
                mod_copy(stage, parity).start()

    def mask(query, key, same):
        usable = (query[0] == key[0]) & (key[1] <= query[1]) & ((key[2] > 0.5) | same)
        return jnp.where(usable, 0.0, MASK_VALUE)

    tokens = codes_ref.shape[0]
    block = tokens // 4

    def masks(index, size):
        at = slice(index * size, (index + 1) * size)
        shape = (size, tokens)
        same = lax.broadcasted_iota(jnp.int32, shape, 0) + index * size == lax.broadcasted_iota(
            jnp.int32, shape, 1
        )
        down = [token_columns[at, i : i + 1] for i in range(3)]
        across = [token_rows[i : i + 1] for i in range(3)]
        bias_ref[at] = mask(down, across, same)
        turned_ref[at] = mask(across, down, same)

    def embed(index):
        at = slice(index * block, (index + 1) * block)
        values = dot_last(codes_ref[at], rows_full[...].reshape(D, 128))
        embedded_ref[at] = values
        center = values - jnp.sum(values, axis=1, keepdims=True) * (1.0 / D)
        rate = lax.rsqrt(jnp.sum(center * center, axis=1, keepdims=True) * (1.0 / D) + NORM_EPSILON)
        unit[at] = center * rate

    masking = iter(range(8))
    steps = iter(range(gather.steps))
    for t in range(6):
        small.step(t)
        gather.step(next(steps))
        if t < 5:
            masks(next(masking), tokens // 8)
    tag_sums[...] = jnp.sum(tags_full[...].reshape(32, 8, 128), axis=0)
    low = jnp.bfloat16
    class_tables = tables_ref[:, :D].astype(low)
    for order, target in ((DIMS, None), (("x", "y", "w", "u", "c"), part)):
        hot = hot_of(slot_labels(tags_full, order))
        cond = dot_last(hot[:, :D], class_tables)
        act = (cond / (1.0 + jnp.exp(-cond))).astype(low)
        if target is None:
            hot_ref[...], cond_ref[...], act_ref[...] = hot, cond, act
        else:
            target[...] = dot_plain(act, ada_ref[...].astype(low)).reshape(2, 2, 2, 8, 6 * D)
    vectors_ref[...] = rows_full[...].reshape(D, 128).astype(jnp.float32).T[0:16]
    for stage in range(6):
        mod_step(stage)
        for step in steps:
            gather.step(step)
            break
        if stage < 4:
            embed(stage)
        for index in masking:
            masks(index, tokens // 8)
            break
    for step in steps:
        gather.step(step)
    store_qkv = pltpu.make_async_copy(qkv_full, qkv_out, copy_sems.at[2])
    store_qkv.start()
    spot = 4 * bit["u"] + 2 * bit["c"]
    row_ids = lax.broadcasted_iota(jnp.int32, (8, D), 0)
    for kind in range(6):
        at = (kind % 3) * D
        group = mod_sums[4][kind // 3, :, at : at + D]
        for slot in range(2):
            row = jnp.sum(jnp.where(row_ids == spot + slot, group, 0.0), axis=0, keepdims=True)
            modulation_ref[slot : slot + 1, kind * D : (kind + 1) * D] = row + vectors_ref[kind : kind + 1]
    stores = []
    for index in range(4):
        at = slice(index * block, (index + 1) * block)
        other = token_columns[at, 0:1] > 0.5
        scale = jnp.where(other, modulation_ref[1:2, 2 * D : 3 * D], modulation_ref[0:1, 2 * D : 3 * D])
        shift = jnp.where(other, modulation_ref[1:2, 4 * D : 5 * D], modulation_ref[0:1, 4 * D : 5 * D])
        normed = (unit[at] * (1.0 + scale) + shift).astype(low)
        normed_ref[at] = normed
        if index >= 2:
            stores[index - 2].wait()
        for column in range(0, 3 * D, 512):
            weight = qkv_full[:, :, :, :, :, :, column : column + 512].reshape(D, 512)
            staged[index % 2, :, column : column + 512] = dot_plain(normed, weight)
        stores.append(
            pltpu.make_async_copy(
                staged.at[index % 2], projected_ref.at[pl.ds(index * block, block)], copy_sems.at[index % 2]
            )
        )
        stores[index].start()
    stores[2].wait()
    stores[3].wait()
    store_qkv.wait()


def begin(rows, tags, tables, ada_weight, qkv_weight, out_weight, codes, token_columns, token_rows):
    depth = rows.shape[0]
    tokens = codes.shape[0]
    f32, low = jnp.float32, jnp.bfloat16
    dma = pltpu.SemaphoreType.DMA
    lanes = 3 * D
    lands = [
        pltpu.VMEM((2, 2, 2, 8, lanes), f32),
        pltpu.VMEM((2, 2, 8, lanes), f32),
    ] + [pltpu.VMEM((2, 8, lanes), f32)] * 3
    shape = jax.ShapeDtypeStruct
    return pl.pallas_call(
        begin_kernel,
        out_shape=(
            shape((tokens, 3 * D), f32),
            shape(FIVE + (depth, 3 * D), low),
            shape(FIVE + (depth, D), low),
            shape((tokens, D), f32),
            shape((tokens, D), low),
            shape((2, 6 * D), f32),
            shape((16, D), f32),
            shape((64, 1152), low),
            shape((64, depth), f32),
            shape((64, depth), low),
            shape((8, 128), f32),
            shape((tokens, tokens), f32),
            shape((tokens, tokens), f32),
        ),
        in_specs=[WHOLE] * 9,
        out_specs=(ANY, ANY, ANY) + (WHOLE,) * 10,
        scratch_shapes=[
            pltpu.VMEM(FIVE + (depth, 128), low),
            pltpu.VMEM(FIVE + (8, 128), f32),
            pltpu.VMEM((depth, 3 * D), low),
            pltpu.VMEM((depth, D), low),
            pltpu.VMEM(FIVE + (depth, 3 * D), low),
            pltpu.VMEM((2, 2, 2, 8, 6 * D), f32),
            pltpu.VMEM((tokens, D), f32),
            pltpu.VMEM((2, tokens // 4, 3 * D), f32),
            dma((3,)),
            dma((5, 2)),
            dma((5, 2)),
        ]
        + lands
        + lands
        + Gather.scratch()
        + Gather.scratch(FIRST_LAG),
        compiler_params=params(0),
        name="begin",
    )(rows, tags, tables, ada_weight, qkv_weight, out_weight, codes, token_columns, token_rows)


def head_mean(values):
    low_lane = lax.broadcasted_iota(jnp.int32, values.shape, 1) < HEAD_DIM
    low_sum = jnp.sum(jnp.where(low_lane, values, 0.0), axis=1, keepdims=True)
    high_sum = jnp.sum(jnp.where(low_lane, 0.0, values), axis=1, keepdims=True)
    return jnp.where(low_lane, low_sum, high_sum) * (1.0 / HEAD_DIM)


def of_head(values, head):
    low_lane = lax.broadcasted_iota(jnp.int32, values.shape, 1) < HEAD_DIM
    zero = jnp.zeros_like(values)
    return jnp.where(low_lane, values, zero) if head == 0 else jnp.where(low_lane, zero, values)


def dot_last(left, right):
    return lax.dot_general(left, right, (((1,), (1,)), ((), ())), preferred_element_type=jnp.float32)


def dot_first(left, right):
    return lax.dot_general(left, right, (((0,), (0,)), ((), ())), preferred_element_type=jnp.float32)


def dot_plain(left, right):
    return lax.dot_general(left, right, (((1,), (0,)), ((), ())), preferred_element_type=jnp.float32)


UNITS = 4


def normed_head(raw, gain):
    return (raw * lax.rsqrt(head_mean(raw * raw) + NORM_EPSILON) * gain).astype(jnp.bfloat16)


def attend_kernel(linked, q_ref, k_ref, v_ref, gain_ref, bias_ref, *refs):
    if linked:
        down_own, half_ref, mixed_ref, exact_ref, total_ref, down_full, up_full = refs[:7]
        qn, kn, vn, pair_sems, passing, pass_sems = refs[7:13]
        sems = refs[13:]
        place = Place()
        core = place.bit["c"]

        def pair_copies():
            target = up_full.at[:, :, :, :, core]
            yield place.send(half_ref, target, pair_sems.at[0, 0], pair_sems.at[1, 0], "c")

        chunks = HEADS // 2
        piece = passing.shape[6]

        def load(i):
            return pltpu.make_async_copy(
                half_ref.at[:, :, :, :, :, i * piece : (i + 1) * piece], passing.at[i % 2], pass_sems.at[0, i % 2]
            )

        def save(i):
            at = i * piece
            return pltpu.make_async_copy(
                passing.at[i % 2], up_full.at[:, :, :, :, core, :, at : at + piece], pass_sems.at[1, i % 2]
            )

        def each_chunk(body):
            for i in range(chunks):
                pl.when(pl.program_id(0) == i)(partial(body, i))

        def begin_chunk(i):
            if i >= 2:
                save(i - 2).wait()
            load(i).start()

        def end_chunk(i):
            load(i).wait()
            save(i).start()
            if i == chunks - 1:
                save(i - 1).wait()
                save(i).wait()

        width = ATTEND_WIDTH
        split = D // (2 * width)
        depth = down_full.shape[6]
        parts = down_full.shape[5]

        def down_source(j, p):
            part, column = lax.div(j, split), lax.rem(j, split)
            return down_own.at[
                pl.ds(pl.multiple_of(part * depth, depth), depth), columns((2 * column + p) * width, width)
            ]

        def down_target(j, p, r):
            part, column = lax.div(j, split), lax.rem(j, split)
            return down_full.at[r + (part, slice(None), columns((2 * column + p) * width, width))]

        gather = Gather(place, [(0, split * parts, down_source, down_target)], *sems, lag=ATTEND_LAG)

        @pl.when(pl.program_id(0) == 0)
        def first():
            place.meet()
            for copy in pair_copies():
                copy.start()

        each_chunk(begin_chunk)
    else:
        mixed_ref, exact_ref, total_ref, qn, kn, vn = refs
    qn[...] = normed_head(q_ref[...], gain_ref[0:1])
    kn[...] = normed_head(k_ref[...], gain_ref[1:2])
    vn[...] = v_ref[...].astype(jnp.bfloat16)
    tokens = q_ref.shape[0]
    both, sums = [], []
    for head in range(2):
        query = of_head(qn[...], head)
        mixed = jnp.zeros((tokens, 128), jnp.float32)
        lanes = jnp.zeros((tokens, 128), jnp.float32)
        for order in range(UNITS // 2):
            if linked:
                gather.step(pl.program_id(0) * UNITS + head * (UNITS // 2) + order)
            size = tokens // (UNITS // 2)
            keys = slice(order * size, (order + 1) * size)
            raised = jnp.exp2(dot_last(query, kn[keys]) * EXP_SCALE + bias_ref[:, keys])
            for lane in range(0, size, 128):
                lanes = lanes + raised[:, lane : lane + 128]
            mixed = mixed + dot_plain(raised.astype(jnp.bfloat16), vn[keys])
        total = jnp.sum(lanes, axis=1, keepdims=True)
        both.append(mixed * (1.0 / total))
        sums.append(total)
    low_lane = lax.broadcasted_iota(jnp.int32, both[0].shape, 1) < HEAD_DIM
    exact = jnp.where(low_lane, both[0], both[1])
    mixed_ref[...] = exact.astype(jnp.bfloat16)
    exact_ref[...] = exact
    total_ref[...] = jnp.log2(jnp.where(low_lane, sums[0], sums[1]))

    if linked:
        finish(gather)
        each_chunk(end_chunk)

        @pl.when(pl.program_id(0) == HEADS // 2 - 1)
        def pair_done():
            for copy in pair_copies():
                copy.wait()


def attend(projected, gains, bias, down_own=None, half=None):
    tokens = projected.shape[0]
    pair = pl.BlockSpec((tokens, 128), lambda i: (0, i))
    specs = [
        pair,
        pl.BlockSpec((tokens, 128), lambda i: (0, i + 8)),
        pl.BlockSpec((tokens, 128), lambda i: (0, i + 16)),
        pl.BlockSpec((8, 128), lambda i: (0, i)),
        pl.BlockSpec((tokens, tokens), lambda i: (0, 0), pipeline_mode=pl.Buffered(1)),
    ]
    outs = [jax.ShapeDtypeStruct((tokens, D), kind) for kind in (jnp.bfloat16, jnp.float32, jnp.float32)]
    out_specs = [pair] * 3
    scratch = [pltpu.VMEM((tokens, 128), jnp.bfloat16)] * 3
    operands = [projected, projected, projected, gains, bias]
    linked = down_own is not None
    if linked:
        depth = half.shape[4]
        specs += [ANY, ANY]
        operands += [down_own, half]
        outs += [jax.ShapeDtypeStruct(FIVE + (down_own.shape[0] // depth, depth, D), jnp.bfloat16)]
        outs += [jax.ShapeDtypeStruct(FIVE + (depth, half.shape[5]), jnp.bfloat16)]
        out_specs += [ANY] * 2
        scratch = scratch + [pltpu.SemaphoreType.DMA((2, 2))]
        scratch += [pltpu.VMEM((2,) + half.shape[:5] + (half.shape[5] // (HEADS // 2),), jnp.bfloat16)]
        scratch += [pltpu.SemaphoreType.DMA((2, 2))] + Gather.scratch(ATTEND_LAG)
    return pl.pallas_call(
        partial(attend_kernel, linked),
        grid=(HEADS // 2,),
        out_shape=tuple(outs),
        in_specs=specs,
        out_specs=tuple(out_specs),
        scratch_shapes=scratch,
        compiler_params=params(2) if linked else pltpu.CompilerParams(vmem_limit_bytes=VMEM_GRANT),
        name="attention_forward",
    )(*operands)


def attend_back_kernel(linked, q_ref, k_ref, v_ref, m_ref, exact_ref, total_ref, gain_ref, bias_ref, *refs):
    if linked:
        up_ref, down_ref, grad_ref, gain_grad_ref, done_ref = refs[:5]
        qn, kn, vn, dk, dv, turned, dq_turned, key_turned = refs[5:13]
        place = Place()
        width = BACK_WIDTH
        wide = up_ref.shape[6] // (2 * width)
        narrow = down_ref.shape[7] // (2 * width)
        parts = down_ref.shape[5]

        def columns_of(ref, first):
            return lambda j, core: ref.at[
                :, :, :, :, core, :, columns(2 * (j - first) * width, 2 * width)
            ]

        def down_source(j, core):
            spread = j - wide
            part, column = lax.div(spread, narrow), lax.rem(spread, narrow)
            return down_ref.at[:, :, :, :, core, part, :, columns(2 * column * width, 2 * width)]

        def store(j, parity, total):
            done_ref[j, :, parity * width : (parity + 1) * width] = total

        pairs = wide + parts * narrow
        scatter = Scatter(
            place,
            [
                (0, wide, columns_of(up_ref, 0)),
                (wide, pairs, down_source),
            ],
            store,
            refs[13:],
            lag=BACK_LAG,
        )
        pl.when(pl.program_id(0) == 0)(place.meet)
    else:
        grad_ref, gain_grad_ref = refs[:2]
        qn, kn, vn, dk, dv, turned, dq_turned, key_turned = refs[2:]
    qn[...] = normed_head(q_ref[...], gain_ref[0:1])
    kn[...] = normed_head(k_ref[...], gain_ref[1:2])
    vn[...] = v_ref[...].astype(jnp.bfloat16)
    for head in range(2):
        key_turned[head] = of_head(kn[...], head).T
    turned[0] = total_ref[...].T
    turned[1] = (head_mean(m_ref[...].astype(jnp.float32) * exact_ref[...]) * HEAD_DIM).T
    tokens = q_ref.shape[0]
    size = tokens // (UNITS // 2)
    for head in range(2):
        query = of_head(qn[...], head)
        mixed = of_head(m_ref[...], head)
        at = head * HEAD_DIM
        total = turned[0, at : at + 1]
        center = turned[1, at : at + 1]
        for order in range(UNITS // 2):
            if linked:
                scatter.step(pl.program_id(0) * UNITS + head * (UNITS // 2) + order)
            keys = slice(order * size, (order + 1) * size)
            scores = dot_last(kn[keys], query) * EXP_SCALE + (bias_ref[keys] - total)
            probs = jnp.exp2(scores)
            prob_grad = dot_last(vn[keys], mixed)
            score_grad = (probs * (prob_grad - center)).astype(jnp.bfloat16)
            key_part = dot_plain(score_grad, query)
            value_part = dot_plain(probs.astype(jnp.bfloat16), mixed)
            query_part = dot_plain(key_turned[head, :, keys], score_grad)
            dk[keys] = key_part if head == 0 else dk[keys] + key_part
            dv[keys] = value_part if head == 0 else dv[keys] + value_part
            dq_turned[...] = query_part if head == 0 and order == 0 else dq_turned[...] + query_part

    gain_rows = []
    for place_at, raw_ref, grad in ((0, q_ref, dq_turned[...].T), (1, k_ref, dk[...])):
        raw = raw_ref[...]
        normed_grad = grad * SCORE_SCALE
        rate = lax.rsqrt(head_mean(raw * raw) + NORM_EPSILON)
        scaled = gain_ref[place_at : place_at + 1] * normed_grad
        back = rate * scaled - raw * (rate * rate * rate) * head_mean(raw * scaled)
        grad_ref[place_at] = back.astype(jnp.bfloat16)
        gain_rows.append(jnp.sum(normed_grad * raw * rate, axis=0, keepdims=True))
    grad_ref[2] = dv[...].astype(jnp.bfloat16)
    gain_grad_ref[...] = jnp.concatenate(gain_rows + [jnp.zeros((6, 128), jnp.float32)], axis=0)
    if linked:
        finish(scatter)


def attend_back(projected, mixed_grad, exact, totals, gains, bias, up_grad=None, down_grad=None):
    tokens = projected.shape[0]
    pair = pl.BlockSpec((tokens, 128), lambda i: (0, i))
    specs = [
        pair,
        pl.BlockSpec((tokens, 128), lambda i: (0, i + 8)),
        pl.BlockSpec((tokens, 128), lambda i: (0, i + 16)),
        pair,
        pair,
        pair,
        pl.BlockSpec((8, 128), lambda i: (0, i)),
        pl.BlockSpec((tokens, tokens), lambda i: (0, 0), pipeline_mode=pl.Buffered(1)),
    ]
    outs = [
        jax.ShapeDtypeStruct((3, tokens, D), jnp.bfloat16),
        jax.ShapeDtypeStruct((8, D), jnp.float32),
    ]
    out_specs = [
        pl.BlockSpec((3, tokens, 128), lambda i: (0, 0, i)),
        pl.BlockSpec((8, 128), lambda i: (0, i)),
    ]
    scratch = [pltpu.VMEM((tokens, 128), jnp.bfloat16)] * 3 + [
        pltpu.VMEM((tokens, 128), jnp.float32)
    ] * 2
    scratch += [
        pltpu.VMEM((2, 128, tokens), jnp.float32),
        pltpu.VMEM((128, tokens), jnp.float32),
        pltpu.VMEM((2, 128, tokens), jnp.bfloat16),
    ]
    operands = [projected, projected, projected, mixed_grad, exact, totals, gains, bias]
    linked = up_grad is not None
    if linked:
        depth = up_grad.shape[5]
        specs += [ANY, ANY]
        operands += [up_grad, down_grad]
        pairs = (up_grad.shape[6] + down_grad.shape[5] * down_grad.shape[7]) // (2 * BACK_WIDTH)
        outs += [jax.ShapeDtypeStruct((pairs, depth, 2 * BACK_WIDTH), jnp.float32)]
        out_specs += [WHOLE]
        scratch = scratch + Scatter.scratch((depth, BACK_WIDTH), jnp.bfloat16, BACK_LAG)
    return pl.pallas_call(
        partial(attend_back_kernel, linked),
        grid=(HEADS // 2,),
        out_shape=tuple(outs),
        in_specs=specs,
        out_specs=tuple(out_specs),
        scratch_shapes=scratch,
        compiler_params=params(3) if linked else pltpu.CompilerParams(vmem_limit_bytes=VMEM_GRANT),
        name="attention_backward",
    )(*operands)


TANH_RATE = math.sqrt(2.0 / math.pi)
DENSE_WIDTH = 512


def dense_back_kernel(
    branch_ref,
    normed_ref,
    pre_ref,
    down_ref,
    up_ref,
    residual_ref,
    grad_ref,
    attended_ref,
    token_columns,
    mods_ref,
    head_ref,
    up_grad,
    down_grad,
    residual_grad,
    attended_grad,
    rows_ref,
    done_ref,
    normed_turned,
    pre_grad,
    hidden,
    back,
    *scratch,
):
    place = Place()
    index = pl.program_id(0)
    width = BACK_WIDTH

    def store(j, parity, total):
        done_ref[j, :, parity * width : (parity + 1) * width] = total

    pairs = head_ref.shape[6] // (2 * width)
    scatter = Scatter(
        place,
        [
            (
                0,
                pairs,
                lambda j, core: head_ref.at[:, :, :, :, core, :, columns(2 * j * width, 2 * width)],
            )
        ],
        store,
        scratch,
        lag=BACK_LAG,
    )

    @pl.when(index == 0)
    def first():
        place.meet()
        normed_turned[...] = normed_ref[...].T
        back[...] = jnp.zeros_like(back)

    tokens = branch_ref.shape[0]
    block = tokens // 4
    blocks = [slice(i * block, (i + 1) * block) for i in range(4)]
    scatter.step(index * 3)
    for rows in blocks:
        act_grad = dot_last(branch_ref[rows], down_ref[...])
        value = pre_ref[rows]
        square = value * value
        bent = jnp.tanh(TANH_RATE * value * (1.0 + 0.044715 * square))
        half = 0.5 * (1.0 + bent)
        slope = half + 0.5 * value * (1.0 - bent * bent) * (TANH_RATE * (1.0 + 3 * 0.044715 * square))
        pre_grad[rows] = (slope * act_grad).astype(jnp.bfloat16)
        hidden[rows] = (value * half).astype(jnp.bfloat16)
    scatter.step(index * 3 + 1)
    down_grad[...] = dot_first(hidden[...], branch_ref[...]).astype(jnp.bfloat16)
    up_grad[...] = dot_plain(normed_turned[...], pre_grad[...]).astype(jnp.bfloat16)
    scatter.step(index * 3 + 2)
    for rows in blocks:
        back[rows] += dot_last(pre_grad[rows], up_ref[...])

    @pl.when(index == pl.num_programs(0) - 1)
    def last():
        sums = [jnp.zeros((1, D), jnp.float32)] * 6
        for rows in blocks:
            values, slope = residual_ref[rows], back[rows]
            center = values - jnp.sum(values, axis=1, keepdims=True) * (1.0 / D)
            rate = lax.rsqrt(
                jnp.sum(center * center, axis=1, keepdims=True) * (1.0 / D) + NORM_EPSILON
            )
            unit = center * rate
            other = token_columns[rows, 0:1] > 0.5
            unit_back = slope * (1.0 + jnp.where(other, mods_ref[1:2], mods_ref[0:1]))
            mean_back = jnp.sum(unit_back, axis=1, keepdims=True) * (1.0 / D)
            mean_along = jnp.sum(unit_back * unit, axis=1, keepdims=True) * (1.0 / D)
            total = grad_ref[rows] + rate * (unit_back - mean_back - unit * mean_along)
            residual_grad[rows] = total
            attended_grad[rows] = (total * jnp.where(other, mods_ref[3:4], mods_ref[2:3])).astype(
                jnp.bfloat16
            )
            for at, value in enumerate((slope * unit, slope, total * attended_ref[rows])):
                second = jnp.sum(jnp.where(other, value, 0.0), axis=0, keepdims=True)
                first_slot = jnp.sum(jnp.where(other, 0.0, value), axis=0, keepdims=True)
                sums[2 * at] = sums[2 * at] + first_slot
                sums[2 * at + 1] = sums[2 * at + 1] + second
        for at in range(6):
            rows_ref[at : at + 1] = sums[at]


def dense_back(branch_grad, normed, pre, down, up, residual, grad, attended, token_columns, mods, head):
    tokens, wide = pre.shape
    depth = head.shape[5]
    pairs = head.shape[6] // (2 * BACK_WIDTH)
    f32, low = jnp.float32, jnp.bfloat16
    width = DENSE_WIDTH

    def fixed(*shape):
        return pl.BlockSpec(shape, lambda i: (0,) * len(shape), pipeline_mode=pl.Buffered(1))

    across = pl.BlockSpec((D, width), lambda i: (0, i))
    along = pl.BlockSpec((width, D), lambda i: (i, 0))
    shape = jax.ShapeDtypeStruct
    return pl.pallas_call(
        dense_back_kernel,
        grid=(wide // width,),
        out_shape=(
            shape((D, wide), low),
            shape((wide, D), low),
            shape((tokens, D), f32),
            shape((tokens, D), low),
            shape((8, D), f32),
            shape((pairs, depth, 2 * BACK_WIDTH), f32),
        ),
        in_specs=[
            fixed(tokens, D),
            fixed(tokens, D),
            pl.BlockSpec((tokens, width), lambda i: (0, i)),
            along,
            across,
            fixed(tokens, D),
            fixed(tokens, D),
            fixed(tokens, D),
            fixed(tokens, 128),
            fixed(8, D),
            ANY,
        ],
        out_specs=(across, along, fixed(tokens, D), fixed(tokens, D), fixed(8, D), WHOLE),
        scratch_shapes=[
            pltpu.VMEM((D, tokens), low),
            pltpu.VMEM((tokens, width), low),
            pltpu.VMEM((tokens, width), low),
            pltpu.VMEM((tokens, D), f32),
        ]
        + Scatter.scratch((depth, BACK_WIDTH), low, BACK_LAG),
        compiler_params=params(5),
        name="dense_backward",
    )(branch_grad, normed, pre, down, up, residual, grad, attended, token_columns, mods, head)


WEIGHT_COLUMNS = (CLASSES + CODE_DIM + LEVELS, 9, 6 * D, 3 * D, D, 4 * D, D, CODES)
SUM_STARTS = (0, None, 1152, 1152 + 6144, 1152 + 9216, 1152 + 10240, 1152 + 14336, 1152 + 15360)
SCALARS = 1152 + 19456
SUM_LANES = SCALARS + 128
SMALL_LANES = CODE_DIM + LEVELS + 9
DECAY = 1.0 - STEP ** (-0.8)


def three_terms(values):
    high = values.astype(jnp.bfloat16)
    rest = values - high.astype(jnp.float32)
    middle = rest.astype(jnp.bfloat16)
    return high, middle, (rest - middle.astype(jnp.float32)).astype(jnp.bfloat16)


def lane_row(scalars):
    lanes = lax.broadcasted_iota(jnp.int32, (1, 128), 1)
    row = jnp.zeros((1, 128), jnp.float32)
    for lane, value in scalars:
        row = jnp.where(lanes == lane, value, row)
    return row


def whole_sum(values):
    return jnp.sum(jnp.sum(values, axis=0, keepdims=True), axis=1, keepdims=True)


def weight_tiles(tables_grad, ada_grad, done_head, done_attention, done_last):
    def blocks(ref, first, count, width):
        return [(lambda at=first + i: ref[at], i * width, width) for i in range(count)]

    near, far = 2 * LAST_WIDTH, 2 * BACK_WIDTH
    tables_columns = WEIGHT_COLUMNS[0]
    wide = CODES // far
    return {
        0: [(0, [(lambda: tables_grad[:, :tables_columns], 0, tables_columns)])],
        2: [(1, [(lambda: ada_grad[...], 0, 6 * D)])],
        3: [(2, blocks(done_last, D // near, 3 * D // near, near))],
        4: [(3, blocks(done_last, 0, D // near, near))],
        5: [(4, blocks(done_attention, 0, wide, far))],
        6: [(6 + part, blocks(done_attention, wide + part * (D // far), D // far, far)) for part in range(4)],
        7: [(5, blocks(done_head, 0, wide, far))],
    }


class Total:
    def __init__(self, place, sums, land, sends, recvs):
        self.place, self.sums, self.land = place, sums, land
        self.sends, self.recvs = sends, recvs

    @staticmethod
    def scratch(lanes):
        dma = pltpu.SemaphoreType.DMA
        return [
            pltpu.VMEM((6, 1, lanes), jnp.float32),
            pltpu.VMEM((5, 1, lanes), jnp.float32),
            dma((5,)),
            dma((5,)),
        ]

    def run(self):
        for stage, dim in enumerate(DIMS):
            copy = self.place.send(
                self.sums.at[stage], self.land.at[stage], self.sends.at[stage], self.recvs.at[stage], dim
            )
            copy.start()
            copy.wait()
            self.sums[stage + 1] = self.sums[stage] + self.land[stage]


def last_kernel(
    out_ref,
    qkv_low,
    embedded_ref,
    grad_ref,
    heads_grad,
    normed_ref,
    codes_ref,
    second_ref,
    scale_ref,
    known_ref,
    gains_ref,
    act_ref,
    cond_ref,
    hot_ref,
    loss_ref,
    done_head,
    attention_ref,
    tables_ref,
    vectors_ref,
    ada_ref,
    qkv_master,
    out_master,
    up_master,
    down_master,
    head_master,
    moments_ref,
    vector_moment_ref,
    column_moment_ref,
    done_ref,
    small_done,
    tables_grad,
    ada_grad,
    rows_ref,
    columns_ref,
    facts_ref,
    *scratch,
):
    place = Place()
    place.meet()
    devices = lax.axis_size(AXES)
    depth = tables_ref.shape[0]
    width = LAST_WIDTH
    narrow = D // (2 * width)
    part_grads, qkv_full, embedded, grad, code_sums, mod_ref, small_ref, load_sems = scratch[40:48]
    loads = [
        pltpu.make_async_copy(source, target, load_sems.at[i])
        for i, (source, target) in enumerate(
            ((qkv_low, qkv_full), (embedded_ref, embedded), (grad_ref, grad))
        )
    ]
    for load in loads:
        load.start()

    def columns_of(ref, first):
        return lambda j, core: ref.at[
            :, :, :, :, core, :, columns(2 * (j - first) * width, 2 * width)
        ]

    def store(j, parity, total):
        done_ref[j, :, parity * width : (parity + 1) * width] = total

    pairs = 4 * narrow
    scatter = Scatter(
        place,
        [(0, narrow, columns_of(out_ref, 0))]
        + [
            ((1 + part) * narrow, (2 + part) * narrow, columns_of(part_grads.at[part], (1 + part) * narrow))
            for part in range(3)
        ],
        store,
        scratch[:13],
        lag=LAST_LAG,
    )
    half = depth // 2

    def small_store(j, parity, total):
        small_done[pl.ds(parity * half, half)] = total

    small = Scatter(
        place,
        [(0, 1, lambda j, core: small_ref.at[:, :, :, :, core])],
        small_store,
        scratch[13:26],
    )
    mod_sums, mod_land, mod_all, mod_sends, mod_recvs = scratch[26:31]
    bit = place.bit

    def mod_copy(stage):
        dim = ("c", "x", "y", "u", "w")[stage]
        if stage < 3:
            source, target = (mod_ref, mod_sums.at[0], mod_sums.at[1])[stage], mod_land.at[stage]
        elif stage == 3:
            source = target = mod_all.at[bit["w"], bit["u"]]
        else:
            source = target = mod_all.at[bit["w"]]
        return place.send(source, target, mod_sends.at[stage], mod_recvs.at[stage], dim)

    def mod_step(stage):
        if stage:
            mod_copy(stage - 1).wait()
        if stage == 1:
            mod_sums[0] = mod_ref[...] + mod_land[0]
        elif stage == 2:
            mod_sums[1] = mod_sums[0] + mod_land[1]
        elif stage == 3:
            mod_all[bit["w"], bit["u"]] = mod_sums[1] + mod_land[2]
        if stage < 5:
            mod_copy(stage).start()

    first_total = Total(place, *scratch[31:35])
    second_total = Total(place, *scratch[35:39])
    sums, facts = first_total.sums, scratch[39]
    tiles = weight_tiles(tables_grad, ada_grad, done_head, attention_ref, done_ref)
    masters = (
        tables_ref,
        vectors_ref,
        ada_ref,
        qkv_master,
        out_master,
        up_master,
        down_master,
        head_master,
    )

    def ada_part():
        slots = mod_all[...].reshape(2 * devices, 6 * D)
        ada_grad[...] = dot_first(act_ref[...], slots)
        activated_grad = dot_last(slots, ada_ref[...].astype(jnp.bfloat16))
        cond = cond_ref[...]
        gate = 1.0 / (1.0 + jnp.exp(-cond))
        cond_grad = activated_grad * (gate * (1.0 + cond * (1.0 - gate)))
        shape = (128, hot_ref.shape[1])
        source = lax.broadcasted_iota(jnp.int32, shape, 0)
        target = lax.broadcasted_iota(jnp.int32, shape, 1)
        moved = (target == source + (CLASSES - 9)) & (source >= 9) & (source < SMALL_LANES)
        shift = jnp.where(moved, 1.0, 0.0).astype(jnp.bfloat16)
        total = jnp.zeros((depth, hot_ref.shape[1]), jnp.float32)
        for term in three_terms(cond_grad)[::-1]:
            total = total + dot_first(term, hot_ref[...])
        for term in three_terms(small_done[...])[::-1]:
            total = total + dot_plain(term, shift)
        tables_grad[...] = total

    def stats(position):
        row_total = jnp.zeros((1, 1), jnp.float32)
        for index, group in tiles[position]:
            row_sum = jnp.zeros((depth, 1), jnp.float32)
            for load, first, size in group:
                gradient = load()
                squared = gradient * gradient + TINY_SQUARE
                row_sum = row_sum + jnp.sum(squared, axis=1, keepdims=True)
                at = SUM_STARTS[position] + first
                sums[0, :, at : at + size] += jnp.sum(squared, axis=0, keepdims=True)
            rows_new = DECAY * moments_ref[index] + (1.0 - DECAY) * (
                row_sum * (1.0 / WEIGHT_COLUMNS[position])
            )
            rows_ref[index] = rows_new
            row_total = row_total + jnp.sum(rows_new, axis=0, keepdims=True)
        facts[...] += lane_row([(position, row_total)])

    def squares(first, end):
        for position in range(first, end):
            master = masters[position][...]
            facts[...] += lane_row([(8 + position, whole_sum(master * master))])

    def part_grad(part):
        @pl.loop(0, D // 256)
        def tile(i):
            at = columns(i * 256, 256)
            product = dot_first(normed_ref[...], heads_grad[part, :, at])
            part_grads[part, :, :, :, :, :, :, at] = product.astype(jnp.bfloat16).reshape(
                FIVE + (depth, 256)
            )

    tokens = normed_ref.shape[0]
    block = tokens // 4
    slot_rows = [jnp.zeros((1, D), jnp.float32)] * 4

    def norm_back(index):
        rows = slice(index * block, (index + 1) * block)
        back = jnp.zeros((block, D), jnp.float32)
        for part in range(3):
            back = back + dot_last(heads_grad[part, rows], qkv_full[:, part * D : (part + 1) * D])
        values = embedded[rows]
        center = values - jnp.sum(values, axis=1, keepdims=True) * (1.0 / D)
        rate = lax.rsqrt(jnp.sum(center * center, axis=1, keepdims=True) * (1.0 / D) + NORM_EPSILON)
        unit = center * rate
        other = second_ref[rows] > 0.5
        scale_back = back * unit
        for at, value in enumerate((scale_back, back)):
            everything = jnp.sum(value, axis=0, keepdims=True)
            second = jnp.sum(jnp.where(other, value, 0.0), axis=0, keepdims=True)
            slot_rows[2 * at] = slot_rows[2 * at] + (everything - second)
            slot_rows[2 * at + 1] = slot_rows[2 * at + 1] + second
        unit_back = back * (1.0 + jnp.where(other, scale_ref[1:2], scale_ref[0:1]))
        mean_back = jnp.sum(unit_back, axis=1, keepdims=True) * (1.0 / D)
        mean_along = jnp.sum(unit_back * unit, axis=1, keepdims=True) * (1.0 / D)
        total = grad[rows] + rate * (unit_back - mean_back - unit * mean_along)
        high = total.astype(jnp.bfloat16)
        rest = (total - high.astype(jnp.float32)).astype(jnp.bfloat16)
        product = dot_first(codes_ref[rows], high) + dot_first(codes_ref[rows], rest)
        code_sums[...] = product if index == 0 else code_sums[...] + product

    def gather_rows():
        spot = 2 * (4 * bit["y"] + 2 * bit["x"] + bit["c"])
        row_ids = lax.broadcasted_iota(jnp.int32, (16, D), 0)
        for kind in range(6):
            if kind in (2, 4):
                first, other = slot_rows[kind - 2 : kind]
            else:
                at = slice(kind * D, (kind + 1) * D)
                first, other = known_ref[0:1, at], known_ref[1:2, at]
            placed = jnp.where(row_ids == spot, first, jnp.where(row_ids == spot + 1, other, 0.0))
            mod_ref[:, kind * D : (kind + 1) * D] = placed.astype(jnp.bfloat16)
            code_sums[kind : kind + 1] = first + other
        code_sums[6:9] = gains_ref[0:3]
        small_ref[...] = code_sums[...].T.reshape(FIVE + (depth, 128))

    sums[0] = jnp.zeros_like(sums[0])
    facts[...] = lane_row([(16, loss_ref[...])])
    steps = iter(range(scatter.steps))
    for _ in range(narrow):
        scatter.step(next(steps))
    for part in range(3):
        part_grad(part)
        for _ in range(narrow):
            scatter.step(next(steps))
    for load in loads:
        load.wait()
    for index in range(4):
        norm_back(index)
        if index % 2:
            scatter.step(next(steps))
    gather_rows()
    beside = [
        partial(stats, 5),
        partial(stats, 6),
        partial(stats, 7),
        partial(squares, 0, 5),
        partial(squares, 5, 8),
    ]
    for t in range(6):
        mod_step(t)
        small.step(t)
        if t < len(beside):
            beside[t]()
        for step in steps:
            scatter.step(step)
            break
    ada_part()
    for step in steps:
        scatter.step(step)
    stats(0)
    stats(2)
    stats(3)
    stats(4)
    sums[0, :, SCALARS:] = facts[...]
    first_total.run()
    columns_ref[...] = DECAY * column_moment_ref[...] + (1.0 - DECAY) * sums[5] * (1.0 / D)
    start, end = SUM_STARTS[6], SUM_STARTS[6] + D
    columns_ref[:, start:end] = DECAY * column_moment_ref[:, start:end] + (1.0 - DECAY) * sums[
        5, :, start:end
    ] * (1.0 / (4 * D))

    def rows_all(position):
        return 4.0 * D if position == 6 else 1.0 * D

    scalars = []
    for position, groups in tiles.items():
        at = SCALARS + position
        row_mean = sums[5, :, at : at + 1] * (1.0 / rows_all(position))
        spread = jnp.zeros((1, 1), jnp.float32)
        for index, group in groups:
            for load, first, size in group:
                lane = SUM_STARTS[position] + first
                estimate = rows_ref[index] * columns_ref[:, lane : lane + size] / row_mean
                update = load() * lax.rsqrt(estimate)
                spread = spread + whole_sum(update * update)
        scalars.append((position, spread))
    gradient = small_done[:, :9]
    moment = DECAY * vector_moment_ref[...] + (1.0 - DECAY) * (gradient * gradient + TINY_SQUARE)
    update = gradient * lax.rsqrt(moment)
    scalars.append((1, whole_sum(update * update)))
    second_total.sums[0] = lane_row(scalars)
    second_total.run()
    spread_row, factor_row = [], []
    for position in range(8):
        count = rows_all(position) * WEIGHT_COLUMNS[position]
        spread = jnp.sqrt(second_total.sums[5, :, position : position + 1] * (1.0 / count))
        at = SCALARS + 8 + position
        scale = jnp.maximum(SCALE_FLOOR, jnp.sqrt(sums[5, :, at : at + 1] * (1.0 / count)))
        spread_row.append((position, spread))
        factor_row.append((position, STEP_RATE * scale / jnp.maximum(1.0, spread / CLIP_LIMIT)))
    facts_ref[0] = lane_row(spread_row)
    facts_ref[1] = lane_row(factor_row)
    facts_ref[2] = sums[5, :, SCALARS:]


def last_exchange(far, near, done, masters, moments):
    depth = far[0].shape[5]
    pairs = 4 * D // (2 * LAST_WIDTH)
    dma = pltpu.SemaphoreType.DMA
    f32, low = jnp.float32, jnp.bfloat16
    tokens = far[2].shape[0]
    operands = list(far) + list(near) + list(done) + list(masters) + list(moments)
    return pl.pallas_call(
        last_kernel,
        out_shape=(
            jax.ShapeDtypeStruct((pairs, depth, 2 * LAST_WIDTH), f32),
            jax.ShapeDtypeStruct((depth, 128), f32),
            jax.ShapeDtypeStruct((depth, 1152), f32),
            jax.ShapeDtypeStruct((depth, 6 * D), f32),
            jax.ShapeDtypeStruct((10, depth, 1), f32),
            jax.ShapeDtypeStruct((1, SUM_LANES), f32),
            jax.ShapeDtypeStruct((3, 1, 128), f32),
        ),
        in_specs=[ANY] * 4 + [WHOLE] * (len(operands) - 4),
        out_specs=(WHOLE,) * 7,
        scratch_shapes=Scatter.scratch((depth, LAST_WIDTH), low, LAST_LAG)
        + Scatter.scratch((depth // 2, 128), f32, 1, True)
        + [
            pltpu.VMEM((2, 16, 6 * D), low),
            pltpu.VMEM((3, 16, 6 * D), low),
            pltpu.VMEM((2, 2, 16, 6 * D), low),
            dma((5,)),
            dma((5,)),
        ]
        + Total.scratch(SUM_LANES)
        + Total.scratch(128)
        + [pltpu.VMEM((1, 128), f32)]
        + [
            pltpu.VMEM((3,) + FIVE + (depth, D), low),
            pltpu.VMEM((D, 3 * D), low),
            pltpu.VMEM((tokens, D), f32),
            pltpu.VMEM((tokens, D), f32),
            pltpu.VMEM((128, D), f32),
            pltpu.VMEM((16, 6 * D), low),
            pltpu.VMEM(FIVE + (depth, 128), f32),
            dma((3,)),
        ],
        compiler_params=params(4),
        name="last_scatter",
    )(*operands)


def step_kernel(
    done_ref,
    small_ref,
    tables_grad,
    ada_grad,
    rows_ref,
    columns_ref,
    facts_ref,
    done_head,
    attention_ref,
    vector_moment_ref,
    tables_ref,
    vectors_ref,
    ada_ref,
    qkv_master,
    out_master,
    up_master,
    down_master,
    head_master,
    *outs,
):
    depth = tables_ref.shape[0]
    masters = (
        tables_ref,
        vectors_ref,
        ada_ref,
        qkv_master,
        out_master,
        up_master,
        down_master,
        head_master,
    )
    vector_stat = outs[16]
    tiles = weight_tiles(tables_grad, ada_grad, done_head, attention_ref, done_ref)
    for position, groups in tiles.items():
        grad_ref, next_ref, master = outs[2 * position], outs[2 * position + 1], masters[position]
        factor = facts_ref[1, :, position : position + 1]
        mean_scale = 1.0 / (4 * D) if position == 6 else 1.0 / D
        row_mean = facts_ref[2, :, position : position + 1] * mean_scale
        for order, (index, group) in enumerate(groups):
            at = slice(order * depth, (order + 1) * depth)
            for load, first, size in group:
                gradient = load()
                lane = SUM_STARTS[position] + first
                estimate = rows_ref[index] * columns_ref[:, lane : lane + size] / row_mean
                grad_ref[at, first : first + size] = gradient
                next_ref[at, first : first + size] = master[at, first : first + size] - factor * (
                    gradient * lax.rsqrt(estimate)
                )
    gradient = small_ref[:, :9]
    moment = DECAY * vector_moment_ref[...] + (1.0 - DECAY) * (gradient * gradient + TINY_SQUARE)
    vector_stat[...] = moment
    outs[2][...] = gradient
    outs[3][...] = vectors_ref[...] - facts_ref[1, :, 1:2] * (gradient * lax.rsqrt(moment))


def take_step(last, done, vector_moment, masters):
    operands = list(last) + list(done) + [vector_moment] + list(masters)
    shapes = []
    for master in masters:
        shapes += [jax.ShapeDtypeStruct(master.shape, jnp.float32)] * 2
    shapes.append(jax.ShapeDtypeStruct(vector_moment.shape, jnp.float32))
    return pl.pallas_call(
        step_kernel,
        out_shape=tuple(shapes),
        in_specs=[WHOLE] * len(operands),
        out_specs=(WHOLE,) * len(shapes),
        compiler_params=pltpu.CompilerParams(vmem_limit_bytes=VMEM_GRANT),
        name="weight_step",
    )(*operands)


def linked_mesh():
    return lax.axis_size("fsdp") == 8 and lax.axis_size("sub") == 4


def gathered(values):
    return lax.all_gather(values, AXES, axis=0, tiled=True)


def scattered(values):
    return lax.psum_scatter(values, AXES, scatter_dimension=0, tiled=True)


def layer_norm(values):
    center = values - jnp.mean(values, axis=-1, keepdims=True)
    return center * lax.rsqrt(jnp.mean(center * center, axis=-1, keepdims=True) + NORM_EPSILON)


def modulate(values, scale_part, shift_part):
    return layer_norm(values) * (1.0 + scale_part) + shift_part


def final_norm(values, gain_vector):
    return layer_norm(values) * gain_vector


def attention_bias(query, key):
    usable = (query[1] == key[1]) & (key[0] <= query[0]) & ((key[2] == 1) | (query[3] == key[3]))
    return jnp.where(usable, 0.0, MASK_VALUE)


def split_product(left_side, right_low):
    high = left_side.astype(jnp.bfloat16)
    rest = (left_side - high.astype(jnp.float32)).astype(jnp.bfloat16)
    return bfloat_product(high, right_low) + bfloat_product(rest, right_low)


def on_device(
    code_vectors,
    scale_ids,
    segment_ids,
    real_mask,
    labels,
    targets,
    loss_weight,
    tables,
    vectors,
    ada_weight,
    qkv_weight,
    out_weight,
    up_weight,
    down_weight,
    head_weight,
    tables_moment,
    ada_moment,
    qkv_moment,
    out_moment,
    up_moment,
    down_moment,
    head_moment,
    vector_moment,
    column_moment,
):
    devices = lax.axis_size(AXES)
    linked = linked_mesh()
    depth = tables.shape[0]
    tokens = code_vectors.shape[0]
    masters = (
        tables,
        vectors,
        ada_weight,
        qkv_weight,
        out_weight,
        up_weight,
        down_weight,
        head_weight,
    )
    local_count = jnp.sum(loss_weight).astype(jnp.float32)
    low = jnp.bfloat16
    part_kind = low if linked else jnp.float32
    tables_low = tables.astype(low)
    ada_low = ada_weight.astype(low)
    qkv_low = qkv_weight.astype(low)
    out_low = out_weight.astype(low)
    down_low = down_weight.astype(low)

    if linked:
        cores = [[core + 2 * chip for chip in range(devices // 2)] for core in range(2)]
        up_half = lax.all_gather(
            up_weight.astype(low),
            AXES,
            axis_index_groups=cores,
            axis=0,
            tiled=True,
        ).reshape(2, 2, 2, 2, depth, -1)
    else:
        full_up = gathered(up_weight.astype(low))
    full_head = gathered(head_weight.astype(low))
    small_rows = jnp.concatenate(
        [vectors.astype(low), tables_low[:, CLASSES:], jnp.zeros((depth, 128 - SMALL_LANES), low)], axis=1
    )
    tag_row = jnp.concatenate([labels.astype(jnp.float32), local_count[None], jnp.zeros((5,), jnp.float32)])
    tags = jnp.broadcast_to(tag_row[:, None], (8, 128))
    level_hot = (scale_ids[:, None] == jnp.arange(LEVELS)[None, :]).astype(low)
    code_levels = jnp.concatenate([code_vectors, level_hot], axis=1)
    codes = jnp.pad(code_levels, ((0, 0), (9, 128 - SMALL_LANES)))
    second = (segment_ids == 1)[:, None]
    if linked:
        token_rows = jnp.stack([segment_ids, scale_ids, real_mask] + [real_mask] * 5).astype(jnp.float32)
        token_columns = jnp.pad(token_rows[:3].T, ((0, 0), (0, 125)))
        (
            projected,
            full_qkv,
            full_out,
            embedded,
            normed,
            modulation,
            vector_rows,
            label_hot,
            class_cond,
            activated,
            tag_sums,
            bias,
            turned_bias,
        ) = begin(
            small_rows, tags, tables, ada_weight, qkv_weight, out_weight, codes, token_columns, token_rows
        )
        full_qkv, full_out = full_qkv.reshape(D, 3 * D), full_out.reshape(D, D)
        weight_total = tag_sums[2, 0]
        gains = vector_rows[6:14]
        head_gain = vector_rows[8]
    else:
        small_full = gathered(small_rows)
        tags_full = gathered(tags).reshape(devices, 8, 128)[:, :, 0]
        labels_all = tags_full[:, :2].reshape(2 * devices)
        weight_total = jnp.sum(tags_full[:, 2])
        gain_vector = small_full[:, :9].astype(jnp.float32)
        label_hot = (labels_all[:, None] == jnp.arange(1152, dtype=jnp.float32)[None, :]).astype(low)
        class_cond = bfloat_product(label_hot[:, :CLASSES], tables_low[:, :CLASSES].T)
        activated = jax.nn.silu(class_cond).astype(low)
        own_modulation, full_qkv = scattered(bfloat_product(activated, ada_low)), gathered(qkv_low)
        modulation = own_modulation + gain_vector[:, :6].T.reshape(1, 6 * D)
        embedded = bfloat_product(codes, small_full.T)
        gains = jnp.pad(gain_vector[:, 6:8].T, ((0, 6), (0, 0)))
        head_gain = gain_vector[:, 8]

    def of_token(block):
        piece = modulation[:, block * D : (block + 1) * D]
        return jnp.where(second, piece[1:2], piece[0:1])

    gamma_one, gamma_two, scale_one, scale_two, shift_one, shift_two = (
        of_token(block) for block in range(6)
    )
    if linked:
        mixed_heads, exact, totals, full_down, full_up = attend(projected, gains, bias, down_low, up_half)
        full_down = full_down.reshape(-1, D)
        full_up = full_up.reshape(D, -1)
    else:
        normed = modulate(embedded, scale_one, shift_one).astype(low)
        projected = bfloat_product(normed, full_qkv)
        places = jnp.arange(tokens)
        masks = (scale_ids, segment_ids, real_mask, places)
        bias = attention_bias([m[:, None] for m in masks], [m[None, :] for m in masks])
        turned_bias = attention_bias([m[None, :] for m in masks], [m[:, None] for m in masks])
        mixed_heads, exact, totals = attend(projected, gains, bias)
        full_out, full_down = gathered(out_low), gathered(down_low)
    attended = bfloat_product(mixed_heads, full_out)
    residual_one = embedded + gamma_one * attended
    normed_two = modulate(residual_one, scale_two, shift_two).astype(low)
    hidden_pre = bfloat_product(normed_two, full_up)
    hidden_act = jax.nn.gelu(hidden_pre, approximate=True).astype(low)
    branch = bfloat_product(hidden_act, full_down)
    residual_two = residual_one + gamma_two * branch
    final_normed = final_norm(residual_two, head_gain).astype(low)
    logits = bfloat_product(final_normed, full_head)
    logit_peak = jnp.max(logits, axis=-1, keepdims=True)
    log_total = logit_peak + jnp.log(jnp.sum(jnp.exp(logits - logit_peak), axis=-1, keepdims=True))
    target_hot = targets[:, None] == jnp.arange(CODES)[None, :]
    picked = jnp.sum(jnp.where(target_hot, logits, 0.0), axis=-1, keepdims=True)
    weight_column = loss_weight.astype(jnp.float32)[:, None]
    local_loss = jnp.sum(weight_column * (log_total - picked))
    logit_grad = (
        (jnp.exp(logits - log_total) - target_hot.astype(jnp.float32))
        * (weight_column / weight_total)
    ).astype(low)

    head_part = bfloat_product(final_normed.T, logit_grad).astype(part_kind)
    final_grad = bfloat_product(logit_grad, full_head.T)
    _, final_back = jax.vjp(final_norm, residual_two, head_gain)
    residual_grad, head_gain_grad = final_back(final_grad)
    branch_grad = (gamma_two * residual_grad).astype(low)

    def slot_sums(token_grad):
        other = jnp.sum(jnp.where(second, token_grad, 0.0), axis=0)
        first = jnp.sum(jnp.where(second, 0.0, token_grad), axis=0)
        return jnp.stack([first, other])

    gamma_two_grad = slot_sums(residual_grad * branch)
    if linked:
        mods = jnp.concatenate([modulation[:, 3 * D : 4 * D], modulation[:, :D], jnp.zeros((4, D), jnp.float32)])
        up_part, down_part, residual_grad, attended_grad, slot_rows, head_done = dense_back(
            branch_grad,
            normed_two,
            hidden_pre,
            full_down,
            full_up,
            residual_one,
            residual_grad,
            attended,
            token_columns,
            mods,
            head_part.reshape(FIVE + (depth, CODES)),
        )
        scale_two_grad, shift_two_grad, gamma_one_grad = slot_rows[0:2], slot_rows[2:4], slot_rows[4:6]
    else:
        down_part = bfloat_product(hidden_act.T, branch_grad).astype(part_kind)
        act_grad = bfloat_product(branch_grad, full_down.T)
        _, gelu_back = jax.vjp(partial(jax.nn.gelu, approximate=True), hidden_pre)
        pre_grad = gelu_back(act_grad)[0].astype(low)
        up_part = bfloat_product(normed_two.T, pre_grad).astype(part_kind)
        normed_two_grad = bfloat_product(pre_grad, full_up.T)
        _, modulate_two_back = jax.vjp(modulate, residual_one, scale_two, shift_two)
        norm_grad, scale_two_grad, shift_two_grad = modulate_two_back(normed_two_grad)
        scale_two_grad, shift_two_grad = slot_sums(scale_two_grad), slot_sums(shift_two_grad)
        residual_grad = residual_grad + norm_grad
        attended_grad = (gamma_one * residual_grad).astype(low)
        gamma_one_grad = slot_sums(residual_grad * attended)
    out_part = bfloat_product(mixed_heads.T, attended_grad).astype(part_kind)
    mixed_grad = bfloat_product(attended_grad, full_out.T).astype(low)
    if linked:
        heads_grad, gain_grads, attention_done = attend_back(
            projected,
            mixed_grad,
            exact,
            totals,
            gains,
            turned_bias,
            up_part.reshape(FIVE + (depth, up_part.shape[1])),
            down_part.reshape(FIVE + (down_part.shape[0] // D, depth, D)),
        )
    else:
        heads_grad, gain_grads = attend_back(projected, mixed_grad, exact, totals, gains, turned_bias)
        head_grad, up_grad, down_grad = scattered(head_part), scattered(up_part), scattered(down_part)
    if linked:
        unknown = jnp.zeros((2, D), jnp.float32)
        factored_rows = [tables_moment, ada_moment, qkv_moment, out_moment, up_moment, head_moment]
        row_moments = jnp.concatenate(factored_rows + [down_moment]).reshape(10, depth, 1)
        padding = jnp.zeros((110,), jnp.float32)
        column_moments = jnp.concatenate(
            [column_moment[:1042], padding, column_moment[1042:], jnp.zeros((128,), jnp.float32)]
        )[None]
        known = jnp.concatenate(
            [gamma_one_grad, gamma_two_grad, unknown, scale_two_grad, unknown, shift_two_grad], axis=1
        )
        gain_rows = jnp.concatenate([gain_grads[:2], head_gain_grad[None], jnp.zeros((5, D), jnp.float32)])
        last = last_exchange(
            (out_part.reshape(FIVE + (depth, D)), full_qkv, embedded, residual_grad),
            (
                heads_grad,
                normed,
                codes,
                second.astype(jnp.float32),
                modulation[:, 2 * D : 3 * D],
                known,
                gain_rows,
                activated,
                class_cond,
                label_hot,
                local_loss[None, None],
            ),
            (head_done, attention_done),
            masters,
            (row_moments, vector_moment, column_moments),
        )
        stepped = take_step(last, (head_done, attention_done), vector_moment, masters)
        rows_new, cols_new, facts = last[4].reshape(10 * depth), last[5][0], last[6][:, 0]
        stats = [rows_new[i * depth : (i + 1) * depth] for i in range(6)] + [rows_new[6 * depth :]]
        moment_of = (stats[0], stepped[16], stats[1], stats[2], stats[3], stats[4], stats[6], stats[5])
        results = [facts[2, 16], weight_total]
        for position in range(8):
            results += [stepped[2 * position], moment_of[position], stepped[2 * position + 1]]
        column_stat = jnp.concatenate([cols_new[:1042], cols_new[1152:SCALARS]])
        return tuple(results + [column_stat, facts[0, :8]])

    qkv_part = jnp.concatenate(
        [bfloat_product(normed.T, heads_grad[part]).astype(part_kind) for part in range(3)], axis=1
    )
    normed_grad = sum(
        bfloat_product(heads_grad[part], full_qkv[:, part * D : (part + 1) * D].T) for part in range(3)
    )
    _, modulate_one_back = jax.vjp(modulate, embedded, scale_one, shift_one)
    norm_grad, scale_one_grad, shift_one_grad = modulate_one_back(normed_grad)
    scale_one_grad, shift_one_grad = slot_sums(scale_one_grad), slot_sums(shift_one_grad)
    embedded_grad = residual_grad + norm_grad
    modulation_grad = jnp.concatenate(
        [
            gamma_one_grad,
            gamma_two_grad,
            scale_one_grad,
            scale_two_grad,
            shift_one_grad,
            shift_two_grad,
        ],
        axis=1,
    )
    bias_grad = jnp.sum(modulation_grad, axis=0).reshape(6, D)
    code_grad = split_product(embedded_grad.T, code_levels)
    small_part = jnp.concatenate(
        [
            bias_grad.T,
            gain_grads[:2].T,
            head_gain_grad[:, None],
            code_grad,
            jnp.zeros((D, 128 - CODE_DIM - LEVELS - 9), jnp.float32),
        ],
        axis=1,
    )
    modulation_low = modulation_grad.astype(low)
    modulation_all = gathered(modulation_low)
    small_grad, qkv_grad, out_grad = scattered(small_part), scattered(qkv_part), scattered(out_part)
    ada_grad = bfloat_product(activated.T, modulation_all)
    activated_grad = bfloat_product(modulation_all, ada_low.T)
    _, silu_back = jax.vjp(jax.nn.silu, class_cond)
    cond_grad = silu_back(activated_grad)[0]
    class_grad = jnp.dot(
        cond_grad.T,
        label_hot[:, :CLASSES].astype(jnp.float32),
        precision=lax.Precision.HIGHEST,
        preferred_element_type=jnp.float32,
    )
    tables_grad = jnp.concatenate([class_grad, small_grad[:, 9:SMALL_LANES]], axis=1)
    vectors_grad = small_grad[:, :9]
    gradients = (
        tables_grad,
        vectors_grad,
        ada_grad,
        qkv_grad,
        out_grad,
        up_grad,
        down_grad,
        head_grad,
    )
    second_decay = DECAY
    factored_index = (0, 2, 3, 4, 5, 6, 7)
    factored_moments = (
        tables_moment,
        ada_moment,
        qkv_moment,
        out_moment,
        up_moment,
        down_moment,
        head_moment,
    )
    local_squares = jnp.stack([jnp.sum(master * master) for master in masters])
    rows_list = []
    column_parts = []
    row_parts = []
    for position, moment in zip(factored_index, factored_moments):
        gradient = gradients[position]
        squared = gradient * gradient + TINY_SQUARE
        rows_new = second_decay * moment + (1.0 - second_decay) * jnp.mean(squared, axis=1)
        rows_list.append(rows_new)
        column_parts.append(jnp.sum(squared, axis=0))
        row_parts.append(jnp.sum(rows_new))
    column_count = column_moment.shape[0]
    sums = lax.psum(
        jnp.concatenate(column_parts + [jnp.stack(row_parts), local_squares, local_loss[None]]), AXES
    )
    column_total = sums[:column_count]
    row_total = sums[column_count : column_count + 7]
    weight_squares = sums[column_count + 7 : column_count + 15]
    loss_sum = sums[column_count + 15]
    updates = [None] * 8
    moments_new = [None] * 8
    column_new = []
    offset = 0
    for factor_slot, position in enumerate(factored_index):
        gradient = gradients[position]
        rows_all = gradient.shape[0] * devices
        column_count = gradient.shape[1]
        cols_new = second_decay * column_moment[offset : offset + column_count] + (
            1.0 - second_decay
        ) * (column_total[offset : offset + column_count] / rows_all)
        offset += column_count
        estimate = (
            rows_list[factor_slot][:, None]
            * cols_new[None, :]
            / (row_total[factor_slot] / rows_all)
        )
        updates[position] = gradient * lax.rsqrt(estimate)
        moments_new[position] = rows_list[factor_slot]
        column_new.append(cols_new)
    vector_new = second_decay * vector_moment + (1.0 - second_decay) * (
        gradients[1] * gradients[1] + TINY_SQUARE
    )
    updates[1] = gradients[1] * lax.rsqrt(vector_new)
    moments_new[1] = vector_new
    local_spread = jnp.stack([jnp.sum(update * update) for update in updates])
    spread_total = lax.psum(local_spread, AXES)
    next_weights = []
    spreads = []
    for position in range(8):
        count_all = gradients[position].size * devices
        spread = jnp.sqrt(spread_total[position] / count_all)
        step_scale = jnp.maximum(SCALE_FLOOR, jnp.sqrt(weight_squares[position] / count_all))
        next_weights.append(
            masters[position]
            - STEP_RATE * step_scale * (updates[position] / jnp.maximum(1.0, spread / CLIP_LIMIT))
        )
        spreads.append(spread)
    column_stat = jnp.concatenate(column_new)
    clip_spread = jnp.stack(spreads)
    results = [loss_sum, weight_total]
    for position in range(8):
        results += [gradients[position], moments_new[position], next_weights[position]]
    return tuple(results + [column_stat, clip_spread])


def solution(mesh):
    in_specs = (
        P(("fsdp", "sub"), None),
        P(("fsdp", "sub")),
        P(("fsdp", "sub")),
        P(("fsdp", "sub")),
        P(("fsdp", "sub")),
        P(("fsdp", "sub")),
        P(("fsdp", "sub")),
        P(("fsdp", "sub"), None),
        P(("fsdp", "sub"), None),
        P(("fsdp", "sub"), None),
        P(("fsdp", "sub"), None),
        P(("fsdp", "sub"), None),
        P(("fsdp", "sub"), None),
        P(("fsdp", "sub"), None),
        P(("fsdp", "sub"), None),
        P(("fsdp", "sub")),
        P(("fsdp", "sub")),
        P(("fsdp", "sub")),
        P(("fsdp", "sub")),
        P(("fsdp", "sub")),
        P(("fsdp", "sub")),
        P(("fsdp", "sub")),
        P(("fsdp", "sub"), None),
        P(),
    )
    out_specs = (
        P(),
        P(),
        P(("fsdp", "sub"), None),
        P(("fsdp", "sub")),
        P(("fsdp", "sub"), None),
        P(("fsdp", "sub"), None),
        P(("fsdp", "sub"), None),
        P(("fsdp", "sub"), None),
        P(("fsdp", "sub"), None),
        P(("fsdp", "sub")),
        P(("fsdp", "sub"), None),
        P(("fsdp", "sub"), None),
        P(("fsdp", "sub")),
        P(("fsdp", "sub"), None),
        P(("fsdp", "sub"), None),
        P(("fsdp", "sub")),
        P(("fsdp", "sub"), None),
        P(("fsdp", "sub"), None),
        P(("fsdp", "sub")),
        P(("fsdp", "sub"), None),
        P(("fsdp", "sub"), None),
        P(("fsdp", "sub")),
        P(("fsdp", "sub"), None),
        P(("fsdp", "sub"), None),
        P(("fsdp", "sub")),
        P(("fsdp", "sub"), None),
        P(),
        P(),
    )
    return jax.shard_map(
        on_device, mesh=mesh, in_specs=in_specs, out_specs=out_specs, check_vma=False
    )
```
